32 devices in a mesh: dp: 8 (over z, y), ctx: 4 (over x, core).
Axes of the slice: x: 2, y: 2, z: 4, core: 2. Of those that a mesh axis runs over, the one named last changes fastest.
Arguments:
- tokens: bfloat16 [8, 2048, 1024], P('dp', 'ctx'), may hold values from -6 to 6
- w_query: bfloat16 [1024, 2048], P(('dp', 'ctx')), may hold values from -0.1875 to 0.1875
- key_weight: bfloat16 [1024, 1024], P(('dp', 'ctx')), may hold values from -0.1875 to 0.1875
- value_weight: bfloat16 [1024, 1024], P(('dp', 'ctx')), may hold values from -0.1875 to 0.1875
- w_out: bfloat16 [2048, 1024], P(('dp', 'ctx')), may hold values from -1.5 to 1.5
- w_gate: bfloat16 [1024, 3072], P(('dp', 'ctx')), may hold values from -0.1875 to 0.1875
- w_up: bfloat16 [1024, 3072], P(('dp', 'ctx')), may hold values from -0.1875 to 0.1875
- w_down: bfloat16 [3072, 1024], P(('dp', 'ctx')), may hold values from -0.109375 to 0.109375
- gains: bfloat16 [2304], P(('dp', 'ctx')), may hold values from 0.25 to 1.75
- segment_ids: int32 [8, 2048], P('dp', 'ctx'), may hold values from 0 to 3, as said below
- positions: int32 [8, 2048], P('dp', 'ctx'), may hold values from 0 to 2047, as said below
- cotangent: bfloat16 [8, 2048, 1024], P('dp', 'ctx'), may hold values from -6 to 6
Outputs:
- output: bfloat16 [8, 2048, 1024], P('dp', 'ctx')
- grad_tokens: float32 [8, 2048, 1024], P('dp', 'ctx')
- grad_w_query: float32 [1024, 2048], P(('dp', 'ctx'))
- grad_w_key: float32 [1024, 1024], P(('dp', 'ctx'))
- grad_w_value: float32 [1024, 1024], P(('dp', 'ctx'))
- grad_w_out: float32 [2048, 1024], P(('dp', 'ctx'))
- grad_w_gate: float32 [1024, 3072], P(('dp', 'ctx'))
- grad_w_up: float32 [1024, 3072], P(('dp', 'ctx'))
- grad_w_down: float32 [3072, 1024], P(('dp', 'ctx'))
- grad_gains: float32 [2304], P(('dp', 'ctx'))
The draws below stay inside these ranges and needn't reach their ends.
Inputs may be any that keep to these rules, and one draw needn't show every extreme that they name: `segment_ids`: segment ids never fall along a sequence and start at 0. Document 0 holds 1 to 511 tokens, document 1 follows it and ends within the last 511 tokens, and one or two further documents (ids 2 and 3, or 3 alone) fill the rest. `positions`: positions rise by one from token to token inside a document; every document but document 0 starts at 0; document 0 continues an earlier document, and its last token has position 2047.
All inputs are finite; a program needn't handle non-finite values.
Results may differ from the reference program's by a relative error of at most 0.015.
Values may be sent and summed in bfloat16 or wider, within the bound.
No kernel may reach another device: no remote copies, remote signals or barrier semaphores. Data moves between devices by JAX's collectives and lax.ppermute only.
A program may use at most 256 MiB of HBM per device.

```python
import jax
import jax.numpy as jnp
from jax import lax

MODEL_WIDTH = 1024
QUERY_HEADS = 16
KEY_VALUE_HEADS = 8
HEAD_SIZE = 128
FF = 3072
SEQUENCE_TOKENS = 2048
TOK_DEV = 512
NSEQ = 8


def document_cuts(key):
    keys_split = jax.random.split(key, 3)
    leading = jax.random.randint(keys_split[0], (NSEQ, 1), 1, TOK_DEV, dtype=jnp.int32)
    trailing = jax.random.randint(keys_split[1], (NSEQ, 1), 1, TOK_DEV, dtype=jnp.int32)
    final_len = jax.random.randint(keys_split[2], (NSEQ, 1), 1, trailing + 1, dtype=jnp.int32)
    column = jnp.arange(SEQUENCE_TOKENS, dtype=jnp.int32)[None, :]
    segments = (column >= leading).astype(jnp.int32) + (column >= SEQUENCE_TOKENS - trailing).astype(jnp.int32) + (column >= SEQUENCE_TOKENS - final_len).astype(jnp.int32)
    begins = jnp.where(segments == 0, 0, jnp.where(segments == 1, leading, jnp.where(segments == 2, SEQUENCE_TOKENS - trailing, SEQUENCE_TOKENS - final_len)))
    token_positions = column - begins + jnp.where(segments == 0, SEQUENCE_TOKENS - leading, 0)
    return (segments.astype(jnp.int32), token_positions.astype(jnp.int32))


def draw_segment_ids(key, part):
    segments, token_positions = document_cuts(key)
    return segments


def draw_positions(key, part):
    segments, token_positions = document_cuts(key)
    return token_positions


def levels(own_key, extent, pieces, low, largest):
    def one(axis_at, blocks):
        heights = jax.random.uniform(jax.random.fold_in(jax.random.fold_in(own_key, 6), axis_at), (blocks,), jnp.float32, low / len(pieces), largest / len(pieces))
        return jnp.repeat(jnp.exp(heights), extent[axis_at] // blocks).reshape((-1,) + (1,) * (len(extent) - axis_at - 1))

    factor_of = one(*pieces[0])
    for cut in pieces[1:]:
        factor_of = factor_of * one(*cut)
    return factor_of


def scatter_about(stream_key, extent, scale, most, shards=(), kind=jnp.bfloat16):
    drawn = jax.random.normal(stream_key, extent, jnp.float32) * scale
    if len(shards) > 0:
        drawn = levels(stream_key, extent, shards, -0.22, 0.18) * drawn
    return jnp.clip(drawn, min=-most, max=most).astype(kind)


def setup_inputs(seed: int = 0) -> dict:
    key_of = jax.random.split(jax.random.key(seed), 13)
    return {
        "tokens": scatter_about(key_of[0], (NSEQ, SEQUENCE_TOKENS, MODEL_WIDTH), 1.0, 6.0, ((0, 8), (1, 4))),
        "w_query": scatter_about(key_of[1], (MODEL_WIDTH, QUERY_HEADS * HEAD_SIZE), MODEL_WIDTH ** -0.5, 0.1875, ((0, 32),)),
        "key_weight": scatter_about(key_of[2], (MODEL_WIDTH, KEY_VALUE_HEADS * HEAD_SIZE), MODEL_WIDTH ** -0.5, 0.1875, ((0, 32),)),
        "value_weight": scatter_about(key_of[3], (MODEL_WIDTH, KEY_VALUE_HEADS * HEAD_SIZE), MODEL_WIDTH ** -0.5, 0.1875, ((0, 32),)),
        "w_out": scatter_about(key_of[4], (QUERY_HEADS * HEAD_SIZE, MODEL_WIDTH), 16 ** -0.5, 1.5, ((0, 32),)),
        "w_gate": scatter_about(key_of[5], (MODEL_WIDTH, FF), MODEL_WIDTH ** -0.5, 0.1875, ((0, 32),)),
        "w_up": scatter_about(key_of[6], (MODEL_WIDTH, FF), MODEL_WIDTH ** -0.5, 0.1875, ((0, 32),)),
        "w_down": scatter_about(key_of[7], (FF, MODEL_WIDTH), FF ** -0.5, 0.109375, ((0, 32),)),
        "gains": jnp.clip(1.0 + 0.15 * jax.random.normal(key_of[8], (2 * MODEL_WIDTH + 2 * HEAD_SIZE,), jnp.float32), 0.25, 1.75).astype(jnp.bfloat16),
        "segment_ids": draw_segment_ids(jax.random.fold_in(key_of[12], 71), 0),
        "positions": draw_positions(jax.random.fold_in(key_of[12], 71), 0),
        "cotangent": scatter_about(key_of[11], (NSEQ, SEQUENCE_TOKENS, MODEL_WIDTH), 1.0, 6.0, ((0, 8), (1, 4))),
    }


EPSILON = 1e-06
THETA = 1000000.0

@jax.custom_vjp
def low(v):
    return lax.optimization_barrier(v.astype(jnp.bfloat16)).astype(jnp.float32)

@jax.custom_vjp
def low_back(v):
    return v

def low_keep(v):
    return (low(v), None)

def low_pass(kept, grad):
    return (grad,)

def back_keep(v):
    return (v, None)

def back_low(kept, grad):
    return (low(grad),)
low.defvjp(low_keep, low_pass)
low_back.defvjp(back_keep, back_low)

def row_norm_apply(value_rows, gain_vec):
    return value_rows * lax.rsqrt(lax.optimization_barrier(jnp.mean(value_rows * value_rows, axis=-1, keepdims=True)) + EPSILON) * gain_vec

def rotary_embed(value_rows, token_positions):
    half_size = value_rows.shape[-1] // 2
    inverse_rates = THETA ** (-2.0 * jnp.arange(half_size, dtype=jnp.float32) / value_rows.shape[-1])
    angles = token_positions.astype(jnp.float32)[:, None] * inverse_rates[None, :]
    cosine = jnp.cos(angles)[:, None, :]
    sine_part = jnp.sin(angles)[:, None, :]
    former = value_rows[..., :half_size]
    second = value_rows[..., half_size:]
    return jnp.concatenate([former * cosine - second * sine_part, second * cosine + former * sine_part], axis=-1)

def decoder_layer(inputs, w_query, key_weight, value_weight, w_out, w_gate, w_up, w_down, gains, segments, token_positions):
    highest_precision = lax.Precision.HIGHEST
    gain_attn = gains[:MODEL_WIDTH]
    gain_mlp = gains[MODEL_WIDTH:2 * MODEL_WIDTH]
    gain_query = gains[2 * MODEL_WIDTH:2 * MODEL_WIDTH + HEAD_SIZE]
    key_norm_gain = gains[2 * MODEL_WIDTH + HEAD_SIZE:]
    normalized_input = low(row_norm_apply(inputs, gain_attn))
    query_raw = low_back(jnp.dot(normalized_input, w_query, precision=highest_precision))
    unrotated_keys = low_back(jnp.dot(normalized_input, key_weight, precision=highest_precision))
    value_rows = low(low_back(jnp.dot(normalized_input, value_weight, precision=highest_precision))).reshape(SEQUENCE_TOKENS, KEY_VALUE_HEADS, HEAD_SIZE)
    query_rows = low(rotary_embed(row_norm_apply(query_raw.reshape(SEQUENCE_TOKENS, QUERY_HEADS, HEAD_SIZE), gain_query), token_positions))
    query_rows = query_rows.reshape(SEQUENCE_TOKENS, KEY_VALUE_HEADS, QUERY_HEADS // KEY_VALUE_HEADS, HEAD_SIZE)
    key_rows = low(rotary_embed(row_norm_apply(unrotated_keys.reshape(SEQUENCE_TOKENS, KEY_VALUE_HEADS, HEAD_SIZE), key_norm_gain), token_positions))
    block_rows = min(512, SEQUENCE_TOKENS)
    key_index = jnp.arange(SEQUENCE_TOKENS, dtype=jnp.int32)

    def attend(start_row):
        query_block = lax.dynamic_slice_in_dim(query_rows, start_row, block_rows, 0)
        segment_block = lax.dynamic_slice_in_dim(segments, start_row, block_rows, 0)
        query_index = start_row + jnp.arange(block_rows, dtype=jnp.int32)
        scores = jnp.einsum('lgrd,kgd->grlk', query_block, key_rows, precision=highest_precision) * HEAD_SIZE ** (-0.5)
        allowed = (segment_block[:, None] == segments[None, :]) & (query_index[:, None] >= key_index[None, :])
        scores = low_back(jnp.where(allowed[None, None], scores, -1e+30))
        prob_low = low(jax.nn.softmax(scores, axis=-1))
        return jnp.einsum('grlk,kgd->lgrd', prob_low, value_rows, precision=highest_precision)
    starts = jnp.arange(0, SEQUENCE_TOKENS, block_rows, dtype=jnp.int32)
    attended = lax.map(jax.checkpoint(attend), starts).reshape(SEQUENCE_TOKENS, QUERY_HEADS * HEAD_SIZE)
    attended = low(low_back(attended))
    middle = inputs + low_back(jnp.dot(attended, w_out, precision=highest_precision))
    normed_mlp = low(row_norm_apply(middle, gain_mlp))
    gate_value = low_back(jnp.dot(normed_mlp, w_gate, precision=highest_precision))
    up_value = low_back(jnp.dot(normed_mlp, w_up, precision=highest_precision))
    hidden = low(jax.nn.silu(gate_value) * up_value)
    return middle + jnp.dot(hidden, w_down, precision=highest_precision)

def reference(tokens, w_query, key_weight, value_weight, w_out, w_gate, w_up, w_down, gains, segment_ids, positions, cotangent):
    weights = tuple((weight_in.astype(jnp.float32) for weight_in in (w_query, key_weight, value_weight, w_out, w_gate, w_up, w_down, gains)))

    def one_sequence(totals, slices):
        inputs, segments, token_positions, cot_rows = slices

        def apply_layer(inputs_f, *params):
            return decoder_layer(inputs_f, *params, segments, token_positions)
        result, pull_back = jax.vjp(apply_layer, inputs.astype(jnp.float32), *weights)
        gradients = pull_back(cot_rows.astype(jnp.float32))
        totals = tuple((summed + adding for summed, adding in zip(totals, gradients[1:])))
        return (totals, (result.astype(jnp.bfloat16), gradients[0]))
    starts = tuple((jnp.zeros_like(weight_in) for weight_in in weights))
    totals, (outputs, grad_tokens) = lax.scan(one_sequence, starts, (tokens, segment_ids, positions, cotangent))
    return (outputs, grad_tokens, totals[0], totals[1], totals[2], totals[3], totals[4], totals[5], totals[6], totals[7])
```

```python
import functools

import jax
import jax.numpy as jnp
from jax import lax
from jax.experimental import pallas as pl
from jax.experimental.pallas import tpu as pltpu
from jax.sharding import PartitionSpec as P

MODEL_WIDTH = 1024
QUERY_HEADS = 16
KEY_VALUE_HEADS = 8
HEAD_SIZE = 128


EPSILON = 1e-06
THETA = 1000000.0


def row_norm_apply(value_rows, gain_vec):
    return (
        value_rows
        * lax.rsqrt(jnp.mean(value_rows * value_rows, axis=-1, keepdims=True) + EPSILON)
        * gain_vec
    )


def rotary_embed(value_rows, token_positions):
    half_size = value_rows.shape[-1] // 2
    inverse_rates = THETA ** (
        -2.0 * jnp.arange(half_size, dtype=jnp.float32) / value_rows.shape[-1]
    )
    angles = token_positions.astype(jnp.float32)[:, None] * inverse_rates[None, :]
    cosine = jnp.cos(angles)[:, None, :]
    sine_part = jnp.sin(angles)[:, None, :]
    former = value_rows[..., :half_size]
    second = value_rows[..., half_size:]
    return jnp.concatenate(
        [former * cosine - second * sine_part, second * cosine + former * sine_part], axis=-1
    )


def heads_per_group(raw_rows, gain_vec, token_positions, head_count):
    return rotary_embed(
        row_norm_apply(raw_rows.reshape(raw_rows.shape[0], head_count, HEAD_SIZE), gain_vec),
        token_positions,
    )


def split_gains(packed):
    packed = packed.astype(jnp.float32)
    return (
        packed[:MODEL_WIDTH],
        packed[MODEL_WIDTH : 2 * MODEL_WIDTH],
        packed[2 * MODEL_WIDTH : 2 * MODEL_WIDTH + HEAD_SIZE],
        packed[2 * MODEL_WIDTH + HEAD_SIZE :],
    )


def owner_major(grad_full, owners):
    return grad_full.reshape(owners, -1)


def local(
    tokens,
    w_query,
    key_weight,
    value_weight,
    w_out,
    w_gate,
    w_up,
    w_down,
    gains,
    segment_ids,
    positions,
    cotangent,
):
    sequence_count = tokens.shape[0]
    device_local_rows = tokens.shape[1]
    every_row_set = sequence_count * device_local_rows
    inputs = tokens.reshape(every_row_set, MODEL_WIDTH).astype(jnp.float32)
    token_positions = positions.reshape(every_row_set)
    cot_rows = cotangent.reshape(every_row_set, MODEL_WIDTH)
    head_groups = QUERY_HEADS // KEY_VALUE_HEADS
    score_scale = HEAD_SIZE ** (-0.5)
    f32 = jnp.float32
    brain_float_half = jnp.bfloat16
    owners = lax.axis_size(("dp", "ctx"))
    shard_shapes = (
        w_query.shape,
        key_weight.shape,
        value_weight.shape,
        w_out.shape,
        w_gate.shape,
        w_up.shape,
        w_down.shape,
        gains.shape,
    )
    gathered = (
        lax.all_gather(w_query, ("dp", "ctx"), axis=0, tiled=True),
        lax.all_gather(key_weight, ("dp", "ctx"), axis=0, tiled=True),
        lax.all_gather(value_weight, ("dp", "ctx"), axis=0, tiled=True),
        lax.all_gather(w_out, ("dp", "ctx"), axis=0, tiled=True),
        lax.all_gather(w_gate, ("dp", "ctx"), axis=0, tiled=True),
        lax.all_gather(w_up, ("dp", "ctx"), axis=0, tiled=True),
        lax.all_gather(w_down, ("dp", "ctx"), axis=0, tiled=True),
        lax.all_gather(gains, ("dp", "ctx"), axis=0, tiled=True),
    )
    full_query, full_key, full_value, full_out, full_gate, full_up, full_down, full_gains = gathered
    gain_attn, gain_mlp, gain_query, key_norm_gain = split_gains(full_gains)
    normalized_input = row_norm_apply(inputs, gain_attn).astype(brain_float_half)
    query_raw = jnp.dot(normalized_input, full_query, preferred_element_type=f32)
    unrotated_keys = jnp.dot(normalized_input, full_key, preferred_element_type=f32)
    value_low = (
        jnp.dot(normalized_input, full_value, preferred_element_type=f32)
        .astype(brain_float_half)
        .reshape(sequence_count, device_local_rows, KEY_VALUE_HEADS * HEAD_SIZE)
    )
    reduced_queries = heads_per_group(query_raw, gain_query, token_positions, QUERY_HEADS).astype(
        brain_float_half
    )
    key_low = (
        heads_per_group(unrotated_keys, key_norm_gain, token_positions, KEY_VALUE_HEADS)
        .astype(brain_float_half)
        .reshape(sequence_count, device_local_rows, KEY_VALUE_HEADS * HEAD_SIZE)
    )
    segment_low = segment_ids.astype(brain_float_half)
    gathered_keys, gathered_values, segment_all = (
        lax.all_gather(key_low, "ctx", axis=1, tiled=True),
        lax.all_gather(value_low, "ctx", axis=1, tiled=True),
        lax.all_gather(segment_low, "ctx", axis=1, tiled=True),
    )
    overall_rows = gathered_keys.shape[1]
    query_index = lax.axis_index("ctx") * device_local_rows + jnp.arange(
        device_local_rows, dtype=jnp.int32
    )
    key_index = jnp.arange(overall_rows, dtype=jnp.int32)
    allowed = (segment_low[:, :, None] == segment_all[:, None, :]) & (
        query_index[None, :, None] >= key_index[None, None, :]
    )
    grouped_queries = reduced_queries.reshape(
        sequence_count, device_local_rows, KEY_VALUE_HEADS, head_groups, HEAD_SIZE
    ).transpose(0, 2, 3, 1, 4)
    grouped_keys = gathered_keys.reshape(
        sequence_count, overall_rows, KEY_VALUE_HEADS, HEAD_SIZE
    ).transpose(0, 2, 1, 3)
    grouped_values = gathered_values.reshape(
        sequence_count, overall_rows, KEY_VALUE_HEADS, HEAD_SIZE
    ).transpose(0, 2, 1, 3)

    def masked_scores(query_head, key_head, mask_rows):
        scores = (
            jnp.einsum("rld,kd->rlk", query_head, key_head, preferred_element_type=f32)
            * score_scale
        )
        return jnp.where(mask_rows[None], scores, -1e30)

    def forward_sequence(slices):
        query_seq, key_seq, value_seq, mask_rows = slices

        def forward_head(head_slices):
            query_head, key_head, value_head = head_slices
            scores = masked_scores(query_head, key_head, mask_rows)
            row_peak = jnp.max(scores, axis=-1, keepdims=True)
            exp_scores = jnp.exp(scores - row_peak)
            denominator = jnp.sum(exp_scores, axis=-1, keepdims=True)
            prob_low = (exp_scores / denominator).astype(brain_float_half)
            mixed_head = jnp.einsum("rlk,kd->rld", prob_low, value_head, preferred_element_type=f32)
            return (mixed_head, row_peak[..., 0] + jnp.log(denominator[..., 0]))

        return lax.map(forward_head, (query_seq, key_seq, value_seq))

    mixed_heads, log_totals = lax.map(
        forward_sequence, (grouped_queries, grouped_keys, grouped_values, allowed)
    )
    attended = (
        mixed_heads.transpose(0, 3, 1, 2, 4)
        .reshape(every_row_set, QUERY_HEADS * HEAD_SIZE)
        .astype(brain_float_half)
    )
    middle = inputs + jnp.dot(attended, full_out, preferred_element_type=f32)
    normed_mlp = row_norm_apply(middle, gain_mlp).astype(brain_float_half)
    gate_value = jnp.dot(normed_mlp, full_gate, preferred_element_type=f32)
    up_value = jnp.dot(normed_mlp, full_up, preferred_element_type=f32)
    hidden = (jax.nn.silu(gate_value) * up_value).astype(brain_float_half)
    output = (middle + jnp.dot(hidden, full_down, preferred_element_type=f32)).astype(
        brain_float_half
    )
    regathered = (
        lax.all_gather(w_query, ("dp", "ctx"), axis=0, tiled=True),
        lax.all_gather(key_weight, ("dp", "ctx"), axis=0, tiled=True),
        lax.all_gather(value_weight, ("dp", "ctx"), axis=0, tiled=True),
        lax.all_gather(w_out, ("dp", "ctx"), axis=0, tiled=True),
        lax.all_gather(w_gate, ("dp", "ctx"), axis=0, tiled=True),
        lax.all_gather(w_up, ("dp", "ctx"), axis=0, tiled=True),
        lax.all_gather(w_down, ("dp", "ctx"), axis=0, tiled=True),
        lax.all_gather(gains, ("dp", "ctx"), axis=0, tiled=True),
    )
    back_query, back_key, back_value, back_out, back_gate, back_up, back_down, back_gains = (
        regathered
    )
    gain_attn, gain_mlp, gain_query, key_norm_gain = split_gains(back_gains)
    d_hidden = jnp.einsum("ld,fd->lf", cot_rows, back_down, preferred_element_type=f32)
    grad_down = jnp.einsum("lf,ld->fd", hidden, cot_rows, preferred_element_type=f32)
    unused, swiglu_pull = jax.vjp(
        lambda gate_in, up_in: jax.nn.silu(gate_in) * up_in, gate_value, up_value
    )
    d_gate, d_up = swiglu_pull(d_hidden)
    d_gate = d_gate.astype(brain_float_half)
    d_up = d_up.astype(brain_float_half)
    grad_gate = jnp.einsum("ld,lf->df", normed_mlp, d_gate, preferred_element_type=f32)
    grad_up = jnp.einsum("ld,lf->df", normed_mlp, d_up, preferred_element_type=f32)
    d_normed = jnp.einsum("lf,df->ld", d_gate, back_gate, preferred_element_type=f32)
    d_normed = d_normed + jnp.einsum("lf,df->ld", d_up, back_up, preferred_element_type=f32)
    unused, norm_pull = jax.vjp(row_norm_apply, middle, gain_mlp)
    d_middle, d_gain_mlp = norm_pull(d_normed)
    d_middle = d_middle + cot_rows.astype(f32)
    d_branch = d_middle.astype(brain_float_half)
    grad_out = jnp.einsum("lh,ld->hd", attended, d_branch, preferred_element_type=f32)
    attended_gradient = jnp.einsum(
        "ld,hd->lh", d_branch, back_out, preferred_element_type=f32
    ).astype(brain_float_half)
    group_gradient = attended_gradient.reshape(
        sequence_count, device_local_rows, KEY_VALUE_HEADS, head_groups, HEAD_SIZE
    ).transpose(0, 2, 3, 1, 4)

    def backward_sequence(slices):
        query_seq, key_seq, value_seq, d_seq, log_seq, mask_rows = slices

        def backward_head(head_slices):
            query_head, key_head, value_head, d_head, log_total = head_slices
            scores = masked_scores(query_head, key_head, mask_rows)
            probs_full = jnp.exp(scores - log_total[..., None])
            prob_low = probs_full.astype(brain_float_half)
            d_value = jnp.einsum("rlk,rld->kd", prob_low, d_head, preferred_element_type=f32)
            d_probs = jnp.einsum("rld,kd->rlk", d_head, value_head, preferred_element_type=f32)
            d_scores = probs_full * (
                d_probs - jnp.sum(probs_full * d_probs, axis=-1, keepdims=True)
            )
            d_scores = d_scores.astype(brain_float_half)
            d_query = (
                jnp.einsum("rlk,kd->rld", d_scores, key_head, preferred_element_type=f32)
                * score_scale
            )
            d_key = (
                jnp.einsum("rlk,rld->kd", d_scores, query_head, preferred_element_type=f32)
                * score_scale
            )
            return (d_query, d_key, d_value)

        return lax.map(backward_head, (query_seq, key_seq, value_seq, d_seq, log_seq))

    d_queries, key_rows_gradient, value_rows_gradient = lax.map(
        backward_sequence,
        (grouped_queries, grouped_keys, grouped_values, group_gradient, log_totals, allowed),
    )
    gathered_key_gradient = key_rows_gradient.transpose(2, 0, 1, 3).reshape(
        overall_rows, sequence_count, KEY_VALUE_HEADS * HEAD_SIZE
    )
    gathered_value_gradient = value_rows_gradient.transpose(2, 0, 1, 3).reshape(
        overall_rows, sequence_count, KEY_VALUE_HEADS * HEAD_SIZE
    )
    local_key_gradient, local_value_gradient = (
        lax.psum_scatter(
            gathered_key_gradient.astype(jnp.bfloat16), "ctx", scatter_dimension=0, tiled=True
        ).astype(jnp.float32),
        lax.psum_scatter(
            gathered_value_gradient.astype(jnp.bfloat16), "ctx", scatter_dimension=0, tiled=True
        ).astype(jnp.float32),
    )
    local_key_gradient = local_key_gradient.transpose(1, 0, 2)
    local_value_gradient = local_value_gradient.transpose(1, 0, 2)
    d_query_heads = d_queries.transpose(0, 3, 1, 2, 4).reshape(
        every_row_set, QUERY_HEADS, HEAD_SIZE
    )
    unused, query_pull = jax.vjp(
        lambda unnormalized_input, input_gain_vector: heads_per_group(
            unnormalized_input, input_gain_vector, token_positions, QUERY_HEADS
        ),
        query_raw,
        gain_query,
    )
    d_query_raw, d_gain_query = query_pull(d_query_heads)
    unused, key_pullback = jax.vjp(
        lambda unnormalized_input, input_gain_vector: heads_per_group(
            unnormalized_input, input_gain_vector, token_positions, KEY_VALUE_HEADS
        ),
        unrotated_keys,
        key_norm_gain,
    )
    unrotated_key_gradient, key_gain_gradient = key_pullback(
        local_key_gradient.reshape(every_row_set, KEY_VALUE_HEADS, HEAD_SIZE)
    )
    d_query_low = d_query_raw.astype(brain_float_half)
    d_key_low = unrotated_key_gradient.astype(brain_float_half)
    reduced_value_gradient = local_value_gradient.reshape(
        every_row_set, KEY_VALUE_HEADS * HEAD_SIZE
    ).astype(brain_float_half)
    grad_query = jnp.einsum("ld,lh->dh", normalized_input, d_query_low, preferred_element_type=f32)
    grad_key = jnp.einsum("ld,lh->dh", normalized_input, d_key_low, preferred_element_type=f32)
    grad_value = jnp.einsum(
        "ld,lh->dh", normalized_input, reduced_value_gradient, preferred_element_type=f32
    )
    d_normed_attn = jnp.einsum("lh,dh->ld", d_query_low, back_query, preferred_element_type=f32)
    d_normed_attn = d_normed_attn + jnp.einsum(
        "lh,dh->ld", d_key_low, back_key, preferred_element_type=f32
    )
    d_normed_attn = d_normed_attn + jnp.einsum(
        "lh,dh->ld", reduced_value_gradient, back_value, preferred_element_type=f32
    )
    unused, first_pull = jax.vjp(row_norm_apply, inputs, gain_attn)
    d_inputs, d_gain_attn = first_pull(d_normed_attn)
    grad_tokens = (d_middle + d_inputs).reshape(sequence_count, device_local_rows, MODEL_WIDTH)
    grad_gains = jnp.concatenate([d_gain_attn, d_gain_mlp, d_gain_query, key_gain_gradient])
    summed = (
        lax.psum_scatter(
            owner_major(grad_query, owners), ("dp", "ctx"), scatter_dimension=0, tiled=True
        ),
        lax.psum_scatter(
            owner_major(grad_key, owners), ("dp", "ctx"), scatter_dimension=0, tiled=True
        ),
        lax.psum_scatter(
            owner_major(grad_value, owners), ("dp", "ctx"), scatter_dimension=0, tiled=True
        ),
        lax.psum_scatter(
            owner_major(grad_out, owners), ("dp", "ctx"), scatter_dimension=0, tiled=True
        ),
        lax.psum_scatter(
            owner_major(grad_gate, owners), ("dp", "ctx"), scatter_dimension=0, tiled=True
        ),
        lax.psum_scatter(
            owner_major(grad_up, owners), ("dp", "ctx"), scatter_dimension=0, tiled=True
        ),
        lax.psum_scatter(
            owner_major(grad_down, owners), ("dp", "ctx"), scatter_dimension=0, tiled=True
        ),
        lax.psum_scatter(
            owner_major(grad_gains, owners), ("dp", "ctx"), scatter_dimension=0, tiled=True
        ),
    )
    grad_query = summed[0].reshape(shard_shapes[0])
    grad_key = summed[1].reshape(shard_shapes[1])
    grad_value = summed[2].reshape(shard_shapes[2])
    grad_out = summed[3].reshape(shard_shapes[3])
    grad_gate = summed[4].reshape(shard_shapes[4])
    grad_up = summed[5].reshape(shard_shapes[5])
    grad_down = summed[6].reshape(shard_shapes[6])
    grad_gains = summed[7].reshape(shard_shapes[7])
    return (
        output.reshape(sequence_count, device_local_rows, MODEL_WIDTH),
        grad_tokens,
        grad_query,
        grad_key,
        grad_value,
        grad_out,
        grad_gate,
        grad_up,
        grad_down,
        grad_gains,
    )

FEATURES = 128
MASK_DEPTH = -4096.0
LOG2_E = 1.4426950408889634
VMEM_BYTES = 56 * 1024 * 1024
bf16 = jnp.bfloat16
f32 = jnp.float32


def xor_permute(value, axis, offset):
    size = lax.axis_size(axis)
    return lax.ppermute(value, axis, [(i, i ^ offset) for i in range(size)])


def pick(stacked, index):
    return lax.dynamic_index_in_dim(stacked, index, 0, keepdims=False)


def exchange(stacked, me):
    size = stacked.shape[0]
    relative = [pick(stacked, me)]
    for offset in range(1, size):
        relative.append(xor_permute(pick(stacked, me ^ offset), "ctx", offset))
    relative = jnp.stack(relative)
    return jnp.stack([pick(relative, me ^ source) for source in range(size)])


def gather_blocks(value):
    across = xor_permute(value, "ctx", 2)
    beside = xor_permute(value, "ctx", 1)
    corner = xor_permute(across, "ctx", 1)
    return [value, beside, across, corner]


def scatter_sum(part):
    corner = xor_permute(part(3).astype(bf16), "ctx", 1)
    toward = part(2) + corner.astype(f32)
    across = xor_permute(toward.astype(bf16), "ctx", 2)
    beside = xor_permute(part(1).astype(bf16), "ctx", 1)
    return part(0) + beside.astype(f32) + across.astype(f32)


def nt_dot(left, right):
    return lax.dot_general(left, right, (((1,), (1,)), ((), ())), preferred_element_type=f32)


def nn_dot(left, right):
    return jnp.dot(left, right, preferred_element_type=f32)


def project_kernel(
    query_heads,
    key_heads,
    x_ref,
    gain_ref,
    weight_ref,
    cos_ref,
    sin_ref,
    gain_q_ref,
    gain_k_ref,
    normed_ref,
    raw_ref,
    q_ref,
    k_ref,
    v_ref,
):
    x = x_ref[...].astype(f32)
    scale = lax.rsqrt(jnp.mean(x * x, axis=-1, keepdims=True) + EPSILON)
    normed = (x * scale * gain_ref[...]).astype(bf16)
    normed_ref[...] = normed
    raw = nn_dot(normed, weight_ref[...])
    turned = (query_heads + key_heads) * HEAD_SIZE
    raw_ref[...] = raw[:, :turned]
    v_ref[...] = raw[:, turned:].astype(bf16)
    cosine = cos_ref[...]
    sine = sin_ref[...]
    for head in range(query_heads + key_heads):
        rows = raw[:, head * HEAD_SIZE : (head + 1) * HEAD_SIZE]
        gain = gain_q_ref[...] if head < query_heads else gain_k_ref[...]
        rows = rows * lax.rsqrt(jnp.mean(rows * rows, axis=-1, keepdims=True) + EPSILON) * gain
        rows = (rows * cosine + pltpu.roll(rows, HEAD_SIZE // 2, 1) * sine).astype(bf16)
        if head < query_heads:
            q_ref[:, head * HEAD_SIZE : (head + 1) * HEAD_SIZE] = rows
        else:
            at = (head - query_heads) * HEAD_SIZE
            k_ref[:, at : at + HEAD_SIZE] = rows


def project(x, gain, weight, cosine, sine, gain_q, gain_k, query_heads, key_heads):
    rows, width = x.shape
    block = 256
    turned = (query_heads + key_heads) * HEAD_SIZE
    columns = weight.shape[1]

    def tall(n):
        return pl.BlockSpec((block, n), lambda i: (i, 0))

    def whole(shape):
        return pl.BlockSpec(shape, lambda i: (0, 0))

    return pl.pallas_call(
        functools.partial(project_kernel, query_heads, key_heads),
        grid=(rows // block,),
        in_specs=[
            tall(width),
            whole((1, width)),
            whole(weight.shape),
            tall(HEAD_SIZE),
            tall(HEAD_SIZE),
            whole((1, HEAD_SIZE)),
            whole((1, HEAD_SIZE)),
        ],
        out_specs=[
            tall(width),
            tall(turned),
            tall(query_heads * HEAD_SIZE),
            tall(key_heads * HEAD_SIZE),
            tall(key_heads * HEAD_SIZE),
        ],
        out_shape=[
            jax.ShapeDtypeStruct((rows, width), bf16),
            jax.ShapeDtypeStruct((rows, turned), f32),
            jax.ShapeDtypeStruct((rows, query_heads * HEAD_SIZE), bf16),
            jax.ShapeDtypeStruct((rows, key_heads * HEAD_SIZE), bf16),
            jax.ShapeDtypeStruct((rows, key_heads * HEAD_SIZE), bf16),
        ],
        compiler_params=pltpu.CompilerParams(vmem_limit_bytes=VMEM_BYTES),
        cost_estimate=pl.CostEstimate(
            flops=2 * rows * width * columns,
            bytes_accessed=rows * (4 * width + 4 * turned + 2 * columns) + 2 * width * columns,
            transcendentals=0,
        ),
        name="project",
    )(x, gain, weight, cosine, sine, gain_q, gain_k)


def unproject_kernel(
    query_heads,
    key_heads,
    dq_ref,
    dk_ref,
    dv_ref,
    raw_ref,
    cos_ref,
    sin_ref,
    gain_q_ref,
    gain_k_ref,
    low_ref,
    dgain_ref,
):
    @pl.when(pl.program_id(0) == 0)
    def _():
        dgain_ref[...] = jnp.zeros_like(dgain_ref)

    cosine = cos_ref[...]
    sine = sin_ref[...]
    total_q = jnp.zeros((1, HEAD_SIZE), f32)
    total_k = jnp.zeros((1, HEAD_SIZE), f32)
    for head in range(query_heads + key_heads):
        at = head * HEAD_SIZE
        raw = raw_ref[:, at : at + HEAD_SIZE]
        if head < query_heads:
            grad = dq_ref[:, at : at + HEAD_SIZE]
            gain = gain_q_ref[...]
        else:
            back = (head - query_heads) * HEAD_SIZE
            grad = dk_ref[:, back : back + HEAD_SIZE]
            gain = gain_k_ref[...]
        grad = grad * cosine - pltpu.roll(grad, HEAD_SIZE // 2, 1) * sine
        scale = lax.rsqrt(jnp.mean(raw * raw, axis=-1, keepdims=True) + EPSILON)
        unit = raw * scale
        summed = jnp.sum(unit * grad, axis=0, keepdims=True)
        if head < query_heads:
            total_q += summed
        else:
            total_k += summed
        grad = grad * gain
        mean = jnp.mean(unit * grad, axis=-1, keepdims=True)
        low_ref[:, at : at + HEAD_SIZE] = (scale * (grad - unit * mean)).astype(bf16)
    low_ref[:, (query_heads + key_heads) * HEAD_SIZE :] = dv_ref[...].astype(bf16)
    dgain_ref[0:1, :] += total_q
    dgain_ref[1:2, :] += total_k


def unproject(dq, dk, dv, raw, cosine, sine, gain_q, gain_k, query_heads, key_heads):
    rows = dq.shape[0]
    block = 256
    columns = (query_heads + 2 * key_heads) * HEAD_SIZE

    def tall(n):
        return pl.BlockSpec((block, n), lambda i: (i, 0))

    def whole(shape):
        return pl.BlockSpec(shape, lambda i: (0, 0))

    return pl.pallas_call(
        functools.partial(unproject_kernel, query_heads, key_heads),
        grid=(rows // block,),
        in_specs=[
            tall(dq.shape[1]),
            tall(dk.shape[1]),
            tall(dv.shape[1]),
            tall(raw.shape[1]),
            tall(HEAD_SIZE),
            tall(HEAD_SIZE),
            whole((1, HEAD_SIZE)),
            whole((1, HEAD_SIZE)),
        ],
        out_specs=[tall(columns), whole((8, HEAD_SIZE))],
        out_shape=[
            jax.ShapeDtypeStruct((rows, columns), bf16),
            jax.ShapeDtypeStruct((8, HEAD_SIZE), f32),
        ],
        compiler_params=pltpu.CompilerParams(vmem_limit_bytes=VMEM_BYTES),
        cost_estimate=pl.CostEstimate(
            flops=20 * rows * columns, bytes_accessed=10 * rows * columns, transcendentals=0
        ),
        name="unproject",
    )(dq, dk, dv, raw, cosine, sine, gain_q, gain_k)


def attend_kernel(
    group, block, me_ref, q_ref, qf_ref, k_ref, kf_ref, v_ref, o_ref, log_ref, total_ref
):
    me = me_ref[0]
    at_query = pl.program_id(1)
    factor = HEAD_SIZE ** (-0.5) * LOG2_E
    query_features = qf_ref[...]
    ones = jnp.ones((block, HEAD_SIZE), bf16)
    total_ref[...] = jnp.zeros_like(total_ref)

    def step(at_key, diagonal):
        rows = pl.ds(pl.multiple_of((at_key ^ me) * block, block), block)
        keys = jnp.concatenate([k_ref[rows, :], kf_ref[rows, :]], axis=1)
        values = jnp.concatenate([v_ref[rows, :], ones], axis=1)
        for head in range(group):
            query = q_ref[:, head * HEAD_SIZE : (head + 1) * HEAD_SIZE]
            scores = nt_dot(jnp.concatenate([query, query_features], axis=1), keys)
            probs = jnp.exp2(scores * factor)
            if diagonal:
                down = lax.broadcasted_iota(jnp.int32, probs.shape, 0)
                right = lax.broadcasted_iota(jnp.int32, probs.shape, 1)
                probs = jnp.where(down >= right, probs, 0.0)
            total_ref[head] += nn_dot(probs.astype(bf16), values)

    @pl.loop(0, at_query)
    def _(at_key):
        step(at_key, False)

    step(at_query, True)
    for head in range(group):
        weighted = total_ref[head, :, :HEAD_SIZE]
        summed = total_ref[head, :, HEAD_SIZE:]
        o_ref[:, head * HEAD_SIZE : (head + 1) * HEAD_SIZE] = (weighted / summed).astype(bf16)
        log_ref[0, head : head + 1, :] = jnp.log2(summed.T[0:1, :])


def attend(me, q, qf, k, kf, v, block, group):
    rows = q.shape[0]
    key_heads = k.shape[1] // HEAD_SIZE
    blocks = rows // block
    pairs = key_heads * group * blocks * (blocks + 1) // 2 * block * block
    return pl.pallas_call(
        functools.partial(attend_kernel, group, block),
        grid_spec=pltpu.PrefetchScalarGridSpec(
            num_scalar_prefetch=1,
            grid=(key_heads, blocks),
            in_specs=[
                pl.BlockSpec((block, group * HEAD_SIZE), lambda g, i, me: (i ^ me[0], g)),
                pl.BlockSpec((block, FEATURES), lambda g, i, me: (i ^ me[0], 0)),
                pl.BlockSpec((rows, HEAD_SIZE), lambda g, i, me: (0, g)),
                pl.BlockSpec((rows, FEATURES), lambda g, i, me: (0, 0)),
                pl.BlockSpec((rows, HEAD_SIZE), lambda g, i, me: (0, g)),
            ],
            out_specs=[
                pl.BlockSpec((block, group * HEAD_SIZE), lambda g, i, me: (i ^ me[0], g)),
                pl.BlockSpec((1, group, block), lambda g, i, me: (g, 0, i ^ me[0])),
            ],
            scratch_shapes=[pltpu.VMEM((group, block, 2 * HEAD_SIZE), f32)],
        ),
        out_shape=[
            jax.ShapeDtypeStruct(q.shape, bf16),
            jax.ShapeDtypeStruct((key_heads, group, rows), f32),
        ],
        compiler_params=pltpu.CompilerParams(vmem_limit_bytes=VMEM_BYTES),
        cost_estimate=pl.CostEstimate(
            flops=8 * pairs * HEAD_SIZE, bytes_accessed=10 * q.size, transcendentals=pairs
        ),
        name="attend",
    )(me, q, qf, k, kf, v)


def unattend_kernel(
    group,
    block,
    me_ref,
    q_ref,
    qf_ref,
    k_ref,
    kf_ref,
    v_ref,
    o_ref,
    do_ref,
    log_ref,
    dq_ref,
    dk_ref,
    dv_ref,
    flipped_ref,
    total_ref,
):
    me = me_ref[0]
    at_query = pl.program_id(1)
    scale = HEAD_SIZE ** (-0.5)
    factor = scale * LOG2_E

    @pl.when(at_query == 0)
    def _():
        dk_ref[...] = jnp.zeros_like(dk_ref)
        dv_ref[...] = jnp.zeros_like(dv_ref)
        flipped_ref[...] = k_ref[...].astype(f32).T.astype(bf16)

    total_ref[...] = jnp.zeros_like(total_ref)
    query_features = qf_ref[...]
    deltas = []
    for head in range(group):
        lanes = slice(head * HEAD_SIZE, (head + 1) * HEAD_SIZE)
        product = do_ref[:, lanes].astype(f32) * o_ref[:, lanes].astype(f32)
        deltas.append(jnp.sum(product.T, axis=0, keepdims=True))

    def step(at_key, diagonal):
        start = pl.multiple_of((at_key ^ me) * block, block)
        rows = pl.ds(start, block)
        keys = jnp.concatenate([k_ref[rows, :], kf_ref[rows, :]], axis=1)
        values = v_ref[rows, :]
        for head in range(group):
            lanes = slice(head * HEAD_SIZE, (head + 1) * HEAD_SIZE)
            query = q_ref[:, lanes]
            d_out = do_ref[:, lanes]
            scores = nt_dot(keys, jnp.concatenate([query, query_features], axis=1))
            probs = jnp.exp2(scores * factor - log_ref[0, head : head + 1, :])
            if diagonal:
                key_at = lax.broadcasted_iota(jnp.int32, probs.shape, 0)
                query_at = lax.broadcasted_iota(jnp.int32, probs.shape, 1)
                probs = jnp.where(query_at >= key_at, probs, 0.0)
            d_scores = (probs * (nt_dot(values, d_out) - deltas[head])).astype(bf16)
            dv_ref[rows, :] += nn_dot(probs.astype(bf16), d_out)
            dk_ref[rows, :] += nn_dot(d_scores, query)
            total_ref[head] += nn_dot(flipped_ref[:, rows], d_scores)

    @pl.loop(0, at_query)
    def _(at_key):
        step(at_key, False)

    step(at_query, True)
    for head in range(group):
        dq_ref[:, head * HEAD_SIZE : (head + 1) * HEAD_SIZE] = total_ref[head].T * scale

    @pl.when(at_query == pl.num_programs(1) - 1)
    def _():
        dk_ref[...] = dk_ref[...] * scale


def unattend(me, q, qf, k, kf, v, o, d_out, logs, block, group):
    rows = q.shape[0]
    key_heads = k.shape[1] // HEAD_SIZE
    blocks = rows // block
    pairs = key_heads * group * blocks * (blocks + 1) // 2 * block * block

    def by_query(n):
        return pl.BlockSpec((block, n), lambda g, i, me: (i ^ me[0], g))

    by_key = pl.BlockSpec((rows, HEAD_SIZE), lambda g, i, me: (0, g))
    return pl.pallas_call(
        functools.partial(unattend_kernel, group, block),
        grid_spec=pltpu.PrefetchScalarGridSpec(
            num_scalar_prefetch=1,
            grid=(key_heads, blocks),
            in_specs=[
                by_query(group * HEAD_SIZE),
                pl.BlockSpec((block, FEATURES), lambda g, i, me: (i ^ me[0], 0)),
                by_key,
                pl.BlockSpec((rows, FEATURES), lambda g, i, me: (0, 0)),
                by_key,
                by_query(group * HEAD_SIZE),
                by_query(group * HEAD_SIZE),
                pl.BlockSpec((1, group, block), lambda g, i, me: (g, 0, i ^ me[0])),
            ],
            out_specs=[by_query(group * HEAD_SIZE), by_key, by_key],
            scratch_shapes=[
                pltpu.VMEM((HEAD_SIZE, rows), bf16),
                pltpu.VMEM((group, HEAD_SIZE, block), f32),
            ],
        ),
        out_shape=[
            jax.ShapeDtypeStruct(q.shape, f32),
            jax.ShapeDtypeStruct(k.shape, f32),
            jax.ShapeDtypeStruct(v.shape, f32),
        ],
        compiler_params=pltpu.CompilerParams(vmem_limit_bytes=VMEM_BYTES),
        cost_estimate=pl.CostEstimate(
            flops=14 * pairs * HEAD_SIZE, bytes_accessed=20 * q.size, transcendentals=pairs
        ),
        name="unattend",
    )(me, q, qf, k, kf, v, o, d_out, logs)


def norm_back(value_rows, gain_vec, grad):
    scale = lax.rsqrt(jnp.mean(value_rows * value_rows, axis=-1, keepdims=True) + EPSILON)
    unit = value_rows * scale
    d_gain = jnp.sum(unit * grad, axis=0)
    grad = grad * gain_vec
    return scale * (grad - unit * jnp.mean(unit * grad, axis=-1, keepdims=True)), d_gain


def split_local(
    tokens,
    w_query,
    key_weight,
    value_weight,
    w_out,
    w_gate,
    w_up,
    w_down,
    gains,
    segment_ids,
    positions,
    cotangent,
):
    size = lax.axis_size("ctx")
    copies = lax.axis_size("dp")
    me = lax.axis_index("ctx")
    me_row = me.reshape(1).astype(jnp.int32)
    block = tokens.shape[1]
    group = QUERY_HEADS // KEY_VALUE_HEADS
    query_heads = QUERY_HEADS // size
    key_heads = KEY_VALUE_HEADS // size
    q_cols = query_heads * HEAD_SIZE
    k_cols = key_heads * HEAD_SIZE
    owned = w_query.shape[0]
    hidden_cols = w_gate.shape[1] // size
    gain_count = gains.shape[0]
    pad_rows = 16
    forward_owner = [
        (b, (b % copies) * size + b // copies) for b in range(size * copies)
    ]
    backward_owner = [(target, source) for source, target in forward_owner]

    def by_columns(weight):
        return weight.reshape(weight.shape[0], size, -1).transpose(1, 0, 2)

    x_own = tokens.reshape(block, MODEL_WIDTH)
    x_blocks = gather_blocks(x_own)
    x_all = jnp.concatenate(x_blocks)
    places = jnp.concatenate([positions, segment_ids]).astype(jnp.int32)
    places = jnp.concatenate(gather_blocks(places), axis=1)

    first = jnp.concatenate(
        [by_columns(w_query), by_columns(key_weight), by_columns(value_weight)], axis=2
    )
    gain_rows = jnp.zeros((pad_rows, first.shape[2]), bf16).at[0, :gain_count].set(gains)
    first = jnp.concatenate(
        [first, jnp.broadcast_to(gain_rows[None], (size,) + gain_rows.shape)], axis=1
    )
    first = exchange(first, me)
    gain_rows = jnp.concatenate(
        [first[:, owned], jnp.zeros((pad_rows - size, first.shape[2]), bf16)]
    )
    first = jnp.concatenate(
        [first[:, :owned].reshape(size * owned, first.shape[2]), gain_rows]
    )
    first = lax.all_gather(first, "dp", axis=0, tiled=True)
    first = first.reshape(copies, size * owned + pad_rows, -1)
    w_first = first[:, : size * owned].reshape(MODEL_WIDTH, -1)
    full_gains = first[:, size * owned : size * owned + size, :gain_count].reshape(-1)
    gain_attn, gain_mlp, gain_query, gain_key = split_gains(full_gains)

    out_rows = lax.ppermute(w_out, ("dp", "ctx"), forward_owner)
    out_full = lax.all_gather(out_rows, "dp", axis=0, tiled=True)
    gate_up = jnp.concatenate([by_columns(w_gate), by_columns(w_up)], axis=2)
    gate_up = exchange(gate_up, me).reshape(size * owned, -1)
    gate_up = lax.all_gather(gate_up, "dp", axis=0, tiled=True)
    down_rows = lax.ppermute(w_down, ("dp", "ctx"), forward_owner)
    down_full = lax.all_gather(down_rows, "dp", axis=0, tiled=True)

    cot_own = cotangent.reshape(block, MODEL_WIDTH)
    cot_tied, unused = lax.optimization_barrier((cot_own, x_blocks[2]))
    cot_all = jnp.concatenate(gather_blocks(cot_tied))

    half = HEAD_SIZE // 2
    rates = THETA ** (-2.0 * jnp.arange(half, dtype=f32) / HEAD_SIZE)
    angles = places[0].astype(f32)[:, None] * rates[None, :]
    cosine, sine = jnp.cos(angles), jnp.sin(angles)
    cosine = jnp.concatenate([cosine, cosine], axis=1)
    sine = jnp.concatenate([-sine, sine], axis=1)
    lane = jnp.arange(FEATURES, dtype=jnp.int32)[None, :]
    same = places[1][:, None] == lane
    key_features = same.astype(bf16)
    query_features = jnp.where(same, 0.0, MASK_DEPTH).astype(bf16)
    gain_q_row, gain_k_row = gain_query[None], gain_key[None]
    normed, raw, q, k, v = project(
        x_all, gain_attn[None], w_first, cosine, sine, gain_q_row, gain_k_row, query_heads, key_heads
    )
    attended, logs = attend(me_row, q, query_features, k, key_features, v, block, group)

    def rows_of(value, r):
        return value[r * block : (r + 1) * block]

    branch = scatter_sum(lambda r: nn_dot(rows_of(attended, r), out_full))
    middle = x_own.astype(f32) + branch
    normed_mlp = jnp.concatenate(gather_blocks(row_norm_apply(middle, gain_mlp).astype(bf16)))
    both = nn_dot(normed_mlp, gate_up)
    gate_value, up_value = both[:, :hidden_cols], both[:, hidden_cols:]
    d_hidden = nt_dot(cot_all, down_full)
    sigmoid = 1.0 / (1.0 + jnp.exp(-gate_value))
    silu = gate_value * sigmoid
    hidden = (silu * up_value).astype(bf16)
    d_gate = (d_hidden * up_value * sigmoid * (1.0 + gate_value * (1.0 - sigmoid))).astype(bf16)
    d_up = (d_hidden * silu).astype(bf16)
    d_both = jnp.concatenate([d_gate, d_up], axis=1)

    d_normed = scatter_sum(lambda r: nt_dot(rows_of(d_both, r), gate_up))
    d_middle, d_gain_mlp = norm_back(middle, gain_mlp, d_normed)
    d_middle = d_middle + cot_own.astype(f32)
    d_branch = jnp.concatenate(gather_blocks(d_middle.astype(bf16)))
    d_attended = nt_dot(d_branch, out_full).astype(bf16)

    down = scatter_sum(lambda r: nn_dot(rows_of(hidden, r), down_full))
    output = (middle + down).astype(bf16)

    def tn_dot(left, right):
        return lax.dot_general(left, right, (((0,), (0,)), ((), ())), preferred_element_type=f32)

    def reduce_rows(grad):
        return lax.psum_scatter(grad.astype(bf16), "dp", scatter_dimension=0, tiled=True)

    grad_down = reduce_rows(tn_dot(hidden, cot_all))
    grad_both = reduce_rows(tn_dot(normed_mlp, d_both))
    grad_out = reduce_rows(tn_dot(attended, d_branch))

    dq, dk, dv = unattend(
        me_row, q, query_features, k, key_features, v, attended, d_attended, logs, block, group
    )
    low, d_gain_heads = unproject(
        dq, dk, dv, raw, cosine, sine, gain_q_row, gain_k_row, query_heads, key_heads
    )
    d_normed_attn = scatter_sum(lambda r: nt_dot(rows_of(low, r), w_first))
    d_inputs, d_gain_attn = norm_back(x_own.astype(f32), gain_attn, d_normed_attn)
    grad_tokens = (d_middle + d_inputs).reshape(tokens.shape)

    grad_first = tn_dot(normed, low).astype(bf16)
    grad_gains = jnp.concatenate(
        [d_gain_attn, d_gain_mlp, d_gain_heads[0], d_gain_heads[1]]
    ).reshape(copies, size, gain_count)
    gain_block = jnp.zeros((copies, pad_rows, grad_first.shape[1]), bf16)
    gain_block = gain_block.at[:, :size, :gain_count].set(grad_gains.astype(bf16))
    grad_first = jnp.concatenate(
        [grad_first.reshape(copies, size * owned, -1), gain_block], axis=1
    ).reshape(-1, grad_first.shape[1])
    grad_first = reduce_rows(grad_first)
    gain_part = grad_first[size * owned :][:size]
    gain_part = jnp.broadcast_to(gain_part[:, None], (size, pad_rows, gain_part.shape[1]))
    grad_first = jnp.concatenate(
        [grad_first[: size * owned].reshape(size, owned, -1), gain_part], axis=1
    )
    grad_first = exchange(grad_first, me).astype(f32)
    grad_gains = jnp.sum(grad_first[:, owned, :gain_count], axis=0)
    grad_first = grad_first[:, :owned]

    def to_rows(pieces):
        return pieces.transpose(1, 0, 2).reshape(owned, -1)

    grad_query = to_rows(grad_first[:, :, :q_cols])
    grad_key = to_rows(grad_first[:, :, q_cols : q_cols + k_cols])
    grad_value = to_rows(grad_first[:, :, q_cols + k_cols :])
    grad_both = exchange(grad_both.reshape(size, owned, -1), me).astype(f32)
    grad_gate = to_rows(grad_both[:, :, :hidden_cols])
    grad_up = to_rows(grad_both[:, :, hidden_cols:])
    grad_out = lax.ppermute(grad_out, ("dp", "ctx"), backward_owner).astype(f32)
    grad_down = lax.ppermute(grad_down, ("dp", "ctx"), backward_owner).astype(f32)
    return (
        output.reshape(tokens.shape),
        grad_tokens,
        grad_query,
        grad_key,
        grad_value,
        grad_out,
        grad_gate,
        grad_up,
        grad_down,
        grad_gains,
    )


def solution(mesh):
    small = mesh.shape["ctx"] == 4
    return jax.shard_map(
        split_local if small else local,
        mesh=mesh,
        in_specs=(
            P("dp", "ctx", None),
            P(("dp", "ctx"), None),
            P(("dp", "ctx"), None),
            P(("dp", "ctx"), None),
            P(("dp", "ctx"), None),
            P(("dp", "ctx"), None),
            P(("dp", "ctx"), None),
            P(("dp", "ctx"), None),
            P(("dp", "ctx")),
            P("dp", "ctx"),
            P("dp", "ctx"),
            P("dp", "ctx", None),
        ),
        out_specs=(
            P("dp", "ctx", None),
            P("dp", "ctx", None),
            P(("dp", "ctx"), None),
            P(("dp", "ctx"), None),
            P(("dp", "ctx"), None),
            P(("dp", "ctx"), None),
            P(("dp", "ctx"), None),
            P(("dp", "ctx"), None),
            P(("dp", "ctx"), None),
            P(("dp", "ctx")),
        ),
        check_vma=False,
    )
```

```python
import functools

import jax
import jax.numpy as jnp
from jax import lax
from jax.experimental import pallas as pl
from jax.experimental.pallas import tpu as pltpu
from jax.sharding import PartitionSpec as P

MODEL_WIDTH = 1024
QUERY_HEADS = 16
KEY_VALUE_HEADS = 8
HEAD_SIZE = 128


EPSILON = 1e-06
THETA = 1000000.0


def row_norm_apply(value_rows, gain_vec):
    return (
        value_rows
        * lax.rsqrt(jnp.mean(value_rows * value_rows, axis=-1, keepdims=True) + EPSILON)
        * gain_vec
    )


def rotary_embed(value_rows, token_positions):
    half_size = value_rows.shape[-1] // 2
    inverse_rates = THETA ** (
        -2.0 * jnp.arange(half_size, dtype=jnp.float32) / value_rows.shape[-1]
    )
    angles = token_positions.astype(jnp.float32)[:, None] * inverse_rates[None, :]
    cosine = jnp.cos(angles)[:, None, :]
    sine_part = jnp.sin(angles)[:, None, :]
    former = value_rows[..., :half_size]
    second = value_rows[..., half_size:]
    return jnp.concatenate(
        [former * cosine - second * sine_part, second * cosine + former * sine_part], axis=-1
    )


def heads_per_group(raw_rows, gain_vec, token_positions, head_count):
    return rotary_embed(
        row_norm_apply(raw_rows.reshape(raw_rows.shape[0], head_count, HEAD_SIZE), gain_vec),
        token_positions,
    )


def split_gains(packed):
    packed = packed.astype(jnp.float32)
    return (
        packed[:MODEL_WIDTH],
        packed[MODEL_WIDTH : 2 * MODEL_WIDTH],
        packed[2 * MODEL_WIDTH : 2 * MODEL_WIDTH + HEAD_SIZE],
        packed[2 * MODEL_WIDTH + HEAD_SIZE :],
    )


def owner_major(grad_full, owners):
    return grad_full.reshape(owners, -1)


def local(
    tokens,
    w_query,
    key_weight,
    value_weight,
    w_out,
    w_gate,
    w_up,
    w_down,
    gains,
    segment_ids,
    positions,
    cotangent,
):
    sequence_count = tokens.shape[0]
    device_local_rows = tokens.shape[1]
    every_row_set = sequence_count * device_local_rows
    inputs = tokens.reshape(every_row_set, MODEL_WIDTH).astype(jnp.float32)
    token_positions = positions.reshape(every_row_set)
    cot_rows = cotangent.reshape(every_row_set, MODEL_WIDTH)
    head_groups = QUERY_HEADS // KEY_VALUE_HEADS
    score_scale = HEAD_SIZE ** (-0.5)
    f32 = jnp.float32
    brain_float_half = jnp.bfloat16
    owners = lax.axis_size(("dp", "ctx"))
    shard_shapes = (
        w_query.shape,
        key_weight.shape,
        value_weight.shape,
        w_out.shape,
        w_gate.shape,
        w_up.shape,
        w_down.shape,
        gains.shape,
    )
    gathered = (
        lax.all_gather(w_query, ("dp", "ctx"), axis=0, tiled=True),
        lax.all_gather(key_weight, ("dp", "ctx"), axis=0, tiled=True),
        lax.all_gather(value_weight, ("dp", "ctx"), axis=0, tiled=True),
        lax.all_gather(w_out, ("dp", "ctx"), axis=0, tiled=True),
        lax.all_gather(w_gate, ("dp", "ctx"), axis=0, tiled=True),
        lax.all_gather(w_up, ("dp", "ctx"), axis=0, tiled=True),
        lax.all_gather(w_down, ("dp", "ctx"), axis=0, tiled=True),
        lax.all_gather(gains, ("dp", "ctx"), axis=0, tiled=True),
    )
    full_query, full_key, full_value, full_out, full_gate, full_up, full_down, full_gains = gathered
    gain_attn, gain_mlp, gain_query, key_norm_gain = split_gains(full_gains)
    normalized_input = row_norm_apply(inputs, gain_attn).astype(brain_float_half)
    query_raw = jnp.dot(normalized_input, full_query, preferred_element_type=f32)
    unrotated_keys = jnp.dot(normalized_input, full_key, preferred_element_type=f32)
    value_low = (
        jnp.dot(normalized_input, full_value, preferred_element_type=f32)
        .astype(brain_float_half)
        .reshape(sequence_count, device_local_rows, KEY_VALUE_HEADS * HEAD_SIZE)
    )
    reduced_queries = heads_per_group(query_raw, gain_query, token_positions, QUERY_HEADS).astype(
        brain_float_half
    )
    key_low = (
        heads_per_group(unrotated_keys, key_norm_gain, token_positions, KEY_VALUE_HEADS)
        .astype(brain_float_half)
        .reshape(sequence_count, device_local_rows, KEY_VALUE_HEADS * HEAD_SIZE)
    )
    segment_low = segment_ids.astype(brain_float_half)
    gathered_keys, gathered_values, segment_all = (
        lax.all_gather(key_low, "ctx", axis=1, tiled=True),
        lax.all_gather(value_low, "ctx", axis=1, tiled=True),
        lax.all_gather(segment_low, "ctx", axis=1, tiled=True),
    )
    overall_rows = gathered_keys.shape[1]
    query_index = lax.axis_index("ctx") * device_local_rows + jnp.arange(
        device_local_rows, dtype=jnp.int32
    )
    key_index = jnp.arange(overall_rows, dtype=jnp.int32)
    allowed = (segment_low[:, :, None] == segment_all[:, None, :]) & (
        query_index[None, :, None] >= key_index[None, None, :]
    )
    grouped_queries = reduced_queries.reshape(
        sequence_count, device_local_rows, KEY_VALUE_HEADS, head_groups, HEAD_SIZE
    ).transpose(0, 2, 3, 1, 4)
    grouped_keys = gathered_keys.reshape(
        sequence_count, overall_rows, KEY_VALUE_HEADS, HEAD_SIZE
    ).transpose(0, 2, 1, 3)
    grouped_values = gathered_values.reshape(
        sequence_count, overall_rows, KEY_VALUE_HEADS, HEAD_SIZE
    ).transpose(0, 2, 1, 3)

    def masked_scores(query_head, key_head, mask_rows):
        scores = (
            jnp.einsum("rld,kd->rlk", query_head, key_head, preferred_element_type=f32)
            * score_scale
        )
        return jnp.where(mask_rows[None], scores, -1e30)

    def forward_sequence(slices):
        query_seq, key_seq, value_seq, mask_rows = slices

        def forward_head(head_slices):
            query_head, key_head, value_head = head_slices
            scores = masked_scores(query_head, key_head, mask_rows)
            row_peak = jnp.max(scores, axis=-1, keepdims=True)
            exp_scores = jnp.exp(scores - row_peak)
            denominator = jnp.sum(exp_scores, axis=-1, keepdims=True)
            prob_low = (exp_scores / denominator).astype(brain_float_half)
            mixed_head = jnp.einsum("rlk,kd->rld", prob_low, value_head, preferred_element_type=f32)
            return (mixed_head, row_peak[..., 0] + jnp.log(denominator[..., 0]))

        return lax.map(forward_head, (query_seq, key_seq, value_seq))

    mixed_heads, log_totals = lax.map(
        forward_sequence, (grouped_queries, grouped_keys, grouped_values, allowed)
    )
    attended = (
        mixed_heads.transpose(0, 3, 1, 2, 4)
        .reshape(every_row_set, QUERY_HEADS * HEAD_SIZE)
        .astype(brain_float_half)
    )
    middle = inputs + jnp.dot(attended, full_out, preferred_element_type=f32)
    normed_mlp = row_norm_apply(middle, gain_mlp).astype(brain_float_half)
    gate_value = jnp.dot(normed_mlp, full_gate, preferred_element_type=f32)
    up_value = jnp.dot(normed_mlp, full_up, preferred_element_type=f32)
    hidden = (jax.nn.silu(gate_value) * up_value).astype(brain_float_half)
    output = (middle + jnp.dot(hidden, full_down, preferred_element_type=f32)).astype(
        brain_float_half
    )
    regathered = (
        lax.all_gather(w_query, ("dp", "ctx"), axis=0, tiled=True),
        lax.all_gather(key_weight, ("dp", "ctx"), axis=0, tiled=True),
        lax.all_gather(value_weight, ("dp", "ctx"), axis=0, tiled=True),
        lax.all_gather(w_out, ("dp", "ctx"), axis=0, tiled=True),
        lax.all_gather(w_gate, ("dp", "ctx"), axis=0, tiled=True),
        lax.all_gather(w_up, ("dp", "ctx"), axis=0, tiled=True),
        lax.all_gather(w_down, ("dp", "ctx"), axis=0, tiled=True),
        lax.all_gather(gains, ("dp", "ctx"), axis=0, tiled=True),
    )
    back_query, back_key, back_value, back_out, back_gate, back_up, back_down, back_gains = (
        regathered
    )
    gain_attn, gain_mlp, gain_query, key_norm_gain = split_gains(back_gains)
    d_hidden = jnp.einsum("ld,fd->lf", cot_rows, back_down, preferred_element_type=f32)
    grad_down = jnp.einsum("lf,ld->fd", hidden, cot_rows, preferred_element_type=f32)
    unused, swiglu_pull = jax.vjp(
        lambda gate_in, up_in: jax.nn.silu(gate_in) * up_in, gate_value, up_value
    )
    d_gate, d_up = swiglu_pull(d_hidden)
    d_gate = d_gate.astype(brain_float_half)
    d_up = d_up.astype(brain_float_half)
    grad_gate = jnp.einsum("ld,lf->df", normed_mlp, d_gate, preferred_element_type=f32)
    grad_up = jnp.einsum("ld,lf->df", normed_mlp, d_up, preferred_element_type=f32)
    d_normed = jnp.einsum("lf,df->ld", d_gate, back_gate, preferred_element_type=f32)
    d_normed = d_normed + jnp.einsum("lf,df->ld", d_up, back_up, preferred_element_type=f32)
    unused, norm_pull = jax.vjp(row_norm_apply, middle, gain_mlp)
    d_middle, d_gain_mlp = norm_pull(d_normed)
    d_middle = d_middle + cot_rows.astype(f32)
    d_branch = d_middle.astype(brain_float_half)
    grad_out = jnp.einsum("lh,ld->hd", attended, d_branch, preferred_element_type=f32)
    attended_gradient = jnp.einsum(
        "ld,hd->lh", d_branch, back_out, preferred_element_type=f32
    ).astype(brain_float_half)
    group_gradient = attended_gradient.reshape(
        sequence_count, device_local_rows, KEY_VALUE_HEADS, head_groups, HEAD_SIZE
    ).transpose(0, 2, 3, 1, 4)

    def backward_sequence(slices):
        query_seq, key_seq, value_seq, d_seq, log_seq, mask_rows = slices

        def backward_head(head_slices):
            query_head, key_head, value_head, d_head, log_total = head_slices
            scores = masked_scores(query_head, key_head, mask_rows)
            probs_full = jnp.exp(scores - log_total[..., None])
            prob_low = probs_full.astype(brain_float_half)
            d_value = jnp.einsum("rlk,rld->kd", prob_low, d_head, preferred_element_type=f32)
            d_probs = jnp.einsum("rld,kd->rlk", d_head, value_head, preferred_element_type=f32)
            d_scores = probs_full * (
                d_probs - jnp.sum(probs_full * d_probs, axis=-1, keepdims=True)
            )
            d_scores = d_scores.astype(brain_float_half)
            d_query = (
                jnp.einsum("rlk,kd->rld", d_scores, key_head, preferred_element_type=f32)
                * score_scale
            )
            d_key = (
                jnp.einsum("rlk,rld->kd", d_scores, query_head, preferred_element_type=f32)
                * score_scale
            )
            return (d_query, d_key, d_value)

        return lax.map(backward_head, (query_seq, key_seq, value_seq, d_seq, log_seq))

    d_queries, key_rows_gradient, value_rows_gradient = lax.map(
        backward_sequence,
        (grouped_queries, grouped_keys, grouped_values, group_gradient, log_totals, allowed),
    )
    gathered_key_gradient = key_rows_gradient.transpose(2, 0, 1, 3).reshape(
        overall_rows, sequence_count, KEY_VALUE_HEADS * HEAD_SIZE
    )
    gathered_value_gradient = value_rows_gradient.transpose(2, 0, 1, 3).reshape(
        overall_rows, sequence_count, KEY_VALUE_HEADS * HEAD_SIZE
    )
    local_key_gradient, local_value_gradient = (
        lax.psum_scatter(
            gathered_key_gradient.astype(jnp.bfloat16), "ctx", scatter_dimension=0, tiled=True
        ).astype(jnp.float32),
        lax.psum_scatter(
            gathered_value_gradient.astype(jnp.bfloat16), "ctx", scatter_dimension=0, tiled=True
        ).astype(jnp.float32),
    )
    local_key_gradient = local_key_gradient.transpose(1, 0, 2)
    local_value_gradient = local_value_gradient.transpose(1, 0, 2)
    d_query_heads = d_queries.transpose(0, 3, 1, 2, 4).reshape(
        every_row_set, QUERY_HEADS, HEAD_SIZE
    )
    unused, query_pull = jax.vjp(
        lambda unnormalized_input, input_gain_vector: heads_per_group(
            unnormalized_input, input_gain_vector, token_positions, QUERY_HEADS
        ),
        query_raw,
        gain_query,
    )
    d_query_raw, d_gain_query = query_pull(d_query_heads)
    unused, key_pullback = jax.vjp(
        lambda unnormalized_input, input_gain_vector: heads_per_group(
            unnormalized_input, input_gain_vector, token_positions, KEY_VALUE_HEADS
        ),
        unrotated_keys,
        key_norm_gain,
    )
    unrotated_key_gradient, key_gain_gradient = key_pullback(
        local_key_gradient.reshape(every_row_set, KEY_VALUE_HEADS, HEAD_SIZE)
    )
    d_query_low = d_query_raw.astype(brain_float_half)
    d_key_low = unrotated_key_gradient.astype(brain_float_half)
    reduced_value_gradient = local_value_gradient.reshape(
        every_row_set, KEY_VALUE_HEADS * HEAD_SIZE
    ).astype(brain_float_half)
    grad_query = jnp.einsum("ld,lh->dh", normalized_input, d_query_low, preferred_element_type=f32)
    grad_key = jnp.einsum("ld,lh->dh", normalized_input, d_key_low, preferred_element_type=f32)
    grad_value = jnp.einsum(
        "ld,lh->dh", normalized_input, reduced_value_gradient, preferred_element_type=f32
    )
    d_normed_attn = jnp.einsum("lh,dh->ld", d_query_low, back_query, preferred_element_type=f32)
    d_normed_attn = d_normed_attn + jnp.einsum(
        "lh,dh->ld", d_key_low, back_key, preferred_element_type=f32
    )
    d_normed_attn = d_normed_attn + jnp.einsum(
        "lh,dh->ld", reduced_value_gradient, back_value, preferred_element_type=f32
    )
    unused, first_pull = jax.vjp(row_norm_apply, inputs, gain_attn)
    d_inputs, d_gain_attn = first_pull(d_normed_attn)
    grad_tokens = (d_middle + d_inputs).reshape(sequence_count, device_local_rows, MODEL_WIDTH)
    grad_gains = jnp.concatenate([d_gain_attn, d_gain_mlp, d_gain_query, key_gain_gradient])
    summed = (
        lax.psum_scatter(
            owner_major(grad_query, owners), ("dp", "ctx"), scatter_dimension=0, tiled=True
        ),
        lax.psum_scatter(
            owner_major(grad_key, owners), ("dp", "ctx"), scatter_dimension=0, tiled=True
        ),
        lax.psum_scatter(
            owner_major(grad_value, owners), ("dp", "ctx"), scatter_dimension=0, tiled=True
        ),
        lax.psum_scatter(
            owner_major(grad_out, owners), ("dp", "ctx"), scatter_dimension=0, tiled=True
        ),
        lax.psum_scatter(
            owner_major(grad_gate, owners), ("dp", "ctx"), scatter_dimension=0, tiled=True
        ),
        lax.psum_scatter(
            owner_major(grad_up, owners), ("dp", "ctx"), scatter_dimension=0, tiled=True
        ),
        lax.psum_scatter(
            owner_major(grad_down, owners), ("dp", "ctx"), scatter_dimension=0, tiled=True
        ),
        lax.psum_scatter(
            owner_major(grad_gains, owners), ("dp", "ctx"), scatter_dimension=0, tiled=True
        ),
    )
    grad_query = summed[0].reshape(shard_shapes[0])
    grad_key = summed[1].reshape(shard_shapes[1])
    grad_value = summed[2].reshape(shard_shapes[2])
    grad_out = summed[3].reshape(shard_shapes[3])
    grad_gate = summed[4].reshape(shard_shapes[4])
    grad_up = summed[5].reshape(shard_shapes[5])
    grad_down = summed[6].reshape(shard_shapes[6])
    grad_gains = summed[7].reshape(shard_shapes[7])
    return (
        output.reshape(sequence_count, device_local_rows, MODEL_WIDTH),
        grad_tokens,
        grad_query,
        grad_key,
        grad_value,
        grad_out,
        grad_gate,
        grad_up,
        grad_down,
        grad_gains,
    )

FEATURES = 128
MASK_DEPTH = -4096.0
LOG2_E = 1.4426950408889634
VMEM_BYTES = 56 * 1024 * 1024
bf16 = jnp.bfloat16
f32 = jnp.float32


def xor_permute(value, axis, offset):
    size = lax.axis_size(axis)
    return lax.ppermute(value, axis, [(i, i ^ offset) for i in range(size)])


def pick(stacked, index):
    return lax.dynamic_index_in_dim(stacked, index, 0, keepdims=False)


def exchange(stacked, me):
    size = stacked.shape[0]
    relative = [pick(stacked, me)]
    for offset in range(1, size):
        relative.append(xor_permute(pick(stacked, me ^ offset), "ctx", offset))
    relative = jnp.stack(relative)
    return jnp.stack([pick(relative, me ^ source) for source in range(size)])


def shift_z(value, offset):
    size = lax.axis_size("dp")
    return lax.ppermute(value, "dp", [(i, (i + 2 * offset) % size) for i in range(size)])


def assemble_kernel(splits, count, places_ref, *refs):
    pieces, results, sems = refs[:count], refs[count:-1], refs[-1]
    copies = []
    for n, piece in enumerate(pieces):
        start = 0
        for m, rows in enumerate(splits):
            copy = pltpu.make_async_copy(
                piece.at[pl.ds(start, rows)], results[m].at[places_ref[n]], sems.at[n, m]
            )
            copy.start()
            copies.append(copy)
            start += rows
    for copy in copies:
        copy.wait()


def assemble(pieces, places, splits=None):
    count = len(pieces)
    rows, columns = pieces[0].shape
    splits = (rows,) if splits is None else splits
    anywhere = pl.BlockSpec(memory_space=pl.ANY)
    results = pl.pallas_call(
        functools.partial(assemble_kernel, splits, count),
        in_specs=[pl.BlockSpec(memory_space=pltpu.SMEM)] + [anywhere] * count,
        out_specs=[anywhere] * len(splits),
        out_shape=[jax.ShapeDtypeStruct((count, n, columns), pieces[0].dtype) for n in splits],
        scratch_shapes=[pltpu.SemaphoreType.DMA((count, len(splits)))],
        cost_estimate=pl.CostEstimate(
            flops=0, bytes_accessed=4 * count * rows * columns, transcendentals=0
        ),
        name="assemble",
    )(places.astype(jnp.int32), *pieces)
    return [result.reshape(-1, columns) for result in results]


def join(blocks):
    return assemble(blocks, jnp.arange(len(blocks)))[0]


def gather_copies(value):
    depth = lax.axis_size("dp") // 2
    at = lax.axis_index("dp")
    along = [value] + [shift_z(value, k) for k in range(1, depth)]
    beside = [xor_permute(piece, "dp", 1) for piece in along]
    rows = jnp.stack([(at // 2 - k) % depth for k in range(depth)])
    places = jnp.concatenate([rows * 2 + at % 2, rows * 2 + 1 - at % 2])
    return along + beside, places


def reduce_beside(grad):
    depth = grad.shape[0] // 2
    y = lax.axis_index("dp") % 2
    grad = grad.reshape((depth, 2) + grad.shape[1:])
    away = lax.dynamic_index_in_dim(grad, 1 - y, 1, keepdims=False)
    kept = lax.dynamic_index_in_dim(grad, y, 1, keepdims=False)
    return (kept.astype(f32) + xor_permute(away, "dp", 1).astype(f32)).astype(bf16)


def reduce_along(pair):
    depth = pair.shape[0]
    z = lax.axis_index("dp") // 2
    sent = [shift_z(pick(pair, (z + k) % depth), k) for k in range(1, depth)]
    return [pick(pair, z)] + sent


def add_all(terms):
    total = terms[0].astype(f32)
    for term in terms[1:]:
        total = total + term.astype(f32)
    return total.astype(bf16)


def after(value, *others):
    return lax.optimization_barrier((value, *others))[0]


def gather_blocks(value):
    across = xor_permute(value, "ctx", 2)
    beside = xor_permute(value, "ctx", 1)
    corner = xor_permute(across, "ctx", 1)
    return [value, beside, across, corner]


def scatter_sum(part, waits=()):
    corner = xor_permute(part(3).astype(bf16), "ctx", 1)
    toward = (part(2) + corner.astype(f32)).astype(bf16)
    if waits:
        toward = after(toward, *waits)
    across = xor_permute(toward, "ctx", 2)
    beside = xor_permute(part(1).astype(bf16), "ctx", 1)
    return part(0) + beside.astype(f32) + across.astype(f32), across


def nt_dot(left, right):
    return lax.dot_general(left, right, (((1,), (1,)), ((), ())), preferred_element_type=f32)


def nn_dot(left, right):
    return jnp.dot(left, right, preferred_element_type=f32)


def project_kernel(
    query_heads,
    key_heads,
    x_ref,
    gain_ref,
    weight_ref,
    cos_ref,
    sin_ref,
    gain_q_ref,
    gain_k_ref,
    normed_ref,
    raw_ref,
    q_ref,
    k_ref,
    v_ref,
):
    x = x_ref[...].astype(f32)
    scale = lax.rsqrt(jnp.mean(x * x, axis=-1, keepdims=True) + EPSILON)
    normed = (x * scale * gain_ref[...]).astype(bf16)
    normed_ref[...] = normed
    raw = nn_dot(normed, weight_ref[...])
    turned = (query_heads + key_heads) * HEAD_SIZE
    raw_ref[...] = raw[:, :turned]
    v_ref[...] = raw[:, turned:].astype(bf16)
    cosine = cos_ref[...]
    sine = sin_ref[...]
    for head in range(query_heads + key_heads):
        rows = raw[:, head * HEAD_SIZE : (head + 1) * HEAD_SIZE]
        gain = gain_q_ref[...] if head < query_heads else gain_k_ref[...]
        rows = rows * lax.rsqrt(jnp.mean(rows * rows, axis=-1, keepdims=True) + EPSILON) * gain
        rows = (rows * cosine + pltpu.roll(rows, HEAD_SIZE // 2, 1) * sine).astype(bf16)
        if head < query_heads:
            q_ref[:, head * HEAD_SIZE : (head + 1) * HEAD_SIZE] = rows
        else:
            at = (head - query_heads) * HEAD_SIZE
            k_ref[:, at : at + HEAD_SIZE] = rows


def project(x, gain, weight, cosine, sine, gain_q, gain_k, query_heads, key_heads):
    rows, width = x.shape
    block = 256
    turned = (query_heads + key_heads) * HEAD_SIZE
    columns = weight.shape[1]

    def tall(n):
        return pl.BlockSpec((block, n), lambda i: (i, 0))

    def whole(shape):
        return pl.BlockSpec(shape, lambda i: (0, 0))

    return pl.pallas_call(
        functools.partial(project_kernel, query_heads, key_heads),
        grid=(rows // block,),
        in_specs=[
            tall(width),
            whole((1, width)),
            whole(weight.shape),
            tall(HEAD_SIZE),
            tall(HEAD_SIZE),
            whole((1, HEAD_SIZE)),
            whole((1, HEAD_SIZE)),
        ],
        out_specs=[
            tall(width),
            tall(turned),
            tall(query_heads * HEAD_SIZE),
            tall(key_heads * HEAD_SIZE),
            tall(key_heads * HEAD_SIZE),
        ],
        out_shape=[
            jax.ShapeDtypeStruct((rows, width), bf16),
            jax.ShapeDtypeStruct((rows, turned), f32),
            jax.ShapeDtypeStruct((rows, query_heads * HEAD_SIZE), bf16),
            jax.ShapeDtypeStruct((rows, key_heads * HEAD_SIZE), bf16),
            jax.ShapeDtypeStruct((rows, key_heads * HEAD_SIZE), bf16),
        ],
        compiler_params=pltpu.CompilerParams(vmem_limit_bytes=VMEM_BYTES),
        cost_estimate=pl.CostEstimate(
            flops=2 * rows * width * columns,
            bytes_accessed=rows * (4 * width + 4 * turned + 2 * columns) + 2 * width * columns,
            transcendentals=0,
        ),
        name="project",
    )(x, gain, weight, cosine, sine, gain_q, gain_k)


def unproject_kernel(
    query_heads,
    key_heads,
    dq_ref,
    dk_ref,
    dv_ref,
    raw_ref,
    cos_ref,
    sin_ref,
    gain_q_ref,
    gain_k_ref,
    low_ref,
    dgain_ref,
):
    @pl.when(pl.program_id(0) == 0)
    def _():
        dgain_ref[...] = jnp.zeros_like(dgain_ref)

    cosine = cos_ref[...]
    sine = sin_ref[...]
    total_q = jnp.zeros((1, HEAD_SIZE), f32)
    total_k = jnp.zeros((1, HEAD_SIZE), f32)
    for head in range(query_heads + key_heads):
        at = head * HEAD_SIZE
        raw = raw_ref[:, at : at + HEAD_SIZE]
        if head < query_heads:
            grad = dq_ref[:, at : at + HEAD_SIZE]
            gain = gain_q_ref[...]
        else:
            back = (head - query_heads) * HEAD_SIZE
            grad = dk_ref[:, back : back + HEAD_SIZE]
            gain = gain_k_ref[...]
        grad = grad * cosine - pltpu.roll(grad, HEAD_SIZE // 2, 1) * sine
        scale = lax.rsqrt(jnp.mean(raw * raw, axis=-1, keepdims=True) + EPSILON)
        unit = raw * scale
        summed = jnp.sum(unit * grad, axis=0, keepdims=True)
        if head < query_heads:
            total_q += summed
        else:
            total_k += summed
        grad = grad * gain
        mean = jnp.mean(unit * grad, axis=-1, keepdims=True)
        low_ref[:, at : at + HEAD_SIZE] = (scale * (grad - unit * mean)).astype(bf16)
    low_ref[:, (query_heads + key_heads) * HEAD_SIZE :] = dv_ref[...].astype(bf16)
    dgain_ref[0:1, :] += total_q
    dgain_ref[1:2, :] += total_k


def unproject(dq, dk, dv, raw, cosine, sine, gain_q, gain_k, query_heads, key_heads):
    rows = dq.shape[0]
    block = 256
    columns = (query_heads + 2 * key_heads) * HEAD_SIZE

    def tall(n):
        return pl.BlockSpec((block, n), lambda i: (i, 0))

    def whole(shape):
        return pl.BlockSpec(shape, lambda i: (0, 0))

    return pl.pallas_call(
        functools.partial(unproject_kernel, query_heads, key_heads),
        grid=(rows // block,),
        in_specs=[
            tall(dq.shape[1]),
            tall(dk.shape[1]),
            tall(dv.shape[1]),
            tall(raw.shape[1]),
            tall(HEAD_SIZE),
            tall(HEAD_SIZE),
            whole((1, HEAD_SIZE)),
            whole((1, HEAD_SIZE)),
        ],
        out_specs=[tall(columns), whole((8, HEAD_SIZE))],
        out_shape=[
            jax.ShapeDtypeStruct((rows, columns), bf16),
            jax.ShapeDtypeStruct((8, HEAD_SIZE), f32),
        ],
        compiler_params=pltpu.CompilerParams(vmem_limit_bytes=VMEM_BYTES),
        cost_estimate=pl.CostEstimate(
            flops=20 * rows * columns, bytes_accessed=10 * rows * columns, transcendentals=0
        ),
        name="unproject",
    )(dq, dk, dv, raw, cosine, sine, gain_q, gain_k)


def attend_kernel(
    group, block, me_ref, q_ref, qf_ref, k_ref, kf_ref, v_ref, o_ref, log_ref, total_ref
):
    me = me_ref[0]
    at_query = pl.program_id(1)
    factor = HEAD_SIZE ** (-0.5) * LOG2_E
    query_features = qf_ref[...]
    ones = jnp.ones((block, HEAD_SIZE), bf16)
    total_ref[...] = jnp.zeros_like(total_ref)

    def step(at_key, diagonal):
        rows = pl.ds(pl.multiple_of((at_key ^ me) * block, block), block)
        keys = jnp.concatenate([k_ref[rows, :], kf_ref[rows, :]], axis=1)
        values = jnp.concatenate([v_ref[rows, :], ones], axis=1)
        for head in range(group):
            query = q_ref[:, head * HEAD_SIZE : (head + 1) * HEAD_SIZE]
            scores = nt_dot(jnp.concatenate([query, query_features], axis=1), keys)
            probs = jnp.exp2(scores * factor)
            if diagonal:
                down = lax.broadcasted_iota(jnp.int32, probs.shape, 0)
                right = lax.broadcasted_iota(jnp.int32, probs.shape, 1)
                probs = jnp.where(down >= right, probs, 0.0)
            total_ref[head] += nn_dot(probs.astype(bf16), values)

    @pl.loop(0, at_query)
    def _(at_key):
        step(at_key, False)

    step(at_query, True)
    for head in range(group):
        weighted = total_ref[head, :, :HEAD_SIZE]
        summed = total_ref[head, :, HEAD_SIZE:]
        o_ref[:, head * HEAD_SIZE : (head + 1) * HEAD_SIZE] = (weighted / summed).astype(bf16)
        log_ref[0, head : head + 1, :] = jnp.log2(summed.T[0:1, :])


def attend(me, q, qf, k, kf, v, block, group):
    rows = q.shape[0]
    key_heads = k.shape[1] // HEAD_SIZE
    blocks = rows // block
    pairs = key_heads * group * blocks * (blocks + 1) // 2 * block * block
    return pl.pallas_call(
        functools.partial(attend_kernel, group, block),
        grid_spec=pltpu.PrefetchScalarGridSpec(
            num_scalar_prefetch=1,
            grid=(key_heads, blocks),
            in_specs=[
                pl.BlockSpec((block, group * HEAD_SIZE), lambda g, i, me: (i ^ me[0], g)),
                pl.BlockSpec((block, FEATURES), lambda g, i, me: (i ^ me[0], 0)),
                pl.BlockSpec((rows, HEAD_SIZE), lambda g, i, me: (0, g)),
                pl.BlockSpec((rows, FEATURES), lambda g, i, me: (0, 0)),
                pl.BlockSpec((rows, HEAD_SIZE), lambda g, i, me: (0, g)),
            ],
            out_specs=[
                pl.BlockSpec((block, group * HEAD_SIZE), lambda g, i, me: (i ^ me[0], g)),
                pl.BlockSpec((1, group, block), lambda g, i, me: (g, 0, i ^ me[0])),
            ],
            scratch_shapes=[pltpu.VMEM((group, block, 2 * HEAD_SIZE), f32)],
        ),
        out_shape=[
            jax.ShapeDtypeStruct(q.shape, bf16),
            jax.ShapeDtypeStruct((key_heads, group, rows), f32),
        ],
        compiler_params=pltpu.CompilerParams(vmem_limit_bytes=VMEM_BYTES),
        cost_estimate=pl.CostEstimate(
            flops=8 * pairs * HEAD_SIZE, bytes_accessed=10 * q.size, transcendentals=pairs
        ),
        name="attend",
    )(me, q, qf, k, kf, v)


def unattend_kernel(
    group,
    block,
    me_ref,
    q_ref,
    qf_ref,
    k_ref,
    kf_ref,
    v_ref,
    o_ref,
    do_ref,
    log_ref,
    dq_ref,
    dk_ref,
    dv_ref,
    flipped_ref,
    total_ref,
):
    me = me_ref[0]
    at_query = pl.program_id(1)
    scale = HEAD_SIZE ** (-0.5)
    factor = scale * LOG2_E

    @pl.when(at_query == 0)
    def _():
        dk_ref[...] = jnp.zeros_like(dk_ref)
        dv_ref[...] = jnp.zeros_like(dv_ref)
        flipped_ref[...] = k_ref[...].astype(f32).T.astype(bf16)

    total_ref[...] = jnp.zeros_like(total_ref)
    query_features = qf_ref[...]
    deltas = []
    for head in range(group):
        lanes = slice(head * HEAD_SIZE, (head + 1) * HEAD_SIZE)
        product = do_ref[:, lanes].astype(f32) * o_ref[:, lanes].astype(f32)
        deltas.append(jnp.sum(product.T, axis=0, keepdims=True))

    def step(at_key, diagonal):
        start = pl.multiple_of((at_key ^ me) * block, block)
        rows = pl.ds(start, block)
        keys = jnp.concatenate([k_ref[rows, :], kf_ref[rows, :]], axis=1)
        values = v_ref[rows, :]
        for head in range(group):
            lanes = slice(head * HEAD_SIZE, (head + 1) * HEAD_SIZE)
            query = q_ref[:, lanes]
            d_out = do_ref[:, lanes]
            scores = nt_dot(keys, jnp.concatenate([query, query_features], axis=1))
            probs = jnp.exp2(scores * factor - log_ref[0, head : head + 1, :])
            if diagonal:
                key_at = lax.broadcasted_iota(jnp.int32, probs.shape, 0)
                query_at = lax.broadcasted_iota(jnp.int32, probs.shape, 1)
                probs = jnp.where(query_at >= key_at, probs, 0.0)
            d_scores = (probs * (nt_dot(values, d_out) - deltas[head])).astype(bf16)
            dv_ref[rows, :] += nn_dot(probs.astype(bf16), d_out)
            dk_ref[rows, :] += nn_dot(d_scores, query)
            total_ref[head] += nn_dot(flipped_ref[:, rows], d_scores)

    @pl.loop(0, at_query)
    def _(at_key):
        step(at_key, False)

    step(at_query, True)
    for head in range(group):
        dq_ref[:, head * HEAD_SIZE : (head + 1) * HEAD_SIZE] = total_ref[head].T * scale

    @pl.when(at_query == pl.num_programs(1) - 1)
    def _():
        dk_ref[...] = dk_ref[...] * scale


def unattend(me, q, qf, k, kf, v, o, d_out, logs, block, group):
    rows = q.shape[0]
    key_heads = k.shape[1] // HEAD_SIZE
    blocks = rows // block
    pairs = key_heads * group * blocks * (blocks + 1) // 2 * block * block

    def by_query(n):
        return pl.BlockSpec((block, n), lambda g, i, me: (i ^ me[0], g))

    by_key = pl.BlockSpec((rows, HEAD_SIZE), lambda g, i, me: (0, g))
    return pl.pallas_call(
        functools.partial(unattend_kernel, group, block),
        grid_spec=pltpu.PrefetchScalarGridSpec(
            num_scalar_prefetch=1,
            grid=(key_heads, blocks),
            in_specs=[
                by_query(group * HEAD_SIZE),
                pl.BlockSpec((block, FEATURES), lambda g, i, me: (i ^ me[0], 0)),
                by_key,
                pl.BlockSpec((rows, FEATURES), lambda g, i, me: (0, 0)),
                by_key,
                by_query(group * HEAD_SIZE),
                by_query(group * HEAD_SIZE),
                pl.BlockSpec((1, group, block), lambda g, i, me: (g, 0, i ^ me[0])),
            ],
            out_specs=[by_query(group * HEAD_SIZE), by_key, by_key],
            scratch_shapes=[
                pltpu.VMEM((HEAD_SIZE, rows), bf16),
                pltpu.VMEM((group, HEAD_SIZE, block), f32),
            ],
        ),
        out_shape=[
            jax.ShapeDtypeStruct(q.shape, f32),
            jax.ShapeDtypeStruct(k.shape, f32),
            jax.ShapeDtypeStruct(v.shape, f32),
        ],
        compiler_params=pltpu.CompilerParams(vmem_limit_bytes=VMEM_BYTES),
        cost_estimate=pl.CostEstimate(
            flops=14 * pairs * HEAD_SIZE, bytes_accessed=20 * q.size, transcendentals=pairs
        ),
        name="unattend",
    )(me, q, qf, k, kf, v, o, d_out, logs)


def norm_back(value_rows, gain_vec, grad):
    scale = lax.rsqrt(jnp.mean(value_rows * value_rows, axis=-1, keepdims=True) + EPSILON)
    unit = value_rows * scale
    d_gain = jnp.sum(unit * grad, axis=0)
    grad = grad * gain_vec
    return scale * (grad - unit * jnp.mean(unit * grad, axis=-1, keepdims=True)), d_gain


def split_local(
    tokens,
    w_query,
    key_weight,
    value_weight,
    w_out,
    w_gate,
    w_up,
    w_down,
    gains,
    segment_ids,
    positions,
    cotangent,
):
    size = lax.axis_size("ctx")
    copies = lax.axis_size("dp")
    me = lax.axis_index("ctx")
    me_row = me.reshape(1).astype(jnp.int32)
    block = tokens.shape[1]
    group = QUERY_HEADS // KEY_VALUE_HEADS
    query_heads = QUERY_HEADS // size
    key_heads = KEY_VALUE_HEADS // size
    q_cols = query_heads * HEAD_SIZE
    k_cols = key_heads * HEAD_SIZE
    owned = w_query.shape[0]
    hidden_cols = w_gate.shape[1] // size
    gain_count = gains.shape[0]
    pad_rows = 16
    forward_owner = [
        (b, (b % copies) * size + b // copies) for b in range(size * copies)
    ]
    backward_owner = [(target, source) for source, target in forward_owner]

    def by_columns(weight):
        return weight.reshape(weight.shape[0], size, -1).transpose(1, 0, 2)

    x_own = tokens.reshape(block, MODEL_WIDTH)
    x_blocks = gather_blocks(x_own)
    x_all = join(x_blocks)
    places = jnp.concatenate([positions, segment_ids]).astype(jnp.int32)
    places = jnp.concatenate(gather_blocks(places), axis=1)

    first = jnp.concatenate(
        [by_columns(w_query), by_columns(key_weight), by_columns(value_weight)], axis=2
    )
    gain_rows = jnp.pad(gains[None], ((0, pad_rows - 1), (0, first.shape[2] - gain_count)))
    first = jnp.concatenate(
        [first, jnp.broadcast_to(gain_rows[None], (size,) + gain_rows.shape)], axis=1
    )
    first = exchange(first, me)
    gain_rows = jnp.concatenate(
        [first[:, owned], jnp.zeros((pad_rows - size, first.shape[2]), bf16)]
    )
    first = jnp.concatenate(
        [first[:, :owned].reshape(size * owned, first.shape[2]), gain_rows]
    )
    first_pieces, places_dp = gather_copies(first)
    cot_own = cotangent.reshape(block, MODEL_WIDTH)
    cot_blocks = gather_blocks(after(cot_own, x_blocks[2]))
    w_first, gain_rows = assemble(first_pieces, places_dp, (size * owned, pad_rows))
    w_first = after(w_first, *cot_blocks)
    full_gains = gain_rows.reshape(copies, pad_rows, -1)[:, :size, :gain_count].reshape(-1)
    gain_attn, gain_mlp, gain_query, gain_key = split_gains(full_gains)

    early = first_pieces[1:copies // 2]
    out_rows = lax.ppermute(w_out, ("dp", "ctx"), forward_owner)
    out_pieces, unused = gather_copies(after(out_rows, *early))
    out_full = assemble(out_pieces, places_dp)[0]
    gate_up = jnp.concatenate([by_columns(w_gate), by_columns(w_up)], axis=2)
    gate_up = exchange(gate_up, me).reshape(size * owned, -1)
    gate_up_pieces, unused = gather_copies(after(gate_up, *early))
    gate_up = assemble(gate_up_pieces, places_dp)[0]
    down_rows = lax.ppermute(w_down, ("dp", "ctx"), forward_owner)
    down_pieces, unused = gather_copies(after(down_rows, *early))
    down_full = assemble(down_pieces, places_dp)[0]
    cot_all = join(cot_blocks)

    half = HEAD_SIZE // 2
    rates = THETA ** (-2.0 * jnp.arange(half, dtype=f32) / HEAD_SIZE)
    angles = places[0].astype(f32)[:, None] * rates[None, :]
    cosine, sine = jnp.cos(angles), jnp.sin(angles)
    cosine = jnp.concatenate([cosine, cosine], axis=1)
    sine = jnp.concatenate([-sine, sine], axis=1)
    lane = jnp.arange(FEATURES, dtype=jnp.int32)[None, :]
    same = places[1][:, None] == lane
    key_features = same.astype(bf16)
    query_features = jnp.where(same, 0.0, MASK_DEPTH).astype(bf16)
    gain_q_row, gain_k_row = gain_query[None], gain_key[None]
    normed, raw, q, k, v = project(
        x_all, gain_attn[None], w_first, cosine, sine, gain_q_row, gain_k_row, query_heads, key_heads
    )
    q = after(q, *out_pieces[1:4], *gate_up_pieces[1:4])
    attended, logs = attend(me_row, q, query_features, k, key_features, v, block, group)

    attended = after(attended, *out_pieces[4:], *gate_up_pieces[4:], *down_pieces[1:4])

    def rows_of(value, r):
        return value[r * block : (r + 1) * block]

    branch, unused = scatter_sum(lambda r: nn_dot(rows_of(attended, r), out_full))
    middle = x_own.astype(f32) + branch
    normed_mlp = join(gather_blocks(row_norm_apply(middle, gain_mlp).astype(bf16)))
    both = nn_dot(normed_mlp, gate_up)
    gate_value, up_value = both[:, :hidden_cols], both[:, hidden_cols:]
    d_hidden = nt_dot(cot_all, down_full)
    sigmoid = 1.0 / (1.0 + jnp.exp(-gate_value))
    silu = gate_value * sigmoid
    hidden = (silu * up_value).astype(bf16)
    d_gate = (d_hidden * up_value * sigmoid * (1.0 + gate_value * (1.0 - sigmoid))).astype(bf16)
    d_up = (d_hidden * silu).astype(bf16)
    d_both = jnp.concatenate([d_gate, d_up], axis=1)

    d_normed, unused = scatter_sum(lambda r: nt_dot(rows_of(d_both, r), gate_up))
    d_middle, d_gain_mlp = norm_back(middle, gain_mlp, d_normed)
    d_middle = d_middle + cot_own.astype(f32)
    d_branch_blocks = gather_blocks(d_middle.astype(bf16))
    d_branch = join(d_branch_blocks)
    d_attended = nt_dot(d_branch, out_full).astype(bf16)

    down, down_across = scatter_sum(lambda r: nn_dot(rows_of(hidden, r), down_full), d_branch_blocks[2:3])
    output = (middle + down).astype(bf16)

    def tn_dot(left, right):
        return lax.dot_general(left, right, (((0,), (0,)), ((), ())), preferred_element_type=f32)

    def by_copy(grad):
        return grad.astype(bf16).reshape(copies, -1, grad.shape[-1])

    pair_down = reduce_beside(by_copy(tn_dot(hidden, cot_all)))
    pair_both = reduce_beside(by_copy(tn_dot(normed_mlp, d_both)))
    pair_out = reduce_beside(by_copy(tn_dot(attended, d_branch)))
    terms_down = reduce_along(after(pair_down, d_branch_blocks[2]))
    terms_both = reduce_along(after(pair_both, d_attended))

    dq, dk, dv = unattend(
        me_row, q, query_features, k, key_features, v, attended, d_attended, logs, block, group
    )
    dq = after(dq, *terms_down, *terms_both, pair_out, down_across)
    terms_out = reduce_along(after(pair_out, dq))
    low, d_gain_heads = unproject(
        dq, dk, dv, raw, cosine, sine, gain_q_row, gain_k_row, query_heads, key_heads
    )
    d_normed_attn, unused = scatter_sum(lambda r: nt_dot(rows_of(low, r), w_first))
    d_inputs, unused = norm_back(x_own.astype(f32), gain_attn, d_normed_attn)
    grad_tokens = (d_middle + d_inputs).reshape(tokens.shape)

    grad_first = tn_dot(normed, low).astype(bf16)
    d_gain_attn = jnp.sum(w_first.astype(f32) * grad_first.astype(f32), axis=1) / gain_attn
    grad_gains = jnp.concatenate(
        [d_gain_attn, d_gain_mlp, d_gain_heads[0], d_gain_heads[1]]
    ).reshape(copies, size, gain_count)
    gain_block = jnp.pad(
        grad_gains.astype(bf16),
        ((0, 0), (0, pad_rows - size), (0, grad_first.shape[1] - gain_count)),
    )
    grad_first = jnp.concatenate(
        [grad_first.reshape(copies, size * owned, -1), gain_block], axis=1
    )
    grad_first = add_all(reduce_along(reduce_beside(grad_first)))
    grad_down, grad_both, grad_out = map(add_all, (terms_down, terms_both, terms_out))
    gain_part = grad_first[size * owned :][:size]
    gain_part = jnp.broadcast_to(gain_part[:, None], (size, pad_rows, gain_part.shape[1]))
    grad_first = jnp.concatenate(
        [grad_first[: size * owned].reshape(size, owned, -1), gain_part], axis=1
    )
    grad_first = exchange(grad_first, me).astype(f32)
    grad_gains = jnp.sum(grad_first[:, owned, :gain_count], axis=0)
    grad_first = grad_first[:, :owned]

    def to_rows(pieces):
        return pieces.transpose(1, 0, 2).reshape(owned, -1)

    grad_query = to_rows(grad_first[:, :, :q_cols])
    grad_key = to_rows(grad_first[:, :, q_cols : q_cols + k_cols])
    grad_value = to_rows(grad_first[:, :, q_cols + k_cols :])
    grad_both = exchange(grad_both.reshape(size, owned, -1), me).astype(f32)
    grad_gate = to_rows(grad_both[:, :, :hidden_cols])
    grad_up = to_rows(grad_both[:, :, hidden_cols:])
    grad_out = lax.ppermute(grad_out, ("dp", "ctx"), backward_owner).astype(f32)
    grad_down = lax.ppermute(grad_down, ("dp", "ctx"), backward_owner).astype(f32)
    return (
        output.reshape(tokens.shape),
        grad_tokens,
        grad_query,
        grad_key,
        grad_value,
        grad_out,
        grad_gate,
        grad_up,
        grad_down,
        grad_gains,
    )


def solution(mesh):
    small = mesh.shape["ctx"] == 4
    return jax.shard_map(
        split_local if small else local,
        mesh=mesh,
        in_specs=(
            P("dp", "ctx", None),
            P(("dp", "ctx"), None),
            P(("dp", "ctx"), None),
            P(("dp", "ctx"), None),
            P(("dp", "ctx"), None),
            P(("dp", "ctx"), None),
            P(("dp", "ctx"), None),
            P(("dp", "ctx"), None),
            P(("dp", "ctx")),
            P("dp", "ctx"),
            P("dp", "ctx"),
            P("dp", "ctx", None),
        ),
        out_specs=(
            P("dp", "ctx", None),
            P("dp", "ctx", None),
            P(("dp", "ctx"), None),
            P(("dp", "ctx"), None),
            P(("dp", "ctx"), None),
            P(("dp", "ctx"), None),
            P(("dp", "ctx"), None),
            P(("dp", "ctx"), None),
            P(("dp", "ctx"), None),
            P(("dp", "ctx")),
        ),
        check_vma=False,
    )
```

```python
import functools

import jax
import jax.numpy as jnp
from jax import lax
from jax.experimental import pallas as pl
from jax.experimental.pallas import tpu as pltpu
from jax.sharding import PartitionSpec as P

MODEL_WIDTH = 1024
QUERY_HEADS = 16
KEY_VALUE_HEADS = 8
HEAD_SIZE = 128


EPSILON = 1e-06
THETA = 1000000.0


def row_norm_apply(value_rows, gain_vec):
    return (
        value_rows
        * lax.rsqrt(jnp.mean(value_rows * value_rows, axis=-1, keepdims=True) + EPSILON)
        * gain_vec
    )


def rotary_embed(value_rows, token_positions):
    half_size = value_rows.shape[-1] // 2
    inverse_rates = THETA ** (
        -2.0 * jnp.arange(half_size, dtype=jnp.float32) / value_rows.shape[-1]
    )
    angles = token_positions.astype(jnp.float32)[:, None] * inverse_rates[None, :]
    cosine = jnp.cos(angles)[:, None, :]
    sine_part = jnp.sin(angles)[:, None, :]
    former = value_rows[..., :half_size]
    second = value_rows[..., half_size:]
    return jnp.concatenate(
        [former * cosine - second * sine_part, second * cosine + former * sine_part], axis=-1
    )


def heads_per_group(raw_rows, gain_vec, token_positions, head_count):
    return rotary_embed(
        row_norm_apply(raw_rows.reshape(raw_rows.shape[0], head_count, HEAD_SIZE), gain_vec),
        token_positions,
    )


def split_gains(packed):
    packed = packed.astype(jnp.float32)
    return (
        packed[:MODEL_WIDTH],
        packed[MODEL_WIDTH : 2 * MODEL_WIDTH],
        packed[2 * MODEL_WIDTH : 2 * MODEL_WIDTH + HEAD_SIZE],
        packed[2 * MODEL_WIDTH + HEAD_SIZE :],
    )


def owner_major(grad_full, owners):
    return grad_full.reshape(owners, -1)


def local(
    tokens,
    w_query,
    key_weight,
    value_weight,
    w_out,
    w_gate,
    w_up,
    w_down,
    gains,
    segment_ids,
    positions,
    cotangent,
):
    sequence_count = tokens.shape[0]
    device_local_rows = tokens.shape[1]
    every_row_set = sequence_count * device_local_rows
    inputs = tokens.reshape(every_row_set, MODEL_WIDTH).astype(jnp.float32)
    token_positions = positions.reshape(every_row_set)
    cot_rows = cotangent.reshape(every_row_set, MODEL_WIDTH)
    head_groups = QUERY_HEADS // KEY_VALUE_HEADS
    score_scale = HEAD_SIZE ** (-0.5)
    f32 = jnp.float32
    brain_float_half = jnp.bfloat16
    owners = lax.axis_size(("dp", "ctx"))
    shard_shapes = (
        w_query.shape,
        key_weight.shape,
        value_weight.shape,
        w_out.shape,
        w_gate.shape,
        w_up.shape,
        w_down.shape,
        gains.shape,
    )
    gathered = (
        lax.all_gather(w_query, ("dp", "ctx"), axis=0, tiled=True),
        lax.all_gather(key_weight, ("dp", "ctx"), axis=0, tiled=True),
        lax.all_gather(value_weight, ("dp", "ctx"), axis=0, tiled=True),
        lax.all_gather(w_out, ("dp", "ctx"), axis=0, tiled=True),
        lax.all_gather(w_gate, ("dp", "ctx"), axis=0, tiled=True),
        lax.all_gather(w_up, ("dp", "ctx"), axis=0, tiled=True),
        lax.all_gather(w_down, ("dp", "ctx"), axis=0, tiled=True),
        lax.all_gather(gains, ("dp", "ctx"), axis=0, tiled=True),
    )
    full_query, full_key, full_value, full_out, full_gate, full_up, full_down, full_gains = gathered
    gain_attn, gain_mlp, gain_query, key_norm_gain = split_gains(full_gains)
    normalized_input = row_norm_apply(inputs, gain_attn).astype(brain_float_half)
    query_raw = jnp.dot(normalized_input, full_query, preferred_element_type=f32)
    unrotated_keys = jnp.dot(normalized_input, full_key, preferred_element_type=f32)
    value_low = (
        jnp.dot(normalized_input, full_value, preferred_element_type=f32)
        .astype(brain_float_half)
        .reshape(sequence_count, device_local_rows, KEY_VALUE_HEADS * HEAD_SIZE)
    )
    reduced_queries = heads_per_group(query_raw, gain_query, token_positions, QUERY_HEADS).astype(
        brain_float_half
    )
    key_low = (
        heads_per_group(unrotated_keys, key_norm_gain, token_positions, KEY_VALUE_HEADS)
        .astype(brain_float_half)
        .reshape(sequence_count, device_local_rows, KEY_VALUE_HEADS * HEAD_SIZE)
    )
    segment_low = segment_ids.astype(brain_float_half)
    gathered_keys, gathered_values, segment_all = (
        lax.all_gather(key_low, "ctx", axis=1, tiled=True),
        lax.all_gather(value_low, "ctx", axis=1, tiled=True),
        lax.all_gather(segment_low, "ctx", axis=1, tiled=True),
    )
    overall_rows = gathered_keys.shape[1]
    query_index = lax.axis_index("ctx") * device_local_rows + jnp.arange(
        device_local_rows, dtype=jnp.int32
    )
    key_index = jnp.arange(overall_rows, dtype=jnp.int32)
    allowed = (segment_low[:, :, None] == segment_all[:, None, :]) & (
        query_index[None, :, None] >= key_index[None, None, :]
    )
    grouped_queries = reduced_queries.reshape(
        sequence_count, device_local_rows, KEY_VALUE_HEADS, head_groups, HEAD_SIZE
    ).transpose(0, 2, 3, 1, 4)
    grouped_keys = gathered_keys.reshape(
        sequence_count, overall_rows, KEY_VALUE_HEADS, HEAD_SIZE
    ).transpose(0, 2, 1, 3)
    grouped_values = gathered_values.reshape(
        sequence_count, overall_rows, KEY_VALUE_HEADS, HEAD_SIZE
    ).transpose(0, 2, 1, 3)

    def masked_scores(query_head, key_head, mask_rows):
        scores = (
            jnp.einsum("rld,kd->rlk", query_head, key_head, preferred_element_type=f32)
            * score_scale
        )
        return jnp.where(mask_rows[None], scores, -1e30)

    def forward_sequence(slices):
        query_seq, key_seq, value_seq, mask_rows = slices

        def forward_head(head_slices):
            query_head, key_head, value_head = head_slices
            scores = masked_scores(query_head, key_head, mask_rows)
            row_peak = jnp.max(scores, axis=-1, keepdims=True)
            exp_scores = jnp.exp(scores - row_peak)
            denominator = jnp.sum(exp_scores, axis=-1, keepdims=True)
            prob_low = (exp_scores / denominator).astype(brain_float_half)
            mixed_head = jnp.einsum("rlk,kd->rld", prob_low, value_head, preferred_element_type=f32)
            return (mixed_head, row_peak[..., 0] + jnp.log(denominator[..., 0]))

        return lax.map(forward_head, (query_seq, key_seq, value_seq))

    mixed_heads, log_totals = lax.map(
        forward_sequence, (grouped_queries, grouped_keys, grouped_values, allowed)
    )
    attended = (
        mixed_heads.transpose(0, 3, 1, 2, 4)
        .reshape(every_row_set, QUERY_HEADS * HEAD_SIZE)
        .astype(brain_float_half)
    )
    middle = inputs + jnp.dot(attended, full_out, preferred_element_type=f32)
    normed_mlp = row_norm_apply(middle, gain_mlp).astype(brain_float_half)
    gate_value = jnp.dot(normed_mlp, full_gate, preferred_element_type=f32)
    up_value = jnp.dot(normed_mlp, full_up, preferred_element_type=f32)
    hidden = (jax.nn.silu(gate_value) * up_value).astype(brain_float_half)
    output = (middle + jnp.dot(hidden, full_down, preferred_element_type=f32)).astype(
        brain_float_half
    )
    regathered = (
        lax.all_gather(w_query, ("dp", "ctx"), axis=0, tiled=True),
        lax.all_gather(key_weight, ("dp", "ctx"), axis=0, tiled=True),
        lax.all_gather(value_weight, ("dp", "ctx"), axis=0, tiled=True),
        lax.all_gather(w_out, ("dp", "ctx"), axis=0, tiled=True),
        lax.all_gather(w_gate, ("dp", "ctx"), axis=0, tiled=True),
        lax.all_gather(w_up, ("dp", "ctx"), axis=0, tiled=True),
        lax.all_gather(w_down, ("dp", "ctx"), axis=0, tiled=True),
        lax.all_gather(gains, ("dp", "ctx"), axis=0, tiled=True),
    )
    back_query, back_key, back_value, back_out, back_gate, back_up, back_down, back_gains = (
        regathered
    )
    gain_attn, gain_mlp, gain_query, key_norm_gain = split_gains(back_gains)
    d_hidden = jnp.einsum("ld,fd->lf", cot_rows, back_down, preferred_element_type=f32)
    grad_down = jnp.einsum("lf,ld->fd", hidden, cot_rows, preferred_element_type=f32)
    unused, swiglu_pull = jax.vjp(
        lambda gate_in, up_in: jax.nn.silu(gate_in) * up_in, gate_value, up_value
    )
    d_gate, d_up = swiglu_pull(d_hidden)
    d_gate = d_gate.astype(brain_float_half)
    d_up = d_up.astype(brain_float_half)
    grad_gate = jnp.einsum("ld,lf->df", normed_mlp, d_gate, preferred_element_type=f32)
    grad_up = jnp.einsum("ld,lf->df", normed_mlp, d_up, preferred_element_type=f32)
    d_normed = jnp.einsum("lf,df->ld", d_gate, back_gate, preferred_element_type=f32)
    d_normed = d_normed + jnp.einsum("lf,df->ld", d_up, back_up, preferred_element_type=f32)
    unused, norm_pull = jax.vjp(row_norm_apply, middle, gain_mlp)
    d_middle, d_gain_mlp = norm_pull(d_normed)
    d_middle = d_middle + cot_rows.astype(f32)
    d_branch = d_middle.astype(brain_float_half)
    grad_out = jnp.einsum("lh,ld->hd", attended, d_branch, preferred_element_type=f32)
    attended_gradient = jnp.einsum(
        "ld,hd->lh", d_branch, back_out, preferred_element_type=f32
    ).astype(brain_float_half)
    group_gradient = attended_gradient.reshape(
        sequence_count, device_local_rows, KEY_VALUE_HEADS, head_groups, HEAD_SIZE
    ).transpose(0, 2, 3, 1, 4)

    def backward_sequence(slices):
        query_seq, key_seq, value_seq, d_seq, log_seq, mask_rows = slices

        def backward_head(head_slices):
            query_head, key_head, value_head, d_head, log_total = head_slices
            scores = masked_scores(query_head, key_head, mask_rows)
            probs_full = jnp.exp(scores - log_total[..., None])
            prob_low = probs_full.astype(brain_float_half)
            d_value = jnp.einsum("rlk,rld->kd", prob_low, d_head, preferred_element_type=f32)
            d_probs = jnp.einsum("rld,kd->rlk", d_head, value_head, preferred_element_type=f32)
            d_scores = probs_full * (
                d_probs - jnp.sum(probs_full * d_probs, axis=-1, keepdims=True)
            )
            d_scores = d_scores.astype(brain_float_half)
            d_query = (
                jnp.einsum("rlk,kd->rld", d_scores, key_head, preferred_element_type=f32)
                * score_scale
            )
            d_key = (
                jnp.einsum("rlk,rld->kd", d_scores, query_head, preferred_element_type=f32)
                * score_scale
            )
            return (d_query, d_key, d_value)

        return lax.map(backward_head, (query_seq, key_seq, value_seq, d_seq, log_seq))

    d_queries, key_rows_gradient, value_rows_gradient = lax.map(
        backward_sequence,
        (grouped_queries, grouped_keys, grouped_values, group_gradient, log_totals, allowed),
    )
    gathered_key_gradient = key_rows_gradient.transpose(2, 0, 1, 3).reshape(
        overall_rows, sequence_count, KEY_VALUE_HEADS * HEAD_SIZE
    )
    gathered_value_gradient = value_rows_gradient.transpose(2, 0, 1, 3).reshape(
        overall_rows, sequence_count, KEY_VALUE_HEADS * HEAD_SIZE
    )
    local_key_gradient, local_value_gradient = (
        lax.psum_scatter(
            gathered_key_gradient.astype(jnp.bfloat16), "ctx", scatter_dimension=0, tiled=True
        ).astype(jnp.float32),
        lax.psum_scatter(
            gathered_value_gradient.astype(jnp.bfloat16), "ctx", scatter_dimension=0, tiled=True
        ).astype(jnp.float32),
    )
    local_key_gradient = local_key_gradient.transpose(1, 0, 2)
    local_value_gradient = local_value_gradient.transpose(1, 0, 2)
    d_query_heads = d_queries.transpose(0, 3, 1, 2, 4).reshape(
        every_row_set, QUERY_HEADS, HEAD_SIZE
    )
    unused, query_pull = jax.vjp(
        lambda unnormalized_input, input_gain_vector: heads_per_group(
            unnormalized_input, input_gain_vector, token_positions, QUERY_HEADS
        ),
        query_raw,
        gain_query,
    )
    d_query_raw, d_gain_query = query_pull(d_query_heads)
    unused, key_pullback = jax.vjp(
        lambda unnormalized_input, input_gain_vector: heads_per_group(
            unnormalized_input, input_gain_vector, token_positions, KEY_VALUE_HEADS
        ),
        unrotated_keys,
        key_norm_gain,
    )
    unrotated_key_gradient, key_gain_gradient = key_pullback(
        local_key_gradient.reshape(every_row_set, KEY_VALUE_HEADS, HEAD_SIZE)
    )
    d_query_low = d_query_raw.astype(brain_float_half)
    d_key_low = unrotated_key_gradient.astype(brain_float_half)
    reduced_value_gradient = local_value_gradient.reshape(
        every_row_set, KEY_VALUE_HEADS * HEAD_SIZE
    ).astype(brain_float_half)
    grad_query = jnp.einsum("ld,lh->dh", normalized_input, d_query_low, preferred_element_type=f32)
    grad_key = jnp.einsum("ld,lh->dh", normalized_input, d_key_low, preferred_element_type=f32)
    grad_value = jnp.einsum(
        "ld,lh->dh", normalized_input, reduced_value_gradient, preferred_element_type=f32
    )
    d_normed_attn = jnp.einsum("lh,dh->ld", d_query_low, back_query, preferred_element_type=f32)
    d_normed_attn = d_normed_attn + jnp.einsum(
        "lh,dh->ld", d_key_low, back_key, preferred_element_type=f32
    )
    d_normed_attn = d_normed_attn + jnp.einsum(
        "lh,dh->ld", reduced_value_gradient, back_value, preferred_element_type=f32
    )
    unused, first_pull = jax.vjp(row_norm_apply, inputs, gain_attn)
    d_inputs, d_gain_attn = first_pull(d_normed_attn)
    grad_tokens = (d_middle + d_inputs).reshape(sequence_count, device_local_rows, MODEL_WIDTH)
    grad_gains = jnp.concatenate([d_gain_attn, d_gain_mlp, d_gain_query, key_gain_gradient])
    summed = (
        lax.psum_scatter(
            owner_major(grad_query, owners), ("dp", "ctx"), scatter_dimension=0, tiled=True
        ),
        lax.psum_scatter(
            owner_major(grad_key, owners), ("dp", "ctx"), scatter_dimension=0, tiled=True
        ),
        lax.psum_scatter(
            owner_major(grad_value, owners), ("dp", "ctx"), scatter_dimension=0, tiled=True
        ),
        lax.psum_scatter(
            owner_major(grad_out, owners), ("dp", "ctx"), scatter_dimension=0, tiled=True
        ),
        lax.psum_scatter(
            owner_major(grad_gate, owners), ("dp", "ctx"), scatter_dimension=0, tiled=True
        ),
        lax.psum_scatter(
            owner_major(grad_up, owners), ("dp", "ctx"), scatter_dimension=0, tiled=True
        ),
        lax.psum_scatter(
            owner_major(grad_down, owners), ("dp", "ctx"), scatter_dimension=0, tiled=True
        ),
        lax.psum_scatter(
            owner_major(grad_gains, owners), ("dp", "ctx"), scatter_dimension=0, tiled=True
        ),
    )
    grad_query = summed[0].reshape(shard_shapes[0])
    grad_key = summed[1].reshape(shard_shapes[1])
    grad_value = summed[2].reshape(shard_shapes[2])
    grad_out = summed[3].reshape(shard_shapes[3])
    grad_gate = summed[4].reshape(shard_shapes[4])
    grad_up = summed[5].reshape(shard_shapes[5])
    grad_down = summed[6].reshape(shard_shapes[6])
    grad_gains = summed[7].reshape(shard_shapes[7])
    return (
        output.reshape(sequence_count, device_local_rows, MODEL_WIDTH),
        grad_tokens,
        grad_query,
        grad_key,
        grad_value,
        grad_out,
        grad_gate,
        grad_up,
        grad_down,
        grad_gains,
    )

FEATURES = 128
NARROW = 512
MASK_DEPTH = -4096.0
LOG2_E = 1.4426950408889634
VMEM_BYTES = 56 * 1024 * 1024
bf16 = jnp.bfloat16
f32 = jnp.float32


def xor_permute(value, axis, offset):
    size = lax.axis_size(axis)
    return lax.ppermute(value, axis, [(i, i ^ offset) for i in range(size)])


def pick(stacked, index):
    return lax.dynamic_index_in_dim(stacked, index, 0, keepdims=False)


def exchange(stacked, me):
    size = stacked.shape[0]
    relative = [pick(stacked, me)]
    for offset in range(1, size):
        relative.append(xor_permute(pick(stacked, me ^ offset), "ctx", offset))
    relative = jnp.stack(relative)
    return jnp.stack([pick(relative, me ^ source) for source in range(size)])


def shift_z(value, offset):
    size = lax.axis_size("dp")
    return lax.ppermute(value, "dp", [(i, (i + 2 * offset) % size) for i in range(size)])


def assemble_kernel(splits, count, places_ref, *refs):
    pieces, results, sems = refs[:count], refs[count:-1], refs[-1]
    copies = []
    for n, piece in enumerate(pieces):
        start = 0
        for m, rows in enumerate(splits):
            copy = pltpu.make_async_copy(
                piece.at[pl.ds(start, rows)], results[m].at[places_ref[n]], sems.at[n, m]
            )
            copy.start()
            copies.append(copy)
            start += rows
    for copy in copies:
        copy.wait()


def assemble(pieces, places, splits=None):
    count = len(pieces)
    rows, columns = pieces[0].shape
    splits = (rows,) if splits is None else splits
    anywhere = pl.BlockSpec(memory_space=pl.ANY)
    results = pl.pallas_call(
        functools.partial(assemble_kernel, splits, count),
        in_specs=[pl.BlockSpec(memory_space=pltpu.SMEM)]
        + [pl.BlockSpec(memory_space=pltpu.VMEM)] * count,
        out_specs=[anywhere] * len(splits),
        out_shape=[jax.ShapeDtypeStruct((count, n, columns), pieces[0].dtype) for n in splits],
        scratch_shapes=[pltpu.SemaphoreType.DMA((count, len(splits)))],
        compiler_params=pltpu.CompilerParams(vmem_limit_bytes=VMEM_BYTES),
        cost_estimate=pl.CostEstimate(
            flops=0, bytes_accessed=4 * count * rows * columns, transcendentals=0
        ),
        name="assemble",
    )(places.astype(jnp.int32), *pieces)
    return [result.reshape(-1, columns) for result in results]


def join(blocks):
    return assemble(blocks, jnp.arange(len(blocks)))[0]


def gather_copies(value):
    depth = lax.axis_size("dp") // 2
    at = lax.axis_index("dp")
    along = [value] + [shift_z(value, k) for k in range(1, depth)]
    beside = [xor_permute(piece, "dp", 1) for piece in along]
    rows = jnp.stack([(at // 2 - k) % depth for k in range(depth)])
    places = jnp.concatenate([rows * 2 + at % 2, rows * 2 + 1 - at % 2])
    return along + beside, places


def reduce_beside(grad):
    depth = grad.shape[0] // 2
    y = lax.axis_index("dp") % 2
    grad = grad.reshape((depth, 2) + grad.shape[1:])
    away = lax.dynamic_index_in_dim(grad, 1 - y, 1, keepdims=False)
    kept = lax.dynamic_index_in_dim(grad, y, 1, keepdims=False)
    return (kept.astype(f32) + xor_permute(away, "dp", 1).astype(f32)).astype(bf16)


def reduce_along(pair):
    depth = pair.shape[0]
    z = lax.axis_index("dp") // 2
    sent = [shift_z(pick(pair, (z + k) % depth), k) for k in range(1, depth)]
    return [pick(pair, z)] + sent


def add_all(terms):
    total = terms[0].astype(f32)
    for term in terms[1:]:
        total = total + term.astype(f32)
    return total.astype(bf16)


def narrow(rows, parts):
    pieces = rows.reshape(parts, rows.shape[0] // parts, -1, NARROW)
    return pieces.transpose(0, 2, 1, 3).reshape(parts, -1, NARROW)


def widen(pieces, height):
    parts = pieces.shape[0]
    pieces = pieces.reshape(parts, -1, height, NARROW).transpose(0, 2, 1, 3)
    return pieces.reshape(parts * height, -1)


def after(value, *others):
    return lax.optimization_barrier((value, *others))[0]


def gather_blocks(value):
    across = xor_permute(value, "ctx", 2)
    beside = xor_permute(value, "ctx", 1)
    corner = xor_permute(across, "ctx", 1)
    return [value, beside, across, corner]


def gather_near(value):
    return [value, xor_permute(value, "ctx", 1)], xor_permute(value, "ctx", 2)


def gather_far(across, *waits):
    across = after(across, *waits)
    return [across, xor_permute(across, "ctx", 1)]


def send_across(part_corner, part_across, *waits):
    corner = xor_permute(part_corner.astype(bf16), "ctx", 1)
    toward = (part_across.astype(f32) + corner.astype(f32)).astype(bf16)
    toward = after(toward, *waits) if waits else toward
    return toward, xor_permute(toward, "ctx", 2)


def sum_own(part_beside, part_own, across):
    beside = xor_permute(part_beside.astype(bf16), "ctx", 1)
    return part_own.astype(f32) + beside.astype(f32) + across.astype(f32)


def nt_dot(left, right):
    return lax.dot_general(left, right, (((1,), (1,)), ((), ())), preferred_element_type=f32)


def nn_dot(left, right):
    return jnp.dot(left, right, preferred_element_type=f32)


def project_kernel(
    query_heads,
    key_heads,
    x_ref,
    gain_ref,
    weight_ref,
    cos_ref,
    sin_ref,
    gain_q_ref,
    gain_k_ref,
    normed_ref,
    raw_ref,
    q_ref,
    k_ref,
    v_ref,
):
    x = x_ref[...].astype(f32)
    scale = lax.rsqrt(jnp.mean(x * x, axis=-1, keepdims=True) + EPSILON)
    normed = (x * scale * gain_ref[...]).astype(bf16)
    normed_ref[...] = normed
    raw = nn_dot(normed, weight_ref[...])
    turned = (query_heads + key_heads) * HEAD_SIZE
    raw_ref[...] = raw[:, :turned]
    v_ref[...] = raw[:, turned:].astype(bf16)
    cosine = cos_ref[...]
    sine = sin_ref[...]
    for head in range(query_heads + key_heads):
        rows = raw[:, head * HEAD_SIZE : (head + 1) * HEAD_SIZE]
        gain = gain_q_ref[...] if head < query_heads else gain_k_ref[...]
        rows = rows * lax.rsqrt(jnp.mean(rows * rows, axis=-1, keepdims=True) + EPSILON) * gain
        rows = (rows * cosine + pltpu.roll(rows, HEAD_SIZE // 2, 1) * sine).astype(bf16)
        if head < query_heads:
            q_ref[:, head * HEAD_SIZE : (head + 1) * HEAD_SIZE] = rows
        else:
            at = (head - query_heads) * HEAD_SIZE
            k_ref[:, at : at + HEAD_SIZE] = rows


def project(x, gain, weight, cosine, sine, gain_q, gain_k, query_heads, key_heads):
    rows, width = x.shape
    block = 256
    turned = (query_heads + key_heads) * HEAD_SIZE
    columns = weight.shape[1]

    def tall(n):
        return pl.BlockSpec((block, n), lambda i: (i, 0))

    def whole(shape):
        return pl.BlockSpec(shape, lambda i: (0, 0))

    return pl.pallas_call(
        functools.partial(project_kernel, query_heads, key_heads),
        grid=(rows // block,),
        in_specs=[
            tall(width),
            whole((1, width)),
            whole(weight.shape),
            tall(HEAD_SIZE),
            tall(HEAD_SIZE),
            whole((1, HEAD_SIZE)),
            whole((1, HEAD_SIZE)),
        ],
        out_specs=[
            tall(width),
            tall(turned),
            tall(query_heads * HEAD_SIZE),
            tall(key_heads * HEAD_SIZE),
            tall(key_heads * HEAD_SIZE),
        ],
        out_shape=[
            jax.ShapeDtypeStruct((rows, width), bf16),
            jax.ShapeDtypeStruct((rows, turned), f32),
            jax.ShapeDtypeStruct((rows, query_heads * HEAD_SIZE), bf16),
            jax.ShapeDtypeStruct((rows, key_heads * HEAD_SIZE), bf16),
            jax.ShapeDtypeStruct((rows, key_heads * HEAD_SIZE), bf16),
        ],
        compiler_params=pltpu.CompilerParams(vmem_limit_bytes=VMEM_BYTES),
        cost_estimate=pl.CostEstimate(
            flops=2 * rows * width * columns,
            bytes_accessed=rows * (4 * width + 4 * turned + 2 * columns) + 2 * width * columns,
            transcendentals=0,
        ),
        name="project",
    )(x, gain, weight, cosine, sine, gain_q, gain_k)


def unproject_kernel(
    query_heads,
    key_heads,
    dq_ref,
    dk_ref,
    dv_ref,
    raw_ref,
    cos_ref,
    sin_ref,
    gain_q_ref,
    gain_k_ref,
    low_ref,
    dgain_ref,
):
    @pl.when(pl.program_id(0) == 0)
    def _():
        dgain_ref[...] = jnp.zeros_like(dgain_ref)

    cosine = cos_ref[...]
    sine = sin_ref[...]
    total_q = jnp.zeros((1, HEAD_SIZE), f32)
    total_k = jnp.zeros((1, HEAD_SIZE), f32)
    for head in range(query_heads + key_heads):
        at = head * HEAD_SIZE
        raw = raw_ref[:, at : at + HEAD_SIZE]
        if head < query_heads:
            grad = dq_ref[:, at : at + HEAD_SIZE]
            gain = gain_q_ref[...]
        else:
            back = (head - query_heads) * HEAD_SIZE
            grad = dk_ref[:, back : back + HEAD_SIZE]
            gain = gain_k_ref[...]
        grad = grad * cosine - pltpu.roll(grad, HEAD_SIZE // 2, 1) * sine
        scale = lax.rsqrt(jnp.mean(raw * raw, axis=-1, keepdims=True) + EPSILON)
        unit = raw * scale
        summed = jnp.sum(unit * grad, axis=0, keepdims=True)
        if head < query_heads:
            total_q += summed
        else:
            total_k += summed
        grad = grad * gain
        mean = jnp.mean(unit * grad, axis=-1, keepdims=True)
        low_ref[:, at : at + HEAD_SIZE] = (scale * (grad - unit * mean)).astype(bf16)
    low_ref[:, (query_heads + key_heads) * HEAD_SIZE :] = dv_ref[...].astype(bf16)
    dgain_ref[0:1, :] += total_q
    dgain_ref[1:2, :] += total_k


def unproject(dq, dk, dv, raw, cosine, sine, gain_q, gain_k, query_heads, key_heads):
    rows = dq.shape[0]
    block = 256
    columns = (query_heads + 2 * key_heads) * HEAD_SIZE

    def tall(n):
        return pl.BlockSpec((block, n), lambda i: (i, 0))

    def whole(shape):
        return pl.BlockSpec(shape, lambda i: (0, 0))

    return pl.pallas_call(
        functools.partial(unproject_kernel, query_heads, key_heads),
        grid=(rows // block,),
        in_specs=[
            tall(dq.shape[1]),
            tall(dk.shape[1]),
            tall(dv.shape[1]),
            tall(raw.shape[1]),
            tall(HEAD_SIZE),
            tall(HEAD_SIZE),
            whole((1, HEAD_SIZE)),
            whole((1, HEAD_SIZE)),
        ],
        out_specs=[tall(columns), whole((8, HEAD_SIZE))],
        out_shape=[
            jax.ShapeDtypeStruct((rows, columns), bf16),
            jax.ShapeDtypeStruct((8, HEAD_SIZE), f32),
        ],
        compiler_params=pltpu.CompilerParams(vmem_limit_bytes=VMEM_BYTES),
        cost_estimate=pl.CostEstimate(
            flops=20 * rows * columns, bytes_accessed=10 * rows * columns, transcendentals=0
        ),
        name="unproject",
    )(dq, dk, dv, raw, cosine, sine, gain_q, gain_k)


def attend_kernel(
    group, block, first, me_ref, q_ref, qf_ref, k_ref, kf_ref, v_ref, o_ref, log_ref, total_ref
):
    me = me_ref[0]
    at_query = (pl.program_id(1) + first) ^ me
    factor = HEAD_SIZE ** (-0.5) * LOG2_E
    query_features = qf_ref[...]
    ones = jnp.ones((block, HEAD_SIZE), bf16)
    total_ref[...] = jnp.zeros_like(total_ref)

    def step(at_key, diagonal):
        rows = pl.ds(pl.multiple_of((at_key ^ me) * block, block), block)
        keys = jnp.concatenate([k_ref[rows, :], kf_ref[rows, :]], axis=1)
        values = jnp.concatenate([v_ref[rows, :], ones], axis=1)
        for head in range(group):
            query = q_ref[:, head * HEAD_SIZE : (head + 1) * HEAD_SIZE]
            scores = nt_dot(jnp.concatenate([query, query_features], axis=1), keys)
            probs = jnp.exp2(scores * factor)
            if diagonal:
                down = lax.broadcasted_iota(jnp.int32, probs.shape, 0)
                right = lax.broadcasted_iota(jnp.int32, probs.shape, 1)
                probs = jnp.where(down >= right, probs, 0.0)
            total_ref[head] += nn_dot(probs.astype(bf16), values)

    @pl.loop(0, at_query)
    def _(at_key):
        step(at_key, False)

    step(at_query, True)
    for head in range(group):
        weighted = total_ref[head, :, :HEAD_SIZE]
        summed = total_ref[head, :, HEAD_SIZE:]
        o_ref[:, head * HEAD_SIZE : (head + 1) * HEAD_SIZE] = (weighted / summed).astype(bf16)
        log_ref[0, head : head + 1, :] = jnp.log2(summed.T[0:1, :])


def attend(me, q, qf, k, kf, v, block, group, first, count):
    rows = k.shape[0]
    key_heads = k.shape[1] // HEAD_SIZE
    pairs = key_heads * group * count * block * rows * 5 // 8
    return pl.pallas_call(
        functools.partial(attend_kernel, group, block, first),
        grid_spec=pltpu.PrefetchScalarGridSpec(
            num_scalar_prefetch=1,
            grid=(key_heads, count),
            in_specs=[
                pl.BlockSpec((block, group * HEAD_SIZE), lambda g, i, me: (i + first, g)),
                pl.BlockSpec((block, FEATURES), lambda g, i, me: (i + first, 0)),
                pl.BlockSpec((rows, HEAD_SIZE), lambda g, i, me: (0, g)),
                pl.BlockSpec((rows, FEATURES), lambda g, i, me: (0, 0)),
                pl.BlockSpec((rows, HEAD_SIZE), lambda g, i, me: (0, g)),
            ],
            out_specs=[
                pl.BlockSpec((block, group * HEAD_SIZE), lambda g, i, me: (i, g)),
                pl.BlockSpec((1, group, block), lambda g, i, me: (g, 0, i)),
            ],
            scratch_shapes=[pltpu.VMEM((group, block, 2 * HEAD_SIZE), f32)],
        ),
        out_shape=[
            jax.ShapeDtypeStruct((count * block, q.shape[1]), bf16),
            jax.ShapeDtypeStruct((key_heads, group, count * block), f32),
        ],
        compiler_params=pltpu.CompilerParams(vmem_limit_bytes=VMEM_BYTES),
        cost_estimate=pl.CostEstimate(
            flops=8 * pairs * HEAD_SIZE, bytes_accessed=10 * q.size, transcendentals=pairs
        ),
        name="attend",
    )(me, q, qf, k, kf, v)


def unattend_kernel(
    group,
    block,
    first,
    resumed,
    me_ref,
    q_ref,
    qf_ref,
    k_ref,
    kf_ref,
    v_ref,
    o_ref,
    do_ref,
    log_ref,
    *rest,
):
    if resumed:
        dk_in_ref, dv_in_ref, *rest = rest
    dq_ref, dk_ref, dv_ref, flipped_ref, total_ref = rest
    me = me_ref[0]
    at_query = (pl.program_id(1) + first) ^ me
    scale = HEAD_SIZE ** (-0.5)
    factor = scale * LOG2_E

    @pl.when(pl.program_id(1) == 0)
    def _():
        dk_ref[...] = dk_in_ref[...] if resumed else jnp.zeros_like(dk_ref)
        dv_ref[...] = dv_in_ref[...] if resumed else jnp.zeros_like(dv_ref)
        flipped_ref[...] = k_ref[...].astype(f32).T.astype(bf16)

    total_ref[...] = jnp.zeros_like(total_ref)
    query_features = qf_ref[...]
    deltas = []
    for head in range(group):
        lanes = slice(head * HEAD_SIZE, (head + 1) * HEAD_SIZE)
        product = do_ref[:, lanes].astype(f32) * o_ref[:, lanes].astype(f32)
        deltas.append(jnp.sum(product.T, axis=0, keepdims=True))

    def step(at_key, diagonal):
        start = pl.multiple_of((at_key ^ me) * block, block)
        rows = pl.ds(start, block)
        keys = jnp.concatenate([k_ref[rows, :], kf_ref[rows, :]], axis=1)
        values = v_ref[rows, :]
        for head in range(group):
            lanes = slice(head * HEAD_SIZE, (head + 1) * HEAD_SIZE)
            query = q_ref[:, lanes]
            d_out = do_ref[:, lanes]
            scores = nt_dot(keys, jnp.concatenate([query, query_features], axis=1))
            probs = jnp.exp2(scores * factor - log_ref[0, head : head + 1, :])
            if diagonal:
                key_at = lax.broadcasted_iota(jnp.int32, probs.shape, 0)
                query_at = lax.broadcasted_iota(jnp.int32, probs.shape, 1)
                probs = jnp.where(query_at >= key_at, probs, 0.0)
            d_scores = (probs * (nt_dot(values, d_out) - deltas[head])).astype(bf16)
            dv_ref[rows, :] += nn_dot(probs.astype(bf16), d_out)
            dk_ref[rows, :] += nn_dot(d_scores, query)
            total_ref[head] += nn_dot(flipped_ref[:, rows], d_scores)

    @pl.loop(0, at_query)
    def _(at_key):
        step(at_key, False)

    step(at_query, True)
    for head in range(group):
        dq_ref[:, head * HEAD_SIZE : (head + 1) * HEAD_SIZE] = total_ref[head].T * scale

    if resumed:

        @pl.when(pl.program_id(1) == pl.num_programs(1) - 1)
        def _():
            dk_ref[...] = dk_ref[...] * scale


def unattend(me, q, qf, k, kf, v, o, d_out, logs, block, group, first, count, earlier=()):
    rows = k.shape[0]
    key_heads = k.shape[1] // HEAD_SIZE
    pairs = key_heads * group * count * block * rows * 5 // 8

    def by_query(n):
        return pl.BlockSpec((block, n), lambda g, i, me: (i, g))

    by_key = pl.BlockSpec((rows, HEAD_SIZE), lambda g, i, me: (0, g))
    return pl.pallas_call(
        functools.partial(unattend_kernel, group, block, first, bool(earlier)),
        grid_spec=pltpu.PrefetchScalarGridSpec(
            num_scalar_prefetch=1,
            grid=(key_heads, count),
            in_specs=[
                pl.BlockSpec((block, group * HEAD_SIZE), lambda g, i, me: (i + first, g)),
                pl.BlockSpec((block, FEATURES), lambda g, i, me: (i + first, 0)),
                by_key,
                pl.BlockSpec((rows, FEATURES), lambda g, i, me: (0, 0)),
                by_key,
                by_query(group * HEAD_SIZE),
                by_query(group * HEAD_SIZE),
                pl.BlockSpec((1, group, block), lambda g, i, me: (g, 0, i)),
            ]
            + [by_key] * len(earlier),
            out_specs=[by_query(group * HEAD_SIZE), by_key, by_key],
            scratch_shapes=[
                pltpu.VMEM((HEAD_SIZE, rows), bf16),
                pltpu.VMEM((group, HEAD_SIZE, block), f32),
            ],
        ),
        out_shape=[
            jax.ShapeDtypeStruct((count * block, q.shape[1]), f32),
            jax.ShapeDtypeStruct(k.shape, f32),
            jax.ShapeDtypeStruct(v.shape, f32),
        ],
        compiler_params=pltpu.CompilerParams(vmem_limit_bytes=VMEM_BYTES),
        cost_estimate=pl.CostEstimate(
            flops=14 * pairs * HEAD_SIZE, bytes_accessed=20 * q.size, transcendentals=pairs
        ),
        name="unattend",
    )(me, q, qf, k, kf, v, o, d_out, logs, *earlier)


def feed_kernel(
    units, h_ref, cot_ref, both_ref, down_ref, hidden_ref, d_both_ref, part_ref, d_part_ref
):
    both = nn_dot(h_ref[...], both_ref[...])
    d_hidden = nt_dot(cot_ref[...], down_ref[...])
    gate, up = both[:, :units], both[:, units:]
    sigmoid = 1.0 / (1.0 + jnp.exp(-gate))
    silu = gate * sigmoid
    hidden = (silu * up).astype(bf16)
    hidden_ref[...] = hidden
    part_ref[...] = nn_dot(hidden, down_ref[...]).astype(bf16)
    d_gate = (d_hidden * up * sigmoid * (1.0 + gate * (1.0 - sigmoid))).astype(bf16)
    d_up = (d_hidden * silu).astype(bf16)
    d_both = jnp.concatenate([d_gate, d_up], axis=1)
    d_both_ref[...] = d_both
    d_part_ref[...] = nt_dot(d_both, both_ref[...]).astype(bf16)


def feed(h, cot, both, down):
    rows, width = h.shape
    units = down.shape[0]
    block = 256

    def tall(n):
        return pl.BlockSpec((block, n), lambda i: (i, 0))

    def whole(shape):
        return pl.BlockSpec(shape, lambda i: (0, 0))

    return pl.pallas_call(
        functools.partial(feed_kernel, units),
        grid=(rows // block,),
        in_specs=[tall(width), tall(width), whole(both.shape), whole(down.shape)],
        out_specs=[tall(units), tall(2 * units), tall(width), tall(width)],
        out_shape=[
            jax.ShapeDtypeStruct((rows, n), bf16) for n in (units, 2 * units, width, width)
        ],
        compiler_params=pltpu.CompilerParams(vmem_limit_bytes=VMEM_BYTES),
        cost_estimate=pl.CostEstimate(
            flops=12 * rows * width * units,
            bytes_accessed=rows * (8 * width + 6 * units) + 6 * width * units,
            transcendentals=rows * units,
        ),
        name="feed",
    )(h, cot, both, down)


def norm_back(value_rows, gain_vec, grad):
    scale = lax.rsqrt(jnp.mean(value_rows * value_rows, axis=-1, keepdims=True) + EPSILON)
    unit = value_rows * scale
    d_gain = jnp.sum(unit * grad, axis=0)
    grad = grad * gain_vec
    return scale * (grad - unit * jnp.mean(unit * grad, axis=-1, keepdims=True)), d_gain


def split_local(
    tokens,
    w_query,
    key_weight,
    value_weight,
    w_out,
    w_gate,
    w_up,
    w_down,
    gains,
    segment_ids,
    positions,
    cotangent,
):
    size = lax.axis_size("ctx")
    copies = lax.axis_size("dp")
    me = lax.axis_index("ctx")
    me_row = me.reshape(1).astype(jnp.int32)
    block = tokens.shape[1]
    group = QUERY_HEADS // KEY_VALUE_HEADS
    query_heads = QUERY_HEADS // size
    key_heads = KEY_VALUE_HEADS // size
    q_cols = query_heads * HEAD_SIZE
    k_cols = key_heads * HEAD_SIZE
    owned = w_query.shape[0]
    hidden_cols = w_gate.shape[1] // size
    gain_count = gains.shape[0]
    pad_rows = 16
    forward_owner = [
        (b, (b % copies) * size + b // copies) for b in range(size * copies)
    ]
    backward_owner = [(target, source) for source, target in forward_owner]

    def by_columns(weight):
        return weight.reshape(weight.shape[0], size, -1).transpose(1, 0, 2)

    x_own = tokens.reshape(block, MODEL_WIDTH)
    x_blocks = gather_blocks(x_own)
    x_all = join(x_blocks)
    places = jnp.concatenate([positions, segment_ids]).astype(jnp.int32)
    places = jnp.concatenate(gather_blocks(places), axis=1)

    first = jnp.concatenate(
        [by_columns(w_query), by_columns(key_weight), by_columns(value_weight)], axis=2
    )
    gain_rows = jnp.pad(gains[None], ((0, pad_rows - 1), (0, first.shape[2] - gain_count)))
    first = jnp.concatenate(
        [first, jnp.broadcast_to(gain_rows[None], (size,) + gain_rows.shape)], axis=1
    )
    first = exchange(first, me)
    gain_rows = jnp.concatenate(
        [first[:, owned], jnp.zeros((pad_rows - size, first.shape[2]), bf16)]
    )
    first = jnp.concatenate(
        [first[:, :owned].reshape(size * owned, first.shape[2]), gain_rows]
    )
    first_pieces, places_dp = gather_copies(first)
    cot_own = cotangent.reshape(block, MODEL_WIDTH)
    cot_blocks = gather_blocks(after(cot_own, x_blocks[2]))
    w_first, gain_rows = assemble(first_pieces, places_dp, (size * owned, pad_rows))
    w_first = after(w_first, *cot_blocks)
    full_gains = gain_rows.reshape(copies, pad_rows, -1)[:, :size, :gain_count].reshape(-1)
    gain_attn, gain_mlp, gain_query, gain_key = split_gains(full_gains)

    rows_out, rows_down, rows_both = w_out.shape[0], w_down.shape[0], size * owned
    per_row = MODEL_WIDTH // NARROW
    feed_rows = rows_both * (2 * hidden_cols // NARROW) + rows_down * per_row
    moved = lax.ppermute(jnp.concatenate([w_out, w_down]), ("dp", "ctx"), forward_owner)
    gate_up = jnp.concatenate([by_columns(w_gate), by_columns(w_up)], axis=2)
    gate_up = exchange(gate_up, me).reshape(rows_both, -1)
    later = jnp.concatenate(
        [narrow(gate_up, 1)[0], narrow(moved[rows_out:], 1)[0], narrow(moved[:rows_out], 1)[0]]
    )
    w_first = after(w_first, later)
    later = lax.all_gather(later, "dp", axis=0, tiled=True).reshape(copies, -1, NARROW)
    out_full = widen(later[:, feed_rows:], rows_out)
    gate_up = widen(later[:, : rows_both * (2 * hidden_cols // NARROW)], rows_both)
    down_full = widen(later[:, rows_both * (2 * hidden_cols // NARROW) : feed_rows], rows_down)
    near, far = slice(0, 2), slice(2, 4)
    cot_near, cot_far = join(cot_blocks[near]), join(cot_blocks[far])

    half = HEAD_SIZE // 2
    rates = THETA ** (-2.0 * jnp.arange(half, dtype=f32) / HEAD_SIZE)
    angles = places[0].astype(f32)[:, None] * rates[None, :]
    cosine, sine = jnp.cos(angles), jnp.sin(angles)
    cosine = jnp.concatenate([cosine, cosine], axis=1)
    sine = jnp.concatenate([-sine, sine], axis=1)
    lane = jnp.arange(FEATURES, dtype=jnp.int32)[None, :]
    same = places[1][:, None] == lane
    key_features = same.astype(bf16)
    query_features = jnp.where(same, 0.0, MASK_DEPTH).astype(bf16)
    gain_q_row, gain_k_row = gain_query[None], gain_key[None]
    normed, raw, q, k, v = project(
        x_all, gain_attn[None], w_first, cosine, sine, gain_q_row, gain_k_row, query_heads, key_heads
    )
    def attend_half(query, first):
        return attend(
            me_row, query, query_features, k, key_features, v, block, group, first, 2
        )

    def halves(value):
        return value[:block], value[block:]

    att_far, logs_far = attend_half(q, 2)
    att_across, att_corner = halves(att_far)
    part_corner, part_across = nn_dot(att_corner, out_full), nn_dot(att_across, out_full)
    toward, across = send_across(part_corner, part_across)
    att_near, logs_near = attend_half(after(q, toward), 0)
    att_own, att_beside = halves(att_near)
    part_beside, part_own = nn_dot(att_beside, out_full), nn_dot(att_own, out_full)
    middle = x_own.astype(f32) + sum_own(part_beside, part_own, across)
    h_blocks, across = gather_near(row_norm_apply(middle, gain_mlp).astype(bf16))
    h_near = join(h_blocks)
    hidden_near, d_both_near, down_near, d_h_near = feed(h_near, cot_near, gate_up, down_full)
    h_far = join(gather_far(across, hidden_near))
    hidden_far, d_both_far, down_far, d_h_far = feed(h_far, cot_far, gate_up, down_full)

    part_across, part_corner = halves(d_h_far)
    unused, across = send_across(part_corner, part_across)
    part_own, part_beside = halves(d_h_near)
    d_normed = sum_own(part_beside, part_own, across)
    d_middle, d_gain_mlp = norm_back(middle, gain_mlp, d_normed)
    d_middle = d_middle + cot_own.astype(f32)
    d_branch_blocks, d_branch_across = gather_near(d_middle.astype(bf16))
    d_branch_near = join(d_branch_blocks)

    def tn_dot(left, right):
        return lax.dot_general(left, right, (((0,), (0,)), ((), ())), preferred_element_type=f32)

    def by_copy(grad):
        return grad.astype(bf16).reshape(copies, -1, grad.shape[-1])

    grad_down = tn_dot(hidden_near, cot_near) + tn_dot(hidden_far, cot_far)
    grad_both = tn_dot(h_near, d_both_near) + tn_dot(h_far, d_both_far)
    feed_parts = jnp.concatenate(
        [narrow(grad_both.astype(bf16), copies), narrow(grad_down.astype(bf16), copies)], axis=1
    ).reshape(-1, NARROW)
    grad_feed = lax.psum_scatter(feed_parts, "dp", scatter_dimension=0, tiled=True)

    def unattend_half(att, d_branch, logs, first, earlier, *waits):
        d_att = after(nt_dot(d_branch, out_full).astype(bf16), *waits)
        return unattend(
            me_row,
            q,
            query_features,
            k,
            key_features,
            v,
            att,
            d_att,
            logs,
            block,
            group,
            first,
            2,
            earlier,
        )

    dq_near, *earlier = unattend_half(att_near, d_branch_near, logs_near, 0, (), feed_parts)
    d_branch_blocks = gather_far(d_branch_across, dq_near)
    d_branch_far = join(d_branch_blocks)
    part_across, part_corner = halves(down_far)
    unused, down_across = send_across(part_corner, part_across, d_branch_blocks[0])
    part_own, part_beside = halves(down_near)
    output = (middle + sum_own(part_beside, part_own, down_across)).astype(bf16)

    grad_out = tn_dot(att_near, d_branch_near) + tn_dot(att_far, d_branch_far)
    pair_out = reduce_beside(by_copy(grad_out))
    dq_far, dk, dv = unattend_half(att_far, d_branch_far, logs_far, 2, earlier)
    dk = after(dk, pair_out, down_across)
    dq = jnp.concatenate([dq_near, dq_far])
    low, d_gain_heads = unproject(
        dq, dk, dv, raw, cosine, sine, gain_q_row, gain_k_row, query_heads, key_heads
    )
    terms_out = reduce_along(after(pair_out, low))
    low_own, low_beside, low_across, low_corner = (
        low[r * block : (r + 1) * block] for r in range(size)
    )
    toward, across = send_across(nt_dot(low_corner, w_first), nt_dot(low_across, w_first))
    part_beside, part_own = nt_dot(low_beside, w_first), nt_dot(low_own, w_first)
    d_normed_attn = sum_own(part_beside, part_own, across)
    d_inputs, unused = norm_back(x_own.astype(f32), gain_attn, d_normed_attn)
    grad_tokens = (d_middle + d_inputs).reshape(tokens.shape)

    grad_first = tn_dot(normed, low).astype(bf16)
    d_gain_attn = jnp.sum(w_first.astype(f32) * grad_first.astype(f32), axis=1) / gain_attn
    grad_gains = jnp.concatenate(
        [d_gain_attn, d_gain_mlp, d_gain_heads[0], d_gain_heads[1]]
    ).reshape(copies, size, gain_count)
    gain_block = jnp.pad(
        grad_gains.astype(bf16),
        ((0, 0), (0, pad_rows - size), (0, grad_first.shape[1] - gain_count)),
    )
    grad_first = jnp.concatenate(
        [grad_first.reshape(copies, size * owned, -1), gain_block], axis=1
    )
    terms_first = reduce_along(after(reduce_beside(grad_first), across))
    grad_first = add_all(terms_first)
    grad_out = add_all(after(terms_out, *terms_first))
    grad_feed = after(grad_feed, *terms_first)
    split = rows_both * (2 * hidden_cols // NARROW)
    grad_both = widen(grad_feed[None, :split], rows_both)
    grad_down = widen(grad_feed[None, split:], rows_down)
    gain_part = grad_first[size * owned :][:size]
    gain_part = jnp.broadcast_to(gain_part[:, None], (size, pad_rows, gain_part.shape[1]))
    grad_first = jnp.concatenate(
        [grad_first[: size * owned].reshape(size, owned, -1), gain_part], axis=1
    )
    grad_first = exchange(grad_first, me).astype(f32)
    grad_gains = jnp.sum(grad_first[:, owned, :gain_count], axis=0)
    grad_first = grad_first[:, :owned]

    def to_rows(pieces):
        return pieces.transpose(1, 0, 2).reshape(owned, -1)

    grad_query = to_rows(grad_first[:, :, :q_cols])
    grad_key = to_rows(grad_first[:, :, q_cols : q_cols + k_cols])
    grad_value = to_rows(grad_first[:, :, q_cols + k_cols :])
    grad_both = exchange(grad_both.reshape(size, owned, -1), me).astype(f32)
    grad_gate = to_rows(grad_both[:, :, :hidden_cols])
    grad_up = to_rows(grad_both[:, :, hidden_cols:])
    grad_out = lax.ppermute(grad_out, ("dp", "ctx"), backward_owner).astype(f32)
    grad_down = lax.ppermute(grad_down, ("dp", "ctx"), backward_owner).astype(f32)
    return (
        output.reshape(tokens.shape),
        grad_tokens,
        grad_query,
        grad_key,
        grad_value,
        grad_out,
        grad_gate,
        grad_up,
        grad_down,
        grad_gains,
    )


def solution(mesh):
    small = mesh.shape["ctx"] == 4
    return jax.shard_map(
        split_local if small else local,
        mesh=mesh,
        in_specs=(
            P("dp", "ctx", None),
            P(("dp", "ctx"), None),
            P(("dp", "ctx"), None),
            P(("dp", "ctx"), None),
            P(("dp", "ctx"), None),
            P(("dp", "ctx"), None),
            P(("dp", "ctx"), None),
            P(("dp", "ctx"), None),
            P(("dp", "ctx")),
            P("dp", "ctx"),
            P("dp", "ctx"),
            P("dp", "ctx", None),
        ),
        out_specs=(
            P("dp", "ctx", None),
            P("dp", "ctx", None),
            P(("dp", "ctx"), None),
            P(("dp", "ctx"), None),
            P(("dp", "ctx"), None),
            P(("dp", "ctx"), None),
            P(("dp", "ctx"), None),
            P(("dp", "ctx"), None),
            P(("dp", "ctx"), None),
            P(("dp", "ctx")),
        ),
        check_vma=False,
    )
```

```python
import functools

import jax
import jax.numpy as jnp
from jax import lax
from jax.experimental import pallas as pl
from jax.experimental.pallas import tpu as pltpu
from jax.sharding import PartitionSpec as P

MODEL_WIDTH = 1024
QUERY_HEADS = 16
KEY_VALUE_HEADS = 8
HEAD_SIZE = 128


EPSILON = 1e-06
THETA = 1000000.0


def row_norm_apply(value_rows, gain_vec):
    return (
        value_rows
        * lax.rsqrt(jnp.mean(value_rows * value_rows, axis=-1, keepdims=True) + EPSILON)
        * gain_vec
    )


def rotary_embed(value_rows, token_positions):
    half_size = value_rows.shape[-1] // 2
    inverse_rates = THETA ** (
        -2.0 * jnp.arange(half_size, dtype=jnp.float32) / value_rows.shape[-1]
    )
    angles = token_positions.astype(jnp.float32)[:, None] * inverse_rates[None, :]
    cosine = jnp.cos(angles)[:, None, :]
    sine_part = jnp.sin(angles)[:, None, :]
    former = value_rows[..., :half_size]
    second = value_rows[..., half_size:]
    return jnp.concatenate(
        [former * cosine - second * sine_part, second * cosine + former * sine_part], axis=-1
    )


def heads_per_group(raw_rows, gain_vec, token_positions, head_count):
    return rotary_embed(
        row_norm_apply(raw_rows.reshape(raw_rows.shape[0], head_count, HEAD_SIZE), gain_vec),
        token_positions,
    )


def split_gains(packed):
    packed = packed.astype(jnp.float32)
    return (
        packed[:MODEL_WIDTH],
        packed[MODEL_WIDTH : 2 * MODEL_WIDTH],
        packed[2 * MODEL_WIDTH : 2 * MODEL_WIDTH + HEAD_SIZE],
        packed[2 * MODEL_WIDTH + HEAD_SIZE :],
    )


def owner_major(grad_full, owners):
    return grad_full.reshape(owners, -1)


def local(
    tokens,
    w_query,
    key_weight,
    value_weight,
    w_out,
    w_gate,
    w_up,
    w_down,
    gains,
    segment_ids,
    positions,
    cotangent,
):
    sequence_count = tokens.shape[0]
    device_local_rows = tokens.shape[1]
    every_row_set = sequence_count * device_local_rows
    inputs = tokens.reshape(every_row_set, MODEL_WIDTH).astype(jnp.float32)
    token_positions = positions.reshape(every_row_set)
    cot_rows = cotangent.reshape(every_row_set, MODEL_WIDTH)
    head_groups = QUERY_HEADS // KEY_VALUE_HEADS
    score_scale = HEAD_SIZE ** (-0.5)
    f32 = jnp.float32
    brain_float_half = jnp.bfloat16
    owners = lax.axis_size(("dp", "ctx"))
    shard_shapes = (
        w_query.shape,
        key_weight.shape,
        value_weight.shape,
        w_out.shape,
        w_gate.shape,
        w_up.shape,
        w_down.shape,
        gains.shape,
    )
    gathered = (
        lax.all_gather(w_query, ("dp", "ctx"), axis=0, tiled=True),
        lax.all_gather(key_weight, ("dp", "ctx"), axis=0, tiled=True),
        lax.all_gather(value_weight, ("dp", "ctx"), axis=0, tiled=True),
        lax.all_gather(w_out, ("dp", "ctx"), axis=0, tiled=True),
        lax.all_gather(w_gate, ("dp", "ctx"), axis=0, tiled=True),
        lax.all_gather(w_up, ("dp", "ctx"), axis=0, tiled=True),
        lax.all_gather(w_down, ("dp", "ctx"), axis=0, tiled=True),
        lax.all_gather(gains, ("dp", "ctx"), axis=0, tiled=True),
    )
    full_query, full_key, full_value, full_out, full_gate, full_up, full_down, full_gains = gathered
    gain_attn, gain_mlp, gain_query, key_norm_gain = split_gains(full_gains)
    normalized_input = row_norm_apply(inputs, gain_attn).astype(brain_float_half)
    query_raw = jnp.dot(normalized_input, full_query, preferred_element_type=f32)
    unrotated_keys = jnp.dot(normalized_input, full_key, preferred_element_type=f32)
    value_low = (
        jnp.dot(normalized_input, full_value, preferred_element_type=f32)
        .astype(brain_float_half)
        .reshape(sequence_count, device_local_rows, KEY_VALUE_HEADS * HEAD_SIZE)
    )
    reduced_queries = heads_per_group(query_raw, gain_query, token_positions, QUERY_HEADS).astype(
        brain_float_half
    )
    key_low = (
        heads_per_group(unrotated_keys, key_norm_gain, token_positions, KEY_VALUE_HEADS)
        .astype(brain_float_half)
        .reshape(sequence_count, device_local_rows, KEY_VALUE_HEADS * HEAD_SIZE)
    )
    segment_low = segment_ids.astype(brain_float_half)
    gathered_keys, gathered_values, segment_all = (
        lax.all_gather(key_low, "ctx", axis=1, tiled=True),
        lax.all_gather(value_low, "ctx", axis=1, tiled=True),
        lax.all_gather(segment_low, "ctx", axis=1, tiled=True),
    )
    overall_rows = gathered_keys.shape[1]
    query_index = lax.axis_index("ctx") * device_local_rows + jnp.arange(
        device_local_rows, dtype=jnp.int32
    )
    key_index = jnp.arange(overall_rows, dtype=jnp.int32)
    allowed = (segment_low[:, :, None] == segment_all[:, None, :]) & (
        query_index[None, :, None] >= key_index[None, None, :]
    )
    grouped_queries = reduced_queries.reshape(
        sequence_count, device_local_rows, KEY_VALUE_HEADS, head_groups, HEAD_SIZE
    ).transpose(0, 2, 3, 1, 4)
    grouped_keys = gathered_keys.reshape(
        sequence_count, overall_rows, KEY_VALUE_HEADS, HEAD_SIZE
    ).transpose(0, 2, 1, 3)
    grouped_values = gathered_values.reshape(
        sequence_count, overall_rows, KEY_VALUE_HEADS, HEAD_SIZE
    ).transpose(0, 2, 1, 3)

    def masked_scores(query_head, key_head, mask_rows):
        scores = (
            jnp.einsum("rld,kd->rlk", query_head, key_head, preferred_element_type=f32)
            * score_scale
        )
        return jnp.where(mask_rows[None], scores, -1e30)

    def forward_sequence(slices):
        query_seq, key_seq, value_seq, mask_rows = slices

        def forward_head(head_slices):
            query_head, key_head, value_head = head_slices
            scores = masked_scores(query_head, key_head, mask_rows)
            row_peak = jnp.max(scores, axis=-1, keepdims=True)
            exp_scores = jnp.exp(scores - row_peak)
            denominator = jnp.sum(exp_scores, axis=-1, keepdims=True)
            prob_low = (exp_scores / denominator).astype(brain_float_half)
            mixed_head = jnp.einsum("rlk,kd->rld", prob_low, value_head, preferred_element_type=f32)
            return (mixed_head, row_peak[..., 0] + jnp.log(denominator[..., 0]))

        return lax.map(forward_head, (query_seq, key_seq, value_seq))

    mixed_heads, log_totals = lax.map(
        forward_sequence, (grouped_queries, grouped_keys, grouped_values, allowed)
    )
    attended = (
        mixed_heads.transpose(0, 3, 1, 2, 4)
        .reshape(every_row_set, QUERY_HEADS * HEAD_SIZE)
        .astype(brain_float_half)
    )
    middle = inputs + jnp.dot(attended, full_out, preferred_element_type=f32)
    normed_mlp = row_norm_apply(middle, gain_mlp).astype(brain_float_half)
    gate_value = jnp.dot(normed_mlp, full_gate, preferred_element_type=f32)
    up_value = jnp.dot(normed_mlp, full_up, preferred_element_type=f32)
    hidden = (jax.nn.silu(gate_value) * up_value).astype(brain_float_half)
    output = (middle + jnp.dot(hidden, full_down, preferred_element_type=f32)).astype(
        brain_float_half
    )
    regathered = (
        lax.all_gather(w_query, ("dp", "ctx"), axis=0, tiled=True),
        lax.all_gather(key_weight, ("dp", "ctx"), axis=0, tiled=True),
        lax.all_gather(value_weight, ("dp", "ctx"), axis=0, tiled=True),
        lax.all_gather(w_out, ("dp", "ctx"), axis=0, tiled=True),
        lax.all_gather(w_gate, ("dp", "ctx"), axis=0, tiled=True),
        lax.all_gather(w_up, ("dp", "ctx"), axis=0, tiled=True),
        lax.all_gather(w_down, ("dp", "ctx"), axis=0, tiled=True),
        lax.all_gather(gains, ("dp", "ctx"), axis=0, tiled=True),
    )
    back_query, back_key, back_value, back_out, back_gate, back_up, back_down, back_gains = (
        regathered
    )
    gain_attn, gain_mlp, gain_query, key_norm_gain = split_gains(back_gains)
    d_hidden = jnp.einsum("ld,fd->lf", cot_rows, back_down, preferred_element_type=f32)
    grad_down = jnp.einsum("lf,ld->fd", hidden, cot_rows, preferred_element_type=f32)
    unused, swiglu_pull = jax.vjp(
        lambda gate_in, up_in: jax.nn.silu(gate_in) * up_in, gate_value, up_value
    )
    d_gate, d_up = swiglu_pull(d_hidden)
    d_gate = d_gate.astype(brain_float_half)
    d_up = d_up.astype(brain_float_half)
    grad_gate = jnp.einsum("ld,lf->df", normed_mlp, d_gate, preferred_element_type=f32)
    grad_up = jnp.einsum("ld,lf->df", normed_mlp, d_up, preferred_element_type=f32)
    d_normed = jnp.einsum("lf,df->ld", d_gate, back_gate, preferred_element_type=f32)
    d_normed = d_normed + jnp.einsum("lf,df->ld", d_up, back_up, preferred_element_type=f32)
    unused, norm_pull = jax.vjp(row_norm_apply, middle, gain_mlp)
    d_middle, d_gain_mlp = norm_pull(d_normed)
    d_middle = d_middle + cot_rows.astype(f32)
    d_branch = d_middle.astype(brain_float_half)
    grad_out = jnp.einsum("lh,ld->hd", attended, d_branch, preferred_element_type=f32)
    attended_gradient = jnp.einsum(
        "ld,hd->lh", d_branch, back_out, preferred_element_type=f32
    ).astype(brain_float_half)
    group_gradient = attended_gradient.reshape(
        sequence_count, device_local_rows, KEY_VALUE_HEADS, head_groups, HEAD_SIZE
    ).transpose(0, 2, 3, 1, 4)

    def backward_sequence(slices):
        query_seq, key_seq, value_seq, d_seq, log_seq, mask_rows = slices

        def backward_head(head_slices):
            query_head, key_head, value_head, d_head, log_total = head_slices
            scores = masked_scores(query_head, key_head, mask_rows)
            probs_full = jnp.exp(scores - log_total[..., None])
            prob_low = probs_full.astype(brain_float_half)
            d_value = jnp.einsum("rlk,rld->kd", prob_low, d_head, preferred_element_type=f32)
            d_probs = jnp.einsum("rld,kd->rlk", d_head, value_head, preferred_element_type=f32)
            d_scores = probs_full * (
                d_probs - jnp.sum(probs_full * d_probs, axis=-1, keepdims=True)
            )
            d_scores = d_scores.astype(brain_float_half)
            d_query = (
                jnp.einsum("rlk,kd->rld", d_scores, key_head, preferred_element_type=f32)
                * score_scale
            )
            d_key = (
                jnp.einsum("rlk,rld->kd", d_scores, query_head, preferred_element_type=f32)
                * score_scale
            )
            return (d_query, d_key, d_value)

        return lax.map(backward_head, (query_seq, key_seq, value_seq, d_seq, log_seq))

    d_queries, key_rows_gradient, value_rows_gradient = lax.map(
        backward_sequence,
        (grouped_queries, grouped_keys, grouped_values, group_gradient, log_totals, allowed),
    )
    gathered_key_gradient = key_rows_gradient.transpose(2, 0, 1, 3).reshape(
        overall_rows, sequence_count, KEY_VALUE_HEADS * HEAD_SIZE
    )
    gathered_value_gradient = value_rows_gradient.transpose(2, 0, 1, 3).reshape(
        overall_rows, sequence_count, KEY_VALUE_HEADS * HEAD_SIZE
    )
    local_key_gradient, local_value_gradient = (
        lax.psum_scatter(
            gathered_key_gradient.astype(jnp.bfloat16), "ctx", scatter_dimension=0, tiled=True
        ).astype(jnp.float32),
        lax.psum_scatter(
            gathered_value_gradient.astype(jnp.bfloat16), "ctx", scatter_dimension=0, tiled=True
        ).astype(jnp.float32),
    )
    local_key_gradient = local_key_gradient.transpose(1, 0, 2)
    local_value_gradient = local_value_gradient.transpose(1, 0, 2)
    d_query_heads = d_queries.transpose(0, 3, 1, 2, 4).reshape(
        every_row_set, QUERY_HEADS, HEAD_SIZE
    )
    unused, query_pull = jax.vjp(
        lambda unnormalized_input, input_gain_vector: heads_per_group(
            unnormalized_input, input_gain_vector, token_positions, QUERY_HEADS
        ),
        query_raw,
        gain_query,
    )
    d_query_raw, d_gain_query = query_pull(d_query_heads)
    unused, key_pullback = jax.vjp(
        lambda unnormalized_input, input_gain_vector: heads_per_group(
            unnormalized_input, input_gain_vector, token_positions, KEY_VALUE_HEADS
        ),
        unrotated_keys,
        key_norm_gain,
    )
    unrotated_key_gradient, key_gain_gradient = key_pullback(
        local_key_gradient.reshape(every_row_set, KEY_VALUE_HEADS, HEAD_SIZE)
    )
    d_query_low = d_query_raw.astype(brain_float_half)
    d_key_low = unrotated_key_gradient.astype(brain_float_half)
    reduced_value_gradient = local_value_gradient.reshape(
        every_row_set, KEY_VALUE_HEADS * HEAD_SIZE
    ).astype(brain_float_half)
    grad_query = jnp.einsum("ld,lh->dh", normalized_input, d_query_low, preferred_element_type=f32)
    grad_key = jnp.einsum("ld,lh->dh", normalized_input, d_key_low, preferred_element_type=f32)
    grad_value = jnp.einsum(
        "ld,lh->dh", normalized_input, reduced_value_gradient, preferred_element_type=f32
    )
    d_normed_attn = jnp.einsum("lh,dh->ld", d_query_low, back_query, preferred_element_type=f32)
    d_normed_attn = d_normed_attn + jnp.einsum(
        "lh,dh->ld", d_key_low, back_key, preferred_element_type=f32
    )
    d_normed_attn = d_normed_attn + jnp.einsum(
        "lh,dh->ld", reduced_value_gradient, back_value, preferred_element_type=f32
    )
    unused, first_pull = jax.vjp(row_norm_apply, inputs, gain_attn)
    d_inputs, d_gain_attn = first_pull(d_normed_attn)
    grad_tokens = (d_middle + d_inputs).reshape(sequence_count, device_local_rows, MODEL_WIDTH)
    grad_gains = jnp.concatenate([d_gain_attn, d_gain_mlp, d_gain_query, key_gain_gradient])
    summed = (
        lax.psum_scatter(
            owner_major(grad_query, owners), ("dp", "ctx"), scatter_dimension=0, tiled=True
        ),
        lax.psum_scatter(
            owner_major(grad_key, owners), ("dp", "ctx"), scatter_dimension=0, tiled=True
        ),
        lax.psum_scatter(
            owner_major(grad_value, owners), ("dp", "ctx"), scatter_dimension=0, tiled=True
        ),
        lax.psum_scatter(
            owner_major(grad_out, owners), ("dp", "ctx"), scatter_dimension=0, tiled=True
        ),
        lax.psum_scatter(
            owner_major(grad_gate, owners), ("dp", "ctx"), scatter_dimension=0, tiled=True
        ),
        lax.psum_scatter(
            owner_major(grad_up, owners), ("dp", "ctx"), scatter_dimension=0, tiled=True
        ),
        lax.psum_scatter(
            owner_major(grad_down, owners), ("dp", "ctx"), scatter_dimension=0, tiled=True
        ),
        lax.psum_scatter(
            owner_major(grad_gains, owners), ("dp", "ctx"), scatter_dimension=0, tiled=True
        ),
    )
    grad_query = summed[0].reshape(shard_shapes[0])
    grad_key = summed[1].reshape(shard_shapes[1])
    grad_value = summed[2].reshape(shard_shapes[2])
    grad_out = summed[3].reshape(shard_shapes[3])
    grad_gate = summed[4].reshape(shard_shapes[4])
    grad_up = summed[5].reshape(shard_shapes[5])
    grad_down = summed[6].reshape(shard_shapes[6])
    grad_gains = summed[7].reshape(shard_shapes[7])
    return (
        output.reshape(sequence_count, device_local_rows, MODEL_WIDTH),
        grad_tokens,
        grad_query,
        grad_key,
        grad_value,
        grad_out,
        grad_gate,
        grad_up,
        grad_down,
        grad_gains,
    )

FEATURES = 128
MASK_DEPTH = -4096.0
LOG2_E = 1.4426950408889634
VMEM_BYTES = 56 * 1024 * 1024
bf16 = jnp.bfloat16
f32 = jnp.float32


def xor_permute(value, axis, offset):
    size = lax.axis_size(axis)
    return lax.ppermute(value, axis, [(i, i ^ offset) for i in range(size)])


def pick(stacked, index):
    return lax.dynamic_index_in_dim(stacked, index, 0, keepdims=False)


def exchange(stacked, me):
    size = stacked.shape[0]
    relative = [pick(stacked, me)]
    for offset in range(1, size):
        relative.append(xor_permute(pick(stacked, me ^ offset), "ctx", offset))
    arrived = relative[1:]
    relative = jnp.stack(relative)
    return jnp.stack([pick(relative, me ^ source) for source in range(size)]), arrived


def shift_z(value, offset):
    size = lax.axis_size("dp")
    return lax.ppermute(value, "dp", [(i, (i + 2 * offset) % size) for i in range(size)])


def assemble_kernel(splits, count, places_ref, *refs):
    pieces, results, sems = refs[:count], refs[count:-1], refs[-1]
    copies = []
    for n, piece in enumerate(pieces):
        start = 0
        for m, rows in enumerate(splits):
            copy = pltpu.make_async_copy(
                piece.at[pl.ds(start, rows)], results[m].at[places_ref[n]], sems.at[n, m]
            )
            copy.start()
            copies.append(copy)
            start += rows
    for copy in copies:
        copy.wait()


def assemble(pieces, places, splits=None):
    count = len(pieces)
    rows, columns = pieces[0].shape
    splits = (rows,) if splits is None else splits
    anywhere = pl.BlockSpec(memory_space=pl.ANY)
    results = pl.pallas_call(
        functools.partial(assemble_kernel, splits, count),
        in_specs=[pl.BlockSpec(memory_space=pltpu.SMEM)]
        + [pl.BlockSpec(memory_space=pltpu.VMEM)] * count,
        out_specs=[anywhere] * len(splits),
        out_shape=[jax.ShapeDtypeStruct((count, n, columns), pieces[0].dtype) for n in splits],
        scratch_shapes=[pltpu.SemaphoreType.DMA((count, len(splits)))],
        compiler_params=pltpu.CompilerParams(vmem_limit_bytes=VMEM_BYTES),
        cost_estimate=pl.CostEstimate(
            flops=0, bytes_accessed=4 * count * rows * columns, transcendentals=0
        ),
        name="assemble",
    )(places.astype(jnp.int32), *pieces)
    return [result.reshape(-1, columns) for result in results]


def join(blocks):
    return assemble(blocks, jnp.arange(len(blocks)))[0]


def gather_copies(value):
    depth = lax.axis_size("dp") // 2
    at = lax.axis_index("dp")
    along = [value] + [shift_z(value, k) for k in range(1, depth)]
    beside = [xor_permute(piece, "dp", 1) for piece in along]
    rows = jnp.stack([(at // 2 - k) % depth for k in range(depth)])
    places = jnp.concatenate([rows * 2 + at % 2, rows * 2 + 1 - at % 2])
    return along + beside, places


def reduce_beside(grad):
    depth = grad.shape[0] // 2
    y = lax.axis_index("dp") % 2
    grad = grad.reshape((depth, 2) + grad.shape[1:])
    away = lax.dynamic_index_in_dim(grad, 1 - y, 1, keepdims=False)
    kept = lax.dynamic_index_in_dim(grad, y, 1, keepdims=False)
    return (kept.astype(f32) + xor_permute(away, "dp", 1).astype(f32)).astype(bf16)


def reduce_along(pair):
    depth = pair.shape[0]
    z = lax.axis_index("dp") // 2
    sent = [shift_z(pick(pair, (z + k) % depth), k) for k in range(1, depth)]
    return [pick(pair, z)] + sent


def add_all(terms):
    total = terms[0].astype(f32)
    for term in terms[1:]:
        total = total + term.astype(f32)
    return total.astype(bf16)


def after(value, *others):
    return lax.optimization_barrier((value, *others))[0]


def gather_blocks(value):
    across = xor_permute(value, "ctx", 2)
    beside = xor_permute(value, "ctx", 1)
    corner = xor_permute(across, "ctx", 1)
    return [value, beside, across, corner]


def gather_near(value):
    return [value, xor_permute(value, "ctx", 1)], xor_permute(value, "ctx", 2)


def gather_far(across, *waits):
    across = after(across, *waits)
    return [across, xor_permute(across, "ctx", 1)]


def send_across(part_corner, part_across, *waits):
    corner = xor_permute(part_corner.astype(bf16), "ctx", 1)
    toward = (part_across.astype(f32) + corner.astype(f32)).astype(bf16)
    toward = after(toward, *waits) if waits else toward
    return toward, xor_permute(toward, "ctx", 2)


def sum_own(part_beside, part_own, across):
    beside = xor_permute(part_beside.astype(bf16), "ctx", 1)
    return part_own.astype(f32) + beside.astype(f32) + across.astype(f32)


def nt_dot(left, right):
    return lax.dot_general(left, right, (((1,), (1,)), ((), ())), preferred_element_type=f32)


def nn_dot(left, right):
    return jnp.dot(left, right, preferred_element_type=f32)


def project_kernel(
    query_heads,
    key_heads,
    per_block,
    x_refs,
    gain_ref,
    weight_ref,
    cos_ref,
    sin_ref,
    gain_q_ref,
    gain_k_ref,
    normed_ref,
    raw_ref,
    q_ref,
    k_ref,
    v_ref,
    held_ref,
):
    for r, x_ref in enumerate(x_refs):

        @pl.when(pl.program_id(0) // per_block == r)
        def _():
            held_ref[...] = x_ref[...]

    x = held_ref[...].astype(f32)
    scale = lax.rsqrt(jnp.mean(x * x, axis=-1, keepdims=True) + EPSILON)
    normed = (x * scale * gain_ref[...]).astype(bf16)
    normed_ref[...] = normed
    raw = nn_dot(normed, weight_ref[...])
    turned = (query_heads + key_heads) * HEAD_SIZE
    raw_ref[...] = raw[:, :turned]
    v_ref[...] = raw[:, turned:].astype(bf16)
    cosine = cos_ref[...]
    sine = sin_ref[...]
    for head in range(query_heads + key_heads):
        rows = raw[:, head * HEAD_SIZE : (head + 1) * HEAD_SIZE]
        gain = gain_q_ref[...] if head < query_heads else gain_k_ref[...]
        rows = rows * lax.rsqrt(jnp.mean(rows * rows, axis=-1, keepdims=True) + EPSILON) * gain
        rows = (rows * cosine + pltpu.roll(rows, HEAD_SIZE // 2, 1) * sine).astype(bf16)
        if head < query_heads:
            q_ref[:, head * HEAD_SIZE : (head + 1) * HEAD_SIZE] = rows
        else:
            at = (head - query_heads) * HEAD_SIZE
            k_ref[:, at : at + HEAD_SIZE] = rows


def project(x_blocks, gain, weight, cosine, sine, gain_q, gain_k, query_heads, key_heads):
    rows, width = x_blocks[0].shape
    block = 256
    per_block = rows // block
    rows = rows * len(x_blocks)
    turned = (query_heads + key_heads) * HEAD_SIZE
    columns = weight.shape[1]

    def tall(n):
        return pl.BlockSpec((block, n), lambda i: (i, 0))

    def whole(shape):
        return pl.BlockSpec(shape, lambda i: (0, 0))

    def part(r):
        return pl.BlockSpec(
            (block, width), lambda i: (jnp.clip(i - r * per_block, 0, per_block - 1), 0)
        )

    return pl.pallas_call(
        functools.partial(project_kernel, query_heads, key_heads, per_block),
        grid=(rows // block,),
        in_specs=[
            [part(r) for r in range(len(x_blocks))],
            whole((1, width)),
            whole(weight.shape),
            tall(HEAD_SIZE),
            tall(HEAD_SIZE),
            whole((1, HEAD_SIZE)),
            whole((1, HEAD_SIZE)),
        ],
        out_specs=[
            tall(width),
            tall(turned),
            tall(query_heads * HEAD_SIZE),
            tall(key_heads * HEAD_SIZE),
            tall(key_heads * HEAD_SIZE),
        ],
        out_shape=[
            jax.ShapeDtypeStruct((rows, width), bf16),
            jax.ShapeDtypeStruct((rows, turned), f32),
            jax.ShapeDtypeStruct((rows, query_heads * HEAD_SIZE), bf16),
            jax.ShapeDtypeStruct((rows, key_heads * HEAD_SIZE), bf16),
            jax.ShapeDtypeStruct((rows, key_heads * HEAD_SIZE), bf16),
        ],
        scratch_shapes=[pltpu.VMEM((block, width), bf16)],
        compiler_params=pltpu.CompilerParams(vmem_limit_bytes=VMEM_BYTES),
        cost_estimate=pl.CostEstimate(
            flops=2 * rows * width * columns,
            bytes_accessed=rows * (4 * width + 4 * turned + 2 * columns) + 2 * width * columns,
            transcendentals=0,
        ),
        name="project",
    )(list(x_blocks), gain, weight, cosine, sine, gain_q, gain_k)


def unproject_kernel(
    query_heads,
    key_heads,
    half,
    dq_near_ref,
    dq_far_ref,
    dk_ref,
    dv_ref,
    raw_ref,
    cos_ref,
    sin_ref,
    gain_q_ref,
    gain_k_ref,
    low_ref,
    dgain_ref,
):
    @pl.when(pl.program_id(0) == 0)
    def _():
        dgain_ref[...] = jnp.zeros_like(dgain_ref)

    cosine = cos_ref[...]
    sine = sin_ref[...]
    total_q = jnp.zeros((1, HEAD_SIZE), f32)
    total_k = jnp.zeros((1, HEAD_SIZE), f32)
    for head in range(query_heads + key_heads):
        at = head * HEAD_SIZE
        raw = raw_ref[:, at : at + HEAD_SIZE]
        if head < query_heads:
            lanes = slice(at, at + HEAD_SIZE)
            grad = jnp.where(pl.program_id(0) < half, dq_near_ref[:, lanes], dq_far_ref[:, lanes])
            gain = gain_q_ref[...]
        else:
            back = (head - query_heads) * HEAD_SIZE
            grad = dk_ref[:, back : back + HEAD_SIZE]
            gain = gain_k_ref[...]
        grad = grad * cosine - pltpu.roll(grad, HEAD_SIZE // 2, 1) * sine
        scale = lax.rsqrt(jnp.mean(raw * raw, axis=-1, keepdims=True) + EPSILON)
        unit = raw * scale
        summed = jnp.sum(unit * grad, axis=0, keepdims=True)
        if head < query_heads:
            total_q += summed
        else:
            total_k += summed
        grad = grad * gain
        mean = jnp.mean(unit * grad, axis=-1, keepdims=True)
        low_ref[:, at : at + HEAD_SIZE] = (scale * (grad - unit * mean)).astype(bf16)
    low_ref[:, (query_heads + key_heads) * HEAD_SIZE :] = dv_ref[...].astype(bf16)
    dgain_ref[0:1, :] += total_q
    dgain_ref[1:2, :] += total_k


def unproject(dq_near, dq_far, dk, dv, raw, cosine, sine, gain_q, gain_k, query_heads, key_heads):
    rows = dk.shape[0]
    block = 256
    half = rows // block // 2
    columns = (query_heads + 2 * key_heads) * HEAD_SIZE

    def tall(n):
        return pl.BlockSpec((block, n), lambda i: (i, 0))

    def whole(shape):
        return pl.BlockSpec(shape, lambda i: (0, 0))

    return pl.pallas_call(
        functools.partial(unproject_kernel, query_heads, key_heads, half),
        grid=(rows // block,),
        in_specs=[
            pl.BlockSpec((block, dq_near.shape[1]), lambda i: (jnp.minimum(i, half - 1), 0)),
            pl.BlockSpec((block, dq_far.shape[1]), lambda i: (jnp.maximum(i - half, 0), 0)),
            tall(dk.shape[1]),
            tall(dv.shape[1]),
            tall(raw.shape[1]),
            tall(HEAD_SIZE),
            tall(HEAD_SIZE),
            whole((1, HEAD_SIZE)),
            whole((1, HEAD_SIZE)),
        ],
        out_specs=[tall(columns), whole((8, HEAD_SIZE))],
        out_shape=[
            jax.ShapeDtypeStruct((rows, columns), bf16),
            jax.ShapeDtypeStruct((8, HEAD_SIZE), f32),
        ],
        compiler_params=pltpu.CompilerParams(vmem_limit_bytes=VMEM_BYTES),
        cost_estimate=pl.CostEstimate(
            flops=20 * rows * columns, bytes_accessed=10 * rows * columns, transcendentals=0
        ),
        name="unproject",
    )(dq_near, dq_far, dk, dv, raw, cosine, sine, gain_q, gain_k)


def attend_kernel(
    group, block, first, me_ref, q_ref, qf_ref, k_ref, kf_ref, v_ref, o_ref, log_ref, total_ref
):
    me = me_ref[0]
    at_query = (pl.program_id(1) + first) ^ me
    factor = HEAD_SIZE ** (-0.5) * LOG2_E
    query_features = qf_ref[...]
    ones = jnp.ones((block, HEAD_SIZE), bf16)
    total_ref[...] = jnp.zeros_like(total_ref)

    def step(at_key, diagonal):
        rows = pl.ds(pl.multiple_of((at_key ^ me) * block, block), block)
        keys = jnp.concatenate([k_ref[rows, :], kf_ref[rows, :]], axis=1)
        values = jnp.concatenate([v_ref[rows, :], ones], axis=1)
        for head in range(group):
            query = q_ref[:, head * HEAD_SIZE : (head + 1) * HEAD_SIZE]
            scores = nt_dot(jnp.concatenate([query, query_features], axis=1), keys)
            probs = jnp.exp2(scores * factor)
            if diagonal:
                down = lax.broadcasted_iota(jnp.int32, probs.shape, 0)
                right = lax.broadcasted_iota(jnp.int32, probs.shape, 1)
                probs = jnp.where(down >= right, probs, 0.0)
            total_ref[head] += nn_dot(probs.astype(bf16), values)

    @pl.loop(0, at_query)
    def _(at_key):
        step(at_key, False)

    step(at_query, True)
    for head in range(group):
        weighted = total_ref[head, :, :HEAD_SIZE]
        summed = total_ref[head, :, HEAD_SIZE:]
        o_ref[:, head * HEAD_SIZE : (head + 1) * HEAD_SIZE] = (weighted / summed).astype(bf16)
        log_ref[0, head : head + 1, :] = jnp.log2(summed.T[0:1, :])


def attend(me, q, qf, k, kf, v, block, group, first, count):
    rows = k.shape[0]
    key_heads = k.shape[1] // HEAD_SIZE
    pairs = key_heads * group * count * block * rows * 5 // 8
    return pl.pallas_call(
        functools.partial(attend_kernel, group, block, first),
        grid_spec=pltpu.PrefetchScalarGridSpec(
            num_scalar_prefetch=1,
            grid=(key_heads, count),
            in_specs=[
                pl.BlockSpec((block, group * HEAD_SIZE), lambda g, i, me: (i + first, g)),
                pl.BlockSpec((block, FEATURES), lambda g, i, me: (i + first, 0)),
                pl.BlockSpec((rows, HEAD_SIZE), lambda g, i, me: (0, g)),
                pl.BlockSpec((rows, FEATURES), lambda g, i, me: (0, 0)),
                pl.BlockSpec((rows, HEAD_SIZE), lambda g, i, me: (0, g)),
            ],
            out_specs=[
                pl.BlockSpec((block, group * HEAD_SIZE), lambda g, i, me: (i, g)),
                pl.BlockSpec((1, group, block), lambda g, i, me: (g, 0, i)),
            ],
            scratch_shapes=[pltpu.VMEM((group, block, 2 * HEAD_SIZE), f32)],
        ),
        out_shape=[
            jax.ShapeDtypeStruct((count * block, q.shape[1]), bf16),
            jax.ShapeDtypeStruct((key_heads, group, count * block), f32),
        ],
        compiler_params=pltpu.CompilerParams(vmem_limit_bytes=VMEM_BYTES),
        cost_estimate=pl.CostEstimate(
            flops=8 * pairs * HEAD_SIZE, bytes_accessed=10 * q.size, transcendentals=pairs
        ),
        name="attend",
    )(me, q, qf, k, kf, v)


def unattend_kernel(
    group,
    block,
    first,
    resumed,
    me_ref,
    q_ref,
    qf_ref,
    k_ref,
    kf_ref,
    v_ref,
    o_ref,
    branch_first_ref,
    branch_second_ref,
    out_ref,
    log_ref,
    *rest,
):
    if resumed:
        dk_in_ref, dv_in_ref, d_weight_in_ref, *rest = rest
    dq_ref, dk_ref, dv_ref, d_weight_ref, flipped_ref, total_ref, do_ref = rest
    me = me_ref[0]
    at_query = (pl.program_id(1) + first) ^ me
    scale = HEAD_SIZE ** (-0.5)
    factor = scale * LOG2_E

    @pl.when(pl.program_id(1) == 0)
    def _():
        dk_ref[...] = dk_in_ref[...] if resumed else jnp.zeros_like(dk_ref)
        dv_ref[...] = dv_in_ref[...] if resumed else jnp.zeros_like(dv_ref)
        d_weight_ref[...] = d_weight_in_ref[...] if resumed else jnp.zeros_like(d_weight_ref)
        flipped_ref[...] = k_ref[...].astype(f32).T.astype(bf16)

    def take(branch_ref):
        do_ref[...] = nt_dot(branch_ref[...], out_ref[...]).astype(bf16)
        turned = o_ref[...].astype(f32).T.astype(bf16)
        d_weight_ref[...] += nn_dot(turned, branch_ref[...])

    @pl.when(pl.program_id(1) == 0)
    def _():
        take(branch_first_ref)

    @pl.when(pl.program_id(1) == 1)
    def _():
        take(branch_second_ref)

    total_ref[...] = jnp.zeros_like(total_ref)
    query_features = qf_ref[...]
    deltas = []
    for head in range(group):
        lanes = slice(head * HEAD_SIZE, (head + 1) * HEAD_SIZE)
        product = do_ref[:, lanes].astype(f32) * o_ref[:, lanes].astype(f32)
        deltas.append(jnp.sum(product.T, axis=0, keepdims=True))

    def step(at_key, diagonal):
        start = pl.multiple_of((at_key ^ me) * block, block)
        rows = pl.ds(start, block)
        keys = jnp.concatenate([k_ref[rows, :], kf_ref[rows, :]], axis=1)
        values = v_ref[rows, :]
        for head in range(group):
            lanes = slice(head * HEAD_SIZE, (head + 1) * HEAD_SIZE)
            query = q_ref[:, lanes]
            d_out = do_ref[:, lanes]
            scores = nt_dot(keys, jnp.concatenate([query, query_features], axis=1))
            probs = jnp.exp2(scores * factor - log_ref[0, head : head + 1, :])
            if diagonal:
                key_at = lax.broadcasted_iota(jnp.int32, probs.shape, 0)
                query_at = lax.broadcasted_iota(jnp.int32, probs.shape, 1)
                probs = jnp.where(query_at >= key_at, probs, 0.0)
            d_scores = (probs * (nt_dot(values, d_out) - deltas[head])).astype(bf16)
            dv_ref[rows, :] += nn_dot(probs.astype(bf16), d_out)
            dk_ref[rows, :] += nn_dot(d_scores, query)
            total_ref[head] += nn_dot(flipped_ref[:, rows], d_scores)

    @pl.loop(0, at_query)
    def _(at_key):
        step(at_key, False)

    step(at_query, True)
    for head in range(group):
        dq_ref[:, head * HEAD_SIZE : (head + 1) * HEAD_SIZE] = total_ref[head].T * scale

    if resumed:

        @pl.when(pl.program_id(1) == pl.num_programs(1) - 1)
        def _():
            dk_ref[...] = dk_ref[...] * scale


def unattend(me, q, qf, k, kf, v, o, branches, out, logs, block, group, first, earlier=()):
    count = len(branches)
    rows = k.shape[0]
    key_heads = k.shape[1] // HEAD_SIZE
    width = out.shape[1]
    lanes = group * HEAD_SIZE
    pairs = key_heads * group * count * block * rows * 5 // 8

    def by_query(n):
        return pl.BlockSpec((block, n), lambda g, i, me: (i, g))

    by_key = pl.BlockSpec((rows, HEAD_SIZE), lambda g, i, me: (0, g))
    by_head = pl.BlockSpec((lanes, width), lambda g, i, me: (g, 0))
    whole = pl.BlockSpec((block, width), lambda g, i, me: (0, 0))
    return pl.pallas_call(
        functools.partial(unattend_kernel, group, block, first, bool(earlier)),
        grid_spec=pltpu.PrefetchScalarGridSpec(
            num_scalar_prefetch=1,
            grid=(key_heads, count),
            in_specs=[
                pl.BlockSpec((block, lanes), lambda g, i, me: (i + first, g)),
                pl.BlockSpec((block, FEATURES), lambda g, i, me: (i + first, 0)),
                by_key,
                pl.BlockSpec((rows, FEATURES), lambda g, i, me: (0, 0)),
                by_key,
                by_query(lanes),
                whole,
                whole,
                by_head,
                pl.BlockSpec((1, group, block), lambda g, i, me: (g, 0, i)),
            ]
            + ([by_key, by_key, by_head] if earlier else []),
            out_specs=[by_query(lanes), by_key, by_key, by_head],
            scratch_shapes=[
                pltpu.VMEM((HEAD_SIZE, rows), bf16),
                pltpu.VMEM((group, HEAD_SIZE, block), f32),
                pltpu.VMEM((block, lanes), bf16),
            ],
        ),
        out_shape=[
            jax.ShapeDtypeStruct((count * block, q.shape[1]), f32),
            jax.ShapeDtypeStruct(k.shape, f32),
            jax.ShapeDtypeStruct(v.shape, f32),
            jax.ShapeDtypeStruct(out.shape, f32),
        ],
        compiler_params=pltpu.CompilerParams(vmem_limit_bytes=VMEM_BYTES),
        cost_estimate=pl.CostEstimate(
            flops=14 * pairs * HEAD_SIZE, bytes_accessed=20 * q.size, transcendentals=pairs
        ),
        name="unattend",
    )(me, q, qf, k, kf, v, o, *branches, out, logs, *earlier)


def feed_kernel(
    units,
    half,
    first_ref,
    second_ref,
    cot_ref,
    both_ref,
    down_ref,
    h_ref,
    hidden_ref,
    d_both_ref,
    part_first_ref,
    part_second_ref,
    d_part_first_ref,
    d_part_second_ref,
):
    in_first = pl.program_id(0) < half

    @pl.when(in_first)
    def _():
        h_ref[...] = first_ref[...]

    @pl.when(jnp.logical_not(in_first))
    def _():
        h_ref[...] = second_ref[...]

    both = nn_dot(h_ref[...], both_ref[...])
    d_hidden = nt_dot(cot_ref[...], down_ref[...])
    gate, up = both[:, :units], both[:, units:]
    sigmoid = 1.0 / (1.0 + jnp.exp(-gate))
    silu = gate * sigmoid
    hidden = (silu * up).astype(bf16)
    hidden_ref[...] = hidden
    part = nn_dot(hidden, down_ref[...]).astype(bf16)
    d_gate = (d_hidden * up * sigmoid * (1.0 + gate * (1.0 - sigmoid))).astype(bf16)
    d_up = (d_hidden * silu).astype(bf16)
    d_both = jnp.concatenate([d_gate, d_up], axis=1)
    d_both_ref[...] = d_both
    d_part = nt_dot(d_both, both_ref[...]).astype(bf16)

    @pl.when(in_first)
    def _():
        part_first_ref[...] = part
        d_part_first_ref[...] = d_part

    @pl.when(jnp.logical_not(in_first))
    def _():
        part_second_ref[...] = part
        d_part_second_ref[...] = d_part


def feed(h_first, h_second, cot, both, down):
    rows, width = cot.shape
    units = down.shape[0]
    block = 256
    half = rows // block // 2

    def tall(n):
        return pl.BlockSpec((block, n), lambda i: (i, 0))

    def whole(shape):
        return pl.BlockSpec(shape, lambda i: (0, 0))

    of_first = pl.BlockSpec((block, width), lambda i: (jnp.minimum(i, half - 1), 0))
    of_second = pl.BlockSpec((block, width), lambda i: (jnp.maximum(i - half, 0), 0))
    shapes = [(rows, width), (rows, units), (rows, 2 * units)] + [(rows // 2, width)] * 4
    return pl.pallas_call(
        functools.partial(feed_kernel, units, half),
        grid=(rows // block,),
        in_specs=[of_first, of_second, tall(width), whole(both.shape), whole(down.shape)],
        out_specs=[tall(width), tall(units), tall(2 * units)] + [of_first, of_second] * 2,
        out_shape=[jax.ShapeDtypeStruct(shape, bf16) for shape in shapes],
        compiler_params=pltpu.CompilerParams(vmem_limit_bytes=VMEM_BYTES),
        cost_estimate=pl.CostEstimate(
            flops=12 * rows * width * units,
            bytes_accessed=rows * (10 * width + 6 * units) + 6 * width * units,
            transcendentals=rows * units,
        ),
        name="feed",
    )(h_first, h_second, cot, both, down)


def norm_back(value_rows, gain_vec, grad):
    scale = lax.rsqrt(jnp.mean(value_rows * value_rows, axis=-1, keepdims=True) + EPSILON)
    unit = value_rows * scale
    d_gain = jnp.sum(unit * grad, axis=0)
    grad = grad * gain_vec
    return scale * (grad - unit * jnp.mean(unit * grad, axis=-1, keepdims=True)), d_gain


def split_local(
    tokens,
    w_query,
    key_weight,
    value_weight,
    w_out,
    w_gate,
    w_up,
    w_down,
    gains,
    segment_ids,
    positions,
    cotangent,
):
    size = lax.axis_size("ctx")
    copies = lax.axis_size("dp")
    me = lax.axis_index("ctx")
    me_row = me.reshape(1).astype(jnp.int32)
    block = tokens.shape[1]
    group = QUERY_HEADS // KEY_VALUE_HEADS
    query_heads = QUERY_HEADS // size
    key_heads = KEY_VALUE_HEADS // size
    q_cols = query_heads * HEAD_SIZE
    k_cols = key_heads * HEAD_SIZE
    owned = w_query.shape[0]
    hidden_cols = w_gate.shape[1] // size
    gain_count = gains.shape[0]
    pad_rows = 16
    forward_owner = [
        (b, (b % copies) * size + b // copies) for b in range(size * copies)
    ]
    backward_owner = [(target, source) for source, target in forward_owner]

    def by_columns(weight):
        return weight.reshape(weight.shape[0], size, -1).transpose(1, 0, 2)

    first = jnp.concatenate(
        [by_columns(w_query), by_columns(key_weight), by_columns(value_weight)], axis=2
    )
    gain_rows = jnp.pad(gains[None], ((0, pad_rows - 1), (0, first.shape[2] - gain_count)))
    first = jnp.concatenate(
        [first, jnp.broadcast_to(gain_rows[None], (size,) + gain_rows.shape)], axis=1
    )
    first, arrived = exchange(first, me)
    gain_rows = jnp.concatenate(
        [first[:, owned], jnp.zeros((pad_rows - size, first.shape[2]), bf16)]
    )
    first = jnp.concatenate(
        [first[:, :owned].reshape(size * owned, first.shape[2]), gain_rows]
    )
    first_pieces, places_dp = gather_copies(first)
    early = first_pieces[1 : copies // 2]

    gate_up = jnp.concatenate([by_columns(w_gate), by_columns(w_up)], axis=2)
    gate_up, arrived = exchange(after(gate_up, *arrived), me)
    moved = after(jnp.concatenate([w_out, w_down]), *arrived)
    moved = lax.ppermute(moved, ("dp", "ctx"), forward_owner)
    places = jnp.concatenate([positions, segment_ids]).astype(jnp.int32)
    places = jnp.concatenate(gather_blocks(after(places, *arrived)), axis=1)
    x_own = tokens.reshape(block, MODEL_WIDTH)
    x_blocks = gather_blocks(after(x_own, *arrived))
    cot_own = cotangent.reshape(block, MODEL_WIDTH)
    cot_blocks = gather_blocks(after(cot_own, x_blocks[2]))
    cot_near, cot_far = join(cot_blocks[:2]), join(cot_blocks[2:])

    gate_up_rows = after(gate_up.reshape(size * owned, -1), *early)
    gate_up = lax.all_gather(gate_up_rows, "dp", axis=0, tiled=True)
    moved_pieces, unused = gather_copies(after(moved, *early))
    w_first, gain_rows = assemble(first_pieces, places_dp, (size * owned, pad_rows))
    w_first = after(w_first, gate_up_rows, *moved_pieces[1 : copies // 2])
    full_gains = gain_rows.reshape(copies, pad_rows, -1)[:, :size, :gain_count].reshape(-1)
    gain_attn, gain_mlp, gain_query, gain_key = split_gains(full_gains)

    half = HEAD_SIZE // 2
    rates = THETA ** (-2.0 * jnp.arange(half, dtype=f32) / HEAD_SIZE)
    angles = places[0].astype(f32)[:, None] * rates[None, :]
    cosine, sine = jnp.cos(angles), jnp.sin(angles)
    cosine = jnp.concatenate([cosine, cosine], axis=1)
    sine = jnp.concatenate([-sine, sine], axis=1)
    lane = jnp.arange(FEATURES, dtype=jnp.int32)[None, :]
    same = places[1][:, None] == lane
    key_features = same.astype(bf16)
    query_features = jnp.where(same, 0.0, MASK_DEPTH).astype(bf16)
    gain_q_row, gain_k_row = gain_query[None], gain_key[None]
    normed, raw, q, k, v = project(
        x_blocks, gain_attn[None], w_first, cosine, sine, gain_q_row, gain_k_row, query_heads, key_heads
    )
    def attend_half(query, first):
        return attend(
            me_row, query, query_features, k, key_features, v, block, group, first, 2
        )

    def halves(value):
        return value[:block], value[block:]

    q, cot_near, cot_far, *moved_pieces = lax.optimization_barrier(
        (q, cot_near, cot_far, *moved_pieces)
    )
    att_far, logs_far = attend_half(q, 2)
    out_full, down_full = assemble(moved_pieces, places_dp, (w_out.shape[0], w_down.shape[0]))
    att_across, att_corner = halves(att_far)
    part_corner, part_across = nn_dot(att_corner, out_full), nn_dot(att_across, out_full)
    toward, across = send_across(part_corner, part_across)
    att_near, logs_near = attend_half(after(q, toward, gate_up), 0)
    att_own, att_beside = halves(att_near)
    beside = [
        xor_permute(nn_dot(piece, out_full).astype(bf16), "ctx", 1)
        for piece in jnp.split(att_beside, 2)
    ]
    part_own = nn_dot(att_own, out_full) + jnp.concatenate(beside).astype(f32)
    middle = x_own.astype(f32) + part_own + across.astype(f32)
    h_blocks, across = gather_near(row_norm_apply(middle, gain_mlp).astype(bf16))
    h_near, hidden_near, d_both_near, down_own, down_beside, d_own, d_beside = feed(
        *h_blocks, cot_near, gate_up, down_full
    )
    h_blocks = gather_far(across, hidden_near)
    h_far, hidden_far, d_both_far, down_across, down_corner, d_across, d_corner = feed(
        *h_blocks, cot_far, gate_up, down_full
    )

    unused, across = send_across(d_corner, d_across)
    d_normed = sum_own(d_beside, d_own, across)
    d_middle, d_gain_mlp = norm_back(middle, gain_mlp, d_normed)
    d_middle = d_middle + cot_own.astype(f32)
    branches_near, branch_across = gather_near(d_middle.astype(bf16))

    def tn_dot(left, right):
        return lax.dot_general(left, right, (((0,), (0,)), ((), ())), preferred_element_type=f32)

    def by_copy(grad):
        return grad.astype(bf16).reshape(copies, -1, grad.shape[-1])

    grad_down = tn_dot(hidden_near, cot_near) + tn_dot(hidden_far, cot_far)
    grad_both = tn_dot(h_near, d_both_near) + tn_dot(h_far, d_both_far)
    grad_both = grad_both.astype(bf16)
    grad_down = grad_down.astype(bf16)
    d_both_sum = lax.psum_scatter(grad_both, "dp", scatter_dimension=0, tiled=True)
    d_down_sum = lax.psum_scatter(grad_down, "dp", scatter_dimension=0, tiled=True)

    def unattend_half(att, branches, logs, first, earlier=()):
        return unattend(
            me_row,
            q,
            query_features,
            k,
            key_features,
            v,
            att,
            branches,
            out_full,
            logs,
            block,
            group,
            first,
            earlier,
        )

    branches_near = [after(branches_near[0], grad_both, grad_down), branches_near[1]]
    dq_near, *earlier = unattend_half(att_near, branches_near, logs_near, 0)
    branches_far = gather_far(branch_across, dq_near)
    unused, across = send_across(down_corner, down_across, branches_far[0])
    output = (middle + sum_own(down_beside, down_own, across)).astype(bf16)
    dq_far, dk, dv, grad_out = unattend_half(att_far, branches_far, logs_far, 2, earlier)
    pair_out = reduce_beside(by_copy(grad_out))
    dk = after(dk, across)
    low, d_gain_heads = unproject(
        dq_near, dq_far, dk, dv, raw, cosine, sine, gain_q_row, gain_k_row, query_heads, key_heads
    )
    terms_out = reduce_along(after(pair_out, low))
    low_own, low_beside, low_across, low_corner = (
        low[r * block : (r + 1) * block] for r in range(size)
    )
    toward, across = send_across(nt_dot(low_corner, w_first), nt_dot(low_across, w_first))
    part_beside, part_own = nt_dot(low_beside, w_first), nt_dot(low_own, w_first)
    d_normed_attn = sum_own(part_beside, part_own, across)
    d_inputs, unused = norm_back(x_own.astype(f32), gain_attn, d_normed_attn)
    grad_tokens = (d_middle + d_inputs).reshape(tokens.shape)

    grad_first = tn_dot(normed, low).astype(bf16)
    d_gain_attn = jnp.sum(w_first.astype(f32) * grad_first.astype(f32), axis=1) / gain_attn
    grad_gains = jnp.concatenate(
        [d_gain_attn, d_gain_mlp, d_gain_heads[0], d_gain_heads[1]]
    ).reshape(copies, size, gain_count)
    gain_block = jnp.pad(
        grad_gains.astype(bf16),
        ((0, 0), (0, pad_rows - size), (0, grad_first.shape[1] - gain_count)),
    )
    grad_first = jnp.concatenate(
        [grad_first.reshape(copies, size * owned, -1), gain_block], axis=1
    )
    pair_first = reduce_beside(grad_first)
    d_both_sum = after(d_both_sum, pair_first)
    terms_first = reduce_along(after(pair_first, across))
    d_down_sum = after(d_down_sum, *terms_first)
    grad_first = add_all(terms_first)
    grad_out = add_all(after(terms_out, *terms_first))
    gain_part = grad_first[size * owned :][:size]
    gain_part = jnp.broadcast_to(gain_part[:, None], (size, pad_rows, gain_part.shape[1]))
    grad_first = jnp.concatenate(
        [grad_first[: size * owned].reshape(size, owned, -1), gain_part], axis=1
    )
    grad_first = exchange(grad_first, me)[0].astype(f32)
    grad_gains = jnp.sum(grad_first[:, owned, :gain_count], axis=0)
    grad_first = grad_first[:, :owned]

    def to_rows(pieces):
        return pieces.transpose(1, 0, 2).reshape(owned, -1)

    grad_query = to_rows(grad_first[:, :, :q_cols])
    grad_key = to_rows(grad_first[:, :, q_cols : q_cols + k_cols])
    grad_value = to_rows(grad_first[:, :, q_cols + k_cols :])
    grad_both = exchange(d_both_sum.reshape(size, owned, -1), me)[0].astype(f32)
    grad_gate = to_rows(grad_both[:, :, :hidden_cols])
    grad_up = to_rows(grad_both[:, :, hidden_cols:])
    grad_out = lax.ppermute(grad_out, ("dp", "ctx"), backward_owner).astype(f32)
    grad_down = lax.ppermute(d_down_sum, ("dp", "ctx"), backward_owner).astype(f32)
    return (
        output.reshape(tokens.shape),
        grad_tokens,
        grad_query,
        grad_key,
        grad_value,
        grad_out,
        grad_gate,
        grad_up,
        grad_down,
        grad_gains,
    )


def solution(mesh):
    small = mesh.shape["ctx"] == 4
    return jax.shard_map(
        split_local if small else local,
        mesh=mesh,
        in_specs=(
            P("dp", "ctx", None),
            P(("dp", "ctx"), None),
            P(("dp", "ctx"), None),
            P(("dp", "ctx"), None),
            P(("dp", "ctx"), None),
            P(("dp", "ctx"), None),
            P(("dp", "ctx"), None),
            P(("dp", "ctx"), None),
            P(("dp", "ctx")),
            P("dp", "ctx"),
            P("dp", "ctx"),
            P("dp", "ctx", None),
        ),
        out_specs=(
            P("dp", "ctx", None),
            P("dp", "ctx", None),
            P(("dp", "ctx"), None),
            P(("dp", "ctx"), None),
            P(("dp", "ctx"), None),
            P(("dp", "ctx"), None),
            P(("dp", "ctx"), None),
            P(("dp", "ctx"), None),
            P(("dp", "ctx"), None),
            P(("dp", "ctx")),
        ),
        check_vma=False,
    )
```

```python
import functools

import jax
import jax.numpy as jnp
from jax import lax
from jax.experimental import pallas as pl
from jax.experimental.pallas import tpu as pltpu
from jax.sharding import PartitionSpec as P

MODEL_WIDTH = 1024
QUERY_HEADS = 16
KEY_VALUE_HEADS = 8
HEAD_SIZE = 128


EPSILON = 1e-06
THETA = 1000000.0


def row_norm_apply(value_rows, gain_vec):
    return (
        value_rows
        * lax.rsqrt(jnp.mean(value_rows * value_rows, axis=-1, keepdims=True) + EPSILON)
        * gain_vec
    )


def rotary_embed(value_rows, token_positions):
    half_size = value_rows.shape[-1] // 2
    inverse_rates = THETA ** (
        -2.0 * jnp.arange(half_size, dtype=jnp.float32) / value_rows.shape[-1]
    )
    angles = token_positions.astype(jnp.float32)[:, None] * inverse_rates[None, :]
    cosine = jnp.cos(angles)[:, None, :]
    sine_part = jnp.sin(angles)[:, None, :]
    former = value_rows[..., :half_size]
    second = value_rows[..., half_size:]
    return jnp.concatenate(
        [former * cosine - second * sine_part, second * cosine + former * sine_part], axis=-1
    )


def heads_per_group(raw_rows, gain_vec, token_positions, head_count):
    return rotary_embed(
        row_norm_apply(raw_rows.reshape(raw_rows.shape[0], head_count, HEAD_SIZE), gain_vec),
        token_positions,
    )


def split_gains(packed):
    packed = packed.astype(jnp.float32)
    return (
        packed[:MODEL_WIDTH],
        packed[MODEL_WIDTH : 2 * MODEL_WIDTH],
        packed[2 * MODEL_WIDTH : 2 * MODEL_WIDTH + HEAD_SIZE],
        packed[2 * MODEL_WIDTH + HEAD_SIZE :],
    )


def owner_major(grad_full, owners):
    return grad_full.reshape(owners, -1)


def local(
    tokens,
    w_query,
    key_weight,
    value_weight,
    w_out,
    w_gate,
    w_up,
    w_down,
    gains,
    segment_ids,
    positions,
    cotangent,
):
    sequence_count = tokens.shape[0]
    device_local_rows = tokens.shape[1]
    every_row_set = sequence_count * device_local_rows
    inputs = tokens.reshape(every_row_set, MODEL_WIDTH).astype(jnp.float32)
    token_positions = positions.reshape(every_row_set)
    cot_rows = cotangent.reshape(every_row_set, MODEL_WIDTH)
    head_groups = QUERY_HEADS // KEY_VALUE_HEADS
    score_scale = HEAD_SIZE ** (-0.5)
    f32 = jnp.float32
    brain_float_half = jnp.bfloat16
    owners = lax.axis_size(("dp", "ctx"))
    shard_shapes = (
        w_query.shape,
        key_weight.shape,
        value_weight.shape,
        w_out.shape,
        w_gate.shape,
        w_up.shape,
        w_down.shape,
        gains.shape,
    )
    gathered = (
        lax.all_gather(w_query, ("dp", "ctx"), axis=0, tiled=True),
        lax.all_gather(key_weight, ("dp", "ctx"), axis=0, tiled=True),
        lax.all_gather(value_weight, ("dp", "ctx"), axis=0, tiled=True),
        lax.all_gather(w_out, ("dp", "ctx"), axis=0, tiled=True),
        lax.all_gather(w_gate, ("dp", "ctx"), axis=0, tiled=True),
        lax.all_gather(w_up, ("dp", "ctx"), axis=0, tiled=True),
        lax.all_gather(w_down, ("dp", "ctx"), axis=0, tiled=True),
        lax.all_gather(gains, ("dp", "ctx"), axis=0, tiled=True),
    )
    full_query, full_key, full_value, full_out, full_gate, full_up, full_down, full_gains = gathered
    gain_attn, gain_mlp, gain_query, key_norm_gain = split_gains(full_gains)
    normalized_input = row_norm_apply(inputs, gain_attn).astype(brain_float_half)
    query_raw = jnp.dot(normalized_input, full_query, preferred_element_type=f32)
    unrotated_keys = jnp.dot(normalized_input, full_key, preferred_element_type=f32)
    value_low = (
        jnp.dot(normalized_input, full_value, preferred_element_type=f32)
        .astype(brain_float_half)
        .reshape(sequence_count, device_local_rows, KEY_VALUE_HEADS * HEAD_SIZE)
    )
    reduced_queries = heads_per_group(query_raw, gain_query, token_positions, QUERY_HEADS).astype(
        brain_float_half
    )
    key_low = (
        heads_per_group(unrotated_keys, key_norm_gain, token_positions, KEY_VALUE_HEADS)
        .astype(brain_float_half)
        .reshape(sequence_count, device_local_rows, KEY_VALUE_HEADS * HEAD_SIZE)
    )
    segment_low = segment_ids.astype(brain_float_half)
    gathered_keys, gathered_values, segment_all = (
        lax.all_gather(key_low, "ctx", axis=1, tiled=True),
        lax.all_gather(value_low, "ctx", axis=1, tiled=True),
        lax.all_gather(segment_low, "ctx", axis=1, tiled=True),
    )
    overall_rows = gathered_keys.shape[1]
    query_index = lax.axis_index("ctx") * device_local_rows + jnp.arange(
        device_local_rows, dtype=jnp.int32
    )
    key_index = jnp.arange(overall_rows, dtype=jnp.int32)
    allowed = (segment_low[:, :, None] == segment_all[:, None, :]) & (
        query_index[None, :, None] >= key_index[None, None, :]
    )
    grouped_queries = reduced_queries.reshape(
        sequence_count, device_local_rows, KEY_VALUE_HEADS, head_groups, HEAD_SIZE
    ).transpose(0, 2, 3, 1, 4)
    grouped_keys = gathered_keys.reshape(
        sequence_count, overall_rows, KEY_VALUE_HEADS, HEAD_SIZE
    ).transpose(0, 2, 1, 3)
    grouped_values = gathered_values.reshape(
        sequence_count, overall_rows, KEY_VALUE_HEADS, HEAD_SIZE
    ).transpose(0, 2, 1, 3)

    def masked_scores(query_head, key_head, mask_rows):
        scores = (
            jnp.einsum("rld,kd->rlk", query_head, key_head, preferred_element_type=f32)
            * score_scale
        )
        return jnp.where(mask_rows[None], scores, -1e30)

    def forward_sequence(slices):
        query_seq, key_seq, value_seq, mask_rows = slices

        def forward_head(head_slices):
            query_head, key_head, value_head = head_slices
            scores = masked_scores(query_head, key_head, mask_rows)
            row_peak = jnp.max(scores, axis=-1, keepdims=True)
            exp_scores = jnp.exp(scores - row_peak)
            denominator = jnp.sum(exp_scores, axis=-1, keepdims=True)
            prob_low = (exp_scores / denominator).astype(brain_float_half)
            mixed_head = jnp.einsum("rlk,kd->rld", prob_low, value_head, preferred_element_type=f32)
            return (mixed_head, row_peak[..., 0] + jnp.log(denominator[..., 0]))

        return lax.map(forward_head, (query_seq, key_seq, value_seq))

    mixed_heads, log_totals = lax.map(
        forward_sequence, (grouped_queries, grouped_keys, grouped_values, allowed)
    )
    attended = (
        mixed_heads.transpose(0, 3, 1, 2, 4)
        .reshape(every_row_set, QUERY_HEADS * HEAD_SIZE)
        .astype(brain_float_half)
    )
    middle = inputs + jnp.dot(attended, full_out, preferred_element_type=f32)
    normed_mlp = row_norm_apply(middle, gain_mlp).astype(brain_float_half)
    gate_value = jnp.dot(normed_mlp, full_gate, preferred_element_type=f32)
    up_value = jnp.dot(normed_mlp, full_up, preferred_element_type=f32)
    hidden = (jax.nn.silu(gate_value) * up_value).astype(brain_float_half)
    output = (middle + jnp.dot(hidden, full_down, preferred_element_type=f32)).astype(
        brain_float_half
    )
    regathered = (
        lax.all_gather(w_query, ("dp", "ctx"), axis=0, tiled=True),
        lax.all_gather(key_weight, ("dp", "ctx"), axis=0, tiled=True),
        lax.all_gather(value_weight, ("dp", "ctx"), axis=0, tiled=True),
        lax.all_gather(w_out, ("dp", "ctx"), axis=0, tiled=True),
        lax.all_gather(w_gate, ("dp", "ctx"), axis=0, tiled=True),
        lax.all_gather(w_up, ("dp", "ctx"), axis=0, tiled=True),
        lax.all_gather(w_down, ("dp", "ctx"), axis=0, tiled=True),
        lax.all_gather(gains, ("dp", "ctx"), axis=0, tiled=True),
    )
    back_query, back_key, back_value, back_out, back_gate, back_up, back_down, back_gains = (
        regathered
    )
    gain_attn, gain_mlp, gain_query, key_norm_gain = split_gains(back_gains)
    d_hidden = jnp.einsum("ld,fd->lf", cot_rows, back_down, preferred_element_type=f32)
    grad_down = jnp.einsum("lf,ld->fd", hidden, cot_rows, preferred_element_type=f32)
    unused, swiglu_pull = jax.vjp(
        lambda gate_in, up_in: jax.nn.silu(gate_in) * up_in, gate_value, up_value
    )
    d_gate, d_up = swiglu_pull(d_hidden)
    d_gate = d_gate.astype(brain_float_half)
    d_up = d_up.astype(brain_float_half)
    grad_gate = jnp.einsum("ld,lf->df", normed_mlp, d_gate, preferred_element_type=f32)
    grad_up = jnp.einsum("ld,lf->df", normed_mlp, d_up, preferred_element_type=f32)
    d_normed = jnp.einsum("lf,df->ld", d_gate, back_gate, preferred_element_type=f32)
    d_normed = d_normed + jnp.einsum("lf,df->ld", d_up, back_up, preferred_element_type=f32)
    unused, norm_pull = jax.vjp(row_norm_apply, middle, gain_mlp)
    d_middle, d_gain_mlp = norm_pull(d_normed)
    d_middle = d_middle + cot_rows.astype(f32)
    d_branch = d_middle.astype(brain_float_half)
    grad_out = jnp.einsum("lh,ld->hd", attended, d_branch, preferred_element_type=f32)
    attended_gradient = jnp.einsum(
        "ld,hd->lh", d_branch, back_out, preferred_element_type=f32
    ).astype(brain_float_half)
    group_gradient = attended_gradient.reshape(
        sequence_count, device_local_rows, KEY_VALUE_HEADS, head_groups, HEAD_SIZE
    ).transpose(0, 2, 3, 1, 4)

    def backward_sequence(slices):
        query_seq, key_seq, value_seq, d_seq, log_seq, mask_rows = slices

        def backward_head(head_slices):
            query_head, key_head, value_head, d_head, log_total = head_slices
            scores = masked_scores(query_head, key_head, mask_rows)
            probs_full = jnp.exp(scores - log_total[..., None])
            prob_low = probs_full.astype(brain_float_half)
            d_value = jnp.einsum("rlk,rld->kd", prob_low, d_head, preferred_element_type=f32)
            d_probs = jnp.einsum("rld,kd->rlk", d_head, value_head, preferred_element_type=f32)
            d_scores = probs_full * (
                d_probs - jnp.sum(probs_full * d_probs, axis=-1, keepdims=True)
            )
            d_scores = d_scores.astype(brain_float_half)
            d_query = (
                jnp.einsum("rlk,kd->rld", d_scores, key_head, preferred_element_type=f32)
                * score_scale
            )
            d_key = (
                jnp.einsum("rlk,rld->kd", d_scores, query_head, preferred_element_type=f32)
                * score_scale
            )
            return (d_query, d_key, d_value)

        return lax.map(backward_head, (query_seq, key_seq, value_seq, d_seq, log_seq))

    d_queries, key_rows_gradient, value_rows_gradient = lax.map(
        backward_sequence,
        (grouped_queries, grouped_keys, grouped_values, group_gradient, log_totals, allowed),
    )
    gathered_key_gradient = key_rows_gradient.transpose(2, 0, 1, 3).reshape(
        overall_rows, sequence_count, KEY_VALUE_HEADS * HEAD_SIZE
    )
    gathered_value_gradient = value_rows_gradient.transpose(2, 0, 1, 3).reshape(
        overall_rows, sequence_count, KEY_VALUE_HEADS * HEAD_SIZE
    )
    local_key_gradient, local_value_gradient = (
        lax.psum_scatter(
            gathered_key_gradient.astype(jnp.bfloat16), "ctx", scatter_dimension=0, tiled=True
        ).astype(jnp.float32),
        lax.psum_scatter(
            gathered_value_gradient.astype(jnp.bfloat16), "ctx", scatter_dimension=0, tiled=True
        ).astype(jnp.float32),
    )
    local_key_gradient = local_key_gradient.transpose(1, 0, 2)
    local_value_gradient = local_value_gradient.transpose(1, 0, 2)
    d_query_heads = d_queries.transpose(0, 3, 1, 2, 4).reshape(
        every_row_set, QUERY_HEADS, HEAD_SIZE
    )
    unused, query_pull = jax.vjp(
        lambda unnormalized_input, input_gain_vector: heads_per_group(
            unnormalized_input, input_gain_vector, token_positions, QUERY_HEADS
        ),
        query_raw,
        gain_query,
    )
    d_query_raw, d_gain_query = query_pull(d_query_heads)
    unused, key_pullback = jax.vjp(
        lambda unnormalized_input, input_gain_vector: heads_per_group(
            unnormalized_input, input_gain_vector, token_positions, KEY_VALUE_HEADS
        ),
        unrotated_keys,
        key_norm_gain,
    )
    unrotated_key_gradient, key_gain_gradient = key_pullback(
        local_key_gradient.reshape(every_row_set, KEY_VALUE_HEADS, HEAD_SIZE)
    )
    d_query_low = d_query_raw.astype(brain_float_half)
    d_key_low = unrotated_key_gradient.astype(brain_float_half)
    reduced_value_gradient = local_value_gradient.reshape(
        every_row_set, KEY_VALUE_HEADS * HEAD_SIZE
    ).astype(brain_float_half)
    grad_query = jnp.einsum("ld,lh->dh", normalized_input, d_query_low, preferred_element_type=f32)
    grad_key = jnp.einsum("ld,lh->dh", normalized_input, d_key_low, preferred_element_type=f32)
    grad_value = jnp.einsum(
        "ld,lh->dh", normalized_input, reduced_value_gradient, preferred_element_type=f32
    )
    d_normed_attn = jnp.einsum("lh,dh->ld", d_query_low, back_query, preferred_element_type=f32)
    d_normed_attn = d_normed_attn + jnp.einsum(
        "lh,dh->ld", d_key_low, back_key, preferred_element_type=f32
    )
    d_normed_attn = d_normed_attn + jnp.einsum(
        "lh,dh->ld", reduced_value_gradient, back_value, preferred_element_type=f32
    )
    unused, first_pull = jax.vjp(row_norm_apply, inputs, gain_attn)
    d_inputs, d_gain_attn = first_pull(d_normed_attn)
    grad_tokens = (d_middle + d_inputs).reshape(sequence_count, device_local_rows, MODEL_WIDTH)
    grad_gains = jnp.concatenate([d_gain_attn, d_gain_mlp, d_gain_query, key_gain_gradient])
    summed = (
        lax.psum_scatter(
            owner_major(grad_query, owners), ("dp", "ctx"), scatter_dimension=0, tiled=True
        ),
        lax.psum_scatter(
            owner_major(grad_key, owners), ("dp", "ctx"), scatter_dimension=0, tiled=True
        ),
        lax.psum_scatter(
            owner_major(grad_value, owners), ("dp", "ctx"), scatter_dimension=0, tiled=True
        ),
        lax.psum_scatter(
            owner_major(grad_out, owners), ("dp", "ctx"), scatter_dimension=0, tiled=True
        ),
        lax.psum_scatter(
            owner_major(grad_gate, owners), ("dp", "ctx"), scatter_dimension=0, tiled=True
        ),
        lax.psum_scatter(
            owner_major(grad_up, owners), ("dp", "ctx"), scatter_dimension=0, tiled=True
        ),
        lax.psum_scatter(
            owner_major(grad_down, owners), ("dp", "ctx"), scatter_dimension=0, tiled=True
        ),
        lax.psum_scatter(
            owner_major(grad_gains, owners), ("dp", "ctx"), scatter_dimension=0, tiled=True
        ),
    )
    grad_query = summed[0].reshape(shard_shapes[0])
    grad_key = summed[1].reshape(shard_shapes[1])
    grad_value = summed[2].reshape(shard_shapes[2])
    grad_out = summed[3].reshape(shard_shapes[3])
    grad_gate = summed[4].reshape(shard_shapes[4])
    grad_up = summed[5].reshape(shard_shapes[5])
    grad_down = summed[6].reshape(shard_shapes[6])
    grad_gains = summed[7].reshape(shard_shapes[7])
    return (
        output.reshape(sequence_count, device_local_rows, MODEL_WIDTH),
        grad_tokens,
        grad_query,
        grad_key,
        grad_value,
        grad_out,
        grad_gate,
        grad_up,
        grad_down,
        grad_gains,
    )

FEATURES = 128
MASK_DEPTH = -4096.0
LOG2_E = 1.4426950408889634
VMEM_BYTES = 56 * 1024 * 1024
SMALL_COST = pl.CostEstimate(flops=1, bytes_accessed=1, transcendentals=0)
bf16 = jnp.bfloat16
f32 = jnp.float32


def xor_permute(value, axis, offset):
    size = lax.axis_size(axis)
    return lax.ppermute(value, axis, [(i, i ^ offset) for i in range(size)])


def pick(stacked, index):
    return lax.dynamic_index_in_dim(stacked, index, 0, keepdims=False)


def exchange(stacked, me):
    size = stacked.shape[0]
    relative = [pick(stacked, me)]
    for offset in range(1, size):
        relative.append(xor_permute(pick(stacked, me ^ offset), "ctx", offset))
    arrived = relative[1:]
    relative = jnp.stack(relative)
    return jnp.stack([pick(relative, me ^ source) for source in range(size)]), arrived


def shift_z(value, offset):
    size = lax.axis_size("dp")
    return lax.ppermute(value, "dp", [(i, (i + 2 * offset) % size) for i in range(size)])


def assemble_kernel(splits, count, places_ref, *refs):
    pieces, results, sems = refs[:count], refs[count:-1], refs[-1]
    copies = []
    for piece in pieces:
        for slot in range(piece.shape[0]):
            n = len(copies) // len(splits)
            start = 0
            for m, rows in enumerate(splits):
                copy = pltpu.make_async_copy(
                    piece.at[slot, pl.ds(start, rows)],
                    results[m].at[places_ref[n]],
                    sems.at[n, m],
                )
                copy.start()
                copies.append(copy)
                start += rows
    for copy in copies:
        copy.wait()


def assemble(pieces, places, splits=None):
    slots = sum(piece.shape[0] for piece in pieces)
    rows, columns = pieces[0].shape[1:]
    splits = (rows,) if splits is None else splits
    anywhere = pl.BlockSpec(memory_space=pl.ANY)
    return pl.pallas_call(
        functools.partial(assemble_kernel, splits, len(pieces)),
        in_specs=[pl.BlockSpec(memory_space=pltpu.SMEM)]
        + [pl.BlockSpec(memory_space=pltpu.VMEM)] * len(pieces),
        out_specs=[anywhere] * len(splits),
        out_shape=[jax.ShapeDtypeStruct((slots, n, columns), pieces[0].dtype) for n in splits],
        scratch_shapes=[pltpu.SemaphoreType.DMA((slots, len(splits)))],
        compiler_params=pltpu.CompilerParams(vmem_limit_bytes=VMEM_BYTES),
        cost_estimate=pl.CostEstimate(
            flops=0, bytes_accessed=4 * slots * rows * columns, transcendentals=0
        ),
        name="assemble",
    )(places.astype(jnp.int32), *pieces)


def join(blocks):
    joined = assemble([block[None] for block in blocks], jnp.arange(len(blocks)))[0]
    return joined.reshape(-1, joined.shape[-1])


def gather_along(value):
    return [value] + [shift_z(value, k) for k in range(1, lax.axis_size("dp") // 2)]


def gather_beside(along, *waits):
    depth = len(along)
    z = lax.axis_index("dp") // 2
    places = jnp.stack([(z - k) % depth for k in range(depth)])
    stack = assemble([piece[None] for piece in along], places)[0]
    stack = after(stack, *waits)
    return [stack, xor_permute(stack, "dp", 1)]


def interleave(stacks, splits):
    depth = stacks[0].shape[0]
    y = lax.axis_index("dp") % 2
    rows = 2 * jnp.arange(depth)
    results = assemble(stacks, jnp.concatenate([rows + y, rows + 1 - y]), splits)
    return [result.reshape(-1, result.shape[-1]) for result in results]


def reduce_beside(grad):
    depth = grad.shape[0] // 2
    y = lax.axis_index("dp") % 2
    grad = grad.reshape((depth, 2) + grad.shape[1:])
    away = lax.dynamic_index_in_dim(grad, 1 - y, 1, keepdims=False)
    kept = lax.dynamic_index_in_dim(grad, y, 1, keepdims=False)
    return (kept.astype(f32) + xor_permute(away, "dp", 1).astype(f32)).astype(bf16)


def reduce_along(pair):
    depth = pair.shape[0]
    z = lax.axis_index("dp") // 2
    sent = [shift_z(pick(pair, (z + k) % depth), k) for k in range(1, depth)]
    return [pick(pair, z)] + sent


def add_all(terms):
    total = terms[0].astype(f32)
    for term in terms[1:]:
        total = total + term.astype(f32)
    return total.astype(bf16)


def after(value, *others):
    return lax.optimization_barrier((value, *others))[0]


def after_all(values, *others):
    return lax.optimization_barrier((*values, *others))[: len(values)]


def gather_blocks(value):
    across = xor_permute(value, "ctx", 2)
    beside = xor_permute(value, "ctx", 1)
    corner = xor_permute(across, "ctx", 1)
    return [value, beside, across, corner]


def gather_near(value):
    return [value, xor_permute(value, "ctx", 1)], xor_permute(value, "ctx", 2)


def gather_far(across, *waits):
    across = after(across, *waits)
    return [across, xor_permute(across, "ctx", 1)]


def send_across(part_corner, part_across, *waits):
    corner = xor_permute(part_corner.astype(bf16), "ctx", 1)
    toward = (part_across.astype(f32) + corner.astype(f32)).astype(bf16)
    toward = after(toward, *waits) if waits else toward
    return toward, xor_permute(toward, "ctx", 2)


def sum_own(part_beside, part_own, across):
    beside = xor_permute(part_beside.astype(bf16), "ctx", 1)
    return part_own.astype(f32) + beside.astype(f32) + across.astype(f32)


def nt_dot(left, right):
    return lax.dot_general(left, right, (((1,), (1,)), ((), ())), preferred_element_type=f32)


def nn_dot(left, right):
    return jnp.dot(left, right, preferred_element_type=f32)


def project_kernel(
    query_heads,
    key_heads,
    per_block,
    x_refs,
    gain_ref,
    weight_ref,
    cos_ref,
    sin_ref,
    gain_q_ref,
    gain_k_ref,
    normed_ref,
    raw_ref,
    q_ref,
    k_ref,
    v_ref,
    held_ref,
):
    for r, x_ref in enumerate(x_refs):

        @pl.when(pl.program_id(0) // per_block == r)
        def _():
            held_ref[...] = x_ref[...]

    x = held_ref[...].astype(f32)
    scale = lax.rsqrt(jnp.mean(x * x, axis=-1, keepdims=True) + EPSILON)
    normed = (x * scale * gain_ref[...]).astype(bf16)
    normed_ref[...] = normed
    raw = nn_dot(normed, weight_ref[...])
    turned = (query_heads + key_heads) * HEAD_SIZE
    raw_ref[...] = raw[:, :turned]
    v_ref[...] = raw[:, turned:].astype(bf16)
    cosine = cos_ref[...]
    sine = sin_ref[...]
    for head in range(query_heads + key_heads):
        rows = raw[:, head * HEAD_SIZE : (head + 1) * HEAD_SIZE]
        gain = gain_q_ref[...] if head < query_heads else gain_k_ref[...]
        rows = rows * lax.rsqrt(jnp.mean(rows * rows, axis=-1, keepdims=True) + EPSILON) * gain
        rows = (rows * cosine + pltpu.roll(rows, HEAD_SIZE // 2, 1) * sine).astype(bf16)
        if head < query_heads:
            q_ref[:, head * HEAD_SIZE : (head + 1) * HEAD_SIZE] = rows
        else:
            at = (head - query_heads) * HEAD_SIZE
            k_ref[:, at : at + HEAD_SIZE] = rows


def project(x_blocks, gain, weight, cosine, sine, gain_q, gain_k, query_heads, key_heads):
    rows, width = x_blocks[0].shape
    block = 256
    per_block = rows // block
    rows = rows * len(x_blocks)
    turned = (query_heads + key_heads) * HEAD_SIZE
    columns = weight.shape[1]

    def tall(n):
        return pl.BlockSpec((block, n), lambda i: (i, 0))

    def whole(shape):
        return pl.BlockSpec(shape, lambda i: (0, 0))

    def part(r):
        return pl.BlockSpec(
            (block, width), lambda i: (jnp.clip(i - r * per_block, 0, per_block - 1), 0)
        )

    return pl.pallas_call(
        functools.partial(project_kernel, query_heads, key_heads, per_block),
        grid=(rows // block,),
        in_specs=[
            [part(r) for r in range(len(x_blocks))],
            whole((1, width)),
            whole(weight.shape),
            tall(HEAD_SIZE),
            tall(HEAD_SIZE),
            whole((1, HEAD_SIZE)),
            whole((1, HEAD_SIZE)),
        ],
        out_specs=[
            tall(width),
            tall(turned),
            tall(query_heads * HEAD_SIZE),
            tall(key_heads * HEAD_SIZE),
            tall(key_heads * HEAD_SIZE),
        ],
        out_shape=[
            jax.ShapeDtypeStruct((rows, width), bf16),
            jax.ShapeDtypeStruct((rows, turned), f32),
            jax.ShapeDtypeStruct((rows, query_heads * HEAD_SIZE), bf16),
            jax.ShapeDtypeStruct((rows, key_heads * HEAD_SIZE), bf16),
            jax.ShapeDtypeStruct((rows, key_heads * HEAD_SIZE), bf16),
        ],
        scratch_shapes=[pltpu.VMEM((block, width), bf16)],
        compiler_params=pltpu.CompilerParams(vmem_limit_bytes=VMEM_BYTES),
        cost_estimate=pl.CostEstimate(
            flops=2 * rows * width * columns,
            bytes_accessed=rows * (4 * width + 4 * turned + 2 * columns) + 2 * width * columns,
            transcendentals=0,
        ),
        name="project",
    )(list(x_blocks), gain, weight, cosine, sine, gain_q, gain_k)


def unproject_kernel(
    query_heads,
    key_heads,
    half,
    dq_near_ref,
    dq_far_ref,
    dk_ref,
    dv_ref,
    raw_ref,
    cos_ref,
    sin_ref,
    gain_q_ref,
    gain_k_ref,
    low_ref,
    dgain_ref,
):
    @pl.when(pl.program_id(0) == 0)
    def _():
        dgain_ref[...] = jnp.zeros_like(dgain_ref)

    cosine = cos_ref[...]
    sine = sin_ref[...]
    total_q = jnp.zeros((1, HEAD_SIZE), f32)
    total_k = jnp.zeros((1, HEAD_SIZE), f32)
    for head in range(query_heads + key_heads):
        at = head * HEAD_SIZE
        raw = raw_ref[:, at : at + HEAD_SIZE]
        if head < query_heads:
            lanes = slice(at, at + HEAD_SIZE)
            grad = jnp.where(pl.program_id(0) < half, dq_near_ref[:, lanes], dq_far_ref[:, lanes])
            gain = gain_q_ref[...]
        else:
            back = (head - query_heads) * HEAD_SIZE
            grad = dk_ref[:, back : back + HEAD_SIZE]
            gain = gain_k_ref[...]
        grad = grad * cosine - pltpu.roll(grad, HEAD_SIZE // 2, 1) * sine
        scale = lax.rsqrt(jnp.mean(raw * raw, axis=-1, keepdims=True) + EPSILON)
        unit = raw * scale
        summed = jnp.sum(unit * grad, axis=0, keepdims=True)
        if head < query_heads:
            total_q += summed
        else:
            total_k += summed
        grad = grad * gain
        mean = jnp.mean(unit * grad, axis=-1, keepdims=True)
        low_ref[:, at : at + HEAD_SIZE] = (scale * (grad - unit * mean)).astype(bf16)
    low_ref[:, (query_heads + key_heads) * HEAD_SIZE :] = dv_ref[...].astype(bf16)
    dgain_ref[0:1, :] += total_q
    dgain_ref[1:2, :] += total_k


def unproject(dq_near, dq_far, dk, dv, raw, cosine, sine, gain_q, gain_k, query_heads, key_heads):
    rows = dk.shape[0]
    block = 256
    half = rows // block // 2
    columns = (query_heads + 2 * key_heads) * HEAD_SIZE

    def tall(n):
        return pl.BlockSpec((block, n), lambda i: (i, 0))

    def whole(shape):
        return pl.BlockSpec(shape, lambda i: (0, 0))

    return pl.pallas_call(
        functools.partial(unproject_kernel, query_heads, key_heads, half),
        grid=(rows // block,),
        in_specs=[
            pl.BlockSpec((block, dq_near.shape[1]), lambda i: (jnp.minimum(i, half - 1), 0)),
            pl.BlockSpec((block, dq_far.shape[1]), lambda i: (jnp.maximum(i - half, 0), 0)),
            tall(dk.shape[1]),
            tall(dv.shape[1]),
            tall(raw.shape[1]),
            tall(HEAD_SIZE),
            tall(HEAD_SIZE),
            whole((1, HEAD_SIZE)),
            whole((1, HEAD_SIZE)),
        ],
        out_specs=[tall(columns), whole((8, HEAD_SIZE))],
        out_shape=[
            jax.ShapeDtypeStruct((rows, columns), bf16),
            jax.ShapeDtypeStruct((8, HEAD_SIZE), f32),
        ],
        compiler_params=pltpu.CompilerParams(vmem_limit_bytes=VMEM_BYTES),
        cost_estimate=pl.CostEstimate(
            flops=20 * rows * columns, bytes_accessed=20 * rows * columns, transcendentals=0
        ),
        name="unproject",
    )(dq_near, dq_far, dk, dv, raw, cosine, sine, gain_q, gain_k)


def attend_kernel(
    group, block, first, me_ref, q_ref, qf_ref, k_ref, kf_ref, v_ref, o_ref, log_ref, total_ref
):
    me = me_ref[0]
    at_query = (pl.program_id(1) + first) ^ me
    factor = HEAD_SIZE ** (-0.5) * LOG2_E
    query_features = qf_ref[...]
    ones = jnp.ones((block, HEAD_SIZE), bf16)
    total_ref[...] = jnp.zeros_like(total_ref)

    def step(at_key, diagonal):
        rows = pl.ds(pl.multiple_of((at_key ^ me) * block, block), block)
        keys = jnp.concatenate([k_ref[rows, :], kf_ref[rows, :]], axis=1)
        values = jnp.concatenate([v_ref[rows, :], ones], axis=1)
        for head in range(group):
            query = q_ref[:, head * HEAD_SIZE : (head + 1) * HEAD_SIZE]
            scores = nt_dot(jnp.concatenate([query, query_features], axis=1), keys)
            probs = jnp.exp2(scores * factor)
            if diagonal:
                down = lax.broadcasted_iota(jnp.int32, probs.shape, 0)
                right = lax.broadcasted_iota(jnp.int32, probs.shape, 1)
                probs = jnp.where(down >= right, probs, 0.0)
            total_ref[head] += nn_dot(probs.astype(bf16), values)

    @pl.loop(0, at_query)
    def _(at_key):
        step(at_key, False)

    step(at_query, True)
    for head in range(group):
        weighted = total_ref[head, :, :HEAD_SIZE]
        summed = total_ref[head, :, HEAD_SIZE:]
        o_ref[:, head * HEAD_SIZE : (head + 1) * HEAD_SIZE] = (weighted / summed).astype(bf16)
        log_ref[0, head : head + 1, :] = jnp.log2(summed.T[0:1, :])


def attend(me, q, qf, k, kf, v, block, group, first, count):
    rows = k.shape[0]
    key_heads = k.shape[1] // HEAD_SIZE
    pairs = key_heads * group * count * block * rows * 5 // 8
    return pl.pallas_call(
        functools.partial(attend_kernel, group, block, first),
        grid_spec=pltpu.PrefetchScalarGridSpec(
            num_scalar_prefetch=1,
            grid=(key_heads, count),
            in_specs=[
                pl.BlockSpec((block, group * HEAD_SIZE), lambda g, i, me: (i + first, g)),
                pl.BlockSpec((block, FEATURES), lambda g, i, me: (i + first, 0)),
                pl.BlockSpec((rows, HEAD_SIZE), lambda g, i, me: (0, g)),
                pl.BlockSpec((rows, FEATURES), lambda g, i, me: (0, 0)),
                pl.BlockSpec((rows, HEAD_SIZE), lambda g, i, me: (0, g)),
            ],
            out_specs=[
                pl.BlockSpec((block, group * HEAD_SIZE), lambda g, i, me: (i, g)),
                pl.BlockSpec((1, group, block), lambda g, i, me: (g, 0, i)),
            ],
            scratch_shapes=[pltpu.VMEM((group, block, 2 * HEAD_SIZE), f32)],
        ),
        out_shape=[
            jax.ShapeDtypeStruct((count * block, q.shape[1]), bf16),
            jax.ShapeDtypeStruct((key_heads, group, count * block), f32),
        ],
        compiler_params=pltpu.CompilerParams(vmem_limit_bytes=VMEM_BYTES),
        cost_estimate=pl.CostEstimate(
            flops=8 * pairs * HEAD_SIZE, bytes_accessed=10 * q.size, transcendentals=pairs
        ),
        name="attend",
    )(me, q, qf, k, kf, v)


def unattend_kernel(
    group,
    block,
    first,
    resumed,
    me_ref,
    q_ref,
    qf_ref,
    k_ref,
    kf_ref,
    v_ref,
    o_ref,
    branch_first_ref,
    branch_second_ref,
    out_ref,
    log_ref,
    *rest,
):
    if resumed:
        dk_in_ref, dv_in_ref, d_weight_in_ref, *rest = rest
    dq_ref, dk_ref, dv_ref, d_weight_ref, flipped_ref, total_ref, do_ref = rest
    me = me_ref[0]
    at_query = (pl.program_id(1) + first) ^ me
    scale = HEAD_SIZE ** (-0.5)
    factor = scale * LOG2_E

    @pl.when(pl.program_id(1) == 0)
    def _():
        dk_ref[...] = dk_in_ref[...] if resumed else jnp.zeros_like(dk_ref)
        dv_ref[...] = dv_in_ref[...] if resumed else jnp.zeros_like(dv_ref)
        d_weight_ref[...] = d_weight_in_ref[...] if resumed else jnp.zeros_like(d_weight_ref)
        flipped_ref[...] = k_ref[...].astype(f32).T.astype(bf16)

    def take(branch_ref):
        do_ref[...] = nt_dot(branch_ref[...], out_ref[...]).astype(bf16)
        turned = o_ref[...].astype(f32).T.astype(bf16)
        d_weight_ref[...] += nn_dot(turned, branch_ref[...])

    @pl.when(pl.program_id(1) == 0)
    def _():
        take(branch_first_ref)

    @pl.when(pl.program_id(1) == 1)
    def _():
        take(branch_second_ref)

    total_ref[...] = jnp.zeros_like(total_ref)
    query_features = qf_ref[...]
    deltas = []
    for head in range(group):
        lanes = slice(head * HEAD_SIZE, (head + 1) * HEAD_SIZE)
        product = do_ref[:, lanes].astype(f32) * o_ref[:, lanes].astype(f32)
        deltas.append(jnp.sum(product.T, axis=0, keepdims=True))

    def step(at_key, diagonal):
        start = pl.multiple_of((at_key ^ me) * block, block)
        rows = pl.ds(start, block)
        keys = jnp.concatenate([k_ref[rows, :], kf_ref[rows, :]], axis=1)
        values = v_ref[rows, :]
        for head in range(group):
            lanes = slice(head * HEAD_SIZE, (head + 1) * HEAD_SIZE)
            query = q_ref[:, lanes]
            d_out = do_ref[:, lanes]
            scores = nt_dot(keys, jnp.concatenate([query, query_features], axis=1))
            probs = jnp.exp2(scores * factor - log_ref[0, head : head + 1, :])
            if diagonal:
                key_at = lax.broadcasted_iota(jnp.int32, probs.shape, 0)
                query_at = lax.broadcasted_iota(jnp.int32, probs.shape, 1)
                probs = jnp.where(query_at >= key_at, probs, 0.0)
            d_scores = (probs * (nt_dot(values, d_out) - deltas[head])).astype(bf16)
            dv_ref[rows, :] += nn_dot(probs.astype(bf16), d_out)
            dk_ref[rows, :] += nn_dot(d_scores, query)
            total_ref[head] += nn_dot(flipped_ref[:, rows], d_scores)

    @pl.loop(0, at_query)
    def _(at_key):
        step(at_key, False)

    step(at_query, True)
    for head in range(group):
        dq_ref[:, head * HEAD_SIZE : (head + 1) * HEAD_SIZE] = total_ref[head].T * scale

    if resumed:

        @pl.when(pl.program_id(1) == pl.num_programs(1) - 1)
        def _():
            dk_ref[...] = dk_ref[...] * scale


def unattend(me, q, qf, k, kf, v, o, branches, out, logs, block, group, first, earlier=()):
    count = len(branches)
    rows = k.shape[0]
    key_heads = k.shape[1] // HEAD_SIZE
    width = out.shape[1]
    lanes = group * HEAD_SIZE

    def by_query(n):
        return pl.BlockSpec((block, n), lambda g, i, me: (i, g))

    by_key = pl.BlockSpec((rows, HEAD_SIZE), lambda g, i, me: (0, g))
    by_head = pl.BlockSpec((lanes, width), lambda g, i, me: (g, 0))
    whole = pl.BlockSpec((block, width), lambda g, i, me: (0, 0))
    return pl.pallas_call(
        functools.partial(unattend_kernel, group, block, first, bool(earlier)),
        grid_spec=pltpu.PrefetchScalarGridSpec(
            num_scalar_prefetch=1,
            grid=(key_heads, count),
            in_specs=[
                pl.BlockSpec((block, lanes), lambda g, i, me: (i + first, g)),
                pl.BlockSpec((block, FEATURES), lambda g, i, me: (i + first, 0)),
                by_key,
                pl.BlockSpec((rows, FEATURES), lambda g, i, me: (0, 0)),
                by_key,
                by_query(lanes),
                whole,
                whole,
                by_head,
                pl.BlockSpec((1, group, block), lambda g, i, me: (g, 0, i)),
            ]
            + ([by_key, by_key, by_head] if earlier else []),
            out_specs=[by_query(lanes), by_key, by_key, by_head],
            scratch_shapes=[
                pltpu.VMEM((HEAD_SIZE, rows), bf16),
                pltpu.VMEM((group, HEAD_SIZE, block), f32),
                pltpu.VMEM((block, lanes), bf16),
            ],
        ),
        out_shape=[
            jax.ShapeDtypeStruct((count * block, q.shape[1]), f32),
            jax.ShapeDtypeStruct(k.shape, f32),
            jax.ShapeDtypeStruct(v.shape, f32),
            jax.ShapeDtypeStruct(out.shape, f32),
        ],
        compiler_params=pltpu.CompilerParams(vmem_limit_bytes=VMEM_BYTES),
        cost_estimate=SMALL_COST,
        name="unattend",
    )(me, q, qf, k, kf, v, o, *branches, out, logs, *earlier)


def feed_kernel(
    units,
    half,
    first_ref,
    second_ref,
    cot_ref,
    both_ref,
    down_ref,
    h_ref,
    hidden_ref,
    d_both_ref,
    part_first_ref,
    part_second_ref,
    d_part_first_ref,
    d_part_second_ref,
):
    in_first = pl.program_id(0) < half

    @pl.when(in_first)
    def _():
        h_ref[...] = first_ref[...]

    @pl.when(jnp.logical_not(in_first))
    def _():
        h_ref[...] = second_ref[...]

    both = nn_dot(h_ref[...], both_ref[...])
    d_hidden = nt_dot(cot_ref[...], down_ref[...])
    gate, up = both[:, :units], both[:, units:]
    sigmoid = 1.0 / (1.0 + jnp.exp(-gate))
    silu = gate * sigmoid
    hidden = (silu * up).astype(bf16)
    hidden_ref[...] = hidden
    part = nn_dot(hidden, down_ref[...]).astype(bf16)
    d_gate = (d_hidden * up * sigmoid * (1.0 + gate * (1.0 - sigmoid))).astype(bf16)
    d_up = (d_hidden * silu).astype(bf16)
    d_both = jnp.concatenate([d_gate, d_up], axis=1)
    d_both_ref[...] = d_both
    d_part = nt_dot(d_both, both_ref[...]).astype(bf16)

    @pl.when(in_first)
    def _():
        part_first_ref[...] = part
        d_part_first_ref[...] = d_part

    @pl.when(jnp.logical_not(in_first))
    def _():
        part_second_ref[...] = part
        d_part_second_ref[...] = d_part


def feed(h_first, h_second, cot, both, down):
    rows, width = cot.shape
    units = down.shape[0]
    block = 256
    half = rows // block // 2

    def tall(n):
        return pl.BlockSpec((block, n), lambda i: (i, 0))

    def whole(shape):
        return pl.BlockSpec(shape, lambda i: (0, 0))

    of_first = pl.BlockSpec((block, width), lambda i: (jnp.minimum(i, half - 1), 0))
    of_second = pl.BlockSpec((block, width), lambda i: (jnp.maximum(i - half, 0), 0))
    shapes = [(rows, width), (rows, units), (rows, 2 * units)] + [(rows // 2, width)] * 4
    return pl.pallas_call(
        functools.partial(feed_kernel, units, half),
        grid=(rows // block,),
        in_specs=[of_first, of_second, tall(width), whole(both.shape), whole(down.shape)],
        out_specs=[tall(width), tall(units), tall(2 * units)] + [of_first, of_second] * 2,
        out_shape=[jax.ShapeDtypeStruct(shape, bf16) for shape in shapes],
        compiler_params=pltpu.CompilerParams(vmem_limit_bytes=VMEM_BYTES),
        cost_estimate=pl.CostEstimate(
            flops=12 * rows * width * units,
            bytes_accessed=rows * (10 * width + 6 * units) + 6 * width * units,
            transcendentals=rows * units,
        ),
        name="feed",
    )(h_first, h_second, cot, both, down)


def norm_back(value_rows, gain_vec, grad):
    scale = lax.rsqrt(jnp.mean(value_rows * value_rows, axis=-1, keepdims=True) + EPSILON)
    unit = value_rows * scale
    d_gain = jnp.sum(unit * grad, axis=0)
    grad = grad * gain_vec
    return scale * (grad - unit * jnp.mean(unit * grad, axis=-1, keepdims=True)), d_gain


def split_local(
    tokens,
    w_query,
    key_weight,
    value_weight,
    w_out,
    w_gate,
    w_up,
    w_down,
    gains,
    segment_ids,
    positions,
    cotangent,
):
    size = lax.axis_size("ctx")
    copies = lax.axis_size("dp")
    me = lax.axis_index("ctx")
    me_row = me.reshape(1).astype(jnp.int32)
    block = tokens.shape[1]
    group = QUERY_HEADS // KEY_VALUE_HEADS
    query_heads = QUERY_HEADS // size
    key_heads = KEY_VALUE_HEADS // size
    q_cols = query_heads * HEAD_SIZE
    k_cols = key_heads * HEAD_SIZE
    owned = w_query.shape[0]
    hidden_cols = w_gate.shape[1] // size
    gain_count = gains.shape[0]
    pad_rows = 16
    forward_owner = [
        (b, (b % copies) * size + b // copies) for b in range(size * copies)
    ]
    backward_owner = [(target, source) for source, target in forward_owner]

    def by_columns(weight):
        return weight.reshape(weight.shape[0], size, -1).transpose(1, 0, 2)

    first = jnp.concatenate(
        [by_columns(w_query), by_columns(key_weight), by_columns(value_weight)], axis=2
    )
    gain_rows = jnp.pad(gains[None], ((0, pad_rows - 1), (0, first.shape[2] - gain_count)))
    first = jnp.concatenate(
        [first, jnp.broadcast_to(gain_rows[None], (size,) + gain_rows.shape)], axis=1
    )
    first, arrived = exchange(first, me)
    gain_rows = jnp.concatenate(
        [first[:, owned], jnp.zeros((pad_rows - size, first.shape[2]), bf16)]
    )
    first = jnp.concatenate(
        [first[:, :owned].reshape(size * owned, first.shape[2]), gain_rows]
    )
    first_along = gather_along(first)
    first_stacks = gather_beside(first_along)

    gate_up = jnp.concatenate([by_columns(w_gate), by_columns(w_up)], axis=2)
    gate_up, arrived = exchange(after(gate_up, *arrived), me)
    moved = after(jnp.concatenate([w_out, w_down]), *arrived)
    moved = lax.ppermute(moved, ("dp", "ctx"), forward_owner)
    places = jnp.concatenate([positions, segment_ids]).astype(jnp.int32)
    places = jnp.concatenate(gather_blocks(after(places, *arrived)), axis=1)
    x_own = tokens.reshape(block, MODEL_WIDTH)
    x_near, across = gather_near(after(x_own, *arrived))
    x_blocks = x_near + gather_far(across, first_stacks[0])
    cot_own = cotangent.reshape(block, MODEL_WIDTH)
    cot_blocks = gather_blocks(after(cot_own, first_stacks[1]))
    cot_near, cot_far = join(cot_blocks[:2]), join(cot_blocks[2:])

    moved_along = gather_along(after(moved, *first_along[1:]))
    moved_stacks = gather_beside(moved_along, first_stacks[1])
    gate_up_rows = after(gate_up.reshape(size * owned, -1), *moved_along[1:])
    gate_up = lax.all_gather(gate_up_rows, "dp", axis=0, tiled=True)
    w_first, gain_rows = interleave(first_stacks, (size * owned, pad_rows))
    w_first = after(w_first, gate_up_rows)
    full_gains = gain_rows.reshape(copies, pad_rows, -1)[:, :size, :gain_count].reshape(-1)
    gain_attn, gain_mlp, gain_query, gain_key = split_gains(full_gains)

    half = HEAD_SIZE // 2
    rates = THETA ** (-2.0 * jnp.arange(half, dtype=f32) / HEAD_SIZE)
    angles = places[0].astype(f32)[:, None] * rates[None, :]
    cosine, sine = jnp.cos(angles), jnp.sin(angles)
    cosine = jnp.concatenate([cosine, cosine], axis=1)
    sine = jnp.concatenate([-sine, sine], axis=1)
    lane = jnp.arange(FEATURES, dtype=jnp.int32)[None, :]
    same = places[1][:, None] == lane
    key_features = same.astype(bf16)
    query_features = jnp.where(same, 0.0, MASK_DEPTH).astype(bf16)
    gain_q_row, gain_k_row = gain_query[None], gain_key[None]
    normed, raw, q, k, v = project(
        x_blocks, gain_attn[None], w_first, cosine, sine, gain_q_row, gain_k_row, query_heads, key_heads
    )
    def attend_half(query, first):
        return attend(
            me_row, query, query_features, k, key_features, v, block, group, first, 2
        )

    def tn_dot(left, right):
        return lax.dot_general(left, right, (((0,), (0,)), ((), ())), preferred_element_type=f32)

    def by_copy(grad):
        return grad.astype(bf16).reshape(copies, -1, grad.shape[-1])

    def halves(value):
        return value[:block], value[block:]

    att_far, logs_far = attend_half(q, 2)
    att_far, *moved_stacks = lax.optimization_barrier((att_far, *moved_stacks))
    out_full, down_full = interleave(moved_stacks, (w_out.shape[0], w_down.shape[0]))
    att_across, att_corner = halves(att_far)
    part_corner, part_across = nn_dot(att_corner, out_full), nn_dot(att_across, out_full)
    toward, across = send_across(part_corner, part_across)
    att_near, logs_near = attend_half(after(q, toward, cot_near, cot_far), 0)
    att_near = after(att_near, gate_up)
    att_own, att_beside = halves(att_near)
    beside = [
        xor_permute(nn_dot(piece, out_full).astype(bf16), "ctx", 1)
        for piece in jnp.split(att_beside, 2)
    ]
    part_own = nn_dot(att_own, out_full) + jnp.concatenate(beside).astype(f32)
    middle = x_own.astype(f32) + part_own + across.astype(f32)
    h_blocks, across = gather_near(row_norm_apply(middle, gain_mlp).astype(bf16))
    h_near, hidden_near, d_both_near, down_own, down_beside, d_own, d_beside = feed(
        *h_blocks, cot_near, gate_up, down_full
    )
    h_blocks = gather_far(across, hidden_near)
    h_far, hidden_far, d_both_far, down_across, down_corner, d_across, d_corner = feed(
        *h_blocks, cot_far, gate_up, down_full
    )

    unused, across = send_across(d_corner, d_across)
    grad_down = (tn_dot(hidden_near, cot_near) + tn_dot(hidden_far, cot_far)).astype(bf16)
    grad_both = (tn_dot(h_near, d_both_near) + tn_dot(h_far, d_both_far)).astype(bf16)
    d_normed = sum_own(d_beside, d_own, after(across, grad_down, grad_both))
    d_middle, d_gain_mlp = norm_back(middle, gain_mlp, d_normed)
    d_middle = d_middle + cot_own.astype(f32)
    branches_near, branch_across = gather_near(d_middle.astype(bf16))

    pair_both = reduce_beside(by_copy(grad_both))
    pair_down = reduce_beside(by_copy(grad_down))

    def unattend_half(att, branches, logs, first, earlier=()):
        return unattend(
            me_row,
            q,
            query_features,
            k,
            key_features,
            v,
            att,
            branches,
            out_full,
            logs,
            block,
            group,
            first,
            earlier,
        )

    dq_near, *earlier = unattend_half(att_near, branches_near, logs_near, 0)
    terms_down = reduce_along(pair_down)
    dq_near, pair_both, *terms_down = lax.optimization_barrier((dq_near, pair_both, *terms_down))
    terms_both = reduce_along(pair_both)
    branches_far = gather_far(branch_across, dq_near)
    dq_far, dk, dv, grad_out = unattend_half(att_far, branches_far, logs_far, 2, earlier)
    pair_out = reduce_beside(by_copy(grad_out))
    dk, *terms_both = lax.optimization_barrier((dk, *terms_both))
    unused, down_across = send_across(down_corner, down_across, dk)
    grad_both = exchange(add_all(terms_both).reshape(size, owned, -1), me)[0]
    low, d_gain_heads = unproject(
        dq_near, dq_far, dk, dv, raw, cosine, sine, gain_q_row, gain_k_row, query_heads, key_heads
    )
    low, d_gain_heads, pair_out, grad_both = lax.optimization_barrier(
        (low, d_gain_heads, pair_out, grad_both)
    )
    terms_down = after_all(terms_down, low)
    terms_out = reduce_along(after(pair_out, low))
    low_own, low_beside, low_across, low_corner = (
        low[r * block : (r + 1) * block] for r in range(size)
    )
    toward, across = send_across(nt_dot(low_corner, w_first), nt_dot(low_across, w_first))
    part_beside, part_own = nt_dot(low_beside, w_first), nt_dot(low_own, w_first)
    d_normed_attn = sum_own(part_beside, part_own, across)
    d_inputs, unused = norm_back(x_own.astype(f32), gain_attn, d_normed_attn)
    grad_tokens = (d_middle + d_inputs).reshape(tokens.shape)

    grad_first = tn_dot(normed, low).astype(bf16)
    d_gain_attn = jnp.sum(w_first.astype(f32) * grad_first.astype(f32), axis=1) / gain_attn
    grad_gains = jnp.concatenate(
        [d_gain_attn, d_gain_mlp, d_gain_heads[0], d_gain_heads[1]]
    ).reshape(copies, size, gain_count)
    gain_block = jnp.pad(
        grad_gains.astype(bf16),
        ((0, 0), (0, pad_rows - size), (0, grad_first.shape[1] - gain_count)),
    )
    grad_first = jnp.concatenate(
        [grad_first.reshape(copies, size * owned, -1), gain_block], axis=1
    )
    pair_first = after(reduce_beside(grad_first), *terms_out, down_across)
    output = sum_own(down_beside, down_own, down_across)
    output = (middle + output).astype(bf16)
    terms_first = lax.optimization_barrier((*reduce_along(pair_first), across))[:-1]
    grad_first = add_all(terms_first)
    grad_out = add_all(after_all(terms_out, *terms_first))
    gain_part = grad_first[size * owned :][:size]
    gain_part = jnp.broadcast_to(gain_part[:, None], (size, pad_rows, gain_part.shape[1]))
    grad_first = jnp.concatenate(
        [grad_first[: size * owned].reshape(size, owned, -1), gain_part], axis=1
    )
    grad_first = exchange(grad_first, me)[0].astype(f32)
    grad_gains = jnp.sum(grad_first[:, owned, :gain_count], axis=0)
    grad_first = grad_first[:, :owned]

    def to_rows(pieces):
        return pieces.transpose(1, 0, 2).reshape(owned, -1)

    grad_query = to_rows(grad_first[:, :, :q_cols])
    grad_key = to_rows(grad_first[:, :, q_cols : q_cols + k_cols])
    grad_value = to_rows(grad_first[:, :, q_cols + k_cols :])
    grad_both = grad_both.astype(f32)
    grad_gate = to_rows(grad_both[:, :, :hidden_cols])
    grad_up = to_rows(grad_both[:, :, hidden_cols:])
    grad_out = lax.ppermute(grad_out, ("dp", "ctx"), backward_owner).astype(f32)
    grad_down = lax.ppermute(add_all(terms_down), ("dp", "ctx"), backward_owner).astype(f32)
    return (
        output.reshape(tokens.shape),
        grad_tokens,
        grad_query,
        grad_key,
        grad_value,
        grad_out,
        grad_gate,
        grad_up,
        grad_down,
        grad_gains,
    )


def solution(mesh):
    small = mesh.shape["ctx"] == 4
    return jax.shard_map(
        split_local if small else local,
        mesh=mesh,
        in_specs=(
            P("dp", "ctx", None),
            P(("dp", "ctx"), None),
            P(("dp", "ctx"), None),
            P(("dp", "ctx"), None),
            P(("dp", "ctx"), None),
            P(("dp", "ctx"), None),
            P(("dp", "ctx"), None),
            P(("dp", "ctx"), None),
            P(("dp", "ctx")),
            P("dp", "ctx"),
            P("dp", "ctx"),
            P("dp", "ctx", None),
        ),
        out_specs=(
            P("dp", "ctx", None),
            P("dp", "ctx", None),
            P(("dp", "ctx"), None),
            P(("dp", "ctx"), None),
            P(("dp", "ctx"), None),
            P(("dp", "ctx"), None),
            P(("dp", "ctx"), None),
            P(("dp", "ctx"), None),
            P(("dp", "ctx"), None),
            P(("dp", "ctx")),
        ),
        check_vma=False,
    )
```

```python
import functools

import jax
import jax.numpy as jnp
from jax import lax
from jax.experimental import pallas as pl
from jax.experimental.pallas import tpu as pltpu
from jax.sharding import PartitionSpec as P

MODEL_WIDTH = 1024
QUERY_HEADS = 16
KEY_VALUE_HEADS = 8
HEAD_SIZE = 128


EPSILON = 1e-06
THETA = 1000000.0


def row_norm_apply(value_rows, gain_vec):
    return (
        value_rows
        * lax.rsqrt(jnp.mean(value_rows * value_rows, axis=-1, keepdims=True) + EPSILON)
        * gain_vec
    )


def rotary_embed(value_rows, token_positions):
    half_size = value_rows.shape[-1] // 2
    inverse_rates = THETA ** (
        -2.0 * jnp.arange(half_size, dtype=jnp.float32) / value_rows.shape[-1]
    )
    angles = token_positions.astype(jnp.float32)[:, None] * inverse_rates[None, :]
    cosine = jnp.cos(angles)[:, None, :]
    sine_part = jnp.sin(angles)[:, None, :]
    former = value_rows[..., :half_size]
    second = value_rows[..., half_size:]
    return jnp.concatenate(
        [former * cosine - second * sine_part, second * cosine + former * sine_part], axis=-1
    )


def heads_per_group(raw_rows, gain_vec, token_positions, head_count):
    return rotary_embed(
        row_norm_apply(raw_rows.reshape(raw_rows.shape[0], head_count, HEAD_SIZE), gain_vec),
        token_positions,
    )


def split_gains(packed):
    packed = packed.astype(jnp.float32)
    return (
        packed[:MODEL_WIDTH],
        packed[MODEL_WIDTH : 2 * MODEL_WIDTH],
        packed[2 * MODEL_WIDTH : 2 * MODEL_WIDTH + HEAD_SIZE],
        packed[2 * MODEL_WIDTH + HEAD_SIZE :],
    )


def owner_major(grad_full, owners):
    return grad_full.reshape(owners, -1)


def local(
    tokens,
    w_query,
    key_weight,
    value_weight,
    w_out,
    w_gate,
    w_up,
    w_down,
    gains,
    segment_ids,
    positions,
    cotangent,
):
    sequence_count = tokens.shape[0]
    device_local_rows = tokens.shape[1]
    every_row_set = sequence_count * device_local_rows
    inputs = tokens.reshape(every_row_set, MODEL_WIDTH).astype(jnp.float32)
    token_positions = positions.reshape(every_row_set)
    cot_rows = cotangent.reshape(every_row_set, MODEL_WIDTH)
    head_groups = QUERY_HEADS // KEY_VALUE_HEADS
    score_scale = HEAD_SIZE ** (-0.5)
    f32 = jnp.float32
    brain_float_half = jnp.bfloat16
    owners = lax.axis_size(("dp", "ctx"))
    shard_shapes = (
        w_query.shape,
        key_weight.shape,
        value_weight.shape,
        w_out.shape,
        w_gate.shape,
        w_up.shape,
        w_down.shape,
        gains.shape,
    )
    gathered = (
        lax.all_gather(w_query, ("dp", "ctx"), axis=0, tiled=True),
        lax.all_gather(key_weight, ("dp", "ctx"), axis=0, tiled=True),
        lax.all_gather(value_weight, ("dp", "ctx"), axis=0, tiled=True),
        lax.all_gather(w_out, ("dp", "ctx"), axis=0, tiled=True),
        lax.all_gather(w_gate, ("dp", "ctx"), axis=0, tiled=True),
        lax.all_gather(w_up, ("dp", "ctx"), axis=0, tiled=True),
        lax.all_gather(w_down, ("dp", "ctx"), axis=0, tiled=True),
        lax.all_gather(gains, ("dp", "ctx"), axis=0, tiled=True),
    )
    full_query, full_key, full_value, full_out, full_gate, full_up, full_down, full_gains = gathered
    gain_attn, gain_mlp, gain_query, key_norm_gain = split_gains(full_gains)
    normalized_input = row_norm_apply(inputs, gain_attn).astype(brain_float_half)
    query_raw = jnp.dot(normalized_input, full_query, preferred_element_type=f32)
    unrotated_keys = jnp.dot(normalized_input, full_key, preferred_element_type=f32)
    value_low = (
        jnp.dot(normalized_input, full_value, preferred_element_type=f32)
        .astype(brain_float_half)
        .reshape(sequence_count, device_local_rows, KEY_VALUE_HEADS * HEAD_SIZE)
    )
    reduced_queries = heads_per_group(query_raw, gain_query, token_positions, QUERY_HEADS).astype(
        brain_float_half
    )
    key_low = (
        heads_per_group(unrotated_keys, key_norm_gain, token_positions, KEY_VALUE_HEADS)
        .astype(brain_float_half)
        .reshape(sequence_count, device_local_rows, KEY_VALUE_HEADS * HEAD_SIZE)
    )
    segment_low = segment_ids.astype(brain_float_half)
    gathered_keys, gathered_values, segment_all = (
        lax.all_gather(key_low, "ctx", axis=1, tiled=True),
        lax.all_gather(value_low, "ctx", axis=1, tiled=True),
        lax.all_gather(segment_low, "ctx", axis=1, tiled=True),
    )
    overall_rows = gathered_keys.shape[1]
    query_index = lax.axis_index("ctx") * device_local_rows + jnp.arange(
        device_local_rows, dtype=jnp.int32
    )
    key_index = jnp.arange(overall_rows, dtype=jnp.int32)
    allowed = (segment_low[:, :, None] == segment_all[:, None, :]) & (
        query_index[None, :, None] >= key_index[None, None, :]
    )
    grouped_queries = reduced_queries.reshape(
        sequence_count, device_local_rows, KEY_VALUE_HEADS, head_groups, HEAD_SIZE
    ).transpose(0, 2, 3, 1, 4)
    grouped_keys = gathered_keys.reshape(
        sequence_count, overall_rows, KEY_VALUE_HEADS, HEAD_SIZE
    ).transpose(0, 2, 1, 3)
    grouped_values = gathered_values.reshape(
        sequence_count, overall_rows, KEY_VALUE_HEADS, HEAD_SIZE
    ).transpose(0, 2, 1, 3)

    def masked_scores(query_head, key_head, mask_rows):
        scores = (
            jnp.einsum("rld,kd->rlk", query_head, key_head, preferred_element_type=f32)
            * score_scale
        )
        return jnp.where(mask_rows[None], scores, -1e30)

    def forward_sequence(slices):
        query_seq, key_seq, value_seq, mask_rows = slices

        def forward_head(head_slices):
            query_head, key_head, value_head = head_slices
            scores = masked_scores(query_head, key_head, mask_rows)
            row_peak = jnp.max(scores, axis=-1, keepdims=True)
            exp_scores = jnp.exp(scores - row_peak)
            denominator = jnp.sum(exp_scores, axis=-1, keepdims=True)
            prob_low = (exp_scores / denominator).astype(brain_float_half)
            mixed_head = jnp.einsum("rlk,kd->rld", prob_low, value_head, preferred_element_type=f32)
            return (mixed_head, row_peak[..., 0] + jnp.log(denominator[..., 0]))

        return lax.map(forward_head, (query_seq, key_seq, value_seq))

    mixed_heads, log_totals = lax.map(
        forward_sequence, (grouped_queries, grouped_keys, grouped_values, allowed)
    )
    attended = (
        mixed_heads.transpose(0, 3, 1, 2, 4)
        .reshape(every_row_set, QUERY_HEADS * HEAD_SIZE)
        .astype(brain_float_half)
    )
    middle = inputs + jnp.dot(attended, full_out, preferred_element_type=f32)
    normed_mlp = row_norm_apply(middle, gain_mlp).astype(brain_float_half)
    gate_value = jnp.dot(normed_mlp, full_gate, preferred_element_type=f32)
    up_value = jnp.dot(normed_mlp, full_up, preferred_element_type=f32)
    hidden = (jax.nn.silu(gate_value) * up_value).astype(brain_float_half)
    output = (middle + jnp.dot(hidden, full_down, preferred_element_type=f32)).astype(
        brain_float_half
    )
    regathered = (
        lax.all_gather(w_query, ("dp", "ctx"), axis=0, tiled=True),
        lax.all_gather(key_weight, ("dp", "ctx"), axis=0, tiled=True),
        lax.all_gather(value_weight, ("dp", "ctx"), axis=0, tiled=True),
        lax.all_gather(w_out, ("dp", "ctx"), axis=0, tiled=True),
        lax.all_gather(w_gate, ("dp", "ctx"), axis=0, tiled=True),
        lax.all_gather(w_up, ("dp", "ctx"), axis=0, tiled=True),
        lax.all_gather(w_down, ("dp", "ctx"), axis=0, tiled=True),
        lax.all_gather(gains, ("dp", "ctx"), axis=0, tiled=True),
    )
    back_query, back_key, back_value, back_out, back_gate, back_up, back_down, back_gains = (
        regathered
    )
    gain_attn, gain_mlp, gain_query, key_norm_gain = split_gains(back_gains)
    d_hidden = jnp.einsum("ld,fd->lf", cot_rows, back_down, preferred_element_type=f32)
    grad_down = jnp.einsum("lf,ld->fd", hidden, cot_rows, preferred_element_type=f32)
    unused, swiglu_pull = jax.vjp(
        lambda gate_in, up_in: jax.nn.silu(gate_in) * up_in, gate_value, up_value
    )
    d_gate, d_up = swiglu_pull(d_hidden)
    d_gate = d_gate.astype(brain_float_half)
    d_up = d_up.astype(brain_float_half)
    grad_gate = jnp.einsum("ld,lf->df", normed_mlp, d_gate, preferred_element_type=f32)
    grad_up = jnp.einsum("ld,lf->df", normed_mlp, d_up, preferred_element_type=f32)
    d_normed = jnp.einsum("lf,df->ld", d_gate, back_gate, preferred_element_type=f32)
    d_normed = d_normed + jnp.einsum("lf,df->ld", d_up, back_up, preferred_element_type=f32)
    unused, norm_pull = jax.vjp(row_norm_apply, middle, gain_mlp)
    d_middle, d_gain_mlp = norm_pull(d_normed)
    d_middle = d_middle + cot_rows.astype(f32)
    d_branch = d_middle.astype(brain_float_half)
    grad_out = jnp.einsum("lh,ld->hd", attended, d_branch, preferred_element_type=f32)
    attended_gradient = jnp.einsum(
        "ld,hd->lh", d_branch, back_out, preferred_element_type=f32
    ).astype(brain_float_half)
    group_gradient = attended_gradient.reshape(
        sequence_count, device_local_rows, KEY_VALUE_HEADS, head_groups, HEAD_SIZE
    ).transpose(0, 2, 3, 1, 4)

    def backward_sequence(slices):
        query_seq, key_seq, value_seq, d_seq, log_seq, mask_rows = slices

        def backward_head(head_slices):
            query_head, key_head, value_head, d_head, log_total = head_slices
            scores = masked_scores(query_head, key_head, mask_rows)
            probs_full = jnp.exp(scores - log_total[..., None])
            prob_low = probs_full.astype(brain_float_half)
            d_value = jnp.einsum("rlk,rld->kd", prob_low, d_head, preferred_element_type=f32)
            d_probs = jnp.einsum("rld,kd->rlk", d_head, value_head, preferred_element_type=f32)
            d_scores = probs_full * (
                d_probs - jnp.sum(probs_full * d_probs, axis=-1, keepdims=True)
            )
            d_scores = d_scores.astype(brain_float_half)
            d_query = (
                jnp.einsum("rlk,kd->rld", d_scores, key_head, preferred_element_type=f32)
                * score_scale
            )
            d_key = (
                jnp.einsum("rlk,rld->kd", d_scores, query_head, preferred_element_type=f32)
                * score_scale
            )
            return (d_query, d_key, d_value)

        return lax.map(backward_head, (query_seq, key_seq, value_seq, d_seq, log_seq))

    d_queries, key_rows_gradient, value_rows_gradient = lax.map(
        backward_sequence,
        (grouped_queries, grouped_keys, grouped_values, group_gradient, log_totals, allowed),
    )
    gathered_key_gradient = key_rows_gradient.transpose(2, 0, 1, 3).reshape(
        overall_rows, sequence_count, KEY_VALUE_HEADS * HEAD_SIZE
    )
    gathered_value_gradient = value_rows_gradient.transpose(2, 0, 1, 3).reshape(
        overall_rows, sequence_count, KEY_VALUE_HEADS * HEAD_SIZE
    )
    local_key_gradient, local_value_gradient = (
        lax.psum_scatter(
            gathered_key_gradient.astype(jnp.bfloat16), "ctx", scatter_dimension=0, tiled=True
        ).astype(jnp.float32),
        lax.psum_scatter(
            gathered_value_gradient.astype(jnp.bfloat16), "ctx", scatter_dimension=0, tiled=True
        ).astype(jnp.float32),
    )
    local_key_gradient = local_key_gradient.transpose(1, 0, 2)
    local_value_gradient = local_value_gradient.transpose(1, 0, 2)
    d_query_heads = d_queries.transpose(0, 3, 1, 2, 4).reshape(
        every_row_set, QUERY_HEADS, HEAD_SIZE
    )
    unused, query_pull = jax.vjp(
        lambda unnormalized_input, input_gain_vector: heads_per_group(
            unnormalized_input, input_gain_vector, token_positions, QUERY_HEADS
        ),
        query_raw,
        gain_query,
    )
    d_query_raw, d_gain_query = query_pull(d_query_heads)
    unused, key_pullback = jax.vjp(
        lambda unnormalized_input, input_gain_vector: heads_per_group(
            unnormalized_input, input_gain_vector, token_positions, KEY_VALUE_HEADS
        ),
        unrotated_keys,
        key_norm_gain,
    )
    unrotated_key_gradient, key_gain_gradient = key_pullback(
        local_key_gradient.reshape(every_row_set, KEY_VALUE_HEADS, HEAD_SIZE)
    )
    d_query_low = d_query_raw.astype(brain_float_half)
    d_key_low = unrotated_key_gradient.astype(brain_float_half)
    reduced_value_gradient = local_value_gradient.reshape(
        every_row_set, KEY_VALUE_HEADS * HEAD_SIZE
    ).astype(brain_float_half)
    grad_query = jnp.einsum("ld,lh->dh", normalized_input, d_query_low, preferred_element_type=f32)
    grad_key = jnp.einsum("ld,lh->dh", normalized_input, d_key_low, preferred_element_type=f32)
    grad_value = jnp.einsum(
        "ld,lh->dh", normalized_input, reduced_value_gradient, preferred_element_type=f32
    )
    d_normed_attn = jnp.einsum("lh,dh->ld", d_query_low, back_query, preferred_element_type=f32)
    d_normed_attn = d_normed_attn + jnp.einsum(
        "lh,dh->ld", d_key_low, back_key, preferred_element_type=f32
    )
    d_normed_attn = d_normed_attn + jnp.einsum(
        "lh,dh->ld", reduced_value_gradient, back_value, preferred_element_type=f32
    )
    unused, first_pull = jax.vjp(row_norm_apply, inputs, gain_attn)
    d_inputs, d_gain_attn = first_pull(d_normed_attn)
    grad_tokens = (d_middle + d_inputs).reshape(sequence_count, device_local_rows, MODEL_WIDTH)
    grad_gains = jnp.concatenate([d_gain_attn, d_gain_mlp, d_gain_query, key_gain_gradient])
    summed = (
        lax.psum_scatter(
            owner_major(grad_query, owners), ("dp", "ctx"), scatter_dimension=0, tiled=True
        ),
        lax.psum_scatter(
            owner_major(grad_key, owners), ("dp", "ctx"), scatter_dimension=0, tiled=True
        ),
        lax.psum_scatter(
            owner_major(grad_value, owners), ("dp", "ctx"), scatter_dimension=0, tiled=True
        ),
        lax.psum_scatter(
            owner_major(grad_out, owners), ("dp", "ctx"), scatter_dimension=0, tiled=True
        ),
        lax.psum_scatter(
            owner_major(grad_gate, owners), ("dp", "ctx"), scatter_dimension=0, tiled=True
        ),
        lax.psum_scatter(
            owner_major(grad_up, owners), ("dp", "ctx"), scatter_dimension=0, tiled=True
        ),
        lax.psum_scatter(
            owner_major(grad_down, owners), ("dp", "ctx"), scatter_dimension=0, tiled=True
        ),
        lax.psum_scatter(
            owner_major(grad_gains, owners), ("dp", "ctx"), scatter_dimension=0, tiled=True
        ),
    )
    grad_query = summed[0].reshape(shard_shapes[0])
    grad_key = summed[1].reshape(shard_shapes[1])
    grad_value = summed[2].reshape(shard_shapes[2])
    grad_out = summed[3].reshape(shard_shapes[3])
    grad_gate = summed[4].reshape(shard_shapes[4])
    grad_up = summed[5].reshape(shard_shapes[5])
    grad_down = summed[6].reshape(shard_shapes[6])
    grad_gains = summed[7].reshape(shard_shapes[7])
    return (
        output.reshape(sequence_count, device_local_rows, MODEL_WIDTH),
        grad_tokens,
        grad_query,
        grad_key,
        grad_value,
        grad_out,
        grad_gate,
        grad_up,
        grad_down,
        grad_gains,
    )

FEATURES = 128
MASK_DEPTH = -4096.0
LOG2_E = 1.4426950408889634
VMEM_BYTES = 56 * 1024 * 1024
bf16 = jnp.bfloat16
f32 = jnp.float32


def xor_permute(value, axis, offset):
    size = lax.axis_size(axis)
    return lax.ppermute(value, axis, [(i, i ^ offset) for i in range(size)])


def pick(stacked, index):
    return lax.dynamic_index_in_dim(stacked, index, 0, keepdims=False)


def exchange(stacked, me):
    size = stacked.shape[0]
    relative = [pick(stacked, me)]
    for offset in range(1, size):
        relative.append(xor_permute(pick(stacked, me ^ offset), "ctx", offset))
    arrived = relative[1:]
    relative = jnp.stack(relative)
    return jnp.stack([pick(relative, me ^ source) for source in range(size)]), arrived


def shift_z(value, offset):
    size = lax.axis_size("dp")
    return lax.ppermute(value, "dp", [(i, (i + 2 * offset) % size) for i in range(size)])


def assemble_kernel(splits, count, places_ref, *refs):
    pieces, results, sems = refs[:count], refs[count:-1], refs[-1]
    copies = []
    for piece in pieces:
        for slot in range(piece.shape[0]):
            n = len(copies) // len(splits)
            start = 0
            for m, rows in enumerate(splits):
                copy = pltpu.make_async_copy(
                    piece.at[slot, pl.ds(start, rows)],
                    results[m].at[places_ref[n]],
                    sems.at[n, m],
                )
                copy.start()
                copies.append(copy)
                start += rows
    for copy in copies:
        copy.wait()


def assemble(pieces, places, splits=None):
    slots = sum(piece.shape[0] for piece in pieces)
    rows, columns = pieces[0].shape[1:]
    splits = (rows,) if splits is None else splits
    anywhere = pl.BlockSpec(memory_space=pl.ANY)
    return pl.pallas_call(
        functools.partial(assemble_kernel, splits, len(pieces)),
        in_specs=[pl.BlockSpec(memory_space=pltpu.SMEM)]
        + [pl.BlockSpec(memory_space=pltpu.VMEM)] * len(pieces),
        out_specs=[anywhere] * len(splits),
        out_shape=[jax.ShapeDtypeStruct((slots, n, columns), pieces[0].dtype) for n in splits],
        scratch_shapes=[pltpu.SemaphoreType.DMA((slots, len(splits)))],
        compiler_params=pltpu.CompilerParams(vmem_limit_bytes=VMEM_BYTES),
        cost_estimate=pl.CostEstimate(
            flops=0, bytes_accessed=4 * slots * rows * columns, transcendentals=0
        ),
        name="assemble",
    )(places.astype(jnp.int32), *pieces)


def gather_along(value):
    return [value] + [shift_z(value, k) for k in range(1, lax.axis_size("dp") // 2)]


def gather_beside(along, *waits):
    depth = len(along)
    z = lax.axis_index("dp") // 2
    places = jnp.stack([(z - k) % depth for k in range(depth)])
    stack = assemble([piece[None] for piece in along], places)[0]
    stack = after(stack, *waits)
    return [stack, xor_permute(stack, "dp", 1)]


def interleave(stacks, splits):
    depth = stacks[0].shape[0]
    y = lax.axis_index("dp") % 2
    rows = 2 * jnp.arange(depth)
    results = assemble(stacks, jnp.concatenate([rows + y, rows + 1 - y]), splits)
    return [result.reshape(-1, result.shape[-1]) for result in results]


def send_beside(grad):
    depth = grad.shape[0] // 2
    y = lax.axis_index("dp") % 2
    grad = grad.reshape((depth, 2) + grad.shape[1:])
    away = lax.dynamic_index_in_dim(grad, 1 - y, 1, keepdims=False)
    kept = lax.dynamic_index_in_dim(grad, y, 1, keepdims=False)
    return kept, away, xor_permute(away, "dp", 1)


def add_beside(kept, away, arrived):
    return (kept.astype(f32) + arrived.astype(f32)).astype(bf16)


def reduce_along(pair):
    depth = pair.shape[0]
    z = lax.axis_index("dp") // 2
    sent = [shift_z(pick(pair, (z + k) % depth), k) for k in range(1, depth)]
    return [pick(pair, z)] + sent


def add_all(terms):
    total = terms[0].astype(f32)
    for term in terms[1:]:
        total = total + term.astype(f32)
    return total.astype(bf16)


def after(value, *others):
    return lax.optimization_barrier((value, *others))[0]


def after_all(values, *others):
    return lax.optimization_barrier((*values, *others))[: len(values)]


def gather_blocks(value):
    across = xor_permute(value, "ctx", 2)
    beside = xor_permute(value, "ctx", 1)
    corner = xor_permute(across, "ctx", 1)
    return [value, beside, across, corner]


def gather_near(value):
    return [value, xor_permute(value, "ctx", 1)], xor_permute(value, "ctx", 2)


def gather_far(across, *waits):
    across = after(across, *waits)
    return [across, xor_permute(across, "ctx", 1)]


def send_across(part_corner, part_across, *waits):
    corner = xor_permute(part_corner.astype(bf16), "ctx", 1)
    toward = (part_across.astype(f32) + corner.astype(f32)).astype(bf16)
    toward = after(toward, *waits) if waits else toward
    return toward, xor_permute(toward, "ctx", 2)


def sum_own(part_beside, part_own, across):
    beside = xor_permute(part_beside.astype(bf16), "ctx", 1)
    return part_own.astype(f32) + beside.astype(f32) + across.astype(f32)


def nt_dot(left, right):
    return lax.dot_general(left, right, (((1,), (1,)), ((), ())), preferred_element_type=f32)


def nn_dot(left, right):
    return jnp.dot(left, right, preferred_element_type=f32)


def project_kernel(
    query_heads,
    key_heads,
    per_block,
    x_refs,
    gain_ref,
    weight_ref,
    cos_ref,
    sin_ref,
    gain_q_ref,
    gain_k_ref,
    normed_ref,
    raw_ref,
    q_ref,
    k_ref,
    v_ref,
    held_ref,
):
    for r, x_ref in enumerate(x_refs):

        @pl.when(pl.program_id(0) // per_block == r)
        def _():
            held_ref[...] = x_ref[...]

    x = held_ref[...].astype(f32)
    scale = lax.rsqrt(jnp.mean(x * x, axis=-1, keepdims=True) + EPSILON)
    normed = (x * scale * gain_ref[...]).astype(bf16)
    normed_ref[...] = normed
    raw = nn_dot(normed, weight_ref[...])
    turned = (query_heads + key_heads) * HEAD_SIZE
    raw_ref[...] = raw[:, :turned]
    v_ref[...] = raw[:, turned:].astype(bf16)
    cosine = cos_ref[...]
    sine = sin_ref[...]
    for head in range(query_heads + key_heads):
        rows = raw[:, head * HEAD_SIZE : (head + 1) * HEAD_SIZE]
        gain = gain_q_ref[...] if head < query_heads else gain_k_ref[...]
        rows = rows * lax.rsqrt(jnp.mean(rows * rows, axis=-1, keepdims=True) + EPSILON) * gain
        rows = (rows * cosine + pltpu.roll(rows, HEAD_SIZE // 2, 1) * sine).astype(bf16)
        if head < query_heads:
            q_ref[:, head * HEAD_SIZE : (head + 1) * HEAD_SIZE] = rows
        else:
            at = (head - query_heads) * HEAD_SIZE
            k_ref[:, at : at + HEAD_SIZE] = rows


def project(x_blocks, gain, weight, cosine, sine, gain_q, gain_k, query_heads, key_heads):
    rows, width = x_blocks[0].shape
    block = 256
    per_block = rows // block
    rows = rows * len(x_blocks)
    turned = (query_heads + key_heads) * HEAD_SIZE
    columns = weight.shape[1]

    def tall(n):
        return pl.BlockSpec((block, n), lambda i: (i, 0))

    def whole(shape):
        return pl.BlockSpec(shape, lambda i: (0, 0))

    def part(r):
        return pl.BlockSpec(
            (block, width), lambda i: (jnp.clip(i - r * per_block, 0, per_block - 1), 0)
        )

    return pl.pallas_call(
        functools.partial(project_kernel, query_heads, key_heads, per_block),
        grid=(rows // block,),
        in_specs=[
            [part(r) for r in range(len(x_blocks))],
            whole((1, width)),
            whole(weight.shape),
            tall(HEAD_SIZE),
            tall(HEAD_SIZE),
            whole((1, HEAD_SIZE)),
            whole((1, HEAD_SIZE)),
        ],
        out_specs=[
            tall(width),
            tall(turned),
            tall(query_heads * HEAD_SIZE),
            tall(key_heads * HEAD_SIZE),
            tall(key_heads * HEAD_SIZE),
        ],
        out_shape=[
            jax.ShapeDtypeStruct((rows, width), bf16),
            jax.ShapeDtypeStruct((rows, turned), f32),
            jax.ShapeDtypeStruct((rows, query_heads * HEAD_SIZE), bf16),
            jax.ShapeDtypeStruct((rows, key_heads * HEAD_SIZE), bf16),
            jax.ShapeDtypeStruct((rows, key_heads * HEAD_SIZE), bf16),
        ],
        scratch_shapes=[pltpu.VMEM((block, width), bf16)],
        compiler_params=pltpu.CompilerParams(vmem_limit_bytes=VMEM_BYTES),
        cost_estimate=pl.CostEstimate(
            flops=2 * rows * width * columns,
            bytes_accessed=rows * (4 * width + 4 * turned + 2 * columns) + 2 * width * columns,
            transcendentals=0,
        ),
        name="project",
    )(list(x_blocks), gain, weight, cosine, sine, gain_q, gain_k)


def unproject_kernel(
    query_heads,
    key_heads,
    half,
    dq_near_ref,
    dq_far_ref,
    dk_ref,
    dv_ref,
    raw_ref,
    cos_ref,
    sin_ref,
    gain_q_ref,
    gain_k_ref,
    low_ref,
    dgain_ref,
):
    @pl.when(pl.program_id(0) == 0)
    def _():
        dgain_ref[...] = jnp.zeros_like(dgain_ref)

    cosine = cos_ref[...]
    sine = sin_ref[...]
    total_q = jnp.zeros((1, HEAD_SIZE), f32)
    total_k = jnp.zeros((1, HEAD_SIZE), f32)
    for head in range(query_heads + key_heads):
        at = head * HEAD_SIZE
        raw = raw_ref[:, at : at + HEAD_SIZE]
        if head < query_heads:
            lanes = slice(at, at + HEAD_SIZE)
            grad = jnp.where(pl.program_id(0) < half, dq_near_ref[:, lanes], dq_far_ref[:, lanes])
            gain = gain_q_ref[...]
        else:
            back = (head - query_heads) * HEAD_SIZE
            grad = dk_ref[:, back : back + HEAD_SIZE]
            gain = gain_k_ref[...]
        grad = grad * cosine - pltpu.roll(grad, HEAD_SIZE // 2, 1) * sine
        scale = lax.rsqrt(jnp.mean(raw * raw, axis=-1, keepdims=True) + EPSILON)
        unit = raw * scale
        summed = jnp.sum(unit * grad, axis=0, keepdims=True)
        if head < query_heads:
            total_q += summed
        else:
            total_k += summed
        grad = grad * gain
        mean = jnp.mean(unit * grad, axis=-1, keepdims=True)
        low_ref[:, at : at + HEAD_SIZE] = (scale * (grad - unit * mean)).astype(bf16)
    low_ref[:, (query_heads + key_heads) * HEAD_SIZE :] = dv_ref[...].astype(bf16)
    dgain_ref[0:1, :] += total_q
    dgain_ref[1:2, :] += total_k


def unproject(dq_near, dq_far, dk, dv, raw, cosine, sine, gain_q, gain_k, query_heads, key_heads):
    rows = dk.shape[0]
    block = 256
    half = rows // block // 2
    columns = (query_heads + 2 * key_heads) * HEAD_SIZE

    def tall(n):
        return pl.BlockSpec((block, n), lambda i: (i, 0))

    def whole(shape):
        return pl.BlockSpec(shape, lambda i: (0, 0))

    return pl.pallas_call(
        functools.partial(unproject_kernel, query_heads, key_heads, half),
        grid=(rows // block,),
        in_specs=[
            pl.BlockSpec((block, dq_near.shape[1]), lambda i: (jnp.minimum(i, half - 1), 0)),
            pl.BlockSpec((block, dq_far.shape[1]), lambda i: (jnp.maximum(i - half, 0), 0)),
            tall(dk.shape[1]),
            tall(dv.shape[1]),
            tall(raw.shape[1]),
            tall(HEAD_SIZE),
            tall(HEAD_SIZE),
            whole((1, HEAD_SIZE)),
            whole((1, HEAD_SIZE)),
        ],
        out_specs=[tall(columns), whole((8, HEAD_SIZE))],
        out_shape=[
            jax.ShapeDtypeStruct((rows, columns), bf16),
            jax.ShapeDtypeStruct((8, HEAD_SIZE), f32),
        ],
        compiler_params=pltpu.CompilerParams(vmem_limit_bytes=VMEM_BYTES),
        cost_estimate=pl.CostEstimate(
            flops=20 * rows * columns, bytes_accessed=20 * rows * columns, transcendentals=0
        ),
        name="unproject",
    )(dq_near, dq_far, dk, dv, raw, cosine, sine, gain_q, gain_k)


def attend_kernel(
    group, block, first, me_ref, q_ref, qf_ref, k_ref, kf_ref, v_ref, o_ref, log_ref, total_ref
):
    me = me_ref[0]
    at_query = (pl.program_id(1) + first) ^ me
    factor = HEAD_SIZE ** (-0.5) * LOG2_E
    query_features = qf_ref[...]
    ones = jnp.ones((block, HEAD_SIZE), bf16)
    total_ref[...] = jnp.zeros_like(total_ref)

    def step(at_key, diagonal):
        rows = pl.ds(pl.multiple_of((at_key ^ me) * block, block), block)
        keys = jnp.concatenate([k_ref[rows, :], kf_ref[rows, :]], axis=1)
        values = jnp.concatenate([v_ref[rows, :], ones], axis=1)
        for head in range(group):
            query = q_ref[:, head * HEAD_SIZE : (head + 1) * HEAD_SIZE]
            scores = nt_dot(jnp.concatenate([query, query_features], axis=1), keys)
            probs = jnp.exp2(scores * factor)
            if diagonal:
                down = lax.broadcasted_iota(jnp.int32, probs.shape, 0)
                right = lax.broadcasted_iota(jnp.int32, probs.shape, 1)
                probs = jnp.where(down >= right, probs, 0.0)
            total_ref[head] += nn_dot(probs.astype(bf16), values)

    @pl.loop(0, at_query)
    def _(at_key):
        step(at_key, False)

    step(at_query, True)
    for head in range(group):
        weighted = total_ref[head, :, :HEAD_SIZE]
        summed = total_ref[head, :, HEAD_SIZE:]
        o_ref[:, head * HEAD_SIZE : (head + 1) * HEAD_SIZE] = (weighted / summed).astype(bf16)
        log_ref[0, head : head + 1, :] = jnp.log2(summed.T[0:1, :])


def attend(me, q, qf, k, kf, v, block, group, first, count):
    rows = k.shape[0]
    key_heads = k.shape[1] // HEAD_SIZE
    pairs = key_heads * group * count * block * rows * 5 // 8
    return pl.pallas_call(
        functools.partial(attend_kernel, group, block, first),
        grid_spec=pltpu.PrefetchScalarGridSpec(
            num_scalar_prefetch=1,
            grid=(key_heads, count),
            in_specs=[
                pl.BlockSpec((block, group * HEAD_SIZE), lambda g, i, me: (i + first, g)),
                pl.BlockSpec((block, FEATURES), lambda g, i, me: (i + first, 0)),
                pl.BlockSpec((rows, HEAD_SIZE), lambda g, i, me: (0, g)),
                pl.BlockSpec((rows, FEATURES), lambda g, i, me: (0, 0)),
                pl.BlockSpec((rows, HEAD_SIZE), lambda g, i, me: (0, g)),
            ],
            out_specs=[
                pl.BlockSpec((block, group * HEAD_SIZE), lambda g, i, me: (i, g)),
                pl.BlockSpec((1, group, block), lambda g, i, me: (g, 0, i)),
            ],
            scratch_shapes=[pltpu.VMEM((group, block, 2 * HEAD_SIZE), f32)],
        ),
        out_shape=[
            jax.ShapeDtypeStruct((count * block, q.shape[1]), bf16),
            jax.ShapeDtypeStruct((key_heads, group, count * block), f32),
        ],
        compiler_params=pltpu.CompilerParams(vmem_limit_bytes=VMEM_BYTES),
        cost_estimate=pl.CostEstimate(
            flops=8 * pairs * HEAD_SIZE, bytes_accessed=10 * q.size, transcendentals=pairs
        ),
        name="attend",
    )(me, q, qf, k, kf, v)


def unattend_kernel(
    group,
    block,
    first,
    resumed,
    me_ref,
    q_ref,
    qf_ref,
    k_ref,
    kf_ref,
    v_ref,
    o_ref,
    branch_first_ref,
    branch_second_ref,
    out_ref,
    log_ref,
    *rest,
):
    if resumed:
        dk_in_ref, dv_in_ref, d_weight_in_ref, *rest = rest
    dq_ref, dk_ref, dv_ref, d_weight_ref, flipped_ref, total_ref, do_ref = rest
    me = me_ref[0]
    at_query = (pl.program_id(1) + first) ^ me
    scale = HEAD_SIZE ** (-0.5)
    factor = scale * LOG2_E

    @pl.when(pl.program_id(1) == 0)
    def _():
        dk_ref[...] = dk_in_ref[...] if resumed else jnp.zeros_like(dk_ref)
        dv_ref[...] = dv_in_ref[...] if resumed else jnp.zeros_like(dv_ref)
        d_weight_ref[...] = d_weight_in_ref[...] if resumed else jnp.zeros_like(d_weight_ref)
        flipped_ref[...] = k_ref[...].astype(f32).T.astype(bf16)

    def take(branch_ref):
        do_ref[...] = nt_dot(branch_ref[...], out_ref[...]).astype(bf16)
        turned = o_ref[...].astype(f32).T.astype(bf16)
        d_weight_ref[...] += nn_dot(turned, branch_ref[...])

    @pl.when(pl.program_id(1) == 0)
    def _():
        take(branch_first_ref)

    @pl.when(pl.program_id(1) == 1)
    def _():
        take(branch_second_ref)

    total_ref[...] = jnp.zeros_like(total_ref)
    query_features = qf_ref[...]
    deltas = []
    for head in range(group):
        lanes = slice(head * HEAD_SIZE, (head + 1) * HEAD_SIZE)
        product = do_ref[:, lanes].astype(f32) * o_ref[:, lanes].astype(f32)
        deltas.append(jnp.sum(product.T, axis=0, keepdims=True))

    def step(at_key, diagonal):
        start = pl.multiple_of((at_key ^ me) * block, block)
        rows = pl.ds(start, block)
        keys = jnp.concatenate([k_ref[rows, :], kf_ref[rows, :]], axis=1)
        values = v_ref[rows, :]
        for head in range(group):
            lanes = slice(head * HEAD_SIZE, (head + 1) * HEAD_SIZE)
            query = q_ref[:, lanes]
            d_out = do_ref[:, lanes]
            scores = nt_dot(keys, jnp.concatenate([query, query_features], axis=1))
            probs = jnp.exp2(scores * factor - log_ref[0, head : head + 1, :])
            if diagonal:
                key_at = lax.broadcasted_iota(jnp.int32, probs.shape, 0)
                query_at = lax.broadcasted_iota(jnp.int32, probs.shape, 1)
                probs = jnp.where(query_at >= key_at, probs, 0.0)
            d_scores = (probs * (nt_dot(values, d_out) - deltas[head])).astype(bf16)
            dv_ref[rows, :] += nn_dot(probs.astype(bf16), d_out)
            dk_ref[rows, :] += nn_dot(d_scores, query)
            total_ref[head] += nn_dot(flipped_ref[:, rows], d_scores)

    @pl.loop(0, at_query)
    def _(at_key):
        step(at_key, False)

    step(at_query, True)
    for head in range(group):
        dq_ref[:, head * HEAD_SIZE : (head + 1) * HEAD_SIZE] = total_ref[head].T * scale

    if resumed:

        @pl.when(pl.program_id(1) == pl.num_programs(1) - 1)
        def _():
            dk_ref[...] = dk_ref[...] * scale


def unattend(me, q, qf, k, kf, v, o, branches, out, logs, block, group, first, earlier=()):
    count = len(branches)
    rows = k.shape[0]
    key_heads = k.shape[1] // HEAD_SIZE
    width = out.shape[1]
    lanes = group * HEAD_SIZE

    def by_query(n):
        return pl.BlockSpec((block, n), lambda g, i, me: (i, g))

    by_key = pl.BlockSpec((rows, HEAD_SIZE), lambda g, i, me: (0, g))
    by_head = pl.BlockSpec((lanes, width), lambda g, i, me: (g, 0))
    whole = pl.BlockSpec((block, width), lambda g, i, me: (0, 0))
    return pl.pallas_call(
        functools.partial(unattend_kernel, group, block, first, bool(earlier)),
        grid_spec=pltpu.PrefetchScalarGridSpec(
            num_scalar_prefetch=1,
            grid=(key_heads, count),
            in_specs=[
                pl.BlockSpec((block, lanes), lambda g, i, me: (i + first, g)),
                pl.BlockSpec((block, FEATURES), lambda g, i, me: (i + first, 0)),
                by_key,
                pl.BlockSpec((rows, FEATURES), lambda g, i, me: (0, 0)),
                by_key,
                by_query(lanes),
                whole,
                whole,
                by_head,
                pl.BlockSpec((1, group, block), lambda g, i, me: (g, 0, i)),
            ]
            + ([by_key, by_key, by_head] if earlier else []),
            out_specs=[by_query(lanes), by_key, by_key, by_head],
            scratch_shapes=[
                pltpu.VMEM((HEAD_SIZE, rows), bf16),
                pltpu.VMEM((group, HEAD_SIZE, block), f32),
                pltpu.VMEM((block, lanes), bf16),
            ],
        ),
        out_shape=[
            jax.ShapeDtypeStruct((count * block, q.shape[1]), f32),
            jax.ShapeDtypeStruct(k.shape, f32),
            jax.ShapeDtypeStruct(v.shape, f32),
            jax.ShapeDtypeStruct(out.shape, f32),
        ],
        compiler_params=pltpu.CompilerParams(vmem_limit_bytes=VMEM_BYTES),
        cost_estimate=pl.CostEstimate(
            flops=70 * count * block * rows * key_heads * group * HEAD_SIZE // 8,
            bytes_accessed=20 * q.size,
            transcendentals=0,
        ),
        name="unattend",
    )(me, q, qf, k, kf, v, o, *branches, out, logs, *earlier)


def feed_kernel(
    units,
    half,
    first_ref,
    second_ref,
    cot_first_ref,
    cot_second_ref,
    both_ref,
    down_ref,
    h_ref,
    cot_ref,
    hidden_ref,
    d_both_ref,
    part_first_ref,
    part_second_ref,
    d_part_first_ref,
    d_part_second_ref,
):
    in_first = pl.program_id(0) < half

    @pl.when(in_first)
    def _():
        h_ref[...] = first_ref[...]
        cot_ref[...] = cot_first_ref[...]

    @pl.when(jnp.logical_not(in_first))
    def _():
        h_ref[...] = second_ref[...]
        cot_ref[...] = cot_second_ref[...]

    both = nn_dot(h_ref[...], both_ref[...])
    d_hidden = nt_dot(cot_ref[...], down_ref[...])
    gate, up = both[:, :units], both[:, units:]
    sigmoid = 1.0 / (1.0 + jnp.exp(-gate))
    silu = gate * sigmoid
    hidden = (silu * up).astype(bf16)
    hidden_ref[...] = hidden
    part = nn_dot(hidden, down_ref[...]).astype(bf16)
    d_gate = (d_hidden * up * sigmoid * (1.0 + gate * (1.0 - sigmoid))).astype(bf16)
    d_up = (d_hidden * silu).astype(bf16)
    d_both = jnp.concatenate([d_gate, d_up], axis=1)
    d_both_ref[...] = d_both
    d_part = nt_dot(d_both, both_ref[...]).astype(bf16)

    @pl.when(in_first)
    def _():
        part_first_ref[...] = part
        d_part_first_ref[...] = d_part

    @pl.when(jnp.logical_not(in_first))
    def _():
        part_second_ref[...] = part
        d_part_second_ref[...] = d_part


def feed(h_first, h_second, cot_first, cot_second, both, down):
    rows, width = 2 * cot_first.shape[0], cot_first.shape[1]
    units = down.shape[0]
    block = 256
    half = rows // block // 2

    def tall(n):
        return pl.BlockSpec((block, n), lambda i: (i, 0))

    def whole(shape):
        return pl.BlockSpec(shape, lambda i: (0, 0))

    of_first = pl.BlockSpec((block, width), lambda i: (jnp.minimum(i, half - 1), 0))
    of_second = pl.BlockSpec((block, width), lambda i: (jnp.maximum(i - half, 0), 0))
    shapes = [(rows, width), (rows, width), (rows, units), (rows, 2 * units)] + [(rows // 2, width)] * 4
    return pl.pallas_call(
        functools.partial(feed_kernel, units, half),
        grid=(rows // block,),
        in_specs=[of_first, of_second] * 2 + [whole(both.shape), whole(down.shape)],
        out_specs=[tall(width), tall(width), tall(units), tall(2 * units)] + [of_first, of_second] * 2,
        out_shape=[jax.ShapeDtypeStruct(shape, bf16) for shape in shapes],
        compiler_params=pltpu.CompilerParams(vmem_limit_bytes=VMEM_BYTES),
        cost_estimate=pl.CostEstimate(
            flops=12 * rows * width * units,
            bytes_accessed=rows * (10 * width + 6 * units) + 6 * width * units,
            transcendentals=rows * units,
        ),
        name="feed",
    )(h_first, h_second, cot_first, cot_second, both, down)


def norm_back(value_rows, gain_vec, grad):
    scale = lax.rsqrt(jnp.mean(value_rows * value_rows, axis=-1, keepdims=True) + EPSILON)
    unit = value_rows * scale
    d_gain = jnp.sum(unit * grad, axis=0)
    grad = grad * gain_vec
    return scale * (grad - unit * jnp.mean(unit * grad, axis=-1, keepdims=True)), d_gain


def split_local(
    tokens,
    w_query,
    key_weight,
    value_weight,
    w_out,
    w_gate,
    w_up,
    w_down,
    gains,
    segment_ids,
    positions,
    cotangent,
):
    size = lax.axis_size("ctx")
    copies = lax.axis_size("dp")
    me = lax.axis_index("ctx")
    me_row = me.reshape(1).astype(jnp.int32)
    block = tokens.shape[1]
    group = QUERY_HEADS // KEY_VALUE_HEADS
    query_heads = QUERY_HEADS // size
    key_heads = KEY_VALUE_HEADS // size
    q_cols = query_heads * HEAD_SIZE
    k_cols = key_heads * HEAD_SIZE
    owned = w_query.shape[0]
    hidden_cols = w_gate.shape[1] // size
    gain_count = gains.shape[0]
    pad_rows = 16
    forward_owner = [
        (b, (b % copies) * size + b // copies) for b in range(size * copies)
    ]
    backward_owner = [(target, source) for source, target in forward_owner]

    def by_columns(weight):
        return weight.reshape(weight.shape[0], size, -1).transpose(1, 0, 2)

    first = jnp.concatenate(
        [by_columns(w_query), by_columns(key_weight), by_columns(value_weight)], axis=2
    )
    gain_rows = jnp.pad(gains[None], ((0, pad_rows - 1), (0, first.shape[2] - gain_count)))
    first = jnp.concatenate(
        [first, jnp.broadcast_to(gain_rows[None], (size,) + gain_rows.shape)], axis=1
    )
    first, arrived = exchange(first, me)
    gain_rows = jnp.concatenate(
        [first[:, owned], jnp.zeros((pad_rows - size, first.shape[2]), bf16)]
    )
    first = jnp.concatenate(
        [first[:, :owned].reshape(size * owned, first.shape[2]), gain_rows]
    )
    first_along = gather_along(first)
    first_stacks = gather_beside(first_along)

    gate_up = jnp.concatenate([by_columns(w_gate), by_columns(w_up)], axis=2)
    gate_up, arrived = exchange(after(gate_up, *arrived), me)
    moved = after(jnp.concatenate([w_out, w_down]), *arrived)
    moved = lax.ppermute(moved, ("dp", "ctx"), forward_owner)
    places = jnp.concatenate([positions, segment_ids]).astype(jnp.int32)
    places = jnp.concatenate(gather_blocks(after(places, *arrived)), axis=1)
    x_own = tokens.reshape(block, MODEL_WIDTH)
    x_near, across = gather_near(after(x_own, *arrived))
    x_blocks = x_near + gather_far(across, first_stacks[0])

    moved_along = gather_along(after(moved, first_stacks[0], x_near[1]))
    first_stacks = [first_stacks[0], after(first_stacks[1], *moved_along[1:])]
    cot_own = cotangent.reshape(block, MODEL_WIDTH)
    cot_near, cot_across = gather_near(after(cot_own, first_stacks[1]))
    moved_stacks = gather_beside(moved_along, first_stacks[1])
    gate_up_rows = after(gate_up.reshape(size * owned, -1), *moved_along[1:])
    gate_up = lax.all_gather(gate_up_rows, "dp", axis=0, tiled=True)
    w_first, gain_rows = interleave(first_stacks, (size * owned, pad_rows))
    w_first = after(w_first, gate_up_rows)
    full_gains = gain_rows.reshape(copies, pad_rows, -1)[:, :size, :gain_count].reshape(-1)
    gain_attn, gain_mlp, gain_query, gain_key = split_gains(full_gains)

    half = HEAD_SIZE // 2
    rates = THETA ** (-2.0 * jnp.arange(half, dtype=f32) / HEAD_SIZE)
    angles = places[0].astype(f32)[:, None] * rates[None, :]
    cosine, sine = jnp.cos(angles), jnp.sin(angles)
    cosine = jnp.concatenate([cosine, cosine], axis=1)
    sine = jnp.concatenate([-sine, sine], axis=1)
    lane = jnp.arange(FEATURES, dtype=jnp.int32)[None, :]
    same = places[1][:, None] == lane
    key_features = same.astype(bf16)
    query_features = jnp.where(same, 0.0, MASK_DEPTH).astype(bf16)
    gain_q_row, gain_k_row = gain_query[None], gain_key[None]
    normed, raw, q, k, v = project(
        x_blocks, gain_attn[None], w_first, cosine, sine, gain_q_row, gain_k_row, query_heads, key_heads
    )
    def attend_half(query, first):
        return attend(
            me_row, query, query_features, k, key_features, v, block, group, first, 2
        )

    def tn_dot(left, right):
        return lax.dot_general(left, right, (((0,), (0,)), ((), ())), preferred_element_type=f32)

    def by_copy(grad):
        return grad.astype(bf16).reshape(copies, -1, grad.shape[-1])

    def halves(value):
        return value[:block], value[block:]

    cot_blocks = cot_near + gather_far(cot_across, q)
    att_far, logs_far = attend_half(q, 2)
    att_far, *both = lax.optimization_barrier((att_far, *moved_stacks, *cot_blocks))
    moved_stacks, cot_blocks = both[:2], both[2:]
    out_full, down_full = interleave(moved_stacks, (w_out.shape[0], w_down.shape[0]))
    att_across, att_corner = halves(att_far)
    part_corner, part_across = nn_dot(att_corner, out_full), nn_dot(att_across, out_full)
    toward, across = send_across(part_corner, part_across)
    att_near, logs_near = attend_half(after(q, toward), 0)
    att_near = after(att_near, gate_up)
    att_own, att_beside = halves(att_near)
    beside = [
        xor_permute(nn_dot(piece, out_full).astype(bf16), "ctx", 1)
        for piece in jnp.split(att_beside, 2)
    ]
    part_own = nn_dot(att_own, out_full) + jnp.concatenate(beside).astype(f32)
    middle = x_own.astype(f32) + part_own + across.astype(f32)
    h_blocks, across = gather_near(row_norm_apply(middle, gain_mlp).astype(bf16))
    h_near, cot_near, hidden_near, d_both_near, down_own, down_beside, d_own, d_beside = feed(
        *h_blocks, *cot_blocks[:2], gate_up, down_full
    )
    h_blocks = gather_far(across, hidden_near)
    h_far, cot_far, hidden_far, d_both_far, down_across, down_corner, d_across, d_corner = feed(
        *h_blocks, *cot_blocks[2:], gate_up, down_full
    )

    toward, across = send_across(d_corner, d_across)
    d_both_far, cot_far = lax.optimization_barrier((d_both_far, cot_far, toward))[:2]
    grad_down = (tn_dot(hidden_near, cot_near) + tn_dot(hidden_far, cot_far)).astype(bf16)
    grad_both = (tn_dot(h_near, d_both_near) + tn_dot(h_far, d_both_far)).astype(bf16)
    d_normed = sum_own(d_beside, d_own, after(across, grad_down, grad_both))
    d_middle, d_gain_mlp = norm_back(middle, gain_mlp, d_normed)
    d_middle = d_middle + cot_own.astype(f32)
    branches_near, branch_across = gather_near(d_middle.astype(bf16))

    grad_down = grad_down.reshape(copies, -1, 2 * hidden_cols)
    grad_feed = jnp.concatenate([by_copy(grad_both), grad_down], axis=1)
    pair_feed = add_beside(*send_beside(grad_feed))

    def unattend_half(att, branches, logs, first, earlier=()):
        return unattend(
            me_row,
            q,
            query_features,
            k,
            key_features,
            v,
            att,
            branches,
            out_full,
            logs,
            block,
            group,
            first,
            earlier,
        )

    dq_near, *earlier = unattend_half(att_near, branches_near, logs_near, 0)
    dq_near, pair_feed = lax.optimization_barrier((dq_near, pair_feed))
    terms_both = reduce_along(pair_feed[:, : size * owned])
    branches_far = gather_far(branch_across, dq_near)
    dq_far, dk, dv, grad_out = unattend_half(att_far, branches_far, logs_far, 2, earlier)
    pair_out = add_beside(*send_beside(by_copy(grad_out)))
    dk, *terms_both = lax.optimization_barrier((dk, *terms_both))
    terms_down = reduce_along(after(pair_feed[:, size * owned :], dk))
    unused, down_across = send_across(down_corner, down_across, dk)
    low, d_gain_heads = unproject(
        dq_near, dq_far, dk, dv, raw, cosine, sine, gain_q_row, gain_k_row, query_heads, key_heads
    )
    low, d_gain_heads, pair_out, *terms_down = lax.optimization_barrier(
        (low, d_gain_heads, pair_out, *terms_down)
    )
    grad_first = tn_dot(normed, low).astype(bf16)
    d_gain_attn = jnp.sum(w_first.astype(f32) * grad_first.astype(f32), axis=1) / gain_attn
    grad_gains = jnp.concatenate(
        [d_gain_attn, d_gain_mlp, d_gain_heads[0], d_gain_heads[1]]
    ).reshape(copies, size, gain_count)
    gain_block = jnp.pad(
        grad_gains.astype(bf16),
        ((0, 0), (0, pad_rows - size), (0, grad_first.shape[1] - gain_count)),
    )
    grad_first = jnp.concatenate(
        [grad_first.reshape(copies, size * owned, -1), gain_block], axis=1
    )
    first_sent = send_beside(grad_first)
    low = after(low, first_sent[1])
    low_own, low_beside, low_across, low_corner = (
        low[r * block : (r + 1) * block] for r in range(size)
    )
    toward, across = send_across(nt_dot(low_corner, w_first), nt_dot(low_across, w_first))
    part_beside, part_own = nt_dot(low_beside, w_first), nt_dot(low_own, w_first)
    d_normed_attn = sum_own(part_beside, part_own, across)
    d_inputs, unused = norm_back(x_own.astype(f32), gain_attn, d_normed_attn)
    grad_tokens = (d_middle + d_inputs).reshape(tokens.shape)

    terms_out = reduce_along(after(pair_out, toward))
    grad_both = add_all(after_all(terms_both, toward)).reshape(size, owned, -1)
    grad_both = exchange(grad_both, me)[0].astype(f32)
    grad_down = add_all(after_all(terms_down, toward)).reshape(w_down.shape)
    pair_first = after(add_beside(*first_sent), *terms_out, down_across)
    output = sum_own(down_beside, down_own, down_across)
    output = (middle + output).astype(bf16)
    terms_first = lax.optimization_barrier((*reduce_along(pair_first), across))[:-1]
    grad_first = add_all(terms_first)
    grad_out = add_all(after_all(terms_out, *terms_first))
    gain_part = grad_first[size * owned :][:size]
    gain_part = jnp.broadcast_to(gain_part[:, None], (size, pad_rows, gain_part.shape[1]))
    grad_first = jnp.concatenate(
        [grad_first[: size * owned].reshape(size, owned, -1), gain_part], axis=1
    )
    grad_first = exchange(grad_first, me)[0].astype(f32)
    grad_gains = jnp.sum(grad_first[:, owned, :gain_count], axis=0)
    grad_first = grad_first[:, :owned]

    def to_rows(pieces):
        return pieces.transpose(1, 0, 2).reshape(owned, -1)

    grad_query = to_rows(grad_first[:, :, :q_cols])
    grad_key = to_rows(grad_first[:, :, q_cols : q_cols + k_cols])
    grad_value = to_rows(grad_first[:, :, q_cols + k_cols :])
    grad_gate = to_rows(grad_both[:, :, :hidden_cols])
    grad_up = to_rows(grad_both[:, :, hidden_cols:])
    grad_out = lax.ppermute(grad_out, ("dp", "ctx"), backward_owner).astype(f32)
    grad_down = lax.ppermute(grad_down, ("dp", "ctx"), backward_owner).astype(f32)
    return (
        output.reshape(tokens.shape),
        grad_tokens,
        grad_query,
        grad_key,
        grad_value,
        grad_out,
        grad_gate,
        grad_up,
        grad_down,
        grad_gains,
    )


def solution(mesh):
    small = mesh.shape["ctx"] == 4
    return jax.shard_map(
        split_local if small else local,
        mesh=mesh,
        in_specs=(
            P("dp", "ctx", None),
            P(("dp", "ctx"), None),
            P(("dp", "ctx"), None),
            P(("dp", "ctx"), None),
            P(("dp", "ctx"), None),
            P(("dp", "ctx"), None),
            P(("dp", "ctx"), None),
            P(("dp", "ctx"), None),
            P(("dp", "ctx")),
            P("dp", "ctx"),
            P("dp", "ctx"),
            P("dp", "ctx", None),
        ),
        out_specs=(
            P("dp", "ctx", None),
            P("dp", "ctx", None),
            P(("dp", "ctx"), None),
            P(("dp", "ctx"), None),
            P(("dp", "ctx"), None),
            P(("dp", "ctx"), None),
            P(("dp", "ctx"), None),
            P(("dp", "ctx"), None),
            P(("dp", "ctx"), None),
            P(("dp", "ctx")),
        ),
        check_vma=False,
    )
```

```python
import functools

import jax
import jax.numpy as jnp
from jax import lax
from jax.experimental import pallas as pl
from jax.experimental.pallas import tpu as pltpu
from jax.sharding import PartitionSpec as P

MODEL_WIDTH = 1024
QUERY_HEADS = 16
KEY_VALUE_HEADS = 8
HEAD_SIZE = 128


EPSILON = 1e-06
THETA = 1000000.0


def row_norm_apply(value_rows, gain_vec):
    return (
        value_rows
        * lax.rsqrt(jnp.mean(value_rows * value_rows, axis=-1, keepdims=True) + EPSILON)
        * gain_vec
    )


def rotary_embed(value_rows, token_positions):
    half_size = value_rows.shape[-1] // 2
    inverse_rates = THETA ** (
        -2.0 * jnp.arange(half_size, dtype=jnp.float32) / value_rows.shape[-1]
    )
    angles = token_positions.astype(jnp.float32)[:, None] * inverse_rates[None, :]
    cosine = jnp.cos(angles)[:, None, :]
    sine_part = jnp.sin(angles)[:, None, :]
    former = value_rows[..., :half_size]
    second = value_rows[..., half_size:]
    return jnp.concatenate(
        [former * cosine - second * sine_part, second * cosine + former * sine_part], axis=-1
    )


def heads_per_group(raw_rows, gain_vec, token_positions, head_count):
    return rotary_embed(
        row_norm_apply(raw_rows.reshape(raw_rows.shape[0], head_count, HEAD_SIZE), gain_vec),
        token_positions,
    )


def split_gains(packed):
    packed = packed.astype(jnp.float32)
    return (
        packed[:MODEL_WIDTH],
        packed[MODEL_WIDTH : 2 * MODEL_WIDTH],
        packed[2 * MODEL_WIDTH : 2 * MODEL_WIDTH + HEAD_SIZE],
        packed[2 * MODEL_WIDTH + HEAD_SIZE :],
    )


def owner_major(grad_full, owners):
    return grad_full.reshape(owners, -1)


def local(
    tokens,
    w_query,
    key_weight,
    value_weight,
    w_out,
    w_gate,
    w_up,
    w_down,
    gains,
    segment_ids,
    positions,
    cotangent,
):
    sequence_count = tokens.shape[0]
    device_local_rows = tokens.shape[1]
    every_row_set = sequence_count * device_local_rows
    inputs = tokens.reshape(every_row_set, MODEL_WIDTH).astype(jnp.float32)
    token_positions = positions.reshape(every_row_set)
    cot_rows = cotangent.reshape(every_row_set, MODEL_WIDTH)
    head_groups = QUERY_HEADS // KEY_VALUE_HEADS
    score_scale = HEAD_SIZE ** (-0.5)
    f32 = jnp.float32
    brain_float_half = jnp.bfloat16
    owners = lax.axis_size(("dp", "ctx"))
    shard_shapes = (
        w_query.shape,
        key_weight.shape,
        value_weight.shape,
        w_out.shape,
        w_gate.shape,
        w_up.shape,
        w_down.shape,
        gains.shape,
    )
    gathered = (
        lax.all_gather(w_query, ("dp", "ctx"), axis=0, tiled=True),
        lax.all_gather(key_weight, ("dp", "ctx"), axis=0, tiled=True),
        lax.all_gather(value_weight, ("dp", "ctx"), axis=0, tiled=True),
        lax.all_gather(w_out, ("dp", "ctx"), axis=0, tiled=True),
        lax.all_gather(w_gate, ("dp", "ctx"), axis=0, tiled=True),
        lax.all_gather(w_up, ("dp", "ctx"), axis=0, tiled=True),
        lax.all_gather(w_down, ("dp", "ctx"), axis=0, tiled=True),
        lax.all_gather(gains, ("dp", "ctx"), axis=0, tiled=True),
    )
    full_query, full_key, full_value, full_out, full_gate, full_up, full_down, full_gains = gathered
    gain_attn, gain_mlp, gain_query, key_norm_gain = split_gains(full_gains)
    normalized_input = row_norm_apply(inputs, gain_attn).astype(brain_float_half)
    query_raw = jnp.dot(normalized_input, full_query, preferred_element_type=f32)
    unrotated_keys = jnp.dot(normalized_input, full_key, preferred_element_type=f32)
    value_low = (
        jnp.dot(normalized_input, full_value, preferred_element_type=f32)
        .astype(brain_float_half)
        .reshape(sequence_count, device_local_rows, KEY_VALUE_HEADS * HEAD_SIZE)
    )
    reduced_queries = heads_per_group(query_raw, gain_query, token_positions, QUERY_HEADS).astype(
        brain_float_half
    )
    key_low = (
        heads_per_group(unrotated_keys, key_norm_gain, token_positions, KEY_VALUE_HEADS)
        .astype(brain_float_half)
        .reshape(sequence_count, device_local_rows, KEY_VALUE_HEADS * HEAD_SIZE)
    )
    segment_low = segment_ids.astype(brain_float_half)
    gathered_keys, gathered_values, segment_all = (
        lax.all_gather(key_low, "ctx", axis=1, tiled=True),
        lax.all_gather(value_low, "ctx", axis=1, tiled=True),
        lax.all_gather(segment_low, "ctx", axis=1, tiled=True),
    )
    overall_rows = gathered_keys.shape[1]
    query_index = lax.axis_index("ctx") * device_local_rows + jnp.arange(
        device_local_rows, dtype=jnp.int32
    )
    key_index = jnp.arange(overall_rows, dtype=jnp.int32)
    allowed = (segment_low[:, :, None] == segment_all[:, None, :]) & (
        query_index[None, :, None] >= key_index[None, None, :]
    )
    grouped_queries = reduced_queries.reshape(
        sequence_count, device_local_rows, KEY_VALUE_HEADS, head_groups, HEAD_SIZE
    ).transpose(0, 2, 3, 1, 4)
    grouped_keys = gathered_keys.reshape(
        sequence_count, overall_rows, KEY_VALUE_HEADS, HEAD_SIZE
    ).transpose(0, 2, 1, 3)
    grouped_values = gathered_values.reshape(
        sequence_count, overall_rows, KEY_VALUE_HEADS, HEAD_SIZE
    ).transpose(0, 2, 1, 3)

    def masked_scores(query_head, key_head, mask_rows):
        scores = (
            jnp.einsum("rld,kd->rlk", query_head, key_head, preferred_element_type=f32)
            * score_scale
        )
        return jnp.where(mask_rows[None], scores, -1e30)

    def forward_sequence(slices):
        query_seq, key_seq, value_seq, mask_rows = slices

        def forward_head(head_slices):
            query_head, key_head, value_head = head_slices
            scores = masked_scores(query_head, key_head, mask_rows)
            row_peak = jnp.max(scores, axis=-1, keepdims=True)
            exp_scores = jnp.exp(scores - row_peak)
            denominator = jnp.sum(exp_scores, axis=-1, keepdims=True)
            prob_low = (exp_scores / denominator).astype(brain_float_half)
            mixed_head = jnp.einsum("rlk,kd->rld", prob_low, value_head, preferred_element_type=f32)
            return (mixed_head, row_peak[..., 0] + jnp.log(denominator[..., 0]))

        return lax.map(forward_head, (query_seq, key_seq, value_seq))

    mixed_heads, log_totals = lax.map(
        forward_sequence, (grouped_queries, grouped_keys, grouped_values, allowed)
    )
    attended = (
        mixed_heads.transpose(0, 3, 1, 2, 4)
        .reshape(every_row_set, QUERY_HEADS * HEAD_SIZE)
        .astype(brain_float_half)
    )
    middle = inputs + jnp.dot(attended, full_out, preferred_element_type=f32)
    normed_mlp = row_norm_apply(middle, gain_mlp).astype(brain_float_half)
    gate_value = jnp.dot(normed_mlp, full_gate, preferred_element_type=f32)
    up_value = jnp.dot(normed_mlp, full_up, preferred_element_type=f32)
    hidden = (jax.nn.silu(gate_value) * up_value).astype(brain_float_half)
    output = (middle + jnp.dot(hidden, full_down, preferred_element_type=f32)).astype(
        brain_float_half
    )
    regathered = (
        lax.all_gather(w_query, ("dp", "ctx"), axis=0, tiled=True),
        lax.all_gather(key_weight, ("dp", "ctx"), axis=0, tiled=True),
        lax.all_gather(value_weight, ("dp", "ctx"), axis=0, tiled=True),
        lax.all_gather(w_out, ("dp", "ctx"), axis=0, tiled=True),
        lax.all_gather(w_gate, ("dp", "ctx"), axis=0, tiled=True),
        lax.all_gather(w_up, ("dp", "ctx"), axis=0, tiled=True),
        lax.all_gather(w_down, ("dp", "ctx"), axis=0, tiled=True),
        lax.all_gather(gains, ("dp", "ctx"), axis=0, tiled=True),
    )
    back_query, back_key, back_value, back_out, back_gate, back_up, back_down, back_gains = (
        regathered
    )
    gain_attn, gain_mlp, gain_query, key_norm_gain = split_gains(back_gains)
    d_hidden = jnp.einsum("ld,fd->lf", cot_rows, back_down, preferred_element_type=f32)
    grad_down = jnp.einsum("lf,ld->fd", hidden, cot_rows, preferred_element_type=f32)
    unused, swiglu_pull = jax.vjp(
        lambda gate_in, up_in: jax.nn.silu(gate_in) * up_in, gate_value, up_value
    )
    d_gate, d_up = swiglu_pull(d_hidden)
    d_gate = d_gate.astype(brain_float_half)
    d_up = d_up.astype(brain_float_half)
    grad_gate = jnp.einsum("ld,lf->df", normed_mlp, d_gate, preferred_element_type=f32)
    grad_up = jnp.einsum("ld,lf->df", normed_mlp, d_up, preferred_element_type=f32)
    d_normed = jnp.einsum("lf,df->ld", d_gate, back_gate, preferred_element_type=f32)
    d_normed = d_normed + jnp.einsum("lf,df->ld", d_up, back_up, preferred_element_type=f32)
    unused, norm_pull = jax.vjp(row_norm_apply, middle, gain_mlp)
    d_middle, d_gain_mlp = norm_pull(d_normed)
    d_middle = d_middle + cot_rows.astype(f32)
    d_branch = d_middle.astype(brain_float_half)
    grad_out = jnp.einsum("lh,ld->hd", attended, d_branch, preferred_element_type=f32)
    attended_gradient = jnp.einsum(
        "ld,hd->lh", d_branch, back_out, preferred_element_type=f32
    ).astype(brain_float_half)
    group_gradient = attended_gradient.reshape(
        sequence_count, device_local_rows, KEY_VALUE_HEADS, head_groups, HEAD_SIZE
    ).transpose(0, 2, 3, 1, 4)

    def backward_sequence(slices):
        query_seq, key_seq, value_seq, d_seq, log_seq, mask_rows = slices

        def backward_head(head_slices):
            query_head, key_head, value_head, d_head, log_total = head_slices
            scores = masked_scores(query_head, key_head, mask_rows)
            probs_full = jnp.exp(scores - log_total[..., None])
            prob_low = probs_full.astype(brain_float_half)
            d_value = jnp.einsum("rlk,rld->kd", prob_low, d_head, preferred_element_type=f32)
            d_probs = jnp.einsum("rld,kd->rlk", d_head, value_head, preferred_element_type=f32)
            d_scores = probs_full * (
                d_probs - jnp.sum(probs_full * d_probs, axis=-1, keepdims=True)
            )
            d_scores = d_scores.astype(brain_float_half)
            d_query = (
                jnp.einsum("rlk,kd->rld", d_scores, key_head, preferred_element_type=f32)
                * score_scale
            )
            d_key = (
                jnp.einsum("rlk,rld->kd", d_scores, query_head, preferred_element_type=f32)
                * score_scale
            )
            return (d_query, d_key, d_value)

        return lax.map(backward_head, (query_seq, key_seq, value_seq, d_seq, log_seq))

    d_queries, key_rows_gradient, value_rows_gradient = lax.map(
        backward_sequence,
        (grouped_queries, grouped_keys, grouped_values, group_gradient, log_totals, allowed),
    )
    gathered_key_gradient = key_rows_gradient.transpose(2, 0, 1, 3).reshape(
        overall_rows, sequence_count, KEY_VALUE_HEADS * HEAD_SIZE
    )
    gathered_value_gradient = value_rows_gradient.transpose(2, 0, 1, 3).reshape(
        overall_rows, sequence_count, KEY_VALUE_HEADS * HEAD_SIZE
    )
    local_key_gradient, local_value_gradient = (
        lax.psum_scatter(
            gathered_key_gradient.astype(jnp.bfloat16), "ctx", scatter_dimension=0, tiled=True
        ).astype(jnp.float32),
        lax.psum_scatter(
            gathered_value_gradient.astype(jnp.bfloat16), "ctx", scatter_dimension=0, tiled=True
        ).astype(jnp.float32),
    )
    local_key_gradient = local_key_gradient.transpose(1, 0, 2)
    local_value_gradient = local_value_gradient.transpose(1, 0, 2)
    d_query_heads = d_queries.transpose(0, 3, 1, 2, 4).reshape(
        every_row_set, QUERY_HEADS, HEAD_SIZE
    )
    unused, query_pull = jax.vjp(
        lambda unnormalized_input, input_gain_vector: heads_per_group(
            unnormalized_input, input_gain_vector, token_positions, QUERY_HEADS
        ),
        query_raw,
        gain_query,
    )
    d_query_raw, d_gain_query = query_pull(d_query_heads)
    unused, key_pullback = jax.vjp(
        lambda unnormalized_input, input_gain_vector: heads_per_group(
            unnormalized_input, input_gain_vector, token_positions, KEY_VALUE_HEADS
        ),
        unrotated_keys,
        key_norm_gain,
    )
    unrotated_key_gradient, key_gain_gradient = key_pullback(
        local_key_gradient.reshape(every_row_set, KEY_VALUE_HEADS, HEAD_SIZE)
    )
    d_query_low = d_query_raw.astype(brain_float_half)
    d_key_low = unrotated_key_gradient.astype(brain_float_half)
    reduced_value_gradient = local_value_gradient.reshape(
        every_row_set, KEY_VALUE_HEADS * HEAD_SIZE
    ).astype(brain_float_half)
    grad_query = jnp.einsum("ld,lh->dh", normalized_input, d_query_low, preferred_element_type=f32)
    grad_key = jnp.einsum("ld,lh->dh", normalized_input, d_key_low, preferred_element_type=f32)
    grad_value = jnp.einsum(
        "ld,lh->dh", normalized_input, reduced_value_gradient, preferred_element_type=f32
    )
    d_normed_attn = jnp.einsum("lh,dh->ld", d_query_low, back_query, preferred_element_type=f32)
    d_normed_attn = d_normed_attn + jnp.einsum(
        "lh,dh->ld", d_key_low, back_key, preferred_element_type=f32
    )
    d_normed_attn = d_normed_attn + jnp.einsum(
        "lh,dh->ld", reduced_value_gradient, back_value, preferred_element_type=f32
    )
    unused, first_pull = jax.vjp(row_norm_apply, inputs, gain_attn)
    d_inputs, d_gain_attn = first_pull(d_normed_attn)
    grad_tokens = (d_middle + d_inputs).reshape(sequence_count, device_local_rows, MODEL_WIDTH)
    grad_gains = jnp.concatenate([d_gain_attn, d_gain_mlp, d_gain_query, key_gain_gradient])
    summed = (
        lax.psum_scatter(
            owner_major(grad_query, owners), ("dp", "ctx"), scatter_dimension=0, tiled=True
        ),
        lax.psum_scatter(
            owner_major(grad_key, owners), ("dp", "ctx"), scatter_dimension=0, tiled=True
        ),
        lax.psum_scatter(
            owner_major(grad_value, owners), ("dp", "ctx"), scatter_dimension=0, tiled=True
        ),
        lax.psum_scatter(
            owner_major(grad_out, owners), ("dp", "ctx"), scatter_dimension=0, tiled=True
        ),
        lax.psum_scatter(
            owner_major(grad_gate, owners), ("dp", "ctx"), scatter_dimension=0, tiled=True
        ),
        lax.psum_scatter(
            owner_major(grad_up, owners), ("dp", "ctx"), scatter_dimension=0, tiled=True
        ),
        lax.psum_scatter(
            owner_major(grad_down, owners), ("dp", "ctx"), scatter_dimension=0, tiled=True
        ),
        lax.psum_scatter(
            owner_major(grad_gains, owners), ("dp", "ctx"), scatter_dimension=0, tiled=True
        ),
    )
    grad_query = summed[0].reshape(shard_shapes[0])
    grad_key = summed[1].reshape(shard_shapes[1])
    grad_value = summed[2].reshape(shard_shapes[2])
    grad_out = summed[3].reshape(shard_shapes[3])
    grad_gate = summed[4].reshape(shard_shapes[4])
    grad_up = summed[5].reshape(shard_shapes[5])
    grad_down = summed[6].reshape(shard_shapes[6])
    grad_gains = summed[7].reshape(shard_shapes[7])
    return (
        output.reshape(sequence_count, device_local_rows, MODEL_WIDTH),
        grad_tokens,
        grad_query,
        grad_key,
        grad_value,
        grad_out,
        grad_gate,
        grad_up,
        grad_down,
        grad_gains,
    )

FEATURES = 128
MASK_DEPTH = -4096.0
LOG2_E = 1.4426950408889634
VMEM_BYTES = 56 * 1024 * 1024
bf16 = jnp.bfloat16
f32 = jnp.float32


def xor_permute(value, axis, offset):
    size = lax.axis_size(axis)
    return lax.ppermute(value, axis, [(i, i ^ offset) for i in range(size)])


def pick(stacked, index):
    return lax.dynamic_index_in_dim(stacked, index, 0, keepdims=False)


def exchange(stacked, me):
    size = stacked.shape[0]
    relative = [pick(stacked, me)]
    for offset in range(1, size):
        relative.append(xor_permute(pick(stacked, me ^ offset), "ctx", offset))
    arrived = relative[1:]
    relative = jnp.stack(relative)
    return jnp.stack([pick(relative, me ^ source) for source in range(size)]), arrived


def shift_z(value, offset):
    size = lax.axis_size("dp")
    return lax.ppermute(value, "dp", [(i, (i + 2 * offset) % size) for i in range(size)])


def assemble_kernel(splits, count, places_ref, *refs):
    pieces, results, sems = refs[:count], refs[count:-1], refs[-1]
    copies = []
    for piece in pieces:
        for slot in range(piece.shape[0]):
            n = len(copies) // len(splits)
            start = 0
            for m, rows in enumerate(splits):
                copy = pltpu.make_async_copy(
                    piece.at[slot, pl.ds(start, rows)],
                    results[m].at[places_ref[n]],
                    sems.at[n, m],
                )
                copy.start()
                copies.append(copy)
                start += rows
    for copy in copies:
        copy.wait()


def assemble(pieces, places, splits=None):
    slots = sum(piece.shape[0] for piece in pieces)
    rows, columns = pieces[0].shape[1:]
    splits = (rows,) if splits is None else splits
    anywhere = pl.BlockSpec(memory_space=pl.ANY)
    return pl.pallas_call(
        functools.partial(assemble_kernel, splits, len(pieces)),
        in_specs=[pl.BlockSpec(memory_space=pltpu.SMEM)]
        + [pl.BlockSpec(memory_space=pltpu.VMEM)] * len(pieces),
        out_specs=[anywhere] * len(splits),
        out_shape=[jax.ShapeDtypeStruct((slots, n, columns), pieces[0].dtype) for n in splits],
        scratch_shapes=[pltpu.SemaphoreType.DMA((slots, len(splits)))],
        compiler_params=pltpu.CompilerParams(vmem_limit_bytes=VMEM_BYTES),
        cost_estimate=pl.CostEstimate(
            flops=0, bytes_accessed=4 * slots * rows * columns, transcendentals=0
        ),
        name="assemble",
    )(places.astype(jnp.int32), *pieces)


def gather_along(value):
    return [value] + [shift_z(value, k) for k in range(1, lax.axis_size("dp") // 2)]


def gather_beside(along, *waits):
    depth = len(along)
    z = lax.axis_index("dp") // 2
    places = jnp.stack([(z - k) % depth for k in range(depth)])
    stack = assemble([piece[None] for piece in along], places)[0]
    stack = after(stack, *waits)
    return [stack, xor_permute(stack, "dp", 1)]


def interleave(stacks, splits):
    depth = stacks[0].shape[0]
    y = lax.axis_index("dp") % 2
    rows = 2 * jnp.arange(depth)
    results = assemble(stacks, jnp.concatenate([rows + y, rows + 1 - y]), splits)
    return [result.reshape(-1, result.shape[-1]) for result in results]


def send_beside(grad):
    depth = grad.shape[0] // 2
    y = lax.axis_index("dp") % 2
    grad = grad.reshape((depth, 2) + grad.shape[1:])
    away = lax.dynamic_index_in_dim(grad, 1 - y, 1, keepdims=False)
    kept = lax.dynamic_index_in_dim(grad, y, 1, keepdims=False)
    return kept, away, xor_permute(away, "dp", 1)


def add_beside(kept, away, arrived):
    return (kept.astype(f32) + arrived.astype(f32)).astype(bf16)


def reduce_along(pair):
    depth = pair.shape[0]
    z = lax.axis_index("dp") // 2
    sent = [shift_z(pick(pair, (z + k) % depth), k) for k in range(1, depth)]
    return [pick(pair, z)] + sent


def add_all(terms):
    total = terms[0].astype(f32)
    for term in terms[1:]:
        total = total + term.astype(f32)
    return total.astype(bf16)


def after(value, *others):
    return lax.optimization_barrier((value, *others))[0]


def after_all(values, *others):
    return lax.optimization_barrier((*values, *others))[: len(values)]


def gather_blocks(value):
    across = xor_permute(value, "ctx", 2)
    beside = xor_permute(value, "ctx", 1)
    corner = xor_permute(across, "ctx", 1)
    return [value, beside, across, corner]


def gather_near(value):
    return [value, xor_permute(value, "ctx", 1)], xor_permute(value, "ctx", 2)


def gather_far(across, *waits):
    across = after(across, *waits)
    return [across, xor_permute(across, "ctx", 1)]


def send_across(part_corner, part_across, *waits):
    corner = xor_permute(part_corner.astype(bf16), "ctx", 1)
    toward = (part_across.astype(f32) + corner.astype(f32)).astype(bf16)
    toward = after(toward, *waits) if waits else toward
    return toward, xor_permute(toward, "ctx", 2)


def sum_own(part_beside, part_own, across):
    beside = xor_permute(part_beside.astype(bf16), "ctx", 1)
    return part_own.astype(f32) + beside.astype(f32) + across.astype(f32)


def nt_dot(left, right):
    return lax.dot_general(left, right, (((1,), (1,)), ((), ())), preferred_element_type=f32)


def nn_dot(left, right):
    return jnp.dot(left, right, preferred_element_type=f32)


def project_kernel(
    query_heads,
    key_heads,
    per_block,
    x_refs,
    gain_ref,
    weight_ref,
    cos_ref,
    sin_ref,
    gain_q_ref,
    gain_k_ref,
    normed_ref,
    raw_ref,
    q_ref,
    k_ref,
    v_ref,
    held_ref,
):
    for r, x_ref in enumerate(x_refs):

        @pl.when(pl.program_id(0) // per_block == r)
        def _():
            held_ref[...] = x_ref[...]

    x = held_ref[...].astype(f32)
    scale = lax.rsqrt(jnp.mean(x * x, axis=-1, keepdims=True) + EPSILON)
    normed = (x * scale * gain_ref[...]).astype(bf16)
    normed_ref[...] = normed
    raw = nn_dot(normed, weight_ref[...])
    turned = (query_heads + key_heads) * HEAD_SIZE
    raw_ref[...] = raw[:, :turned]
    v_ref[...] = raw[:, turned:].astype(bf16)
    cosine = cos_ref[...]
    sine = sin_ref[...]
    for head in range(query_heads + key_heads):
        rows = raw[:, head * HEAD_SIZE : (head + 1) * HEAD_SIZE]
        gain = gain_q_ref[...] if head < query_heads else gain_k_ref[...]
        rows = rows * lax.rsqrt(jnp.mean(rows * rows, axis=-1, keepdims=True) + EPSILON) * gain
        rows = (rows * cosine + pltpu.roll(rows, HEAD_SIZE // 2, 1) * sine).astype(bf16)
        if head < query_heads:
            q_ref[:, head * HEAD_SIZE : (head + 1) * HEAD_SIZE] = rows
        else:
            at = (head - query_heads) * HEAD_SIZE
            k_ref[:, at : at + HEAD_SIZE] = rows


def project(x_blocks, gain, weight, cosine, sine, gain_q, gain_k, query_heads, key_heads):
    rows, width = x_blocks[0].shape
    block = 256
    per_block = rows // block
    rows = rows * len(x_blocks)
    turned = (query_heads + key_heads) * HEAD_SIZE
    columns = weight.shape[1]

    def tall(n):
        return pl.BlockSpec((block, n), lambda i: (i, 0))

    def whole(shape):
        return pl.BlockSpec(shape, lambda i: (0, 0))

    def part(r):
        return pl.BlockSpec(
            (block, width), lambda i: (jnp.clip(i - r * per_block, 0, per_block - 1), 0)
        )

    return pl.pallas_call(
        functools.partial(project_kernel, query_heads, key_heads, per_block),
        grid=(rows // block,),
        in_specs=[
            [part(r) for r in range(len(x_blocks))],
            whole((1, width)),
            whole(weight.shape),
            tall(HEAD_SIZE),
            tall(HEAD_SIZE),
            whole((1, HEAD_SIZE)),
            whole((1, HEAD_SIZE)),
        ],
        out_specs=[
            tall(width),
            tall(turned),
            tall(query_heads * HEAD_SIZE),
            tall(key_heads * HEAD_SIZE),
            tall(key_heads * HEAD_SIZE),
        ],
        out_shape=[
            jax.ShapeDtypeStruct((rows, width), bf16),
            jax.ShapeDtypeStruct((rows, turned), f32),
            jax.ShapeDtypeStruct((rows, query_heads * HEAD_SIZE), bf16),
            jax.ShapeDtypeStruct((rows, key_heads * HEAD_SIZE), bf16),
            jax.ShapeDtypeStruct((rows, key_heads * HEAD_SIZE), bf16),
        ],
        scratch_shapes=[pltpu.VMEM((block, width), bf16)],
        compiler_params=pltpu.CompilerParams(vmem_limit_bytes=VMEM_BYTES),
        cost_estimate=pl.CostEstimate(
            flops=2 * rows * width * columns,
            bytes_accessed=rows * (4 * width + 4 * turned + 2 * columns) + 2 * width * columns,
            transcendentals=0,
        ),
        name="project",
    )(list(x_blocks), gain, weight, cosine, sine, gain_q, gain_k)


def unproject_kernel(
    query_heads,
    key_heads,
    half,
    dq_near_ref,
    dq_far_ref,
    dk_ref,
    dv_ref,
    raw_ref,
    cos_ref,
    sin_ref,
    gain_q_ref,
    gain_k_ref,
    low_ref,
    dgain_ref,
):
    @pl.when(pl.program_id(0) == 0)
    def _():
        dgain_ref[...] = jnp.zeros_like(dgain_ref)

    cosine = cos_ref[...]
    sine = sin_ref[...]
    total_q = jnp.zeros((1, HEAD_SIZE), f32)
    total_k = jnp.zeros((1, HEAD_SIZE), f32)
    for head in range(query_heads + key_heads):
        at = head * HEAD_SIZE
        raw = raw_ref[:, at : at + HEAD_SIZE]
        if head < query_heads:
            lanes = slice(at, at + HEAD_SIZE)
            grad = jnp.where(pl.program_id(0) < half, dq_near_ref[:, lanes], dq_far_ref[:, lanes])
            gain = gain_q_ref[...]
        else:
            back = (head - query_heads) * HEAD_SIZE
            grad = dk_ref[:, back : back + HEAD_SIZE]
            gain = gain_k_ref[...]
        grad = grad * cosine - pltpu.roll(grad, HEAD_SIZE // 2, 1) * sine
        scale = lax.rsqrt(jnp.mean(raw * raw, axis=-1, keepdims=True) + EPSILON)
        unit = raw * scale
        summed = jnp.sum(unit * grad, axis=0, keepdims=True)
        if head < query_heads:
            total_q += summed
        else:
            total_k += summed
        grad = grad * gain
        mean = jnp.mean(unit * grad, axis=-1, keepdims=True)
        low_ref[:, at : at + HEAD_SIZE] = (scale * (grad - unit * mean)).astype(bf16)
    low_ref[:, (query_heads + key_heads) * HEAD_SIZE :] = dv_ref[...].astype(bf16)
    dgain_ref[0:1, :] += total_q
    dgain_ref[1:2, :] += total_k


def unproject(dq_near, dq_far, dk, dv, raw, cosine, sine, gain_q, gain_k, query_heads, key_heads):
    rows = dk.shape[0]
    block = 256
    half = rows // block // 2
    columns = (query_heads + 2 * key_heads) * HEAD_SIZE

    def tall(n):
        return pl.BlockSpec((block, n), lambda i: (i, 0))

    def whole(shape):
        return pl.BlockSpec(shape, lambda i: (0, 0))

    return pl.pallas_call(
        functools.partial(unproject_kernel, query_heads, key_heads, half),
        grid=(rows // block,),
        in_specs=[
            pl.BlockSpec((block, dq_near.shape[1]), lambda i: (jnp.minimum(i, half - 1), 0)),
            pl.BlockSpec((block, dq_far.shape[1]), lambda i: (jnp.maximum(i - half, 0), 0)),
            tall(dk.shape[1]),
            tall(dv.shape[1]),
            tall(raw.shape[1]),
            tall(HEAD_SIZE),
            tall(HEAD_SIZE),
            whole((1, HEAD_SIZE)),
            whole((1, HEAD_SIZE)),
        ],
        out_specs=[tall(columns), whole((8, HEAD_SIZE))],
        out_shape=[
            jax.ShapeDtypeStruct((rows, columns), bf16),
            jax.ShapeDtypeStruct((8, HEAD_SIZE), f32),
        ],
        compiler_params=pltpu.CompilerParams(vmem_limit_bytes=VMEM_BYTES),
        cost_estimate=pl.CostEstimate(
            flops=20 * rows * columns, bytes_accessed=20 * rows * columns, transcendentals=0
        ),
        name="unproject",
    )(dq_near, dq_far, dk, dv, raw, cosine, sine, gain_q, gain_k)


def attend_kernel(
    group, block, first, me_ref, q_ref, qf_ref, k_ref, kf_ref, v_ref, o_ref, log_ref, total_ref
):
    me = me_ref[0]
    at_query = (pl.program_id(1) + first) ^ me
    factor = HEAD_SIZE ** (-0.5) * LOG2_E
    query_features = qf_ref[...]
    ones = jnp.ones((block, HEAD_SIZE), bf16)
    total_ref[...] = jnp.zeros_like(total_ref)

    def step(at_key, diagonal):
        rows = pl.ds(pl.multiple_of((at_key ^ me) * block, block), block)
        keys = jnp.concatenate([k_ref[rows, :], kf_ref[rows, :]], axis=1)
        values = jnp.concatenate([v_ref[rows, :], ones], axis=1)
        for head in range(group):
            query = q_ref[:, head * HEAD_SIZE : (head + 1) * HEAD_SIZE]
            scores = nt_dot(jnp.concatenate([query, query_features], axis=1), keys)
            probs = jnp.exp2(scores * factor)
            if diagonal:
                down = lax.broadcasted_iota(jnp.int32, probs.shape, 0)
                right = lax.broadcasted_iota(jnp.int32, probs.shape, 1)
                probs = jnp.where(down >= right, probs, 0.0)
            total_ref[head] += nn_dot(probs.astype(bf16), values)

    @pl.loop(0, at_query)
    def _(at_key):
        step(at_key, False)

    step(at_query, True)
    for head in range(group):
        weighted = total_ref[head, :, :HEAD_SIZE]
        summed = total_ref[head, :, HEAD_SIZE:]
        o_ref[:, head * HEAD_SIZE : (head + 1) * HEAD_SIZE] = (weighted / summed).astype(bf16)
        log_ref[0, head : head + 1, :] = jnp.log2(summed.T[0:1, :])


def attend(me, q, qf, k, kf, v, block, group, first, count):
    rows = k.shape[0]
    key_heads = k.shape[1] // HEAD_SIZE
    pairs = key_heads * group * count * block * rows * 5 // 8
    return pl.pallas_call(
        functools.partial(attend_kernel, group, block, first),
        grid_spec=pltpu.PrefetchScalarGridSpec(
            num_scalar_prefetch=1,
            grid=(key_heads, count),
            in_specs=[
                pl.BlockSpec((block, group * HEAD_SIZE), lambda g, i, me: (i + first, g)),
                pl.BlockSpec((block, FEATURES), lambda g, i, me: (i + first, 0)),
                pl.BlockSpec((rows, HEAD_SIZE), lambda g, i, me: (0, g)),
                pl.BlockSpec((rows, FEATURES), lambda g, i, me: (0, 0)),
                pl.BlockSpec((rows, HEAD_SIZE), lambda g, i, me: (0, g)),
            ],
            out_specs=[
                pl.BlockSpec((block, group * HEAD_SIZE), lambda g, i, me: (i, g)),
                pl.BlockSpec((1, group, block), lambda g, i, me: (g, 0, i)),
            ],
            scratch_shapes=[pltpu.VMEM((group, block, 2 * HEAD_SIZE), f32)],
        ),
        out_shape=[
            jax.ShapeDtypeStruct((count * block, q.shape[1]), bf16),
            jax.ShapeDtypeStruct((key_heads, group, count * block), f32),
        ],
        compiler_params=pltpu.CompilerParams(vmem_limit_bytes=VMEM_BYTES),
        cost_estimate=pl.CostEstimate(
            flops=8 * pairs * HEAD_SIZE, bytes_accessed=10 * q.size, transcendentals=pairs
        ),
        name="attend",
    )(me, q, qf, k, kf, v)


def unattend_kernel(
    group,
    block,
    first,
    resumed,
    me_ref,
    q_ref,
    qf_ref,
    k_ref,
    kf_ref,
    v_ref,
    o_ref,
    branch_first_ref,
    branch_second_ref,
    out_ref,
    log_ref,
    *rest,
):
    if resumed:
        dk_in_ref, dv_in_ref, d_weight_in_ref, *rest = rest
    dq_ref, dk_ref, dv_ref, d_weight_ref, flipped_ref, total_ref, do_ref = rest
    me = me_ref[0]
    at_query = (pl.program_id(1) + first) ^ me
    scale = HEAD_SIZE ** (-0.5)
    factor = scale * LOG2_E

    @pl.when(pl.program_id(1) == 0)
    def _():
        dk_ref[...] = dk_in_ref[...] if resumed else jnp.zeros_like(dk_ref)
        dv_ref[...] = dv_in_ref[...] if resumed else jnp.zeros_like(dv_ref)
        d_weight_ref[...] = d_weight_in_ref[...] if resumed else jnp.zeros_like(d_weight_ref)
        flipped_ref[...] = k_ref[...].astype(f32).T.astype(bf16)

    def take(branch_ref):
        do_ref[...] = nt_dot(branch_ref[...], out_ref[...]).astype(bf16)
        turned = o_ref[...].astype(f32).T.astype(bf16)
        d_weight_ref[...] += nn_dot(turned, branch_ref[...])

    @pl.when(pl.program_id(1) == 0)
    def _():
        take(branch_first_ref)

    @pl.when(pl.program_id(1) == 1)
    def _():
        take(branch_second_ref)

    total_ref[...] = jnp.zeros_like(total_ref)
    query_features = qf_ref[...]
    deltas = []
    for head in range(group):
        lanes = slice(head * HEAD_SIZE, (head + 1) * HEAD_SIZE)
        product = do_ref[:, lanes].astype(f32) * o_ref[:, lanes].astype(f32)
        deltas.append(jnp.sum(product.T, axis=0, keepdims=True))

    def step(at_key, diagonal):
        start = pl.multiple_of((at_key ^ me) * block, block)
        rows = pl.ds(start, block)
        keys = jnp.concatenate([k_ref[rows, :], kf_ref[rows, :]], axis=1)
        values = v_ref[rows, :]
        for head in range(group):
            lanes = slice(head * HEAD_SIZE, (head + 1) * HEAD_SIZE)
            query = q_ref[:, lanes]
            d_out = do_ref[:, lanes]
            scores = nt_dot(keys, jnp.concatenate([query, query_features], axis=1))
            probs = jnp.exp2(scores * factor - log_ref[0, head : head + 1, :])
            if diagonal:
                key_at = lax.broadcasted_iota(jnp.int32, probs.shape, 0)
                query_at = lax.broadcasted_iota(jnp.int32, probs.shape, 1)
                probs = jnp.where(query_at >= key_at, probs, 0.0)
            d_scores = (probs * (nt_dot(values, d_out) - deltas[head])).astype(bf16)
            dv_ref[rows, :] += nn_dot(probs.astype(bf16), d_out)
            dk_ref[rows, :] += nn_dot(d_scores, query)
            total_ref[head] += nn_dot(flipped_ref[:, rows], d_scores)

    @pl.loop(0, at_query)
    def _(at_key):
        step(at_key, False)

    step(at_query, True)
    for head in range(group):
        dq_ref[:, head * HEAD_SIZE : (head + 1) * HEAD_SIZE] = total_ref[head].T * scale

    if resumed:

        @pl.when(pl.program_id(1) == pl.num_programs(1) - 1)
        def _():
            dk_ref[...] = dk_ref[...] * scale


def unattend(me, q, qf, k, kf, v, o, branches, out, logs, block, group, first, earlier=()):
    count = len(branches)
    rows = k.shape[0]
    key_heads = k.shape[1] // HEAD_SIZE
    width = out.shape[1]
    lanes = group * HEAD_SIZE

    def by_query(n):
        return pl.BlockSpec((block, n), lambda g, i, me: (i, g))

    by_key = pl.BlockSpec((rows, HEAD_SIZE), lambda g, i, me: (0, g))
    by_head = pl.BlockSpec((lanes, width), lambda g, i, me: (g, 0))
    whole = pl.BlockSpec((block, width), lambda g, i, me: (0, 0))
    return pl.pallas_call(
        functools.partial(unattend_kernel, group, block, first, bool(earlier)),
        grid_spec=pltpu.PrefetchScalarGridSpec(
            num_scalar_prefetch=1,
            grid=(key_heads, count),
            in_specs=[
                pl.BlockSpec((block, lanes), lambda g, i, me: (i + first, g)),
                pl.BlockSpec((block, FEATURES), lambda g, i, me: (i + first, 0)),
                by_key,
                pl.BlockSpec((rows, FEATURES), lambda g, i, me: (0, 0)),
                by_key,
                by_query(lanes),
                whole,
                whole,
                by_head,
                pl.BlockSpec((1, group, block), lambda g, i, me: (g, 0, i)),
            ]
            + ([by_key, by_key, by_head] if earlier else []),
            out_specs=[by_query(lanes), by_key, by_key, by_head],
            scratch_shapes=[
                pltpu.VMEM((HEAD_SIZE, rows), bf16),
                pltpu.VMEM((group, HEAD_SIZE, block), f32),
                pltpu.VMEM((block, lanes), bf16),
            ],
        ),
        out_shape=[
            jax.ShapeDtypeStruct((count * block, q.shape[1]), f32),
            jax.ShapeDtypeStruct(k.shape, f32),
            jax.ShapeDtypeStruct(v.shape, f32),
            jax.ShapeDtypeStruct(out.shape, f32),
        ],
        compiler_params=pltpu.CompilerParams(vmem_limit_bytes=VMEM_BYTES),
        cost_estimate=pl.CostEstimate(
            flops=(70 if earlier else 7) * count * block * rows * key_heads * group * HEAD_SIZE // 8,
            bytes_accessed=(20 if earlier else 2) * q.size,
            transcendentals=0,
        ),
        name="unattend",
    )(me, q, qf, k, kf, v, o, *branches, out, logs, *earlier)


def feed_kernel(
    units,
    half,
    first_ref,
    second_ref,
    cot_first_ref,
    cot_second_ref,
    both_ref,
    down_ref,
    h_ref,
    cot_ref,
    hidden_ref,
    d_both_ref,
    part_first_ref,
    part_second_ref,
    d_part_first_ref,
    d_part_second_ref,
):
    in_first = pl.program_id(0) < half

    @pl.when(in_first)
    def _():
        h_ref[...] = first_ref[...]
        cot_ref[...] = cot_first_ref[...]

    @pl.when(jnp.logical_not(in_first))
    def _():
        h_ref[...] = second_ref[...]
        cot_ref[...] = cot_second_ref[...]

    both = nn_dot(h_ref[...], both_ref[...])
    d_hidden = nt_dot(cot_ref[...], down_ref[...])
    gate, up = both[:, :units], both[:, units:]
    sigmoid = 1.0 / (1.0 + jnp.exp(-gate))
    silu = gate * sigmoid
    hidden = (silu * up).astype(bf16)
    hidden_ref[...] = hidden
    part = nn_dot(hidden, down_ref[...]).astype(bf16)
    d_gate = (d_hidden * up * sigmoid * (1.0 + gate * (1.0 - sigmoid))).astype(bf16)
    d_up = (d_hidden * silu).astype(bf16)
    d_both = jnp.concatenate([d_gate, d_up], axis=1)
    d_both_ref[...] = d_both
    d_part = nt_dot(d_both, both_ref[...]).astype(bf16)

    @pl.when(in_first)
    def _():
        part_first_ref[...] = part
        d_part_first_ref[...] = d_part

    @pl.when(jnp.logical_not(in_first))
    def _():
        part_second_ref[...] = part
        d_part_second_ref[...] = d_part


def feed(h_first, h_second, cot_first, cot_second, both, down):
    rows, width = 2 * cot_first.shape[0], cot_first.shape[1]
    units = down.shape[0]
    block = 256
    half = rows // block // 2

    def tall(n):
        return pl.BlockSpec((block, n), lambda i: (i, 0))

    def whole(shape):
        return pl.BlockSpec(shape, lambda i: (0, 0))

    of_first = pl.BlockSpec((block, width), lambda i: (jnp.minimum(i, half - 1), 0))
    of_second = pl.BlockSpec((block, width), lambda i: (jnp.maximum(i - half, 0), 0))
    shapes = [(rows, width), (rows, width), (rows, units), (rows, 2 * units)] + [(rows // 2, width)] * 4
    return pl.pallas_call(
        functools.partial(feed_kernel, units, half),
        grid=(rows // block,),
        in_specs=[of_first, of_second] * 2 + [whole(both.shape), whole(down.shape)],
        out_specs=[tall(width), tall(width), tall(units), tall(2 * units)] + [of_first, of_second] * 2,
        out_shape=[jax.ShapeDtypeStruct(shape, bf16) for shape in shapes],
        compiler_params=pltpu.CompilerParams(vmem_limit_bytes=VMEM_BYTES),
        cost_estimate=pl.CostEstimate(
            flops=12 * rows * width * units,
            bytes_accessed=rows * (10 * width + 6 * units) + 6 * width * units,
            transcendentals=rows * units,
        ),
        name="feed",
    )(h_first, h_second, cot_first, cot_second, both, down)


def norm_back(value_rows, gain_vec, grad):
    scale = lax.rsqrt(jnp.mean(value_rows * value_rows, axis=-1, keepdims=True) + EPSILON)
    unit = value_rows * scale
    d_gain = jnp.sum(unit * grad, axis=0)
    grad = grad * gain_vec
    return scale * (grad - unit * jnp.mean(unit * grad, axis=-1, keepdims=True)), d_gain


def split_local(
    tokens,
    w_query,
    key_weight,
    value_weight,
    w_out,
    w_gate,
    w_up,
    w_down,
    gains,
    segment_ids,
    positions,
    cotangent,
):
    size = lax.axis_size("ctx")
    copies = lax.axis_size("dp")
    me = lax.axis_index("ctx")
    me_row = me.reshape(1).astype(jnp.int32)
    block = tokens.shape[1]
    group = QUERY_HEADS // KEY_VALUE_HEADS
    query_heads = QUERY_HEADS // size
    key_heads = KEY_VALUE_HEADS // size
    q_cols = query_heads * HEAD_SIZE
    k_cols = key_heads * HEAD_SIZE
    owned = w_query.shape[0]
    hidden_cols = w_gate.shape[1] // size
    gain_count = gains.shape[0]
    pad_rows = 16
    forward_owner = [
        (b, (b % copies) * size + b // copies) for b in range(size * copies)
    ]
    backward_owner = [(target, source) for source, target in forward_owner]

    def by_columns(weight):
        return weight.reshape(weight.shape[0], size, -1).transpose(1, 0, 2)

    first = jnp.concatenate(
        [by_columns(w_query), by_columns(key_weight), by_columns(value_weight)], axis=2
    )
    gain_rows = jnp.pad(gains[None], ((0, pad_rows - 1), (0, first.shape[2] - gain_count)))
    first = jnp.concatenate(
        [first, jnp.broadcast_to(gain_rows[None], (size,) + gain_rows.shape)], axis=1
    )
    first, arrived = exchange(first, me)
    gain_rows = jnp.concatenate(
        [first[:, owned], jnp.zeros((pad_rows - size, first.shape[2]), bf16)]
    )
    first = jnp.concatenate(
        [first[:, :owned].reshape(size * owned, first.shape[2]), gain_rows]
    )
    first_along = gather_along(first)
    places = jnp.concatenate([positions, segment_ids]).astype(jnp.int32)
    places = jnp.concatenate(gather_blocks(after(places, *arrived)), axis=1)
    half = HEAD_SIZE // 2
    rates = THETA ** (-2.0 * jnp.arange(half, dtype=f32) / HEAD_SIZE)
    angles = places[0].astype(f32)[:, None] * rates[None, :]
    cosine, sine = jnp.cos(angles), jnp.sin(angles)
    cosine = jnp.concatenate([cosine, cosine], axis=1)
    sine = jnp.concatenate([-sine, sine], axis=1)
    lane = jnp.arange(FEATURES, dtype=jnp.int32)[None, :]
    same = places[1][:, None] == lane
    key_features = same.astype(bf16)
    query_features = jnp.where(same, 0.0, MASK_DEPTH).astype(bf16)
    first_stacks = gather_beside(
        after_all(first_along, cosine, sine, key_features, query_features)
    )

    gate_up = jnp.concatenate([by_columns(w_gate), by_columns(w_up)], axis=2)
    gate_up, arrived = exchange(after(gate_up, *arrived), me)
    moved = after(jnp.concatenate([w_out, w_down]), *arrived)
    moved = lax.ppermute(moved, ("dp", "ctx"), forward_owner)
    x_own = tokens.reshape(block, MODEL_WIDTH)
    x_near, across = gather_near(after(x_own, *arrived))
    x_blocks = x_near + gather_far(across, first_stacks[0])

    moved_along = gather_along(after(moved, first_stacks[0], x_near[1]))
    first_stacks = [first_stacks[0], after(first_stacks[1], *moved_along[1:])]
    cot_own = cotangent.reshape(block, MODEL_WIDTH)
    cot_near, cot_across = gather_near(after(cot_own, first_stacks[1]))
    moved_stacks = gather_beside(moved_along, first_stacks[1])
    gate_up_rows = after(gate_up.reshape(size * owned, -1), *moved_along[1:])
    gate_up = lax.all_gather(gate_up_rows, "dp", axis=0, tiled=True)
    w_first, gain_rows = interleave(first_stacks, (size * owned, pad_rows))
    w_first = after(w_first, gate_up_rows)
    full_gains = gain_rows.reshape(copies, pad_rows, -1)[:, :size, :gain_count].reshape(-1)
    gain_attn, gain_mlp, gain_query, gain_key = split_gains(full_gains)

    gain_q_row, gain_k_row = gain_query[None], gain_key[None]
    normed, raw, q, k, v = project(
        x_blocks, gain_attn[None], w_first, cosine, sine, gain_q_row, gain_k_row, query_heads, key_heads
    )
    def attend_half(query, first):
        return attend(
            me_row, query, query_features, k, key_features, v, block, group, first, 2
        )

    def tn_dot(left, right):
        return lax.dot_general(left, right, (((0,), (0,)), ((), ())), preferred_element_type=f32)

    def by_copy(grad):
        return grad.astype(bf16).reshape(copies, -1, grad.shape[-1])

    def halves(value):
        return value[:block], value[block:]

    cot_blocks = cot_near + gather_far(cot_across, q)
    att_far, logs_far = attend_half(q, 2)
    att_far, *both = lax.optimization_barrier((att_far, *moved_stacks, *cot_blocks))
    moved_stacks, cot_blocks = both[:2], both[2:]
    out_full, down_full = interleave(moved_stacks, (w_out.shape[0], w_down.shape[0]))
    att_across, att_corner = halves(att_far)
    part_corner, part_across = nn_dot(att_corner, out_full), nn_dot(att_across, out_full)
    toward, across = send_across(part_corner, part_across)
    att_near, logs_near = attend_half(after(q, toward), 0)
    att_near = after(att_near, gate_up)
    att_own, att_beside = halves(att_near)
    beside = [
        xor_permute(nn_dot(piece, out_full).astype(bf16), "ctx", 1)
        for piece in jnp.split(att_beside, 2)
    ]
    part_own = nn_dot(att_own, out_full) + jnp.concatenate(beside).astype(f32)
    middle = x_own.astype(f32) + part_own + across.astype(f32)
    h_blocks, across = gather_near(row_norm_apply(middle, gain_mlp).astype(bf16))
    h_near, cot_near, hidden_near, d_both_near, down_own, down_beside, d_own, d_beside = feed(
        *h_blocks, *cot_blocks[:2], gate_up, down_full
    )
    h_blocks = gather_far(across, hidden_near)
    h_far, cot_far, hidden_far, d_both_far, down_across, down_corner, d_across, d_corner = feed(
        *h_blocks, *cot_blocks[2:], gate_up, down_full
    )

    toward, across = send_across(d_corner, d_across)
    d_both_far, cot_far = lax.optimization_barrier((d_both_far, cot_far, toward))[:2]
    grad_both = (tn_dot(h_near, d_both_near) + tn_dot(h_far, d_both_far)).astype(bf16)
    both_sent = send_beside(by_copy(grad_both))
    hidden_far = after(hidden_far, both_sent[1])
    grad_down = (tn_dot(hidden_near, cot_near) + tn_dot(hidden_far, cot_far)).astype(bf16)
    d_normed = sum_own(d_beside, d_own, after(across, grad_down))
    d_middle, d_gain_mlp = norm_back(middle, gain_mlp, d_normed)
    d_middle = d_middle + cot_own.astype(f32)
    branches_near, branch_across = gather_near(d_middle.astype(bf16))

    def unattend_half(att, branches, logs, first, earlier=()):
        return unattend(
            me_row,
            q,
            query_features,
            k,
            key_features,
            v,
            att,
            branches,
            out_full,
            logs,
            block,
            group,
            first,
            earlier,
        )

    dq_near, *earlier = unattend_half(att_near, branches_near, logs_near, 0)
    pair_both = add_beside(after(both_sent[0], dq_near), *both_sent[1:])
    terms_both = reduce_along(pair_both)
    down_sent = send_beside(after(by_copy(grad_down), dq_near))
    branches_far = gather_far(branch_across, dq_near)
    dq_far, dk, dv, grad_out = unattend_half(att_far, branches_far, logs_far, 2, earlier)
    pair_out = add_beside(*send_beside(by_copy(grad_out)))
    dk, pair_down, *terms_both = lax.optimization_barrier(
        (dk, add_beside(*down_sent), *terms_both)
    )
    terms_down = reduce_along(pair_down)
    low, d_gain_heads = unproject(
        dq_near, dq_far, dk, dv, raw, cosine, sine, gain_q_row, gain_k_row, query_heads, key_heads
    )
    low, d_gain_heads, pair_out, *terms_down = lax.optimization_barrier(
        (low, d_gain_heads, pair_out, *terms_down)
    )
    grad_first = tn_dot(normed, low).astype(bf16)
    d_gain_attn = jnp.sum(w_first.astype(f32) * grad_first.astype(f32), axis=1) / gain_attn
    grad_gains = jnp.concatenate(
        [d_gain_attn, d_gain_mlp, d_gain_heads[0], d_gain_heads[1]]
    ).reshape(copies, size, gain_count)
    gain_block = jnp.pad(
        grad_gains.astype(bf16),
        ((0, 0), (0, pad_rows - size), (0, grad_first.shape[1] - gain_count)),
    )
    grad_first = jnp.concatenate(
        [grad_first.reshape(copies, size * owned, -1), gain_block], axis=1
    )
    first_sent = send_beside(grad_first)
    low = after(low, first_sent[1])
    low_own, low_beside, low_across, low_corner = (
        low[r * block : (r + 1) * block] for r in range(size)
    )
    toward, across = send_across(nt_dot(low_corner, w_first), nt_dot(low_across, w_first))
    part_beside, part_own = nt_dot(low_beside, w_first), nt_dot(low_own, w_first)
    d_normed_attn = sum_own(part_beside, part_own, across)
    d_inputs, unused = norm_back(x_own.astype(f32), gain_attn, d_normed_attn)
    grad_tokens = (d_middle + d_inputs).reshape(tokens.shape)

    terms_out = reduce_along(after(pair_out, toward))
    grad_both = add_all(after_all(terms_both, toward)).reshape(size, owned, -1)
    grad_down = add_all(after_all(terms_down, toward))
    pair_first = after(add_beside(*first_sent), *terms_out)
    unused, down_across = send_across(down_corner, down_across, pair_first)
    output = (middle + sum_own(down_beside, down_own, down_across)).astype(bf16)
    terms_first = after_all(reduce_along(pair_first), across, down_across)
    grad_first = add_all(terms_first)
    grad_out = add_all(after_all(terms_out, *terms_first))
    gain_part = grad_first[size * owned :][:size]
    gain_part = jnp.broadcast_to(gain_part[:, None], (size, pad_rows, gain_part.shape[1]))
    grad_first = jnp.concatenate(
        [grad_first[: size * owned].reshape(size, owned, -1), gain_part], axis=1
    )
    both_rows = grad_both.size // size // grad_first.shape[2]
    grad_both = grad_both.reshape(size, both_rows, -1)
    grad_first = exchange(jnp.concatenate([grad_first, grad_both], axis=1), me)[0].astype(f32)
    grad_both = grad_first[:, -both_rows:].reshape(size, owned, -1)
    grad_gains = jnp.sum(grad_first[:, owned, :gain_count], axis=0)
    grad_first = grad_first[:, :owned]

    def to_rows(pieces):
        return pieces.transpose(1, 0, 2).reshape(owned, -1)

    grad_query = to_rows(grad_first[:, :, :q_cols])
    grad_key = to_rows(grad_first[:, :, q_cols : q_cols + k_cols])
    grad_value = to_rows(grad_first[:, :, q_cols + k_cols :])
    grad_gate = to_rows(grad_both[:, :, :hidden_cols])
    grad_up = to_rows(grad_both[:, :, hidden_cols:])
    moved = jnp.concatenate([grad_out, grad_down])
    moved = lax.ppermute(moved, ("dp", "ctx"), backward_owner).astype(f32)
    grad_out, grad_down = moved[: w_out.shape[0]], moved[w_out.shape[0] :]
    return (
        output.reshape(tokens.shape),
        grad_tokens,
        grad_query,
        grad_key,
        grad_value,
        grad_out,
        grad_gate,
        grad_up,
        grad_down,
        grad_gains,
    )


def solution(mesh):
    small = mesh.shape["ctx"] == 4
    return jax.shard_map(
        split_local if small else local,
        mesh=mesh,
        in_specs=(
            P("dp", "ctx", None),
            P(("dp", "ctx"), None),
            P(("dp", "ctx"), None),
            P(("dp", "ctx"), None),
            P(("dp", "ctx"), None),
            P(("dp", "ctx"), None),
            P(("dp", "ctx"), None),
            P(("dp", "ctx"), None),
            P(("dp", "ctx")),
            P("dp", "ctx"),
            P("dp", "ctx"),
            P("dp", "ctx", None),
        ),
        out_specs=(
            P("dp", "ctx", None),
            P("dp", "ctx", None),
            P(("dp", "ctx"), None),
            P(("dp", "ctx"), None),
            P(("dp", "ctx"), None),
            P(("dp", "ctx"), None),
            P(("dp", "ctx"), None),
            P(("dp", "ctx"), None),
            P(("dp", "ctx"), None),
            P(("dp", "ctx")),
        ),
        check_vma=False,
    )
```

```python
import functools

import jax
import jax.numpy as jnp
from jax import lax
from jax.experimental import pallas as pl
from jax.experimental.pallas import tpu as pltpu
from jax.sharding import PartitionSpec as P

MODEL_WIDTH = 1024
QUERY_HEADS = 16
KEY_VALUE_HEADS = 8
HEAD_SIZE = 128


EPSILON = 1e-06
THETA = 1000000.0


def row_norm_apply(value_rows, gain_vec):
    return (
        value_rows
        * lax.rsqrt(jnp.mean(value_rows * value_rows, axis=-1, keepdims=True) + EPSILON)
        * gain_vec
    )


def rotary_embed(value_rows, token_positions):
    half_size = value_rows.shape[-1] // 2
    inverse_rates = THETA ** (
        -2.0 * jnp.arange(half_size, dtype=jnp.float32) / value_rows.shape[-1]
    )
    angles = token_positions.astype(jnp.float32)[:, None] * inverse_rates[None, :]
    cosine = jnp.cos(angles)[:, None, :]
    sine_part = jnp.sin(angles)[:, None, :]
    former = value_rows[..., :half_size]
    second = value_rows[..., half_size:]
    return jnp.concatenate(
        [former * cosine - second * sine_part, second * cosine + former * sine_part], axis=-1
    )


def heads_per_group(raw_rows, gain_vec, token_positions, head_count):
    return rotary_embed(
        row_norm_apply(raw_rows.reshape(raw_rows.shape[0], head_count, HEAD_SIZE), gain_vec),
        token_positions,
    )


def split_gains(packed):
    packed = packed.astype(jnp.float32)
    return (
        packed[:MODEL_WIDTH],
        packed[MODEL_WIDTH : 2 * MODEL_WIDTH],
        packed[2 * MODEL_WIDTH : 2 * MODEL_WIDTH + HEAD_SIZE],
        packed[2 * MODEL_WIDTH + HEAD_SIZE :],
    )


def owner_major(grad_full, owners):
    return grad_full.reshape(owners, -1)


def local(
    tokens,
    w_query,
    key_weight,
    value_weight,
    w_out,
    w_gate,
    w_up,
    w_down,
    gains,
    segment_ids,
    positions,
    cotangent,
):
    sequence_count = tokens.shape[0]
    device_local_rows = tokens.shape[1]
    every_row_set = sequence_count * device_local_rows
    inputs = tokens.reshape(every_row_set, MODEL_WIDTH).astype(jnp.float32)
    token_positions = positions.reshape(every_row_set)
    cot_rows = cotangent.reshape(every_row_set, MODEL_WIDTH)
    head_groups = QUERY_HEADS // KEY_VALUE_HEADS
    score_scale = HEAD_SIZE ** (-0.5)
    f32 = jnp.float32
    brain_float_half = jnp.bfloat16
    owners = lax.axis_size(("dp", "ctx"))
    shard_shapes = (
        w_query.shape,
        key_weight.shape,
        value_weight.shape,
        w_out.shape,
        w_gate.shape,
        w_up.shape,
        w_down.shape,
        gains.shape,
    )
    gathered = (
        lax.all_gather(w_query, ("dp", "ctx"), axis=0, tiled=True),
        lax.all_gather(key_weight, ("dp", "ctx"), axis=0, tiled=True),
        lax.all_gather(value_weight, ("dp", "ctx"), axis=0, tiled=True),
        lax.all_gather(w_out, ("dp", "ctx"), axis=0, tiled=True),
        lax.all_gather(w_gate, ("dp", "ctx"), axis=0, tiled=True),
        lax.all_gather(w_up, ("dp", "ctx"), axis=0, tiled=True),
        lax.all_gather(w_down, ("dp", "ctx"), axis=0, tiled=True),
        lax.all_gather(gains, ("dp", "ctx"), axis=0, tiled=True),
    )
    full_query, full_key, full_value, full_out, full_gate, full_up, full_down, full_gains = gathered
    gain_attn, gain_mlp, gain_query, key_norm_gain = split_gains(full_gains)
    normalized_input = row_norm_apply(inputs, gain_attn).astype(brain_float_half)
    query_raw = jnp.dot(normalized_input, full_query, preferred_element_type=f32)
    unrotated_keys = jnp.dot(normalized_input, full_key, preferred_element_type=f32)
    value_low = (
        jnp.dot(normalized_input, full_value, preferred_element_type=f32)
        .astype(brain_float_half)
        .reshape(sequence_count, device_local_rows, KEY_VALUE_HEADS * HEAD_SIZE)
    )
    reduced_queries = heads_per_group(query_raw, gain_query, token_positions, QUERY_HEADS).astype(
        brain_float_half
    )
    key_low = (
        heads_per_group(unrotated_keys, key_norm_gain, token_positions, KEY_VALUE_HEADS)
        .astype(brain_float_half)
        .reshape(sequence_count, device_local_rows, KEY_VALUE_HEADS * HEAD_SIZE)
    )
    segment_low = segment_ids.astype(brain_float_half)
    gathered_keys, gathered_values, segment_all = (
        lax.all_gather(key_low, "ctx", axis=1, tiled=True),
        lax.all_gather(value_low, "ctx", axis=1, tiled=True),
        lax.all_gather(segment_low, "ctx", axis=1, tiled=True),
    )
    overall_rows = gathered_keys.shape[1]
    query_index = lax.axis_index("ctx") * device_local_rows + jnp.arange(
        device_local_rows, dtype=jnp.int32
    )
    key_index = jnp.arange(overall_rows, dtype=jnp.int32)
    allowed = (segment_low[:, :, None] == segment_all[:, None, :]) & (
        query_index[None, :, None] >= key_index[None, None, :]
    )
    grouped_queries = reduced_queries.reshape(
        sequence_count, device_local_rows, KEY_VALUE_HEADS, head_groups, HEAD_SIZE
    ).transpose(0, 2, 3, 1, 4)
    grouped_keys = gathered_keys.reshape(
        sequence_count, overall_rows, KEY_VALUE_HEADS, HEAD_SIZE
    ).transpose(0, 2, 1, 3)
    grouped_values = gathered_values.reshape(
        sequence_count, overall_rows, KEY_VALUE_HEADS, HEAD_SIZE
    ).transpose(0, 2, 1, 3)

    def masked_scores(query_head, key_head, mask_rows):
        scores = (
            jnp.einsum("rld,kd->rlk", query_head, key_head, preferred_element_type=f32)
            * score_scale
        )
        return jnp.where(mask_rows[None], scores, -1e30)

    def forward_sequence(slices):
        query_seq, key_seq, value_seq, mask_rows = slices

        def forward_head(head_slices):
            query_head, key_head, value_head = head_slices
            scores = masked_scores(query_head, key_head, mask_rows)
            row_peak = jnp.max(scores, axis=-1, keepdims=True)
            exp_scores = jnp.exp(scores - row_peak)
            denominator = jnp.sum(exp_scores, axis=-1, keepdims=True)
            prob_low = (exp_scores / denominator).astype(brain_float_half)
            mixed_head = jnp.einsum("rlk,kd->rld", prob_low, value_head, preferred_element_type=f32)
            return (mixed_head, row_peak[..., 0] + jnp.log(denominator[..., 0]))

        return lax.map(forward_head, (query_seq, key_seq, value_seq))

    mixed_heads, log_totals = lax.map(
        forward_sequence, (grouped_queries, grouped_keys, grouped_values, allowed)
    )
    attended = (
        mixed_heads.transpose(0, 3, 1, 2, 4)
        .reshape(every_row_set, QUERY_HEADS * HEAD_SIZE)
        .astype(brain_float_half)
    )
    middle = inputs + jnp.dot(attended, full_out, preferred_element_type=f32)
    normed_mlp = row_norm_apply(middle, gain_mlp).astype(brain_float_half)
    gate_value = jnp.dot(normed_mlp, full_gate, preferred_element_type=f32)
    up_value = jnp.dot(normed_mlp, full_up, preferred_element_type=f32)
    hidden = (jax.nn.silu(gate_value) * up_value).astype(brain_float_half)
    output = (middle + jnp.dot(hidden, full_down, preferred_element_type=f32)).astype(
        brain_float_half
    )
    regathered = (
        lax.all_gather(w_query, ("dp", "ctx"), axis=0, tiled=True),
        lax.all_gather(key_weight, ("dp", "ctx"), axis=0, tiled=True),
        lax.all_gather(value_weight, ("dp", "ctx"), axis=0, tiled=True),
        lax.all_gather(w_out, ("dp", "ctx"), axis=0, tiled=True),
        lax.all_gather(w_gate, ("dp", "ctx"), axis=0, tiled=True),
        lax.all_gather(w_up, ("dp", "ctx"), axis=0, tiled=True),
        lax.all_gather(w_down, ("dp", "ctx"), axis=0, tiled=True),
        lax.all_gather(gains, ("dp", "ctx"), axis=0, tiled=True),
    )
    back_query, back_key, back_value, back_out, back_gate, back_up, back_down, back_gains = (
        regathered
    )
    gain_attn, gain_mlp, gain_query, key_norm_gain = split_gains(back_gains)
    d_hidden = jnp.einsum("ld,fd->lf", cot_rows, back_down, preferred_element_type=f32)
    grad_down = jnp.einsum("lf,ld->fd", hidden, cot_rows, preferred_element_type=f32)
    unused, swiglu_pull = jax.vjp(
        lambda gate_in, up_in: jax.nn.silu(gate_in) * up_in, gate_value, up_value
    )
    d_gate, d_up = swiglu_pull(d_hidden)
    d_gate = d_gate.astype(brain_float_half)
    d_up = d_up.astype(brain_float_half)
    grad_gate = jnp.einsum("ld,lf->df", normed_mlp, d_gate, preferred_element_type=f32)
    grad_up = jnp.einsum("ld,lf->df", normed_mlp, d_up, preferred_element_type=f32)
    d_normed = jnp.einsum("lf,df->ld", d_gate, back_gate, preferred_element_type=f32)
    d_normed = d_normed + jnp.einsum("lf,df->ld", d_up, back_up, preferred_element_type=f32)
    unused, norm_pull = jax.vjp(row_norm_apply, middle, gain_mlp)
    d_middle, d_gain_mlp = norm_pull(d_normed)
    d_middle = d_middle + cot_rows.astype(f32)
    d_branch = d_middle.astype(brain_float_half)
    grad_out = jnp.einsum("lh,ld->hd", attended, d_branch, preferred_element_type=f32)
    attended_gradient = jnp.einsum(
        "ld,hd->lh", d_branch, back_out, preferred_element_type=f32
    ).astype(brain_float_half)
    group_gradient = attended_gradient.reshape(
        sequence_count, device_local_rows, KEY_VALUE_HEADS, head_groups, HEAD_SIZE
    ).transpose(0, 2, 3, 1, 4)

    def backward_sequence(slices):
        query_seq, key_seq, value_seq, d_seq, log_seq, mask_rows = slices

        def backward_head(head_slices):
            query_head, key_head, value_head, d_head, log_total = head_slices
            scores = masked_scores(query_head, key_head, mask_rows)
            probs_full = jnp.exp(scores - log_total[..., None])
            prob_low = probs_full.astype(brain_float_half)
            d_value = jnp.einsum("rlk,rld->kd", prob_low, d_head, preferred_element_type=f32)
            d_probs = jnp.einsum("rld,kd->rlk", d_head, value_head, preferred_element_type=f32)
            d_scores = probs_full * (
                d_probs - jnp.sum(probs_full * d_probs, axis=-1, keepdims=True)
            )
            d_scores = d_scores.astype(brain_float_half)
            d_query = (
                jnp.einsum("rlk,kd->rld", d_scores, key_head, preferred_element_type=f32)
                * score_scale
            )
            d_key = (
                jnp.einsum("rlk,rld->kd", d_scores, query_head, preferred_element_type=f32)
                * score_scale
            )
            return (d_query, d_key, d_value)

        return lax.map(backward_head, (query_seq, key_seq, value_seq, d_seq, log_seq))

    d_queries, key_rows_gradient, value_rows_gradient = lax.map(
        backward_sequence,
        (grouped_queries, grouped_keys, grouped_values, group_gradient, log_totals, allowed),
    )
    gathered_key_gradient = key_rows_gradient.transpose(2, 0, 1, 3).reshape(
        overall_rows, sequence_count, KEY_VALUE_HEADS * HEAD_SIZE
    )
    gathered_value_gradient = value_rows_gradient.transpose(2, 0, 1, 3).reshape(
        overall_rows, sequence_count, KEY_VALUE_HEADS * HEAD_SIZE
    )
    local_key_gradient, local_value_gradient = (
        lax.psum_scatter(
            gathered_key_gradient.astype(jnp.bfloat16), "ctx", scatter_dimension=0, tiled=True
        ).astype(jnp.float32),
        lax.psum_scatter(
            gathered_value_gradient.astype(jnp.bfloat16), "ctx", scatter_dimension=0, tiled=True
        ).astype(jnp.float32),
    )
    local_key_gradient = local_key_gradient.transpose(1, 0, 2)
    local_value_gradient = local_value_gradient.transpose(1, 0, 2)
    d_query_heads = d_queries.transpose(0, 3, 1, 2, 4).reshape(
        every_row_set, QUERY_HEADS, HEAD_SIZE
    )
    unused, query_pull = jax.vjp(
        lambda unnormalized_input, input_gain_vector: heads_per_group(
            unnormalized_input, input_gain_vector, token_positions, QUERY_HEADS
        ),
        query_raw,
        gain_query,
    )
    d_query_raw, d_gain_query = query_pull(d_query_heads)
    unused, key_pullback = jax.vjp(
        lambda unnormalized_input, input_gain_vector: heads_per_group(
            unnormalized_input, input_gain_vector, token_positions, KEY_VALUE_HEADS
        ),
        unrotated_keys,
        key_norm_gain,
    )
    unrotated_key_gradient, key_gain_gradient = key_pullback(
        local_key_gradient.reshape(every_row_set, KEY_VALUE_HEADS, HEAD_SIZE)
    )
    d_query_low = d_query_raw.astype(brain_float_half)
    d_key_low = unrotated_key_gradient.astype(brain_float_half)
    reduced_value_gradient = local_value_gradient.reshape(
        every_row_set, KEY_VALUE_HEADS * HEAD_SIZE
    ).astype(brain_float_half)
    grad_query = jnp.einsum("ld,lh->dh", normalized_input, d_query_low, preferred_element_type=f32)
    grad_key = jnp.einsum("ld,lh->dh", normalized_input, d_key_low, preferred_element_type=f32)
    grad_value = jnp.einsum(
        "ld,lh->dh", normalized_input, reduced_value_gradient, preferred_element_type=f32
    )
    d_normed_attn = jnp.einsum("lh,dh->ld", d_query_low, back_query, preferred_element_type=f32)
    d_normed_attn = d_normed_attn + jnp.einsum(
        "lh,dh->ld", d_key_low, back_key, preferred_element_type=f32
    )
    d_normed_attn = d_normed_attn + jnp.einsum(
        "lh,dh->ld", reduced_value_gradient, back_value, preferred_element_type=f32
    )
    unused, first_pull = jax.vjp(row_norm_apply, inputs, gain_attn)
    d_inputs, d_gain_attn = first_pull(d_normed_attn)
    grad_tokens = (d_middle + d_inputs).reshape(sequence_count, device_local_rows, MODEL_WIDTH)
    grad_gains = jnp.concatenate([d_gain_attn, d_gain_mlp, d_gain_query, key_gain_gradient])
    summed = (
        lax.psum_scatter(
            owner_major(grad_query, owners), ("dp", "ctx"), scatter_dimension=0, tiled=True
        ),
        lax.psum_scatter(
            owner_major(grad_key, owners), ("dp", "ctx"), scatter_dimension=0, tiled=True
        ),
        lax.psum_scatter(
            owner_major(grad_value, owners), ("dp", "ctx"), scatter_dimension=0, tiled=True
        ),
        lax.psum_scatter(
            owner_major(grad_out, owners), ("dp", "ctx"), scatter_dimension=0, tiled=True
        ),
        lax.psum_scatter(
            owner_major(grad_gate, owners), ("dp", "ctx"), scatter_dimension=0, tiled=True
        ),
        lax.psum_scatter(
            owner_major(grad_up, owners), ("dp", "ctx"), scatter_dimension=0, tiled=True
        ),
        lax.psum_scatter(
            owner_major(grad_down, owners), ("dp", "ctx"), scatter_dimension=0, tiled=True
        ),
        lax.psum_scatter(
            owner_major(grad_gains, owners), ("dp", "ctx"), scatter_dimension=0, tiled=True
        ),
    )
    grad_query = summed[0].reshape(shard_shapes[0])
    grad_key = summed[1].reshape(shard_shapes[1])
    grad_value = summed[2].reshape(shard_shapes[2])
    grad_out = summed[3].reshape(shard_shapes[3])
    grad_gate = summed[4].reshape(shard_shapes[4])
    grad_up = summed[5].reshape(shard_shapes[5])
    grad_down = summed[6].reshape(shard_shapes[6])
    grad_gains = summed[7].reshape(shard_shapes[7])
    return (
        output.reshape(sequence_count, device_local_rows, MODEL_WIDTH),
        grad_tokens,
        grad_query,
        grad_key,
        grad_value,
        grad_out,
        grad_gate,
        grad_up,
        grad_down,
        grad_gains,
    )

FEATURES = 128
MASK_DEPTH = -4096.0
LOG2_E = 1.4426950408889634
VMEM_BYTES = 56 * 1024 * 1024
bf16 = jnp.bfloat16
f32 = jnp.float32


def xor_permute(value, axis, offset):
    size = lax.axis_size(axis)
    return lax.ppermute(value, axis, [(i, i ^ offset) for i in range(size)])


def pick(stacked, index):
    return lax.dynamic_index_in_dim(stacked, index, 0, keepdims=False)


def exchange(stacked, me):
    size = stacked.shape[0]
    relative = [pick(stacked, me)]
    for offset in range(1, size):
        relative.append(xor_permute(pick(stacked, me ^ offset), "ctx", offset))
    arrived = relative[1:]
    relative = jnp.stack(relative)
    return jnp.stack([pick(relative, me ^ source) for source in range(size)]), arrived


def shift_z(value, offset):
    size = lax.axis_size("dp")
    return lax.ppermute(value, "dp", [(i, (i + 2 * offset) % size) for i in range(size)])


def assemble_kernel(splits, count, places_ref, *refs):
    pieces, results, sems = refs[:count], refs[count:-1], refs[-1]
    copies = []
    for piece in pieces:
        for slot in range(piece.shape[0]):
            n = len(copies) // len(splits)
            start = 0
            for m, rows in enumerate(splits):
                copy = pltpu.make_async_copy(
                    piece.at[slot, pl.ds(start, rows)],
                    results[m].at[places_ref[n]],
                    sems.at[n, m],
                )
                copy.start()
                copies.append(copy)
                start += rows
    for copy in copies:
        copy.wait()


def assemble(pieces, places, splits=None):
    slots = sum(piece.shape[0] for piece in pieces)
    rows, columns = pieces[0].shape[1:]
    splits = (rows,) if splits is None else splits
    anywhere = pl.BlockSpec(memory_space=pl.ANY)
    return pl.pallas_call(
        functools.partial(assemble_kernel, splits, len(pieces)),
        in_specs=[pl.BlockSpec(memory_space=pltpu.SMEM)]
        + [pl.BlockSpec(memory_space=pltpu.VMEM)] * len(pieces),
        out_specs=[anywhere] * len(splits),
        out_shape=[jax.ShapeDtypeStruct((slots, n, columns), pieces[0].dtype) for n in splits],
        scratch_shapes=[pltpu.SemaphoreType.DMA((slots, len(splits)))],
        compiler_params=pltpu.CompilerParams(vmem_limit_bytes=VMEM_BYTES),
        cost_estimate=pl.CostEstimate(
            flops=0, bytes_accessed=4 * slots * rows * columns, transcendentals=0
        ),
        name="assemble",
    )(places.astype(jnp.int32), *pieces)


def gather_along(value):
    return [value] + [shift_z(value, k) for k in range(1, lax.axis_size("dp") // 2)]


def gather_beside(along, *waits):
    depth = len(along)
    z = lax.axis_index("dp") // 2
    places = jnp.stack([(z - k) % depth for k in range(depth)])
    stack = assemble([piece[None] for piece in along], places)[0]
    stack = after(stack, *waits)
    return [stack, xor_permute(stack, "dp", 1)]


def interleave(stacks, splits):
    depth = stacks[0].shape[0]
    y = lax.axis_index("dp") % 2
    rows = 2 * jnp.arange(depth)
    results = assemble(stacks, jnp.concatenate([rows + y, rows + 1 - y]), splits)
    return [result.reshape(-1, result.shape[-1]) for result in results]


def send_beside(grad):
    depth = grad.shape[0] // 2
    y = lax.axis_index("dp") % 2
    grad = grad.reshape((depth, 2) + grad.shape[1:])
    away = lax.dynamic_index_in_dim(grad, 1 - y, 1, keepdims=False)
    kept = lax.dynamic_index_in_dim(grad, y, 1, keepdims=False)
    return kept, away, xor_permute(away, "dp", 1)


def add_beside(kept, away, arrived):
    return (kept.astype(f32) + arrived.astype(f32)).astype(bf16)


def reduce_along(pair):
    depth = pair.shape[0]
    z = lax.axis_index("dp") // 2
    sent = [shift_z(pick(pair, (z + k) % depth), k) for k in range(1, depth)]
    return [pick(pair, z)] + sent


def add_all(terms):
    total = terms[0].astype(f32)
    for term in terms[1:]:
        total = total + term.astype(f32)
    return total.astype(bf16)


def after(value, *others):
    return lax.optimization_barrier((value, *others))[0]


def after_all(values, *others):
    return lax.optimization_barrier((*values, *others))[: len(values)]


def gather_blocks(value):
    across = xor_permute(value, "ctx", 2)
    beside = xor_permute(value, "ctx", 1)
    corner = xor_permute(across, "ctx", 1)
    return [value, beside, across, corner]


def gather_near(value):
    return [value, xor_permute(value, "ctx", 1)], xor_permute(value, "ctx", 2)


def gather_far(across, *waits):
    across = after(across, *waits)
    return [across, xor_permute(across, "ctx", 1)]


def send_across(part_corner, part_across, *waits):
    corner = xor_permute(part_corner.astype(bf16), "ctx", 1)
    toward = (part_across.astype(f32) + corner.astype(f32)).astype(bf16)
    toward = after(toward, *waits) if waits else toward
    return toward, xor_permute(toward, "ctx", 2)


def sum_own(part_beside, part_own, across):
    beside = xor_permute(part_beside.astype(bf16), "ctx", 1)
    return part_own.astype(f32) + beside.astype(f32) + across.astype(f32)


def nt_dot(left, right):
    return lax.dot_general(left, right, (((1,), (1,)), ((), ())), preferred_element_type=f32)


def nn_dot(left, right):
    return jnp.dot(left, right, preferred_element_type=f32)


def project_kernel(
    query_heads,
    key_heads,
    per_block,
    x_refs,
    gain_ref,
    weight_ref,
    cos_ref,
    sin_ref,
    gain_q_ref,
    gain_k_ref,
    normed_ref,
    raw_ref,
    q_ref,
    k_ref,
    v_ref,
    held_ref,
):
    for r, x_ref in enumerate(x_refs):

        @pl.when(pl.program_id(0) // per_block == r)
        def _():
            held_ref[...] = x_ref[...]

    x = held_ref[...].astype(f32)
    scale = lax.rsqrt(jnp.mean(x * x, axis=-1, keepdims=True) + EPSILON)
    normed = (x * scale * gain_ref[...]).astype(bf16)
    normed_ref[...] = normed
    raw = nn_dot(normed, weight_ref[...])
    turned = (query_heads + key_heads) * HEAD_SIZE
    raw_ref[...] = raw[:, :turned]
    v_ref[...] = raw[:, turned:].astype(bf16)
    cosine = cos_ref[...]
    sine = sin_ref[...]
    for head in range(query_heads + key_heads):
        rows = raw[:, head * HEAD_SIZE : (head + 1) * HEAD_SIZE]
        gain = gain_q_ref[...] if head < query_heads else gain_k_ref[...]
        rows = rows * lax.rsqrt(jnp.mean(rows * rows, axis=-1, keepdims=True) + EPSILON) * gain
        rows = (rows * cosine + pltpu.roll(rows, HEAD_SIZE // 2, 1) * sine).astype(bf16)
        if head < query_heads:
            q_ref[:, head * HEAD_SIZE : (head + 1) * HEAD_SIZE] = rows
        else:
            at = (head - query_heads) * HEAD_SIZE
            k_ref[:, at : at + HEAD_SIZE] = rows


def project(x_blocks, gain, weight, cosine, sine, gain_q, gain_k, query_heads, key_heads):
    rows, width = x_blocks[0].shape
    block = 256
    per_block = rows // block
    rows = rows * len(x_blocks)
    turned = (query_heads + key_heads) * HEAD_SIZE
    columns = weight.shape[1]

    def tall(n):
        return pl.BlockSpec((block, n), lambda i: (i, 0))

    def whole(shape):
        return pl.BlockSpec(shape, lambda i: (0, 0))

    def part(r):
        return pl.BlockSpec(
            (block, width), lambda i: (jnp.clip(i - r * per_block, 0, per_block - 1), 0)
        )

    return pl.pallas_call(
        functools.partial(project_kernel, query_heads, key_heads, per_block),
        grid=(rows // block,),
        in_specs=[
            [part(r) for r in range(len(x_blocks))],
            whole((1, width)),
            whole(weight.shape),
            tall(HEAD_SIZE),
            tall(HEAD_SIZE),
            whole((1, HEAD_SIZE)),
            whole((1, HEAD_SIZE)),
        ],
        out_specs=[
            tall(width),
            tall(turned),
            tall(query_heads * HEAD_SIZE),
            tall(key_heads * HEAD_SIZE),
            tall(key_heads * HEAD_SIZE),
        ],
        out_shape=[
            jax.ShapeDtypeStruct((rows, width), bf16),
            jax.ShapeDtypeStruct((rows, turned), f32),
            jax.ShapeDtypeStruct((rows, query_heads * HEAD_SIZE), bf16),
            jax.ShapeDtypeStruct((rows, key_heads * HEAD_SIZE), bf16),
            jax.ShapeDtypeStruct((rows, key_heads * HEAD_SIZE), bf16),
        ],
        scratch_shapes=[pltpu.VMEM((block, width), bf16)],
        compiler_params=pltpu.CompilerParams(vmem_limit_bytes=VMEM_BYTES),
        cost_estimate=pl.CostEstimate(
            flops=2 * rows * width * columns,
            bytes_accessed=rows * (4 * width + 4 * turned + 2 * columns) + 2 * width * columns,
            transcendentals=0,
        ),
        name="project",
    )(list(x_blocks), gain, weight, cosine, sine, gain_q, gain_k)


def unproject_kernel(
    query_heads,
    key_heads,
    half,
    dq_near_ref,
    dq_far_ref,
    dk_ref,
    dv_ref,
    raw_ref,
    cos_ref,
    sin_ref,
    gain_q_ref,
    gain_k_ref,
    low_ref,
    dgain_ref,
):
    @pl.when(pl.program_id(0) == 0)
    def _():
        dgain_ref[...] = jnp.zeros_like(dgain_ref)

    cosine = cos_ref[...]
    sine = sin_ref[...]
    total_q = jnp.zeros((1, HEAD_SIZE), f32)
    total_k = jnp.zeros((1, HEAD_SIZE), f32)
    for head in range(query_heads + key_heads):
        at = head * HEAD_SIZE
        raw = raw_ref[:, at : at + HEAD_SIZE]
        if head < query_heads:
            lanes = slice(at, at + HEAD_SIZE)
            grad = jnp.where(pl.program_id(0) < half, dq_near_ref[:, lanes], dq_far_ref[:, lanes])
            gain = gain_q_ref[...]
        else:
            back = (head - query_heads) * HEAD_SIZE
            grad = dk_ref[:, back : back + HEAD_SIZE]
            gain = gain_k_ref[...]
        grad = grad * cosine - pltpu.roll(grad, HEAD_SIZE // 2, 1) * sine
        scale = lax.rsqrt(jnp.mean(raw * raw, axis=-1, keepdims=True) + EPSILON)
        unit = raw * scale
        summed = jnp.sum(unit * grad, axis=0, keepdims=True)
        if head < query_heads:
            total_q += summed
        else:
            total_k += summed
        grad = grad * gain
        mean = jnp.mean(unit * grad, axis=-1, keepdims=True)
        low_ref[:, at : at + HEAD_SIZE] = (scale * (grad - unit * mean)).astype(bf16)
    low_ref[:, (query_heads + key_heads) * HEAD_SIZE :] = dv_ref[...].astype(bf16)
    dgain_ref[0:1, :] += total_q
    dgain_ref[1:2, :] += total_k


def unproject(dq_near, dq_far, dk, dv, raw, cosine, sine, gain_q, gain_k, query_heads, key_heads):
    rows = dk.shape[0]
    block = 256
    half = rows // block // 2
    columns = (query_heads + 2 * key_heads) * HEAD_SIZE

    def tall(n):
        return pl.BlockSpec((block, n), lambda i: (i, 0))

    def whole(shape):
        return pl.BlockSpec(shape, lambda i: (0, 0))

    return pl.pallas_call(
        functools.partial(unproject_kernel, query_heads, key_heads, half),
        grid=(rows // block,),
        in_specs=[
            pl.BlockSpec((block, dq_near.shape[1]), lambda i: (jnp.minimum(i, half - 1), 0)),
            pl.BlockSpec((block, dq_far.shape[1]), lambda i: (jnp.maximum(i - half, 0), 0)),
            tall(dk.shape[1]),
            tall(dv.shape[1]),
            tall(raw.shape[1]),
            tall(HEAD_SIZE),
            tall(HEAD_SIZE),
            whole((1, HEAD_SIZE)),
            whole((1, HEAD_SIZE)),
        ],
        out_specs=[tall(columns), whole((8, HEAD_SIZE))],
        out_shape=[
            jax.ShapeDtypeStruct((rows, columns), bf16),
            jax.ShapeDtypeStruct((8, HEAD_SIZE), f32),
        ],
        compiler_params=pltpu.CompilerParams(vmem_limit_bytes=VMEM_BYTES),
        cost_estimate=pl.CostEstimate(
            flops=20 * rows * columns, bytes_accessed=20 * rows * columns, transcendentals=0
        ),
        name="unproject",
    )(dq_near, dq_far, dk, dv, raw, cosine, sine, gain_q, gain_k)


def attend_kernel(
    group, block, first, me_ref, q_ref, qf_ref, k_ref, kf_ref, v_ref, o_ref, log_ref, total_ref
):
    me = me_ref[0]
    at_query = (pl.program_id(1) + first) ^ me
    factor = HEAD_SIZE ** (-0.5) * LOG2_E
    query_features = qf_ref[...]
    ones = jnp.ones((block, HEAD_SIZE), bf16)
    total_ref[...] = jnp.zeros_like(total_ref)

    def step(at_key, diagonal):
        rows = pl.ds(pl.multiple_of((at_key ^ me) * block, block), block)
        keys = jnp.concatenate([k_ref[rows, :], kf_ref[rows, :]], axis=1)
        values = jnp.concatenate([v_ref[rows, :], ones], axis=1)
        for head in range(group):
            query = q_ref[:, head * HEAD_SIZE : (head + 1) * HEAD_SIZE]
            scores = nt_dot(jnp.concatenate([query, query_features], axis=1), keys)
            probs = jnp.exp2(scores * factor)
            if diagonal:
                down = lax.broadcasted_iota(jnp.int32, probs.shape, 0)
                right = lax.broadcasted_iota(jnp.int32, probs.shape, 1)
                probs = jnp.where(down >= right, probs, 0.0)
            total_ref[head] += nn_dot(probs.astype(bf16), values)

    @pl.loop(0, at_query)
    def _(at_key):
        step(at_key, False)

    step(at_query, True)
    for head in range(group):
        weighted = total_ref[head, :, :HEAD_SIZE]
        summed = total_ref[head, :, HEAD_SIZE:]
        o_ref[:, head * HEAD_SIZE : (head + 1) * HEAD_SIZE] = (weighted / summed).astype(bf16)
        log_ref[0, head : head + 1, :] = jnp.log2(summed.T[0:1, :])


def attend(me, q, qf, k, kf, v, block, group, first, count):
    rows = k.shape[0]
    key_heads = k.shape[1] // HEAD_SIZE
    pairs = key_heads * group * count * block * rows * 5 // 8
    return pl.pallas_call(
        functools.partial(attend_kernel, group, block, first),
        grid_spec=pltpu.PrefetchScalarGridSpec(
            num_scalar_prefetch=1,
            grid=(key_heads, count),
            in_specs=[
                pl.BlockSpec((block, group * HEAD_SIZE), lambda g, i, me: (i + first, g)),
                pl.BlockSpec((block, FEATURES), lambda g, i, me: (i + first, 0)),
                pl.BlockSpec((rows, HEAD_SIZE), lambda g, i, me: (0, g)),
                pl.BlockSpec((rows, FEATURES), lambda g, i, me: (0, 0)),
                pl.BlockSpec((rows, HEAD_SIZE), lambda g, i, me: (0, g)),
            ],
            out_specs=[
                pl.BlockSpec((block, group * HEAD_SIZE), lambda g, i, me: (i, g)),
                pl.BlockSpec((1, group, block), lambda g, i, me: (g, 0, i)),
            ],
            scratch_shapes=[pltpu.VMEM((group, block, 2 * HEAD_SIZE), f32)],
        ),
        out_shape=[
            jax.ShapeDtypeStruct((count * block, q.shape[1]), bf16),
            jax.ShapeDtypeStruct((key_heads, group, count * block), f32),
        ],
        compiler_params=pltpu.CompilerParams(vmem_limit_bytes=VMEM_BYTES),
        cost_estimate=pl.CostEstimate(
            flops=8 * pairs * HEAD_SIZE, bytes_accessed=10 * q.size, transcendentals=pairs
        ),
        name="attend",
    )(me, q, qf, k, kf, v)


def unattend_kernel(
    group,
    block,
    first,
    resumed,
    me_ref,
    q_ref,
    qf_ref,
    k_ref,
    kf_ref,
    v_ref,
    o_ref,
    branch_first_ref,
    branch_second_ref,
    out_ref,
    log_ref,
    *rest,
):
    if resumed:
        dk_in_ref, dv_in_ref, d_weight_in_ref, *rest = rest
    dq_ref, dk_ref, dv_ref, d_weight_ref, flipped_ref, total_ref, do_ref = rest
    me = me_ref[0]
    at_query = (pl.program_id(1) + first) ^ me
    scale = HEAD_SIZE ** (-0.5)
    factor = scale * LOG2_E

    @pl.when(pl.program_id(1) == 0)
    def _():
        dk_ref[...] = dk_in_ref[...] if resumed else jnp.zeros_like(dk_ref)
        dv_ref[...] = dv_in_ref[...] if resumed else jnp.zeros_like(dv_ref)
        d_weight_ref[...] = d_weight_in_ref[...] if resumed else jnp.zeros_like(d_weight_ref)
        flipped_ref[...] = k_ref[...].astype(f32).T.astype(bf16)

    def take(branch_ref):
        do_ref[...] = nt_dot(branch_ref[...], out_ref[...]).astype(bf16)
        turned = o_ref[...].astype(f32).T.astype(bf16)
        d_weight_ref[...] += nn_dot(turned, branch_ref[...])

    @pl.when(pl.program_id(1) == 0)
    def _():
        take(branch_first_ref)

    @pl.when(pl.program_id(1) == 1)
    def _():
        take(branch_second_ref)

    total_ref[...] = jnp.zeros_like(total_ref)
    query_features = qf_ref[...]
    deltas = []
    for head in range(group):
        lanes = slice(head * HEAD_SIZE, (head + 1) * HEAD_SIZE)
        product = do_ref[:, lanes].astype(f32) * o_ref[:, lanes].astype(f32)
        deltas.append(jnp.sum(product.T, axis=0, keepdims=True))

    def step(at_key, diagonal):
        start = pl.multiple_of((at_key ^ me) * block, block)
        rows = pl.ds(start, block)
        keys = jnp.concatenate([k_ref[rows, :], kf_ref[rows, :]], axis=1)
        values = v_ref[rows, :]
        for head in range(group):
            lanes = slice(head * HEAD_SIZE, (head + 1) * HEAD_SIZE)
            query = q_ref[:, lanes]
            d_out = do_ref[:, lanes]
            scores = nt_dot(keys, jnp.concatenate([query, query_features], axis=1))
            probs = jnp.exp2(scores * factor - log_ref[0, head : head + 1, :])
            if diagonal:
                key_at = lax.broadcasted_iota(jnp.int32, probs.shape, 0)
                query_at = lax.broadcasted_iota(jnp.int32, probs.shape, 1)
                probs = jnp.where(query_at >= key_at, probs, 0.0)
            d_scores = (probs * (nt_dot(values, d_out) - deltas[head])).astype(bf16)
            dv_ref[rows, :] += nn_dot(probs.astype(bf16), d_out)
            dk_ref[rows, :] += nn_dot(d_scores, query)
            total_ref[head] += nn_dot(flipped_ref[:, rows], d_scores)

    @pl.loop(0, at_query)
    def _(at_key):
        step(at_key, False)

    step(at_query, True)
    for head in range(group):
        dq_ref[:, head * HEAD_SIZE : (head + 1) * HEAD_SIZE] = total_ref[head].T * scale

    if resumed:

        @pl.when(pl.program_id(1) == pl.num_programs(1) - 1)
        def _():
            dk_ref[...] = dk_ref[...] * scale


def unattend(me, q, qf, k, kf, v, o, branches, out, logs, block, group, first, earlier=()):
    count = len(branches)
    rows = k.shape[0]
    key_heads = k.shape[1] // HEAD_SIZE
    width = out.shape[1]
    lanes = group * HEAD_SIZE

    def by_query(n):
        return pl.BlockSpec((block, n), lambda g, i, me: (i, g))

    by_key = pl.BlockSpec((rows, HEAD_SIZE), lambda g, i, me: (0, g))
    by_head = pl.BlockSpec((lanes, width), lambda g, i, me: (g, 0))
    whole = pl.BlockSpec((block, width), lambda g, i, me: (0, 0))
    return pl.pallas_call(
        functools.partial(unattend_kernel, group, block, first, bool(earlier)),
        grid_spec=pltpu.PrefetchScalarGridSpec(
            num_scalar_prefetch=1,
            grid=(key_heads, count),
            in_specs=[
                pl.BlockSpec((block, lanes), lambda g, i, me: (i + first, g)),
                pl.BlockSpec((block, FEATURES), lambda g, i, me: (i + first, 0)),
                by_key,
                pl.BlockSpec((rows, FEATURES), lambda g, i, me: (0, 0)),
                by_key,
                by_query(lanes),
                whole,
                whole,
                by_head,
                pl.BlockSpec((1, group, block), lambda g, i, me: (g, 0, i)),
            ]
            + ([by_key, by_key, by_head] if earlier else []),
            out_specs=[by_query(lanes), by_key, by_key, by_head],
            scratch_shapes=[
                pltpu.VMEM((HEAD_SIZE, rows), bf16),
                pltpu.VMEM((group, HEAD_SIZE, block), f32),
                pltpu.VMEM((block, lanes), bf16),
            ],
        ),
        out_shape=[
            jax.ShapeDtypeStruct((count * block, q.shape[1]), f32),
            jax.ShapeDtypeStruct(k.shape, f32),
            jax.ShapeDtypeStruct(v.shape, f32),
            jax.ShapeDtypeStruct(out.shape, f32),
        ],
        compiler_params=pltpu.CompilerParams(vmem_limit_bytes=VMEM_BYTES),
        cost_estimate=pl.CostEstimate(
            flops=(70 if earlier else 7) * count * block * rows * key_heads * group * HEAD_SIZE // 8,
            bytes_accessed=(20 if earlier else 2) * q.size,
            transcendentals=0,
        ),
        name="unattend",
    )(me, q, qf, k, kf, v, o, *branches, out, logs, *earlier)


def feed_kernel(
    units,
    half,
    first_ref,
    second_ref,
    cot_first_ref,
    cot_second_ref,
    both_ref,
    down_ref,
    h_ref,
    cot_ref,
    hidden_ref,
    d_both_ref,
    part_first_ref,
    part_second_ref,
    d_part_first_ref,
    d_part_second_ref,
):
    in_first = pl.program_id(0) < half

    @pl.when(in_first)
    def _():
        h_ref[...] = first_ref[...]
        cot_ref[...] = cot_first_ref[...]

    @pl.when(jnp.logical_not(in_first))
    def _():
        h_ref[...] = second_ref[...]
        cot_ref[...] = cot_second_ref[...]

    both = nn_dot(h_ref[...], both_ref[...])
    d_hidden = nt_dot(cot_ref[...], down_ref[...])
    gate, up = both[:, :units], both[:, units:]
    sigmoid = 1.0 / (1.0 + jnp.exp(-gate))
    silu = gate * sigmoid
    hidden = (silu * up).astype(bf16)
    hidden_ref[...] = hidden
    part = nn_dot(hidden, down_ref[...]).astype(bf16)
    d_gate = (d_hidden * up * sigmoid * (1.0 + gate * (1.0 - sigmoid))).astype(bf16)
    d_up = (d_hidden * silu).astype(bf16)
    d_both = jnp.concatenate([d_gate, d_up], axis=1)
    d_both_ref[...] = d_both
    d_part = nt_dot(d_both, both_ref[...]).astype(bf16)

    @pl.when(in_first)
    def _():
        part_first_ref[...] = part
        d_part_first_ref[...] = d_part

    @pl.when(jnp.logical_not(in_first))
    def _():
        part_second_ref[...] = part
        d_part_second_ref[...] = d_part


def feed(h_first, h_second, cot_first, cot_second, both, down):
    rows, width = 2 * cot_first.shape[0], cot_first.shape[1]
    units = down.shape[0]
    block = 256
    half = rows // block // 2

    def tall(n):
        return pl.BlockSpec((block, n), lambda i: (i, 0))

    def whole(shape):
        return pl.BlockSpec(shape, lambda i: (0, 0))

    of_first = pl.BlockSpec((block, width), lambda i: (jnp.minimum(i, half - 1), 0))
    of_second = pl.BlockSpec((block, width), lambda i: (jnp.maximum(i - half, 0), 0))
    shapes = [(rows, width), (rows, width), (rows, units), (rows, 2 * units)] + [(rows // 2, width)] * 4
    return pl.pallas_call(
        functools.partial(feed_kernel, units, half),
        grid=(rows // block,),
        in_specs=[of_first, of_second] * 2 + [whole(both.shape), whole(down.shape)],
        out_specs=[tall(width), tall(width), tall(units), tall(2 * units)] + [of_first, of_second] * 2,
        out_shape=[jax.ShapeDtypeStruct(shape, bf16) for shape in shapes],
        compiler_params=pltpu.CompilerParams(vmem_limit_bytes=VMEM_BYTES),
        cost_estimate=pl.CostEstimate(
            flops=12 * rows * width * units,
            bytes_accessed=rows * (10 * width + 6 * units) + 6 * width * units,
            transcendentals=rows * units,
        ),
        name="feed",
    )(h_first, h_second, cot_first, cot_second, both, down)


def norm_back(value_rows, gain_vec, grad):
    scale = lax.rsqrt(jnp.mean(value_rows * value_rows, axis=-1, keepdims=True) + EPSILON)
    unit = value_rows * scale
    d_gain = jnp.sum(unit * grad, axis=0)
    grad = grad * gain_vec
    return scale * (grad - unit * jnp.mean(unit * grad, axis=-1, keepdims=True)), d_gain


def split_local(
    tokens,
    w_query,
    key_weight,
    value_weight,
    w_out,
    w_gate,
    w_up,
    w_down,
    gains,
    segment_ids,
    positions,
    cotangent,
):
    size = lax.axis_size("ctx")
    copies = lax.axis_size("dp")
    me = lax.axis_index("ctx")
    me_row = me.reshape(1).astype(jnp.int32)
    block = tokens.shape[1]
    group = QUERY_HEADS // KEY_VALUE_HEADS
    query_heads = QUERY_HEADS // size
    key_heads = KEY_VALUE_HEADS // size
    q_cols = query_heads * HEAD_SIZE
    k_cols = key_heads * HEAD_SIZE
    owned = w_query.shape[0]
    hidden_cols = w_gate.shape[1] // size
    gain_count = gains.shape[0]
    pad_rows = 16
    forward_owner = [
        (b, (b % copies) * size + b // copies) for b in range(size * copies)
    ]
    backward_owner = [(target, source) for source, target in forward_owner]

    def by_columns(weight):
        return weight.reshape(weight.shape[0], size, -1).transpose(1, 0, 2)

    first = jnp.concatenate(
        [by_columns(w_query), by_columns(key_weight), by_columns(value_weight)], axis=2
    )
    gain_rows = jnp.pad(gains[None], ((0, pad_rows - 1), (0, first.shape[2] - gain_count)))
    first = jnp.concatenate(
        [first, jnp.broadcast_to(gain_rows[None], (size,) + gain_rows.shape)], axis=1
    )
    first, arrived = exchange(first, me)
    gain_rows = jnp.concatenate(
        [first[:, owned], jnp.zeros((pad_rows - size, first.shape[2]), bf16)]
    )
    first = jnp.concatenate(
        [first[:, :owned].reshape(size * owned, first.shape[2]), gain_rows]
    )
    first_along = gather_along(first)
    first_stacks = gather_beside(first_along)

    gate_up = jnp.concatenate([by_columns(w_gate), by_columns(w_up)], axis=2)
    gate_up, arrived = exchange(after(gate_up, *arrived), me)
    moved = after(jnp.concatenate([w_out, w_down]), *arrived)
    moved = lax.ppermute(moved, ("dp", "ctx"), forward_owner)
    places = jnp.concatenate([positions, segment_ids]).astype(jnp.int32)
    places = jnp.concatenate(gather_blocks(after(places, *arrived)), axis=1)
    x_own = tokens.reshape(block, MODEL_WIDTH)
    x_near, across = gather_near(after(x_own, *arrived))
    x_blocks = x_near + gather_far(across, first_stacks[0])

    moved_along = gather_along(after(moved, first_stacks[0], x_near[1]))
    first_stacks = [first_stacks[0], after(first_stacks[1], *moved_along[1:])]
    cot_own = cotangent.reshape(block, MODEL_WIDTH)
    cot_near, cot_across = gather_near(after(cot_own, first_stacks[1]))
    moved_stacks = gather_beside(moved_along, first_stacks[1])
    gate_up_rows = after(gate_up.reshape(size * owned, -1), *moved_along[1:])
    gate_up = lax.all_gather(gate_up_rows, "dp", axis=0, tiled=True)
    w_first, gain_rows = interleave(first_stacks, (size * owned, pad_rows))
    w_first = after(w_first, gate_up_rows)
    full_gains = gain_rows.reshape(copies, pad_rows, -1)[:, :size, :gain_count].reshape(-1)
    gain_attn, gain_mlp, gain_query, gain_key = split_gains(full_gains)

    half = HEAD_SIZE // 2
    rates = THETA ** (-2.0 * jnp.arange(half, dtype=f32) / HEAD_SIZE)
    angles = places[0].astype(f32)[:, None] * rates[None, :]
    cosine, sine = jnp.cos(angles), jnp.sin(angles)
    cosine = jnp.concatenate([cosine, cosine], axis=1)
    sine = jnp.concatenate([-sine, sine], axis=1)
    lane = jnp.arange(FEATURES, dtype=jnp.int32)[None, :]
    same = places[1][:, None] == lane
    key_features = same.astype(bf16)
    query_features = jnp.where(same, 0.0, MASK_DEPTH).astype(bf16)
    gain_q_row, gain_k_row = gain_query[None], gain_key[None]
    normed, raw, q, k, v = project(
        x_blocks, gain_attn[None], w_first, cosine, sine, gain_q_row, gain_k_row, query_heads, key_heads
    )
    def attend_half(query, first):
        return attend(
            me_row, query, query_features, k, key_features, v, block, group, first, 2
        )

    def tn_dot(left, right):
        return lax.dot_general(left, right, (((0,), (0,)), ((), ())), preferred_element_type=f32)

    def by_copy(grad):
        return grad.astype(bf16).reshape(copies, -1, grad.shape[-1])

    def halves(value):
        return value[:block], value[block:]

    cot_blocks = cot_near + gather_far(cot_across, q)
    att_far, logs_far = attend_half(q, 2)
    att_far, *both = lax.optimization_barrier((att_far, *moved_stacks, *cot_blocks))
    moved_stacks, cot_blocks = both[:2], both[2:]
    out_full, down_full = interleave(moved_stacks, (w_out.shape[0], w_down.shape[0]))
    att_across, att_corner = halves(att_far)
    part_corner, part_across = nn_dot(att_corner, out_full), nn_dot(att_across, out_full)
    toward, across = send_across(part_corner, part_across)
    att_near, logs_near = attend_half(after(q, toward), 0)
    att_near = after(att_near, gate_up)
    att_own, att_beside = halves(att_near)
    beside = [
        xor_permute(nn_dot(piece, out_full).astype(bf16), "ctx", 1)
        for piece in jnp.split(att_beside, 2)
    ]
    part_own = nn_dot(att_own, out_full) + jnp.concatenate(beside).astype(f32)
    middle = x_own.astype(f32) + part_own + across.astype(f32)
    h_blocks, across = gather_near(row_norm_apply(middle, gain_mlp).astype(bf16))
    h_near, cot_near, hidden_near, d_both_near, down_own, down_beside, d_own, d_beside = feed(
        *h_blocks, *cot_blocks[:2], gate_up, down_full
    )
    h_blocks = gather_far(across, hidden_near)
    h_far, cot_far, hidden_far, d_both_far, down_across, down_corner, d_across, d_corner = feed(
        *h_blocks, *cot_blocks[2:], gate_up, down_full
    )

    toward, across = send_across(d_corner, d_across)
    d_both_far, cot_far = lax.optimization_barrier((d_both_far, cot_far, toward))[:2]
    grad_both = (tn_dot(h_near, d_both_near) + tn_dot(h_far, d_both_far)).astype(bf16)
    both_sent = send_beside(by_copy(grad_both))
    hidden_far = after(hidden_far, both_sent[1])
    grad_down = (tn_dot(hidden_near, cot_near) + tn_dot(hidden_far, cot_far)).astype(bf16)
    d_normed = sum_own(d_beside, d_own, after(across, grad_down))
    d_middle, d_gain_mlp = norm_back(middle, gain_mlp, d_normed)
    d_middle = d_middle + cot_own.astype(f32)
    branches_near, branch_across = gather_near(d_middle.astype(bf16))

    def unattend_half(att, branches, logs, first, earlier=()):
        return unattend(
            me_row,
            q,
            query_features,
            k,
            key_features,
            v,
            att,
            branches,
            out_full,
            logs,
            block,
            group,
            first,
            earlier,
        )

    dq_near, *earlier = unattend_half(att_near, branches_near, logs_near, 0)
    pair_both = add_beside(after(both_sent[0], dq_near), *both_sent[1:])
    terms_both = reduce_along(pair_both)
    down_sent = send_beside(after(by_copy(grad_down), dq_near))
    branches_far = gather_far(branch_across, dq_near)
    dq_far, dk, dv, grad_out = unattend_half(att_far, branches_far, logs_far, 2, earlier)
    pair_out = add_beside(*send_beside(by_copy(grad_out)))
    dk, pair_down, *terms_both = lax.optimization_barrier(
        (dk, add_beside(*down_sent), *terms_both)
    )
    terms_down = reduce_along(pair_down)
    low, d_gain_heads = unproject(
        dq_near, dq_far, dk, dv, raw, cosine, sine, gain_q_row, gain_k_row, query_heads, key_heads
    )
    low, d_gain_heads, pair_out, *terms_down = lax.optimization_barrier(
        (low, d_gain_heads, pair_out, *terms_down)
    )
    grad_first = tn_dot(normed, low).astype(bf16)
    d_gain_attn = jnp.sum(w_first.astype(f32) * grad_first.astype(f32), axis=1) / gain_attn
    grad_gains = jnp.concatenate(
        [d_gain_attn, d_gain_mlp, d_gain_heads[0], d_gain_heads[1]]
    ).reshape(copies, size, gain_count)
    gain_block = jnp.pad(
        grad_gains.astype(bf16),
        ((0, 0), (0, pad_rows - size), (0, grad_first.shape[1] - gain_count)),
    )
    grad_first = jnp.concatenate(
        [grad_first.reshape(copies, size * owned, -1), gain_block], axis=1
    )
    first_sent = send_beside(grad_first)
    low = after(low, first_sent[1])
    low_own, low_beside, low_across, low_corner = (
        low[r * block : (r + 1) * block] for r in range(size)
    )
    toward, across = send_across(nt_dot(low_corner, w_first), nt_dot(low_across, w_first))
    part_beside, part_own = nt_dot(low_beside, w_first), nt_dot(low_own, w_first)
    d_normed_attn = sum_own(part_beside, part_own, across)
    d_inputs, unused = norm_back(x_own.astype(f32), gain_attn, d_normed_attn)
    grad_tokens = (d_middle + d_inputs).reshape(tokens.shape)

    terms_out = reduce_along(after(pair_out, toward))
    grad_both = add_all(after_all(terms_both, toward)).reshape(size, owned, -1)
    grad_down = add_all(after_all(terms_down, toward))
    pair_first = after(add_beside(*first_sent), *terms_out)
    unused, down_across = send_across(down_corner, down_across, pair_first)
    output = (middle + sum_own(down_beside, down_own, down_across)).astype(bf16)
    terms_first = after_all(reduce_along(pair_first), across, down_across)
    grad_first = add_all(terms_first)
    grad_out = add_all(after_all(terms_out, *terms_first))
    gain_part = grad_first[size * owned :][:size]
    gain_part = jnp.broadcast_to(gain_part[:, None], (size, pad_rows, gain_part.shape[1]))
    grad_first = jnp.concatenate(
        [grad_first[: size * owned].reshape(size, owned, -1), gain_part], axis=1
    )
    both_rows = grad_both.size // size // grad_first.shape[2]
    grad_both = grad_both.reshape(size, both_rows, -1)
    grad_first = exchange(jnp.concatenate([grad_first, grad_both], axis=1), me)[0].astype(f32)
    grad_both = grad_first[:, -both_rows:].reshape(size, owned, -1)
    grad_gains = jnp.sum(grad_first[:, owned, :gain_count], axis=0)
    grad_first = grad_first[:, :owned]

    def to_rows(pieces):
        return pieces.transpose(1, 0, 2).reshape(owned, -1)

    grad_query = to_rows(grad_first[:, :, :q_cols])
    grad_key = to_rows(grad_first[:, :, q_cols : q_cols + k_cols])
    grad_value = to_rows(grad_first[:, :, q_cols + k_cols :])
    grad_gate = to_rows(grad_both[:, :, :hidden_cols])
    grad_up = to_rows(grad_both[:, :, hidden_cols:])
    moved = jnp.concatenate([grad_out, grad_down])
    moved = lax.ppermute(moved, ("dp", "ctx"), backward_owner).astype(f32)
    grad_out, grad_down = moved[: w_out.shape[0]], moved[w_out.shape[0] :]
    return (
        output.reshape(tokens.shape),
        grad_tokens,
        grad_query,
        grad_key,
        grad_value,
        grad_out,
        grad_gate,
        grad_up,
        grad_down,
        grad_gains,
    )


def solution(mesh):
    small = mesh.shape["ctx"] == 4
    return jax.shard_map(
        split_local if small else local,
        mesh=mesh,
        in_specs=(
            P("dp", "ctx", None),
            P(("dp", "ctx"), None),
            P(("dp", "ctx"), None),
            P(("dp", "ctx"), None),
            P(("dp", "ctx"), None),
            P(("dp", "ctx"), None),
            P(("dp", "ctx"), None),
            P(("dp", "ctx"), None),
            P(("dp", "ctx")),
            P("dp", "ctx"),
            P("dp", "ctx"),
            P("dp", "ctx", None),
        ),
        out_specs=(
            P("dp", "ctx", None),
            P("dp", "ctx", None),
            P(("dp", "ctx"), None),
            P(("dp", "ctx"), None),
            P(("dp", "ctx"), None),
            P(("dp", "ctx"), None),
            P(("dp", "ctx"), None),
            P(("dp", "ctx"), None),
            P(("dp", "ctx"), None),
            P(("dp", "ctx")),
        ),
        check_vma=False,
    )
```
